128 devices in a mesh: dp: 64 (over z, x, y_lo, core), mp: 2 (over y_hi).
Axes of the slice: x: 4, y: 4 (y_hi: 2, y_lo: 2; y = y_hi * 2 + y_lo), z: 4, core: 2. Of those that a mesh axis runs over, the one named last changes fastest.
Arguments:
- tokens: bfloat16 [16384, 2048], P(('dp', 'mp')), may hold values from -6 to 6
- cotangent: bfloat16 [16384, 2048], P(('dp', 'mp')), may hold values from -6 to 6
- norm_params: float32 [4, 2048], P(None, ('dp', 'mp')), may hold values from -1.5 to 2.1
- qkv_weight: bfloat16 [3, 2048, 2048], P(None, 'dp', 'mp'), may hold values from -0.125 to 0.125
- qkv_bias: bfloat16 [3, 32, 64], P(None, 'mp', 'dp'), may hold values from -3 to 3
- out_weight: bfloat16 [2048, 2048], P('mp', 'dp'), may hold values from -0.375 to 0.375
- gate_up_weight: bfloat16 [2, 2048, 5632], P(None, 'dp', 'mp'), may hold values from -0.125 to 0.125
- down_weight: bfloat16 [5632, 2048], P('mp', 'dp'), may hold values from -0.078125 to 0.078125
Outputs:
- mixed: bfloat16 [16384, 2048], P(('dp', 'mp'))
- grad_tokens: float32 [16384, 2048], P(('dp', 'mp'))
- grad_norm: float32 [4, 2048], P(None, ('dp', 'mp'))
- grad_qkv: float32 [3, 2048, 2048], P(None, 'dp', 'mp')
- grad_qkv_bias: float32 [3, 32, 64], P(None, 'mp', 'dp')
- grad_out: float32 [2048, 2048], P('mp', 'dp')
- grad_gate_up: float32 [2, 2048, 5632], P(None, 'dp', 'mp')
- grad_down: float32 [5632, 2048], P('mp', 'dp')
The draws below stay inside these ranges and needn't reach their ends.
All inputs are finite; a program needn't handle non-finite values.
Results may differ from the reference program's by a relative error of at most 0.013.
Values may be sent and summed in bfloat16 or wider, within the bound.
A program may use at most 384 MiB of HBM per device.

```python
import jax
import jax.numpy as jnp
from jax import lax

D = 2048
HEADS = 32
FF = 5632
HEAD_DIM = 64
ROTARY = 16
TOK_GROUP = 256
TOKENS = 16384
N_DP = 64


def draw_norm_params(key, part):
    key = jax.random.fold_in(key, 7)
    key_gain, key_shift = jax.random.split(key)
    gains = jnp.exp(jax.random.uniform(key_gain, (2, D), jnp.float32, -0.7, 0.7))
    shifts = jnp.clip(0.3 * jax.random.normal(key_shift, (2, D), jnp.float32), -1.5, 1.5)
    return jnp.stack([gains[0], shifts[0], gains[1], shifts[1]]).astype(jnp.float32)


def level_of(rng, shape, cuts, low, largest):
    loudness, own = 1.0, jax.random.fold_in(rng, 6)
    for dim, shards_of in cuts:
        draws = jnp.exp(jax.random.uniform(jax.random.fold_in(own, dim), (shards_of,), jnp.float32, low / len(cuts), largest / len(cuts)))
        loudness = loudness * jnp.repeat(draws, shape[dim] // shards_of).reshape([-1 if axis == dim else 1 for axis in range(len(shape))])
    return loudness


def gaussian(own_key, dims, width, most, cuts=(), dtype=jnp.bfloat16):
    array = width * jax.random.normal(own_key, dims, jnp.float32)
    if cuts:
        array = array * level_of(own_key, dims, cuts, -0.22, 0.18)
    return jnp.clip(array, -most, most).astype(dtype)


def setup_inputs(seed: int = 0) -> dict:
    splits = jax.random.split(jax.random.key(seed), 9)
    tokens = gaussian(splits[0], (TOKENS, D), 1.0, 6.0, ((0, 128),))
    cotangent = gaussian(splits[1], (TOKENS, D), 1.0, 6.0, ((0, 128),))
    norm_params = draw_norm_params(jax.random.fold_in(splits[8], 71), 0)
    qkv_weight = gaussian(splits[3], (3, D, D), D ** -0.5, 0.125, ((1, 64), (2, 2)))
    qkv_bias = gaussian(splits[4], (3, HEADS, HEAD_DIM), 0.5, 3.0, ((1, 2), (2, 64)))
    out_weight = gaussian(splits[5], (D, D), (D // 8) ** -0.5, 0.375, ((0, 2), (1, 64)))
    gate_up_weight = gaussian(splits[6], (2, D, FF), D ** -0.5, 0.125, ((1, 64), (2, 2)))
    down_weight = gaussian(splits[7], (FF, D), FF ** -0.5, 0.078125, ((0, 2), (1, 64)))
    return {"tokens": tokens, "cotangent": cotangent, "norm_params": norm_params, "qkv_weight": qkv_weight, "qkv_bias": qkv_bias, "out_weight": out_weight, "gate_up_weight": gate_up_weight, "down_weight": down_weight}


epsilon = 1e-05
score_scale = 0.125

@jax.custom_vjp
def low(v):
    return lax.optimization_barrier(v.astype(jnp.bfloat16)).astype(jnp.float32)

@jax.custom_vjp
def low_back(v):
    return v

def low_keep(v):
    return (low(v), None)

def low_pass(kept, grad):
    return (grad,)

def back_keep(v):
    return (v, None)

def back_low(kept, grad):
    return (low(grad),)
low.defvjp(low_keep, low_pass)
low_back.defvjp(back_keep, back_low)

def normalize(values, gain, shift):
    row_mean = lax.optimization_barrier(jnp.mean(values, -1, keepdims=True))
    centered = values - row_mean
    variance = lax.optimization_barrier(jnp.mean(centered * centered, -1, keepdims=True))
    return centered * lax.rsqrt(variance + epsilon) * gain + shift

def rotary_tables(length):
    position = jnp.arange(length).astype(jnp.float32)
    frequency = jnp.power(10000.0, -jnp.arange(ROTARY // 2).astype(jnp.float32) * (2.0 / ROTARY))
    angles = position[:, None] * frequency[None, :]
    return (jnp.cos(angles)[:, None, :], jnp.sin(angles)[:, None, :])

def rotate(values, cosine, sine_table):
    half_rot = ROTARY // 2
    lower_part = values[..., :half_rot]
    upper_part = values[..., half_rot:ROTARY]
    return jnp.concatenate([lower_part * cosine - upper_part * sine_table, upper_part * cosine + lower_part * sine_table, values[..., ROTARY:]], -1)

def layer(inputs, norm_table, qkv_full, qkv_shift, out_full, gate_up_full, down_full):
    length = inputs.shape[0]
    highest = lax.Precision.HIGHEST
    normed_one = low(normalize(inputs, norm_table[0], norm_table[1]))
    projected = jnp.einsum('sd,tde->tse', normed_one, qkv_full, precision=highest) + qkv_shift.reshape(3, 1, D)
    projected = low_back(projected)
    cosine, sine_table = rotary_tables(length)
    queries = low(rotate(projected[0].reshape(length, HEADS, HEAD_DIM), cosine, sine_table))
    key_heads = low(rotate(projected[1].reshape(length, HEADS, HEAD_DIM), cosine, sine_table))
    value_heads = low(projected[2].reshape(length, HEADS, HEAD_DIM))
    causal = jnp.arange(length)[:, None] >= jnp.arange(length)[None, :]
    scores = jnp.einsum('shd,thd->hst', queries, key_heads, precision=highest) * score_scale
    scores = low_back(jnp.where(causal[None], scores, -1000000000.0))
    soft_low = low(jax.nn.softmax(scores, axis=-1))
    head_mix = jnp.einsum('hst,thd->shd', soft_low, value_heads, precision=highest).reshape(length, D)
    head_mix = low_back(low(head_mix))
    first_sum = inputs + low_back(jnp.dot(head_mix, out_full, precision=highest))
    normed_two = low(normalize(first_sum, norm_table[2], norm_table[3]))
    gate_up = low_back(jnp.einsum('sd,tdf->tsf', normed_two, gate_up_full, precision=highest))
    hidden = low(jax.nn.silu(gate_up[0]) * gate_up[1])
    return first_sum + jnp.dot(hidden, down_full, precision=highest)

def reference(tokens, cotangent, norm_params, qkv_weight, qkv_bias, out_weight, gate_up_weight, down_weight):
    params = (norm_params.astype(jnp.float32), qkv_weight.astype(jnp.float32), qkv_bias.astype(jnp.float32), out_weight.astype(jnp.float32), gate_up_weight.astype(jnp.float32), down_weight.astype(jnp.float32))
    inputs = tokens.astype(jnp.float32).reshape(N_DP, TOK_GROUP, D)
    cotangents = cotangent.astype(jnp.float32).reshape(N_DP, TOK_GROUP, D)

    def scan_step(totals, sequence_pair):
        inputs_one, cotangent_one = sequence_pair
        output, puller = jax.vjp(layer, inputs_one, *params)
        grads = puller(cotangent_one)
        totals = tuple((earlier + later for earlier, later in zip(totals, grads[1:])))
        return (totals, (output.astype(jnp.bfloat16), grads[0]))
    start = tuple((jnp.zeros(param.shape, jnp.float32) for param in params))
    totals, (outputs, grad_inputs) = lax.scan(scan_step, start, (inputs, cotangents))
    return (outputs.reshape(TOKENS, D), grad_inputs.reshape(TOKENS, D), totals[0], totals[1], totals[2], totals[3], totals[4], totals[5])
```

```python
import jax
import jax.numpy as jnp
from jax import lax
from jax.sharding import Mesh
from jax.sharding import PartitionSpec as P

HEAD_DIM = 64
ROTARY = 16
EPSILON = 1e-05
SCALE = 0.125

GRID = ("z", "x", "yl", "c", "yh")
ROWS = ("z", "x", "yl", "c")
SPREAD = ("z", "x", "c")
RING = ("yl", "yh")
PAIR = ("yl", "c")
EXTRA = 128

SAME = [(0, 0), (1, 2), (2, 1), (3, 3)]
CROSS = [(0, 2), (1, 0), (2, 3), (3, 1)]

bf16 = jnp.bfloat16
f32 = jnp.float32


def turn(k):
    place = [0, 2, 1, 3]
    return [(place[y], place[(y + k) % 4]) for y in range(4)]


def mm(a, b, ca, cb):
    return lax.dot_general(a, b, (((ca,), (cb,)), ((), ())), preferred_element_type=f32)


def to_quarters(quarters):
    yl, c = lax.axis_index("yl"), lax.axis_index("c")
    one = lax.ppermute(lax.dynamic_index_in_dim(quarters, c, 0, False), PAIR, SAME)
    two = lax.ppermute(lax.dynamic_index_in_dim(quarters, 1 - c, 0, False), PAIR, CROSS)
    low = jnp.where(yl == 0, one, two)
    high = jnp.where(yl == 0, two, one)
    return jnp.concatenate([low, high], axis=0)


def from_quarters(rows):
    yl, c = lax.axis_index("yl"), lax.axis_index("c")
    halves = rows.reshape(2, 32, rows.shape[1])
    one = lax.ppermute(
        lax.dynamic_index_in_dim(halves, yl, 0, False), PAIR, [(b, a) for a, b in SAME]
    )
    two = lax.ppermute(
        lax.dynamic_index_in_dim(halves, 1 - yl, 0, False), PAIR, [(b, a) for a, b in CROSS]
    )
    return jnp.stack([jnp.where(c == 0, one, two), jnp.where(c == 0, two, one)])


def gather_ring(block):
    got = [block]
    for k in (2, 1, 3):
        got.append(lax.ppermute(block, RING, turn(-k)))
    return jnp.concatenate(got, axis=0)


def sum_ring(parts):
    blocks = parts.reshape(4, -1, parts.shape[1])
    total = blocks[0]
    low = blocks.astype(bf16)
    for place, k in ((1, 2), (2, 1), (3, 3)):
        total = total + lax.ppermute(
            low[place], RING, turn(k)
        ).astype(f32)
    return total


def unit_of(values):
    centered = values - jnp.mean(values, -1, keepdims=True)
    variance = jnp.mean(centered * centered, -1, keepdims=True)
    inverse = lax.rsqrt(variance + EPSILON)
    return centered * inverse, inverse


def normalize_back(incoming, unit_rows, inverse, gain):
    grad_unit = incoming * gain
    return inverse * (
        grad_unit
        - jnp.mean(grad_unit, -1, keepdims=True)
        - unit_rows * jnp.mean(grad_unit * unit_rows, -1, keepdims=True)
    )


def rotate(values, cosine, sine):
    half = ROTARY // 2
    low, high = values[..., :half], values[..., half:ROTARY]
    return jnp.concatenate(
        [low * cosine - high * sine, high * cosine + low * sine, values[..., ROTARY:]], -1
    )


def shards(
    tokens, cotangent, norm_params, qkv_weight, qkv_bias, out_weight, gate_up_weight, down_weight
):
    yl, yh = lax.axis_index("yl"), lax.axis_index("yh")
    y = yh * 2 + yl
    rows = qkv_weight.shape[1]
    hq = qkv_weight.shape[2] // 2
    fq = gate_up_weight.shape[2] // 2
    heads = hq // HEAD_DIM
    here = tokens.shape[0]
    length = 2 * here

    qkv_q = qkv_weight.reshape(3, rows, 2, hq).transpose(2, 1, 0, 3).reshape(2, rows, 3 * hq)
    out_q = out_weight.T.reshape(rows, 2, hq).transpose(1, 0, 2)
    gu_q = gate_up_weight.reshape(2, rows, 2, fq).transpose(2, 1, 0, 3).reshape(2, rows, 2 * fq)
    down_q = down_weight.T.reshape(rows, 2, fq).transpose(1, 0, 2)
    other = lax.ppermute(norm_params, "yh", [(0, 1), (1, 0)])
    norm_rows = jnp.where(
        yh == 0,
        jnp.concatenate([norm_params, other], 1),
        jnp.concatenate([other, norm_params], 1),
    ).T
    norm_high = norm_rows.astype(bf16)
    norm_low = (norm_rows - norm_high.astype(f32)).astype(bf16)
    bias_q = qkv_bias.reshape(3, 2, heads).transpose(1, 0, 2).reshape(2, 1, 3 * heads)
    bias_q = jnp.pad(bias_q, ((0, 0), (0, rows - 1), (8, EXTRA - 8 - 3 * heads)))
    extra = jnp.pad(jnp.concatenate([norm_high, norm_low], 1), ((0, 0), (0, EXTRA - 8)))
    extra_q = bias_q + extra[None]

    first = to_quarters(jnp.concatenate([qkv_q, out_q, extra_q], axis=2))
    second = to_quarters(jnp.concatenate([gu_q, down_q], axis=2))
    first = lax.all_gather(first, SPREAD, axis=0, tiled=True)
    second = lax.all_gather(second, SPREAD, axis=0, tiled=True)
    w_qkv, w_out = first[:, : 3 * hq], first[:, 3 * hq : 4 * hq]
    extras = first[:, 4 * hq :]
    w_gu, w_down = second[:, : 2 * fq], second[:, 2 * fq :]
    width = extras.shape[0]
    norm_table = (extras[:, :4].astype(f32) + extras[:, 4:8].astype(f32)).T
    bias = extras.reshape(HEAD_DIM, rows, EXTRA)[:, 0, 8 : 8 + 3 * heads].T.reshape(3 * hq)

    token_rows = gather_ring(tokens).astype(f32)
    cot_rows = gather_ring(cotangent)
    unit_rows, inverse_rows = unit_of(token_rows)
    unit_one, scale_one = unit_rows[:here], inverse_rows[:here]
    normed_one = (unit_rows * norm_table[0] + norm_table[1]).astype(bf16)
    projected = mm(normed_one, w_qkv, 1, 0) + bias.astype(f32)
    place = jnp.stack([((y + k) % 4) // 2 for k in (0, 2, 1, 3)])
    position = (place[:, None] * here + jnp.arange(here)[None, :]).reshape(2, length)
    frequency = jnp.power(10000.0, -jnp.arange(ROTARY // 2).astype(f32) * (2.0 / ROTARY))
    angles = position.astype(f32)[:, :, None] * frequency
    cosine, sine = jnp.cos(angles)[:, :, None, :], jnp.sin(angles)[:, :, None, :]
    split = projected.reshape(2, length, 3, heads, HEAD_DIM)
    queries = rotate(split[:, :, 0], cosine, sine).astype(bf16)
    key_heads = rotate(split[:, :, 1], cosine, sine).astype(bf16)
    value_heads = split[:, :, 2].astype(bf16)
    causal = position[:, :, None] >= position[:, None, :]
    scores = (
        jnp.einsum("bshd,bthd->bhst", queries, key_heads, preferred_element_type=f32) * SCALE
    )
    scores = jnp.where(causal[:, None], scores, -1000000000.0)
    powers = jnp.exp(scores - jnp.max(scores, -1, keepdims=True))
    soft = powers / jnp.sum(powers, -1, keepdims=True)
    soft_low = soft.astype(bf16)
    head_mix = jnp.einsum("bhst,bthd->bshd", soft_low, value_heads, preferred_element_type=f32)
    head_mix = head_mix.reshape(2 * length, hq).astype(bf16)
    first_sum = tokens.astype(f32) + sum_ring(mm(head_mix, w_out, 1, 1))

    unit_two, scale_two = unit_of(first_sum)
    normed_two = gather_ring((unit_two * norm_table[2] + norm_table[3]).astype(bf16))
    gate_up = mm(normed_two, w_gu, 1, 0)
    gate_pre, up_pre = gate_up[:, :fq], gate_up[:, fq:]
    sigmoid = jax.nn.sigmoid(gate_pre)
    activated = gate_pre * sigmoid
    hidden = (activated * up_pre).astype(bf16)
    grad_down = mm(cot_rows, hidden, 0, 0).astype(bf16)
    down_sums = lax.psum_scatter(grad_down, SPREAD, scatter_dimension=0, tiled=True)
    mixed = (first_sum + sum_ring(mm(hidden, w_down, 1, 1))).astype(bf16)
    grad_hidden = mm(cot_rows, w_down, 1, 0)
    grad_gate = grad_hidden * up_pre * sigmoid * (1.0 + gate_pre * (1.0 - sigmoid))
    grad_pair = jnp.concatenate([grad_gate, grad_hidden * activated], 1).astype(bf16)
    grad_gu = mm(normed_two, grad_pair, 0, 0).astype(bf16)
    gu_sums = lax.psum_scatter(grad_gu, SPREAD, scatter_dimension=0, tiled=True)
    grad_second = sum_ring(mm(grad_pair, w_gu, 1, 1))
    grad_resid = cotangent.astype(f32) + normalize_back(
        grad_second, unit_two, scale_two, norm_table[2]
    )
    gain_two = jnp.sum(grad_second * unit_two, 0)
    shift_two = jnp.sum(grad_second, 0)

    resid_rows = gather_ring(grad_resid.astype(bf16))
    grad_mix = mm(resid_rows, w_out, 1, 0).astype(bf16).reshape(2, length, heads, HEAD_DIM)
    grad_out = mm(resid_rows, head_mix, 0, 0).astype(bf16)
    grad_soft = jnp.einsum("bshd,bthd->bhst", grad_mix, value_heads, preferred_element_type=f32)
    row_dot = jnp.sum(grad_soft * soft, -1, keepdims=True)
    grad_score = (soft * (grad_soft - row_dot)).astype(bf16)
    grad_query = (
        jnp.einsum("bhst,bthd->bshd", grad_score, key_heads, preferred_element_type=f32) * SCALE
    )
    grad_key = (
        jnp.einsum("bhst,bshd->bthd", grad_score, queries, preferred_element_type=f32) * SCALE
    )
    grad_value = jnp.einsum("bhst,bshd->bthd", soft_low, grad_mix, preferred_element_type=f32)
    grad_proj = jnp.concatenate(
        [
            rotate(grad_query, cosine, -sine).reshape(2 * length, hq),
            rotate(grad_key, cosine, -sine).reshape(2 * length, hq),
            grad_value.reshape(2 * length, hq),
        ],
        1,
    ).astype(bf16)
    grad_qkv = mm(normed_one, grad_proj, 0, 0).astype(bf16)
    first_parts = mm(grad_proj, w_qkv, 1, 1)
    gain_one = jnp.sum(first_parts * unit_rows, 0)
    shift_one = jnp.sum(first_parts, 0)
    grad_bias = jnp.sum(grad_proj.astype(f32), 0).reshape(3 * heads, HEAD_DIM).T
    norm_terms = jnp.stack([gain_one, shift_one, gain_two, shift_two], 1)
    grad_extra = jnp.pad(norm_terms, ((0, 0), (0, EXTRA - 4))) + jnp.pad(
        grad_bias[:, None, :], ((0, 0), (0, rows - 1), (8, EXTRA - 8 - 3 * heads))
    ).reshape(width, EXTRA)
    grad_first = jnp.concatenate([grad_qkv, grad_out, grad_extra.astype(bf16)], 1)
    first_sums = lax.psum_scatter(grad_first, SPREAD, scatter_dimension=0, tiled=True)
    grad_input = grad_resid + normalize_back(
        sum_ring(first_parts), unit_one, scale_one, norm_table[0]
    )

    down_back = from_quarters(down_sums)
    gu_back = from_quarters(gu_sums)
    first_back = from_quarters(first_sums)
    out_down = down_back.transpose(0, 2, 1).reshape(2 * fq, rows).astype(f32)
    out_gu = (
        gu_back.reshape(2, rows, 2, fq).transpose(2, 1, 0, 3).reshape(2, rows, 2 * fq).astype(f32)
    )
    out_qkv = (
        first_back[:, :, : 3 * hq]
        .reshape(2, rows, 3, hq)
        .transpose(2, 1, 0, 3)
        .reshape(3, rows, 2 * hq)
        .astype(f32)
    )
    out_out = (
        first_back[:, :, 3 * hq : 4 * hq].transpose(0, 2, 1).reshape(2 * hq, rows).astype(f32)
    )
    extra_back = first_back[:, :, 4 * hq :].astype(f32)
    out_bias = (
        extra_back[:, 0, 8 : 8 + 3 * heads]
        .reshape(2, 3, heads)
        .transpose(1, 0, 2)
        .reshape(3, 2 * heads, 1)
    )
    norm_back = (extra_back[0, :, :4] + extra_back[1, :, :4]).T.reshape(4, 2, rows // 2)
    mine = lax.dynamic_index_in_dim(norm_back, yh, 1, False)
    theirs = lax.dynamic_index_in_dim(norm_back, 1 - yh, 1, False)
    out_norm = mine + lax.ppermute(theirs, "yh", [(0, 1), (1, 0)])
    return (mixed, grad_input, out_norm, out_qkv, out_bias, out_out, out_gu, out_down)


def solution(mesh):
    grid = Mesh(mesh.devices.reshape(4, 4, 2, 2, 2), GRID)
    placed = (
        P(GRID, None),
        P(GRID, None),
        P(None, GRID),
        P(None, ROWS, "yh"),
        P(None, "yh", ROWS),
        P("yh", ROWS),
        P(None, ROWS, "yh"),
        P("yh", ROWS),
    )
    return jax.shard_map(
        shards,
        mesh=grid,
        in_specs=placed,
        out_specs=(
            P(GRID, None),
            P(GRID, None),
            P(None, GRID),
            P(None, ROWS, "yh"),
            P(None, "yh", ROWS),
            P("yh", ROWS),
            P(None, ROWS, "yh"),
            P("yh", ROWS),
        ),
        check_vma=False,
    )
```

```python
import functools

import jax
import jax.numpy as jnp
from jax import lax
from jax.experimental import pallas as pl
from jax.experimental.pallas import tpu as pltpu
from jax.sharding import Mesh
from jax.sharding import PartitionSpec as P

HEAD_DIM = 64
ROTARY = 16
EPSILON = 1e-05
SCALE = 0.125

GRID = ("z", "x", "yl", "c", "yh")
ROWS = ("z", "x", "yl", "c")
SPREAD = ("z", "x", "c")
PAIR = ("yl", "c")
EXTRA = 128

SAME = [(0, 0), (1, 2), (2, 1), (3, 3)]
CROSS = [(0, 2), (1, 0), (2, 3), (3, 1)]

bf16 = jnp.bfloat16
f32 = jnp.float32


MESH = pl.DeviceIdType.MESH
VMEM = pltpu.VMEM
DMA = pltpu.SemaphoreType.DMA
VMEM_LIMIT = 60 * 1024 * 1024


def at_y(k):
    y = (lax.axis_index("yh") * 2 + lax.axis_index("yl") + k) % 4
    return {"yl": y % 2, "yh": y // 2}


def at_z(k):
    return {"z": (lax.axis_index("z") + k) % 4}


def at_x(k):
    return {"x": (lax.axis_index("x") + k) % 4}


def sibling():
    return {"c": 1 - lax.axis_index("c")}


def greet(devices):
    barrier = pltpu.get_barrier_semaphore()
    for device in devices:
        pl.semaphore_signal(barrier, inc=1, device_id=device, device_id_type=MESH)
    pl.semaphore_wait(barrier, len(devices))


def remote(src, dst, sems, index, device):
    send, recv = sems
    return pltpu.make_async_remote_copy(
        src_ref=src,
        dst_ref=dst,
        send_sem=send.at[index],
        recv_sem=recv.at[index],
        device_id=device,
        device_id_type=MESH,
    )


def ring_sum(parts, mid, sent, far, near, sems):
    started = ring_sum_start(parts, mid, near, sems, 0)
    middle = ring_sum_middle(parts, started, mid, sent, far, sems, 0)
    return ring_sum_finish(parts, started, middle, far, near), started + middle


def ring_gather_half(out, top, sems, base):
    here = out.shape[0] // 4
    half = here // 2
    copies = []
    for way, step, block in ((0, 1, 3), (1, -1, 2)):
        copies.append(
            remote(
                out.at[pl.ds(top * half, half)],
                out.at[pl.ds(block * here + top * half, half)],
                sems,
                base + 2 * way + top,
                at_y(step),
            )
        )
        copies[-1].start()
    return copies


def ring_gather_pass(out, halves, sems, base):
    here = out.shape[0] // 4
    half = here // 2
    passed = []
    for way, step, block in ((0, 1, 3), (1, -1, 2)):
        halves[way][way].wait_recv()
        passed.append(
            remote(
                out.at[pl.ds(block * here + way * half, half)],
                out.at[pl.ds(here + way * half, half)],
                sems,
                base + 4 + way,
                at_y(step),
            )
        )
        passed[-1].start()
    return passed


def second_norm_kernel(parts, tokens, gains, summed, unit, scale, normed, mid, sent, far, near, send, recv):
    sems = (send, recv)
    greet([at_y(1), at_y(3)])
    finish, copies = ring_sum(parts, mid, sent, far, near, sems)
    half = tokens.shape[0] // 2
    halves = []
    for top in range(2):
        rows = pl.ds(top * half, half)
        total = tokens[rows].astype(f32) + finish(top)
        summed[rows] = total
        centered = total - jnp.mean(total, -1, keepdims=True)
        inverse = lax.rsqrt(jnp.mean(centered * centered, -1, keepdims=True) + EPSILON)
        unit_rows = centered * inverse
        unit[rows] = unit_rows
        scale[rows] = inverse
        normed[rows] = (unit_rows * gains[0:1] + gains[1:2]).astype(bf16)
        halves.append(ring_gather_half(normed, top, sems, 6))
    passed = ring_gather_pass(normed, halves, sems, 6)
    for copy in passed + [halves[1][0], halves[0][1]]:
        copy.wait_recv()
    for copy in copies + halves[0] + halves[1] + passed:
        copy.wait_send()


def second_norm(parts, tokens, gains):
    here, width = tokens.shape
    half = here // 2
    full = pl.BlockSpec(memory_space=VMEM)
    return pl.pallas_call(
        second_norm_kernel,
        out_shape=(
            jax.ShapeDtypeStruct((here, width), f32),
            jax.ShapeDtypeStruct((here, width), f32),
            jax.ShapeDtypeStruct((here, 1), f32),
            jax.ShapeDtypeStruct((4 * here, width), bf16),
        ),
        in_specs=[full] * 3,
        out_specs=(full,) * 4,
        scratch_shapes=[VMEM((2, half, width), bf16)] * 4 + [DMA((12,)), DMA((12,))],
        compiler_params=pltpu.CompilerParams(
            collective_id=1, has_side_effects=True, vmem_limit_bytes=VMEM_LIMIT
        ),
    )(parts, tokens, gains)


def second_norm_back_kernel(
    parts, cotangent, unit, scale, gains, resid, sums, spread, mid, sent, far, near, send, recv
):
    sems = (send, recv)
    greet([at_y(1), at_y(3)])
    finish, copies = ring_sum(parts, mid, sent, far, near, sems)
    half = cotangent.shape[0] // 2
    halves = []
    for top in range(2):
        rows = pl.ds(top * half, half)
        total = finish(top)
        unit_rows = unit[rows]
        incoming = total * gains[0:1]
        result = cotangent[rows].astype(f32) + scale[rows] * (
            incoming
            - jnp.mean(incoming, -1, keepdims=True)
            - unit_rows * jnp.mean(incoming * unit_rows, -1, keepdims=True)
        )
        resid[rows] = result
        spread[rows] = result.astype(bf16)
        halves.append(ring_gather_half(spread, top, sems, 6))
        both = jnp.concatenate(
            [
                jnp.sum(total * unit_rows, 0, keepdims=True),
                jnp.sum(total, 0, keepdims=True),
            ],
            0,
        )
        sums[...] = both if top == 0 else sums[...] + both
    passed = ring_gather_pass(spread, halves, sems, 6)
    for copy in passed + [halves[1][0], halves[0][1]]:
        copy.wait_recv()
    for copy in copies + halves[0] + halves[1] + passed:
        copy.wait_send()


def second_norm_back(parts, cotangent, unit, scale, gains):
    here, width = cotangent.shape
    half = here // 2
    full = pl.BlockSpec(memory_space=VMEM)
    return pl.pallas_call(
        second_norm_back_kernel,
        out_shape=(
            jax.ShapeDtypeStruct((here, width), f32),
            jax.ShapeDtypeStruct((2, width), f32),
            jax.ShapeDtypeStruct((4 * here, width), bf16),
        ),
        in_specs=[full] * 5,
        out_specs=(full,) * 3,
        scratch_shapes=[VMEM((2, half, width), bf16)] * 4 + [DMA((12,)), DMA((12,))],
        compiler_params=pltpu.CompilerParams(
            collective_id=2, has_side_effects=True, vmem_limit_bytes=VMEM_LIMIT
        ),
    )(parts, cotangent, unit, scale, gains)


def pair_moves():
    yl, c = lax.axis_index("yl"), lax.axis_index("c")
    return {"yl": c, "c": yl}, {"yl": 1 - c, "c": yl}


def diagonal():
    return {"yl": 1 - lax.axis_index("yl"), "c": 1 - lax.axis_index("c")}


def everyone_near():
    return [at_z(1), at_z(3), at_x(1), at_x(3), at_y(1), at_y(3), sibling(), diagonal()]


def stay_or_go(src, dst, sems, index, device, local_sem):
    yl, c = lax.axis_index("yl"), lax.axis_index("c")

    @pl.when(yl == c)
    def _():
        pltpu.make_async_copy(src, dst, local_sem).start()

    @pl.when(yl != c)
    def _():
        remote(src, dst, sems, index, device).start()


def stay_or_go_wait(src, dst, sems, index, device, local_sem):
    yl, c = lax.axis_index("yl"), lax.axis_index("c")

    @pl.when(yl == c)
    def _():
        pltpu.make_async_copy(src, dst, local_sem).wait()

    @pl.when(yl != c)
    def _():
        copy = remote(src, dst, sems, index, device)
        copy.wait_recv()
        copy.wait_send()


def first_gather_kernel(
    one_q, two_q, tokens, cotangent, one, two, token_rows, cot_rows,
    pair_send, pair_recv, local_sem, y_send, y_recv, send, recv, core_send, core_recv,
):
    z, x = lax.axis_index("z"), lax.axis_index("x")
    yl, c = lax.axis_index("yl"), lax.axis_index("c")
    pair_sems, y_sems, sems, core_sems = (
        (pair_send, pair_recv),
        (y_send, y_recv),
        (send, recv),
        (core_send, core_recv),
    )
    rows = one_q.shape[1]
    here = tokens.shape[0]
    piece = rows // 2
    same, cross = pair_moves()
    token_rows[pl.ds(0, here)] = tokens[...]
    cot_rows[pl.ds(0, here)] = cotangent[...]
    greet(everyone_near())

    def start_of(dz, dx, half):
        return (((z + dz) % 4) * 4 + (x + dx) % 4) * 4 * rows + c * 2 * rows + half * rows

    target = ((z * 4 + x) * 4 + yl * 2 + c) * rows
    moves = [
        (one_q.at[c], one.at[pl.ds(target, rows)], 0, same),
        (one_q.at[1 - c], one.at[pl.ds(target, rows)], 1, cross),
        (two_q.at[c], two.at[pl.ds(c * rows, rows)], 2, same),
        (two_q.at[1 - c], two.at[pl.ds(c * rows, rows)], 3, cross),
    ]

    def launch(k):
        src, dst, index, device = moves[k]
        if device is same:
            stay_or_go(src, dst, pair_sems, index, device, local_sem.at[index // 2])
        else:
            remote(src, dst, pair_sems, index, device).start()

    def land(k):
        src, dst, index, device = moves[k]
        if device is same:
            stay_or_go_wait(src, dst, pair_sems, index, device, local_sem.at[index // 2])
        else:
            copy = remote(src, dst, pair_sems, index, device)
            copy.wait_recv()
            copy.wait_send()

    launch(0)
    launch(1)
    y_halves = {}
    y_passed = {}
    for top in range(2):
        y_halves[0, top] = ring_gather_half(token_rows, top, y_sems, 0)
    land(0)
    land(1)

    done = []

    def index_of(half, df, dg, part):
        return ((half * 4 + df % 4) * 4 + dg % 4) * 2 + part

    def block(half, df, dg):
        return start_of(df, dg, half) if half == 0 else start_of(dg, df, half)

    def push(half, df, dg, axis, step, part):
        along_z = (half == 0) == (axis == 0)
        device = at_z(step) if along_z else at_x(step)
        to = (df - step, dg) if axis == 0 else (df, dg - step)
        rng = pl.ds(block(half, df, dg) + part * piece, piece)
        copy = remote(one.at[rng], one.at[rng], sems, index_of(half, *to, part), device)
        copy.start()
        done.append(copy)

    def arrived(half, df, dg, part):
        rng = pl.ds(block(half, df, dg) + part * piece, piece)
        remote(one.at[rng], one.at[rng], sems, index_of(half, df, dg, part), at_z(1)).wait_recv()

    def to_sibling(half, df, dg):
        rng = pl.ds(block(half, df, dg), rows)
        copy = remote(
            one.at[rng], one.at[rng], core_sems, (half * 4 + df % 4) * 4 + dg % 4, sibling()
        )
        copy.start()
        done.append(copy)
        core.append(copy)

    core = []
    for axis in range(2):
        for half in range(2):
            for part in range(2):
                push(half, 0, 0, axis, 1, part)
                push(half, 0, 0, axis, -1, 1 - part)
    launch(2)
    launch(3)
    for half in range(2):
        to_sibling(half, 0, 0)
    for half in range(2):
        arrived(half, 3, 0, 0)
        push(half, 3, 0, 0, 1, 0)
        arrived(half, 1, 0, 1)
        push(half, 1, 0, 0, -1, 1)
    for half in range(2):
        arrived(half, 3, 0, 1)
        arrived(half, 1, 0, 0)
        for df in (3, 1):
            for part in range(2):
                push(half, df, 0, 1, 1, part)
                push(half, df, 0, 1, -1, 1 - part)
            to_sibling(half, df, 0)
    y_passed[0] = ring_gather_pass(token_rows, [y_halves[0, 0], y_halves[0, 1]], y_sems, 0)
    for top in range(2):
        y_halves[1, top] = ring_gather_half(cot_rows, top, y_sems, 6)

    def second_axis(df):
        for half in range(2):
            arrived(half, df, 3, 0)
            push(half, df, 3, 1, 1, 0)
            arrived(half, df, 1, 1)
            push(half, df, 1, 1, -1, 1)
        for half in range(2):
            arrived(half, df, 3, 1)
            to_sibling(half, df, 3)
            arrived(half, df, 1, 0)
            to_sibling(half, df, 1)

    second_axis(0)
    for half in range(2):
        arrived(half, 2, 0, 0)
        arrived(half, 2, 0, 1)
        for part in range(2):
            push(half, 2, 0, 1, 1, part)
            push(half, 2, 0, 1, -1, 1 - part)
        to_sibling(half, 2, 0)
    second_axis(3)
    second_axis(1)
    y_passed[1] = ring_gather_pass(cot_rows, [y_halves[1, 0], y_halves[1, 1]], y_sems, 6)
    second_axis(2)
    for df in (0, 3, 1, 2):
        for half in range(2):
            for part in range(2):
                arrived(half, df, 2, part)
            to_sibling(half, df, 2)
    land(2)
    land(3)
    for which in range(2):
        for copy in y_passed[which] + [y_halves[which, 1][0], y_halves[which, 0][1]]:
            copy.wait_recv()
        for copy in y_passed[which] + y_halves[which, 0] + y_halves[which, 1]:
            copy.wait_send()
    for copy in core:
        copy.wait_recv()
    for copy in done:
        copy.wait_send()


def first_gather(one_q, two_q, tokens, cotangent):
    rows = one_q.shape[1]
    here, width = tokens.shape
    anywhere = pl.BlockSpec(memory_space=pl.ANY)
    full = pl.BlockSpec(memory_space=VMEM)
    return pl.pallas_call(
        first_gather_kernel,
        out_shape=(
            jax.ShapeDtypeStruct((64 * rows, one_q.shape[2]), bf16),
            jax.ShapeDtypeStruct((2 * rows, two_q.shape[2]), bf16),
            jax.ShapeDtypeStruct((4 * here, width), bf16),
            jax.ShapeDtypeStruct((4 * here, width), bf16),
        ),
        in_specs=[full] * 4,
        out_specs=(anywhere, anywhere, full, full),
        scratch_shapes=[
            DMA((4,)), DMA((4,)), DMA((2,)), DMA((12,)), DMA((12,)),
            DMA((64,)), DMA((64,)), DMA((32,)), DMA((32,)),
        ],
        compiler_params=pltpu.CompilerParams(
            collective_id=0, has_side_effects=True, vmem_limit_bytes=VMEM_LIMIT
        ),
    )(one_q, two_q, tokens, cotangent)


def last_sum_kernel(
    grads, first_parts, mixed_parts, resid, unit, scale, gains, first_sum,
    result, grad_tokens, mixed,
    sib, mid, sent, far, near, stage, mid2, sent2, far2, near2, packed,
    ymid, ysent, yfar, ynear,
    core_send, core_recv, send, recv, send2, recv2, pair_send, pair_recv, local_sem, y_send, y_recv,
):
    z, x = lax.axis_index("z"), lax.axis_index("x")
    yl, c = lax.axis_index("yl"), lax.axis_index("c")
    core_sems, sems, sems2, pair_sems, y_sems = (
        (core_send, core_recv),
        (send, recv),
        (send2, recv2),
        (pair_send, pair_recv),
        (y_send, y_recv),
    )
    rows = result.shape[1]
    piece = rows // 2
    greet(everyone_near())
    done = []

    def begin(copy):
        copy.start()
        done.append(copy)
        return copy

    def start_of(dz, dx, core):
        return (((z + dz) % 4) * 4 + (x + dx) % 4) * 4 * rows + core * 2 * rows

    order = []
    for d in (2, 1, 3, 0):
        for e in (2, 1, 3, 0):
            for pair in ((d, e), (e, d)):
                if pair not in order:
                    order.append(pair)
    core = {}
    for dz, dx in order:
        core[dz, dx] = begin(
            remote(
                grads.at[pl.ds(start_of(dz, dx, 1 - c), 2 * rows)],
                sib.at[dz, dx],
                core_sems,
                dz * 4 + dx,
                sibling(),
            )
        )
    y_jobs = [
        ring_sum_start(first_parts, ymid.at[0], ynear.at[0], y_sems, 0),
        ring_sum_start(mixed_parts, ymid.at[1], ynear.at[1], y_sems, 6),
    ]
    summed = set()

    def core_sum(dz, dx):
        if (dz, dx) in summed:
            return
        summed.add((dz, dx))
        core[dz, dx].wait_recv()
        sib[dz, dx] = (
            sib[dz, dx].astype(f32)
            + grads[pl.ds(start_of(dz, dx, c), 2 * rows)].astype(f32)
        ).astype(bf16)

    def view(half, df, part):
        rng = pl.ds(half * rows + part * piece, piece)
        return sib.at[df, :, rng] if half == 0 else sib.at[:, df, rng]

    def device(half, axis, step):
        return at_z(step) if (half == 0) == (axis == 0) else at_x(step)

    def ring_first(half, axis, src, mids, nears, some_sems):
        base = half * 6
        got = {}
        for way, step in ((0, 1), (1, -1)):
            got["first", way] = begin(
                remote(src(2, way), mids.at[half, way], some_sems, base + way, device(half, axis, step))
            )
        return got

    def ring_second(half, axis, src, nears, some_sems, got):
        base = half * 6
        for way, step in ((0, 1), (1, -1)):
            got["second", way] = begin(
                remote(
                    src(step % 4, 1 - way), nears.at[half, way], some_sems, base + 2 + way,
                    device(half, axis, step),
                )
            )

    def ring_third(half, axis, src, mids, sents, fars, some_sems, got):
        base = half * 6
        for way, step in ((0, 1), (1, -1)):
            got["first", way].wait_recv()
            sents[half, way] = (
                src(step % 4, way)[...].astype(f32) + mids[half, way].astype(f32)
            ).astype(bf16)
            got["third", way] = begin(
                remote(
                    sents.at[half, way], fars.at[half, way], some_sems, base + 4 + way,
                    device(half, axis, step),
                )
            )

    def ring_last(half, part, src, fars, nears, got):
        got["third", part].wait_recv()
        got["second", 1 - part].wait_recv()
        return (
            src(0, part)[...].astype(f32)
            + fars[half, part].astype(f32)
            + nears[half, 1 - part].astype(f32)
        )

    got = {}
    sources = [functools.partial(view, half) for half in range(2)]
    for half in range(2):
        for d in (2, 1, 3, 0):
            core_sum(*((2, d) if half == 0 else (d, 2)))
        got[half] = ring_first(half, 0, sources[half], mid, near, sems)
    for half in range(2):
        for step in (1, 3):
            for d in (2, 1, 3, 0):
                core_sum(*((step, d) if half == 0 else (d, step)))
        ring_second(half, 0, sources[half], near, sems, got[half])
    y_more = [
        ring_sum_middle(first_parts, y_jobs[0], ymid.at[0], ysent.at[0], yfar.at[0], y_sems, 0)
    ]
    for half in range(2):
        ring_third(half, 0, sources[half], mid, sent, far, sems, got[half])
    core_sum(0, 0)
    y_more.append(
        ring_sum_middle(mixed_parts, y_jobs[1], ymid.at[1], ysent.at[1], yfar.at[1], y_sems, 6)
    )
    finish = ring_sum_finish(first_parts, y_jobs[0], y_more[0], yfar.at[0], ynear.at[0])
    here = grad_tokens.shape[0] // 2
    for top in range(2):
        rng = pl.ds(top * here, here)
        incoming = finish(top) * gains[0:1]
        unit_rows = unit[rng]
        grad_tokens[rng] = resid[rng] + scale[rng] * (
            incoming
            - jnp.mean(incoming, -1, keepdims=True)
            - unit_rows * jnp.mean(incoming * unit_rows, -1, keepdims=True)
        )
    for half in range(2):
        for part in range(2):
            stage[half, :, part * piece : (part + 1) * piece] = ring_last(
                half, part, sources[half], far, near, got[half]
            ).astype(bf16)

    def stage_view(half, dg, part):
        return stage.at[half, dg, pl.ds(part * piece, piece)]

    sources = [functools.partial(stage_view, half) for half in range(2)]
    got = {}
    for half in range(2):
        got[half] = ring_first(half, 1, sources[half], mid2, near2, sems2)
    for half in range(2):
        ring_second(half, 1, sources[half], near2, sems2, got[half])
    for half in range(2):
        ring_third(half, 1, sources[half], mid2, sent2, far2, sems2, got[half])
    finish = ring_sum_finish(mixed_parts, y_jobs[1], y_more[1], yfar.at[1], ynear.at[1])
    for top in range(2):
        rng = pl.ds(top * here, here)
        mixed[rng] = (first_sum[rng] + finish(top)).astype(bf16)
    for half in range(2):
        for part in range(2):
            packed[half, part * piece : (part + 1) * piece] = ring_last(
                half, part, sources[half], far2, near2, got[half]
            ).astype(bf16)

    home, away = {"yl": c, "c": yl}, {"yl": c, "c": 1 - yl}
    stay_or_go(packed.at[yl], result.at[yl], pair_sems, 0, home, local_sem)
    cross = remote(packed.at[1 - yl], result.at[yl], pair_sems, 1, away)
    cross.start()
    cross.wait_recv()
    cross.wait_send()
    stay_or_go_wait(packed.at[yl], result.at[yl], pair_sems, 0, home, local_sem)
    for jobs in y_jobs + y_more:
        for copy in jobs:
            copy.wait_send()
    for copy in done:
        copy.wait_send()


def ring_sum_start(parts, mid, near, sems, base):
    here = parts.shape[0] // 4
    half = here // 2
    copies = []
    for way, step in ((0, 1), (1, -1)):
        copies.append(
            remote(
                parts.at[pl.ds(here + way * half, half)], mid.at[way], sems, base + way, at_y(step)
            )
        )
    for way, step, block in ((0, 1, 2), (1, -1, 3)):
        copies.append(
            remote(
                parts.at[pl.ds(block * here + (1 - way) * half, half)],
                near.at[way],
                sems,
                base + 2 + way,
                at_y(step),
            )
        )
    for copy in copies:
        copy.start()
    return copies


def ring_sum_middle(parts, started, mid, sent, far, sems, base):
    here = parts.shape[0] // 4
    half = here // 2
    copies = []
    for way, step, block in ((0, 1, 2), (1, -1, 3)):
        started[way].wait_recv()
        sent[way] = (
            parts[pl.ds(block * here + way * half, half)].astype(f32) + mid[way].astype(f32)
        ).astype(bf16)
        copies.append(remote(sent.at[way], far.at[way], sems, base + 4 + way, at_y(step)))
        copies[-1].start()
    return copies


def ring_sum_finish(parts, started, middle, far, near):
    half = parts.shape[0] // 8

    def finish(top):
        started[2 + 1 - top].wait_recv()
        middle[top].wait_recv()
        return (
            parts[pl.ds(top * half, half)].astype(f32)
            + far[top].astype(f32)
            + near[1 - top].astype(f32)
        )

    return finish


def last_sum(grads, first_parts, mixed_parts, resid, unit, scale, gains, first_sum):
    rows = grads.shape[0] // 64
    wide = grads.shape[1]
    here, width = resid.shape
    full = pl.BlockSpec(memory_space=VMEM)
    piece = rows // 2
    return pl.pallas_call(
        last_sum_kernel,
        out_shape=(
            jax.ShapeDtypeStruct((2, rows, wide), bf16),
            jax.ShapeDtypeStruct((here, width), f32),
            jax.ShapeDtypeStruct((here, width), bf16),
        ),
        in_specs=[full] * 8,
        out_specs=(full,) * 3,
        scratch_shapes=[
            VMEM((4, 4, 2 * rows, wide), bf16),
            VMEM((2, 2, 4, piece, wide), bf16),
            VMEM((2, 2, 4, piece, wide), bf16),
            VMEM((2, 2, 4, piece, wide), bf16),
            VMEM((2, 2, 4, piece, wide), bf16),
            VMEM((2, 4, rows, wide), bf16),
            VMEM((2, 2, piece, wide), bf16),
            VMEM((2, 2, piece, wide), bf16),
            VMEM((2, 2, piece, wide), bf16),
            VMEM((2, 2, piece, wide), bf16),
            VMEM((2, rows, wide), bf16),
            VMEM((2, 2, here // 2, width), bf16),
            VMEM((2, 2, here // 2, width), bf16),
            VMEM((2, 2, here // 2, width), bf16),
            VMEM((2, 2, here // 2, width), bf16),
            DMA((16,)), DMA((16,)), DMA((12,)), DMA((12,)), DMA((12,)), DMA((12,)),
            DMA((2,)), DMA((2,)), DMA, DMA((12,)), DMA((12,)),
        ],
        compiler_params=pltpu.CompilerParams(
            collective_id=3, has_side_effects=True, vmem_limit_bytes=VMEM_LIMIT
        ),
    )(grads, first_parts, mixed_parts, resid, unit, scale, gains, first_sum)


def mm(a, b, ca, cb):
    return lax.dot_general(a, b, (((ca,), (cb,)), ((), ())), preferred_element_type=f32)


def from_quarters(rows):
    yl, c = lax.axis_index("yl"), lax.axis_index("c")
    halves = rows.reshape(2, 32, rows.shape[1])
    one = lax.ppermute(
        lax.dynamic_index_in_dim(halves, yl, 0, False), PAIR, [(b, a) for a, b in SAME]
    )
    two = lax.ppermute(
        lax.dynamic_index_in_dim(halves, 1 - yl, 0, False), PAIR, [(b, a) for a, b in CROSS]
    )
    return jnp.stack([jnp.where(c == 0, one, two), jnp.where(c == 0, two, one)])


def unit_of(values):
    centered = values - jnp.mean(values, -1, keepdims=True)
    variance = jnp.mean(centered * centered, -1, keepdims=True)
    inverse = lax.rsqrt(variance + EPSILON)
    return centered * inverse, inverse


def rotate(values, cosine, sine):
    half = ROTARY // 2
    low, high = values[..., :half], values[..., half:ROTARY]
    return jnp.concatenate(
        [low * cosine - high * sine, high * cosine + low * sine, values[..., ROTARY:]], -1
    )


def shards(
    tokens, cotangent, norm_params, qkv_weight, qkv_bias, out_weight, gate_up_weight, down_weight
):
    yl, yh = lax.axis_index("yl"), lax.axis_index("yh")
    y = yh * 2 + yl
    rows = qkv_weight.shape[1]
    hq = qkv_weight.shape[2] // 2
    fq = gate_up_weight.shape[2] // 2
    heads = hq // HEAD_DIM
    here = tokens.shape[0]
    length = 2 * here

    qkv_q = qkv_weight.reshape(3, rows, 2, hq).transpose(2, 1, 0, 3).reshape(2, rows, 3 * hq)
    out_q = out_weight.T.reshape(rows, 2, hq).transpose(1, 0, 2)
    gu_q = gate_up_weight.reshape(2, rows, 2, fq).transpose(2, 1, 0, 3).reshape(2, rows, 2 * fq)
    down_q = down_weight.T.reshape(rows, 2, fq).transpose(1, 0, 2)
    other = lax.ppermute(norm_params, "yh", [(0, 1), (1, 0)])
    norm_rows = jnp.where(
        yh == 0,
        jnp.concatenate([norm_params, other], 1),
        jnp.concatenate([other, norm_params], 1),
    ).T
    norm_high = norm_rows.astype(bf16)
    norm_low = (norm_rows - norm_high.astype(f32)).astype(bf16)
    bias_q = qkv_bias.reshape(3, 2, heads).transpose(1, 0, 2).reshape(2, 1, 3 * heads)
    bias_q = jnp.pad(bias_q, ((0, 0), (0, rows - 1), (8, EXTRA - 8 - 3 * heads)))
    extra = jnp.pad(jnp.concatenate([norm_high, norm_low], 1), ((0, 0), (0, EXTRA - 8)))
    extra_q = bias_q + extra[None]

    first, second, token_rows, cot_rows = first_gather(
        jnp.concatenate([qkv_q, out_q, extra_q], axis=2),
        jnp.concatenate([gu_q, down_q], axis=2),
        tokens,
        cotangent,
    )
    second = lax.all_gather(second, SPREAD, axis=0, tiled=True)
    w_qkv, w_out = first[:, : 3 * hq], first[:, 3 * hq : 4 * hq]
    extras = first[:, 4 * hq :]
    w_gu, w_down = second[:, : 2 * fq], second[:, 2 * fq :]
    width = extras.shape[0]
    norm_table = (extras[:, :4].astype(f32) + extras[:, 4:8].astype(f32)).T
    bias = extras.reshape(HEAD_DIM, rows, EXTRA)[:, 0, 8 : 8 + 3 * heads].T.reshape(3 * hq)

    unit_rows, inverse_rows = unit_of(token_rows.astype(f32))
    unit_one, scale_one = unit_rows[:here], inverse_rows[:here]
    normed_one = (unit_rows * norm_table[0] + norm_table[1]).astype(bf16)
    projected = mm(normed_one, w_qkv, 1, 0) + bias.astype(f32)
    place = jnp.stack([((y + k) % 4) // 2 for k in (0, 2, 1, 3)])
    position = (place[:, None] * here + jnp.arange(here)[None, :]).reshape(2, length)
    frequency = jnp.power(10000.0, -jnp.arange(ROTARY // 2).astype(f32) * (2.0 / ROTARY))
    angles = position.astype(f32)[:, :, None] * frequency
    cosine, sine = jnp.cos(angles)[:, :, None, :], jnp.sin(angles)[:, :, None, :]
    split = projected.reshape(2, length, 3, heads, HEAD_DIM)
    queries = rotate(split[:, :, 0], cosine, sine).astype(bf16)
    key_heads = rotate(split[:, :, 1], cosine, sine).astype(bf16)
    value_heads = split[:, :, 2].astype(bf16)
    causal = position[:, :, None] >= position[:, None, :]
    scores = (
        jnp.einsum("bshd,bthd->bhst", queries, key_heads, preferred_element_type=f32) * SCALE
    )
    scores = jnp.where(causal[:, None], scores, -1000000000.0)
    powers = jnp.exp(scores - jnp.max(scores, -1, keepdims=True))
    soft = powers / jnp.sum(powers, -1, keepdims=True)
    soft_low = soft.astype(bf16)
    head_mix = jnp.einsum("bhst,bthd->bshd", soft_low, value_heads, preferred_element_type=f32)
    head_mix = head_mix.reshape(2 * length, hq).astype(bf16)

    first_sum, unit_two, scale_two, normed_two = second_norm(
        mm(head_mix, w_out, 1, 1).astype(bf16), tokens, norm_table[2:]
    )
    gate_up = mm(normed_two, w_gu, 1, 0)
    gate_pre, up_pre = gate_up[:, :fq], gate_up[:, fq:]
    sigmoid = jax.nn.sigmoid(gate_pre)
    activated = gate_pre * sigmoid
    hidden = (activated * up_pre).astype(bf16)
    grad_down = mm(cot_rows, hidden, 0, 0).astype(bf16)
    mixed_parts = mm(hidden, w_down, 1, 1).astype(bf16)
    grad_hidden = mm(cot_rows, w_down, 1, 0)
    grad_gate = grad_hidden * up_pre * sigmoid * (1.0 + gate_pre * (1.0 - sigmoid))
    grad_pair = jnp.concatenate([grad_gate, grad_hidden * activated], 1).astype(bf16)
    grad_gu = mm(normed_two, grad_pair, 0, 0).astype(bf16)
    second_cores = jnp.concatenate([grad_gu, grad_down], 1).reshape(16, 2, 2 * rows, 3 * fq)
    core = lax.axis_index("c")
    arriving = lax.ppermute(
        lax.dynamic_index_in_dim(second_cores, 1 - core, 1, False), "c", [(0, 1), (1, 0)]
    )
    second_parts = mm(grad_pair, w_gu, 1, 1).astype(bf16)
    second_chip = (
        lax.dynamic_index_in_dim(second_cores, core, 1, False).astype(f32) + arriving.astype(f32)
    ).astype(bf16)
    second_parts, second_chip = lax.optimization_barrier((second_parts, second_chip))
    second_sums = lax.psum_scatter(
        second_chip.reshape(width // 2, 3 * fq), ("z", "x"), scatter_dimension=0, tiled=True
    )
    grad_resid, second_terms, resid_rows = second_norm_back(
        second_parts, cotangent, unit_two, scale_two, norm_table[2:]
    )

    grad_mix = mm(resid_rows, w_out, 1, 0).astype(bf16).reshape(2, length, heads, HEAD_DIM)
    grad_out = mm(resid_rows, head_mix, 0, 0).astype(bf16)
    grad_soft = jnp.einsum("bshd,bthd->bhst", grad_mix, value_heads, preferred_element_type=f32)
    row_dot = jnp.sum(grad_soft * soft, -1, keepdims=True)
    grad_score = (soft * (grad_soft - row_dot)).astype(bf16)
    grad_query = (
        jnp.einsum("bhst,bthd->bshd", grad_score, key_heads, preferred_element_type=f32) * SCALE
    )
    grad_key = (
        jnp.einsum("bhst,bshd->bthd", grad_score, queries, preferred_element_type=f32) * SCALE
    )
    grad_value = jnp.einsum("bhst,bshd->bthd", soft_low, grad_mix, preferred_element_type=f32)
    grad_proj = jnp.concatenate(
        [
            rotate(grad_query, cosine, -sine).reshape(2 * length, hq),
            rotate(grad_key, cosine, -sine).reshape(2 * length, hq),
            grad_value.reshape(2 * length, hq),
        ],
        1,
    ).astype(bf16)
    grad_qkv = mm(normed_one, grad_proj, 0, 0).astype(bf16)
    first_parts = mm(grad_proj, w_qkv, 1, 1)
    gain_one = jnp.sum(first_parts * unit_rows, 0)
    shift_one = jnp.sum(first_parts, 0)
    grad_bias = jnp.sum(grad_proj.astype(f32), 0).reshape(3 * heads, HEAD_DIM).T
    norm_terms = jnp.concatenate([jnp.stack([gain_one, shift_one]), second_terms], 0).T
    grad_extra = jnp.pad(norm_terms, ((0, 0), (0, EXTRA - 4))) + jnp.pad(
        grad_bias[:, None, :], ((0, 0), (0, rows - 1), (8, EXTRA - 8 - 3 * heads))
    ).reshape(width, EXTRA)
    grad_first = jnp.concatenate([grad_qkv, grad_out, grad_extra.astype(bf16)], 1)
    first_back, grad_input, mixed = last_sum(
        grad_first,
        first_parts.astype(bf16),
        mixed_parts,
        grad_resid,
        unit_one,
        scale_one,
        norm_table[:2],
        first_sum,
    )

    second_back = from_quarters(second_sums)
    gu_back, down_back = second_back[:, :, : 2 * fq], second_back[:, :, 2 * fq :]
    out_down = down_back.transpose(0, 2, 1).reshape(2 * fq, rows).astype(f32)
    out_gu = (
        gu_back.reshape(2, rows, 2, fq).transpose(2, 1, 0, 3).reshape(2, rows, 2 * fq).astype(f32)
    )
    out_qkv = (
        first_back[:, :, : 3 * hq]
        .reshape(2, rows, 3, hq)
        .transpose(2, 1, 0, 3)
        .reshape(3, rows, 2 * hq)
        .astype(f32)
    )
    out_out = (
        first_back[:, :, 3 * hq : 4 * hq].transpose(0, 2, 1).reshape(2 * hq, rows).astype(f32)
    )
    extra_back = first_back[:, :, 4 * hq :].astype(f32)
    out_bias = (
        extra_back[:, 0, 8 : 8 + 3 * heads]
        .reshape(2, 3, heads)
        .transpose(1, 0, 2)
        .reshape(3, 2 * heads, 1)
    )
    norm_back = (extra_back[0, :, :4] + extra_back[1, :, :4]).T.reshape(4, 2, rows // 2)
    mine = lax.dynamic_index_in_dim(norm_back, yh, 1, False)
    theirs = lax.dynamic_index_in_dim(norm_back, 1 - yh, 1, False)
    out_norm = mine + lax.ppermute(theirs, "yh", [(0, 1), (1, 0)])
    return (mixed, grad_input, out_norm, out_qkv, out_bias, out_out, out_gu, out_down)


def solution(mesh):
    grid = Mesh(mesh.devices.reshape(4, 4, 2, 2, 2), GRID)
    placed = (
        P(GRID, None),
        P(GRID, None),
        P(None, GRID),
        P(None, ROWS, "yh"),
        P(None, "yh", ROWS),
        P("yh", ROWS),
        P(None, ROWS, "yh"),
        P("yh", ROWS),
    )
    return jax.shard_map(
        shards,
        mesh=grid,
        in_specs=placed,
        out_specs=(
            P(GRID, None),
            P(GRID, None),
            P(None, GRID),
            P(None, ROWS, "yh"),
            P(None, "yh", ROWS),
            P("yh", ROWS),
            P(None, ROWS, "yh"),
            P("yh", ROWS),
        ),
        check_vma=False,
    )
```

```python
import functools

import jax
import jax.numpy as jnp
import numpy as np
from jax import lax
from jax.experimental import pallas as pl
from jax.experimental.pallas import tpu as pltpu
from jax.sharding import Mesh
from jax.sharding import PartitionSpec as P

HEAD_DIM = 64
ROTARY = 16
EPSILON = 1e-05
SCALE = 0.125

GRID = ("z", "x", "yl", "c", "yh")
ROWS = ("z", "x", "yl", "c")
EXTRA = 128

bf16 = jnp.bfloat16
f32 = jnp.float32

MESH = pl.DeviceIdType.MESH
VMEM = pltpu.VMEM
DMA = pltpu.SemaphoreType.DMA
VMEM_LIMIT = 60 * 1024 * 1024


def at_y(k):
    y = (lax.axis_index("yh") * 2 + lax.axis_index("yl") + k) % 4
    return {"yl": y % 2, "yh": y // 2}


def at_z(k):
    return {"z": (lax.axis_index("z") + k) % 4}


def at_x(k):
    return {"x": (lax.axis_index("x") + k) % 4}


def sibling():
    return {"c": 1 - lax.axis_index("c")}


def greet(devices):
    barrier = pltpu.get_barrier_semaphore()
    for device in devices:
        pl.semaphore_signal(barrier, inc=1, device_id=device, device_id_type=MESH)
    pl.semaphore_wait(barrier, len(devices))


def remote(src, dst, sems, index, device):
    send, recv = sems
    return pltpu.make_async_remote_copy(
        src_ref=src,
        dst_ref=dst,
        send_sem=send.at[index],
        recv_sem=recv.at[index],
        device_id=device,
        device_id_type=MESH,
    )


def ring_sum(parts, mid, sent, far, near, sems):
    started = ring_sum_start(parts, mid, near, sems, 0)
    middle = ring_sum_middle(parts, started, mid, sent, far, sems, 0)
    return ring_sum_finish(parts, started, middle, far, near), started + middle


def ring_gather_half(out, top, sems, base):
    here = out.shape[0] // 4
    half = here // 2
    copies = []
    for way, step, block in ((0, 1, 3), (1, -1, 2)):
        copies.append(
            remote(
                out.at[pl.ds(top * half, half)],
                out.at[pl.ds(block * here + top * half, half)],
                sems,
                base + 2 * way + top,
                at_y(step),
            )
        )
        copies[-1].start()
    return copies


def ring_gather_pass(out, halves, sems, base):
    here = out.shape[0] // 4
    half = here // 2
    passed = []
    for way, step, block in ((0, 1, 3), (1, -1, 2)):
        halves[way][way].wait_recv()
        passed.append(
            remote(
                out.at[pl.ds(block * here + way * half, half)],
                out.at[pl.ds(here + way * half, half)],
                sems,
                base + 4 + way,
                at_y(step),
            )
        )
        passed[-1].start()
    return passed


def second_norm_kernel(parts, tokens, gains, summed, unit, scale, normed, mid, sent, far, near, send, recv):
    sems = (send, recv)
    greet([at_y(1), at_y(3)])
    finish, copies = ring_sum(parts, mid, sent, far, near, sems)
    half = tokens.shape[0] // 2
    halves = []
    for top in range(2):
        rows = pl.ds(top * half, half)
        total = tokens[rows].astype(f32) + finish(top)
        summed[rows] = total
        centered = total - jnp.mean(total, -1, keepdims=True)
        inverse = lax.rsqrt(jnp.mean(centered * centered, -1, keepdims=True) + EPSILON)
        unit_rows = centered * inverse
        unit[rows] = unit_rows
        scale[rows] = inverse
        normed[rows] = (unit_rows * gains[0:1] + gains[1:2]).astype(bf16)
        halves.append(ring_gather_half(normed, top, sems, 6))
    passed = ring_gather_pass(normed, halves, sems, 6)
    for copy in passed + [halves[1][0], halves[0][1]]:
        copy.wait_recv()
    for copy in copies + halves[0] + halves[1] + passed:
        copy.wait_send()


def second_norm(parts, tokens, gains):
    here, width = tokens.shape
    half = here // 2
    full = pl.BlockSpec(memory_space=VMEM)
    return pl.pallas_call(
        second_norm_kernel,
        out_shape=(
            jax.ShapeDtypeStruct((here, width), f32),
            jax.ShapeDtypeStruct((here, width), f32),
            jax.ShapeDtypeStruct((here, 1), f32),
            jax.ShapeDtypeStruct((4 * here, width), bf16),
        ),
        in_specs=[full] * 3,
        out_specs=(full,) * 4,
        scratch_shapes=[VMEM((2, half, width), bf16)] * 4 + [DMA((12,)), DMA((12,))],
        compiler_params=pltpu.CompilerParams(
            collective_id=1, has_side_effects=True, vmem_limit_bytes=VMEM_LIMIT
        ),
    )(parts, tokens, gains)


def pair_moves():
    yl, c = lax.axis_index("yl"), lax.axis_index("c")
    return {"yl": c, "c": yl}, {"yl": 1 - c, "c": yl}


def diagonal():
    return {"yl": 1 - lax.axis_index("yl"), "c": 1 - lax.axis_index("c")}


def everyone_near():
    return [at_z(1), at_z(3), at_x(1), at_x(3), at_y(1), at_y(3), sibling(), diagonal()]


def stay_or_go(src, dst, sems, index, device, local_sem):
    yl, c = lax.axis_index("yl"), lax.axis_index("c")

    @pl.when(yl == c)
    def _():
        pltpu.make_async_copy(src, dst, local_sem).start()

    @pl.when(yl != c)
    def _():
        remote(src, dst, sems, index, device).start()


def stay_or_go_wait(src, dst, sems, index, device, local_sem):
    yl, c = lax.axis_index("yl"), lax.axis_index("c")

    @pl.when(yl == c)
    def _():
        pltpu.make_async_copy(src, dst, local_sem).wait()

    @pl.when(yl != c)
    def _():
        copy = remote(src, dst, sems, index, device)
        copy.wait_recv()
        copy.wait_send()


def first_gather_kernel(
    one_q, two_q, tokens, cotangent, one, two, token_rows, cot_rows,
    pair_send, pair_recv, local_sem, y_send, y_recv, send, recv, core_send, core_recv,
):
    z, x = lax.axis_index("z"), lax.axis_index("x")
    yl, c = lax.axis_index("yl"), lax.axis_index("c")
    pair_sems, y_sems, sems, core_sems = (
        (pair_send, pair_recv),
        (y_send, y_recv),
        (send, recv),
        (core_send, core_recv),
    )
    rows = one_q.shape[1]
    here = tokens.shape[0]
    piece = rows // 2
    same, cross = pair_moves()
    token_rows[pl.ds(0, here)] = tokens[...]
    cot_rows[pl.ds(0, here)] = cotangent[...]
    greet(everyone_near())

    def start_of(dz, dx, half):
        return (((z + dz) % 4) * 4 + (x + dx) % 4) * 4 * rows + c * 2 * rows + half * rows

    target = ((z * 4 + x) * 4 + yl * 2 + c) * rows
    moves = [
        (one_q.at[c], one.at[pl.ds(target, rows)], 0, same),
        (one_q.at[1 - c], one.at[pl.ds(target, rows)], 1, cross),
        (two_q.at[c], two.at[pl.ds(c * rows, rows)], 2, same),
        (two_q.at[1 - c], two.at[pl.ds(c * rows, rows)], 3, cross),
    ]

    def launch(k):
        src, dst, index, device = moves[k]
        if device is same:
            stay_or_go(src, dst, pair_sems, index, device, local_sem.at[index // 2])
        else:
            remote(src, dst, pair_sems, index, device).start()

    def land(k):
        src, dst, index, device = moves[k]
        if device is same:
            stay_or_go_wait(src, dst, pair_sems, index, device, local_sem.at[index // 2])
        else:
            copy = remote(src, dst, pair_sems, index, device)
            copy.wait_recv()
            copy.wait_send()

    launch(0)
    launch(1)
    y_halves = {}
    y_passed = {}
    for top in range(2):
        y_halves[0, top] = ring_gather_half(token_rows, top, y_sems, 0)
    land(0)
    land(1)

    done = []

    def index_of(half, df, dg, part):
        return ((half * 4 + df % 4) * 4 + dg % 4) * 2 + part

    def block(half, df, dg):
        return start_of(df, dg, half) if half == 0 else start_of(dg, df, half)

    def push(half, df, dg, axis, step, part):
        along_z = (half == 0) == (axis == 0)
        device = at_z(step) if along_z else at_x(step)
        to = (df - step, dg) if axis == 0 else (df, dg - step)
        rng = pl.ds(block(half, df, dg) + part * piece, piece)
        copy = remote(one.at[rng], one.at[rng], sems, index_of(half, *to, part), device)
        copy.start()
        done.append(copy)

    def arrived(half, df, dg, part):
        rng = pl.ds(block(half, df, dg) + part * piece, piece)
        remote(one.at[rng], one.at[rng], sems, index_of(half, df, dg, part), at_z(1)).wait_recv()

    def to_sibling(half, df, dg):
        rng = pl.ds(block(half, df, dg), rows)
        copy = remote(
            one.at[rng], one.at[rng], core_sems, (half * 4 + df % 4) * 4 + dg % 4, sibling()
        )
        copy.start()
        done.append(copy)
        core.append(copy)

    core = []
    for axis in range(2):
        for half in range(2):
            for part in range(2):
                push(half, 0, 0, axis, 1, part)
                push(half, 0, 0, axis, -1, 1 - part)
    launch(2)
    launch(3)
    for half in range(2):
        to_sibling(half, 0, 0)
    for half in range(2):
        arrived(half, 3, 0, 0)
        push(half, 3, 0, 0, 1, 0)
        arrived(half, 1, 0, 1)
        push(half, 1, 0, 0, -1, 1)
    for half in range(2):
        arrived(half, 3, 0, 1)
        arrived(half, 1, 0, 0)
        for df in (3, 1):
            for part in range(2):
                push(half, df, 0, 1, 1, part)
                push(half, df, 0, 1, -1, 1 - part)
            to_sibling(half, df, 0)
    y_passed[0] = ring_gather_pass(token_rows, [y_halves[0, 0], y_halves[0, 1]], y_sems, 0)
    for top in range(2):
        y_halves[1, top] = ring_gather_half(cot_rows, top, y_sems, 6)

    def second_axis(df):
        for half in range(2):
            arrived(half, df, 3, 0)
            push(half, df, 3, 1, 1, 0)
            arrived(half, df, 1, 1)
            push(half, df, 1, 1, -1, 1)
        for half in range(2):
            arrived(half, df, 3, 1)
            to_sibling(half, df, 3)
            arrived(half, df, 1, 0)
            to_sibling(half, df, 1)

    second_axis(0)
    for half in range(2):
        arrived(half, 2, 0, 0)
        arrived(half, 2, 0, 1)
        for part in range(2):
            push(half, 2, 0, 1, 1, part)
            push(half, 2, 0, 1, -1, 1 - part)
        to_sibling(half, 2, 0)
    second_axis(3)
    second_axis(1)
    y_passed[1] = ring_gather_pass(cot_rows, [y_halves[1, 0], y_halves[1, 1]], y_sems, 6)
    second_axis(2)
    for df in (0, 3, 1, 2):
        for half in range(2):
            for part in range(2):
                arrived(half, df, 2, part)
            to_sibling(half, df, 2)
    land(2)
    land(3)
    for which in range(2):
        for copy in y_passed[which] + [y_halves[which, 1][0], y_halves[which, 0][1]]:
            copy.wait_recv()
        for copy in y_passed[which] + y_halves[which, 0] + y_halves[which, 1]:
            copy.wait_send()
    for copy in core:
        copy.wait_recv()
    for copy in done:
        copy.wait_send()


def first_gather(one_q, two_q, tokens, cotangent):
    rows = one_q.shape[1]
    here, width = tokens.shape
    anywhere = pl.BlockSpec(memory_space=pl.ANY)
    full = pl.BlockSpec(memory_space=VMEM)
    return pl.pallas_call(
        first_gather_kernel,
        out_shape=(
            jax.ShapeDtypeStruct((64 * rows, one_q.shape[2]), bf16),
            jax.ShapeDtypeStruct((2 * rows, two_q.shape[2]), bf16),
            jax.ShapeDtypeStruct((4 * here, width), bf16),
            jax.ShapeDtypeStruct((4 * here, width), bf16),
        ),
        in_specs=[full] * 4,
        out_specs=(anywhere, anywhere, full, full),
        scratch_shapes=[
            DMA((4,)), DMA((4,)), DMA((2,)), DMA((12,)), DMA((12,)),
            DMA((64,)), DMA((64,)), DMA((32,)), DMA((32,)),
        ],
        compiler_params=pltpu.CompilerParams(
            collective_id=0, has_side_effects=True, vmem_limit_bytes=VMEM_LIMIT
        ),
    )(one_q, two_q, tokens, cotangent)


def last_sum_kernel(
    grads, first_parts, mixed_parts, resid, tokens, stats, gains, first_sum,
    result, grad_tokens, mixed,
    sib, mid, sent, far, near, stage, mid2, sent2, far2, near2, packed,
    ymid, ysent, yfar, ynear,
    core_send, core_recv, send, recv, send2, recv2, pair_send, pair_recv, local_sem, y_send, y_recv,
):
    z, x = lax.axis_index("z"), lax.axis_index("x")
    yl, c = lax.axis_index("yl"), lax.axis_index("c")
    core_sems, sems, sems2, pair_sems, y_sems = (
        (core_send, core_recv),
        (send, recv),
        (send2, recv2),
        (pair_send, pair_recv),
        (y_send, y_recv),
    )
    rows = result.shape[1]
    piece = rows // 2
    greet(everyone_near())
    done = []

    def begin(copy):
        copy.start()
        done.append(copy)
        return copy

    def start_of(dz, dx, core):
        return (((z + dz) % 4) * 4 + (x + dx) % 4) * 4 * rows + core * 2 * rows

    order = []
    for d in (2, 1, 3, 0):
        for e in (2, 1, 3, 0):
            for pair in ((d, e), (e, d)):
                if pair not in order:
                    order.append(pair)
    core = {}
    for dz, dx in order:
        core[dz, dx] = begin(
            remote(
                grads.at[pl.ds(start_of(dz, dx, 1 - c), 2 * rows)],
                sib.at[dz, dx],
                core_sems,
                dz * 4 + dx,
                sibling(),
            )
        )
    y_jobs = [
        ring_sum_start(first_parts, ymid.at[0], ynear.at[0], y_sems, 0),
        ring_sum_start(mixed_parts, ymid.at[1], ynear.at[1], y_sems, 6),
    ]
    summed = set()

    def core_sum(dz, dx):
        if (dz, dx) in summed:
            return
        summed.add((dz, dx))
        core[dz, dx].wait_recv()
        sib[dz, dx] = (
            sib[dz, dx].astype(f32)
            + grads[pl.ds(start_of(dz, dx, c), 2 * rows)].astype(f32)
        ).astype(bf16)

    def view(half, df, part):
        rng = pl.ds(half * rows + part * piece, piece)
        return sib.at[df, :, rng] if half == 0 else sib.at[:, df, rng]

    def device(half, axis, step):
        return at_z(step) if (half == 0) == (axis == 0) else at_x(step)

    def ring_first(half, axis, src, mids, nears, some_sems):
        base = half * 6
        got = {}
        for way, step in ((0, 1), (1, -1)):
            got["first", way] = begin(
                remote(src(2, way), mids.at[half, way], some_sems, base + way, device(half, axis, step))
            )
        return got

    def ring_second(half, axis, src, nears, some_sems, got):
        base = half * 6
        for way, step in ((0, 1), (1, -1)):
            got["second", way] = begin(
                remote(
                    src(step % 4, 1 - way), nears.at[half, way], some_sems, base + 2 + way,
                    device(half, axis, step),
                )
            )

    def ring_third(half, axis, src, mids, sents, fars, some_sems, got):
        base = half * 6
        for way, step in ((0, 1), (1, -1)):
            got["first", way].wait_recv()
            sents[half, way] = (
                src(step % 4, way)[...].astype(f32) + mids[half, way].astype(f32)
            ).astype(bf16)
            got["third", way] = begin(
                remote(
                    sents.at[half, way], fars.at[half, way], some_sems, base + 4 + way,
                    device(half, axis, step),
                )
            )

    def ring_last(half, part, src, fars, nears, got):
        got["third", part].wait_recv()
        got["second", 1 - part].wait_recv()
        return (
            src(0, part)[...].astype(f32)
            + fars[half, part].astype(f32)
            + nears[half, 1 - part].astype(f32)
        )

    got = {}
    sources = [functools.partial(view, half) for half in range(2)]
    for half in range(2):
        for d in (2, 1, 3, 0):
            core_sum(*((2, d) if half == 0 else (d, 2)))
        got[half] = ring_first(half, 0, sources[half], mid, near, sems)
    for half in range(2):
        for step in (1, 3):
            for d in (2, 1, 3, 0):
                core_sum(*((step, d) if half == 0 else (d, step)))
        ring_second(half, 0, sources[half], near, sems, got[half])
    y_more = [
        ring_sum_middle(first_parts, y_jobs[0], ymid.at[0], ysent.at[0], yfar.at[0], y_sems, 0)
    ]
    for half in range(2):
        ring_third(half, 0, sources[half], mid, sent, far, sems, got[half])
    core_sum(0, 0)
    y_more.append(
        ring_sum_middle(mixed_parts, y_jobs[1], ymid.at[1], ysent.at[1], yfar.at[1], y_sems, 6)
    )
    finish = ring_sum_finish(first_parts, y_jobs[0], y_more[0], yfar.at[0], ynear.at[0])
    here = grad_tokens.shape[0] // 2
    for top in range(2):
        rng = pl.ds(top * here, here)
        incoming = finish(top) * gains[0:1]
        inverse = stats[1, rng]
        unit_rows = (tokens[rng].astype(f32) - stats[0, rng]) * inverse
        grad_tokens[rng] = resid[rng] + inverse * (
            incoming
            - jnp.mean(incoming, -1, keepdims=True)
            - unit_rows * jnp.mean(incoming * unit_rows, -1, keepdims=True)
        )
    for half in range(2):
        for part in range(2):
            stage[half, :, part * piece : (part + 1) * piece] = ring_last(
                half, part, sources[half], far, near, got[half]
            ).astype(bf16)

    def stage_view(half, dg, part):
        return stage.at[half, dg, pl.ds(part * piece, piece)]

    sources = [functools.partial(stage_view, half) for half in range(2)]
    got = {}
    for half in range(2):
        got[half] = ring_first(half, 1, sources[half], mid2, near2, sems2)
    for half in range(2):
        ring_second(half, 1, sources[half], near2, sems2, got[half])
    for half in range(2):
        ring_third(half, 1, sources[half], mid2, sent2, far2, sems2, got[half])
    finish = ring_sum_finish(mixed_parts, y_jobs[1], y_more[1], yfar.at[1], ynear.at[1])
    for top in range(2):
        rng = pl.ds(top * here, here)
        mixed[rng] = (first_sum[rng] + finish(top)).astype(bf16)
    for half in range(2):
        for part in range(2):
            packed[half, part * piece : (part + 1) * piece] = ring_last(
                half, part, sources[half], far2, near2, got[half]
            ).astype(bf16)

    home, away = {"yl": c, "c": yl}, {"yl": c, "c": 1 - yl}
    stay_or_go(packed.at[yl], result.at[yl], pair_sems, 0, home, local_sem)
    cross = remote(packed.at[1 - yl], result.at[yl], pair_sems, 1, away)
    cross.start()
    cross.wait_recv()
    cross.wait_send()
    stay_or_go_wait(packed.at[yl], result.at[yl], pair_sems, 0, home, local_sem)
    for jobs in y_jobs + y_more:
        for copy in jobs:
            copy.wait_send()
    for copy in done:
        copy.wait_send()


def ring_sum_start(parts, mid, near, sems, base):
    here = parts.shape[0] // 4
    half = here // 2
    copies = []
    for way, step in ((0, 1), (1, -1)):
        copies.append(
            remote(
                parts.at[pl.ds(here + way * half, half)], mid.at[way], sems, base + way, at_y(step)
            )
        )
    for way, step, block in ((0, 1, 2), (1, -1, 3)):
        copies.append(
            remote(
                parts.at[pl.ds(block * here + (1 - way) * half, half)],
                near.at[way],
                sems,
                base + 2 + way,
                at_y(step),
            )
        )
    for copy in copies:
        copy.start()
    return copies


def ring_sum_middle(parts, started, mid, sent, far, sems, base):
    here = parts.shape[0] // 4
    half = here // 2
    copies = []
    for way, step, block in ((0, 1, 2), (1, -1, 3)):
        started[way].wait_recv()
        sent[way] = (
            parts[pl.ds(block * here + way * half, half)].astype(f32) + mid[way].astype(f32)
        ).astype(bf16)
        copies.append(remote(sent.at[way], far.at[way], sems, base + 4 + way, at_y(step)))
        copies[-1].start()
    return copies


def ring_sum_finish(parts, started, middle, far, near):
    half = parts.shape[0] // 8

    def finish(top):
        started[2 + 1 - top].wait_recv()
        middle[top].wait_recv()
        return (
            parts[pl.ds(top * half, half)].astype(f32)
            + far[top].astype(f32)
            + near[1 - top].astype(f32)
        )

    return finish


def last_sum(grads, first_parts, mixed_parts, resid, tokens, stats, gains, first_sum):
    rows = grads.shape[0] // 64
    wide = grads.shape[1]
    here, width = resid.shape
    full = pl.BlockSpec(memory_space=VMEM)
    piece = rows // 2
    return pl.pallas_call(
        last_sum_kernel,
        out_shape=(
            jax.ShapeDtypeStruct((2, rows, wide), bf16),
            jax.ShapeDtypeStruct((here, width), f32),
            jax.ShapeDtypeStruct((here, width), bf16),
        ),
        in_specs=[full] * 8,
        out_specs=(full,) * 3,
        scratch_shapes=[
            VMEM((4, 4, 2 * rows, wide), bf16),
            VMEM((2, 2, 4, piece, wide), bf16),
            VMEM((2, 2, 4, piece, wide), bf16),
            VMEM((2, 2, 4, piece, wide), bf16),
            VMEM((2, 2, 4, piece, wide), bf16),
            VMEM((2, 4, rows, wide), bf16),
            VMEM((2, 2, piece, wide), bf16),
            VMEM((2, 2, piece, wide), bf16),
            VMEM((2, 2, piece, wide), bf16),
            VMEM((2, 2, piece, wide), bf16),
            VMEM((2, rows, wide), bf16),
            VMEM((2, 2, here // 2, width), bf16),
            VMEM((2, 2, here // 2, width), bf16),
            VMEM((2, 2, here // 2, width), bf16),
            VMEM((2, 2, here // 2, width), bf16),
            DMA((16,)), DMA((16,)), DMA((12,)), DMA((12,)), DMA((12,)), DMA((12,)),
            DMA((2,)), DMA((2,)), DMA, DMA((12,)), DMA((12,)),
        ],
        compiler_params=pltpu.CompilerParams(
            collective_id=3, has_side_effects=True, vmem_limit_bytes=VMEM_LIMIT
        ),
    )(grads, first_parts, mixed_parts, resid, tokens, stats, gains, first_sum)


def tables():
    half = ROTARY // 2
    position = np.arange(256, dtype=np.float32)
    frequency = np.power(np.float32(10000.0), -np.arange(half, dtype=np.float32) * np.float32(2.0 / ROTARY))
    angles = position[:, None] * frequency[None, :].astype(np.float32)
    cosine, sine = np.cos(angles), np.sin(angles)
    own = np.ones((256, 2, HEAD_DIM), np.float32)
    up = np.zeros((256, 2, HEAD_DIM), np.float32)
    down = np.zeros((256, 2, HEAD_DIM), np.float32)
    for head in range(2):
        own[:, head, :half] = cosine
        own[:, head, half:ROTARY] = cosine
        up[:, head, :half] = -sine
        down[:, head, half:ROTARY] = sine
    return np.concatenate([a.reshape(256, 128) for a in (own, up, down)], 1)


def dot(a, b, ca, cb):
    return lax.dot_general(a, b, (((ca,), (cb,)), ((), ())), preferred_element_type=f32)


def turn_heads(value, table, sign):
    own, up, down = table[:, :128], table[:, 128:256], table[:, 256:]
    return value * own + sign * (
        pltpu.roll(value, 120, 1) * up + pltpu.roll(value, 8, 1) * down
    )


def half_of_place(place):
    y = lax.axis_index("yh") * 2 + lax.axis_index("yl")
    return ((y + (0, 2, 1, 3)[place]) % 4) // 2


def causal_mask(sequence, here):
    length = 2 * here
    first = half_of_place(2 * sequence)

    def position(dim):
        index = lax.broadcasted_iota(jnp.int32, (length, length), dim)
        return jnp.where(index < here, index + first * here, index - first * here)

    return position(0) >= position(1)


def soft_of(queries, keys, mask):
    scores = dot(queries, keys, 1, 1) * SCALE
    scores = jnp.where(mask, scores, -1000000000.0)
    powers = jnp.exp(scores - jnp.max(scores, -1, keepdims=True))
    return powers * (1.0 / jnp.sum(powers, -1, keepdims=True))


def read_extras(one, first_column, norm_table, bias):
    total = None
    for group in range(one.shape[0] // 128):
        block = one[pl.ds(group * 128, 128), pl.ds(first_column, 128)].astype(f32)
        block = block[0:32] + block[32:64] + block[64:96] + block[96:128]
        norm_table[:, pl.ds(group * 128, 128)] = block[12:16] + block[16:20]
        total = block[0:12] if total is None else total + block[0:12]
    bias[...] = total


def attention_forward_kernel(token_rows, one, table, normed, stats, qkv, head_mix, parts, norm_table, bias):
    here = token_rows.shape[0] // 4
    hq = head_mix.shape[1]
    read_extras(one, 4 * hq, norm_table, bias)

    def norm_rows(k, _):
        rng = pl.ds(pl.multiple_of(k * here, here), here)
        values = token_rows[rng].astype(f32)
        mean = jnp.mean(values, -1, keepdims=True)
        centered = values - mean
        inverse = lax.rsqrt(jnp.mean(centered * centered, -1, keepdims=True) + EPSILON)
        stats[0, rng] = mean
        stats[1, rng] = inverse
        normed[rng] = (centered * inverse * norm_table[0:1] + norm_table[1:2]).astype(bf16)
        return 0

    lax.fori_loop(0, 4, norm_rows, 0)
    wide = 256

    def project(k, _):
        cols = pl.ds(pl.multiple_of(k * wide, wide), wide)
        value = dot(normed[...], one[:, cols], 1, 0)
        shift = jnp.concatenate(
            [bias[pl.ds(2 * k, 1)], bias[pl.ds(2 * k + 1, 1)]], 1
        )
        value = value + shift

        @pl.when(k < 2 * hq // wide)
        def _():
            for place in range(4):
                rng = pl.ds(place * here, here)
                turn = table[pl.ds(pl.multiple_of(half_of_place(place) * here, here), here)]
                for pair in range(wide // 128):
                    qkv[rng, pl.ds(pl.multiple_of(k * wide + pair * 128, 128), 128)] = turn_heads(
                        value[place * here : (place + 1) * here, pair * 128 : (pair + 1) * 128],
                        turn,
                        1.0,
                    ).astype(bf16)

        @pl.when(k >= 2 * hq // wide)
        def _():
            qkv[:, cols] = value.astype(bf16)

        return 0

    lax.fori_loop(0, 3 * hq // wide, project, 0)
    for sequence in range(2):
        mask = causal_mask(sequence, here)
        rng = pl.ds(sequence * 2 * here, 2 * here)

        def heads(k, _):
            def pair(t):
                return qkv[rng, pl.ds(pl.multiple_of(t * hq + k * 128, 128), 128)]

            q, key, value = pair(0), pair(1), pair(2)
            mixes = []
            for head in range(2):
                cut = slice(head * HEAD_DIM, (head + 1) * HEAD_DIM)
                soft = soft_of(q[:, cut], key[:, cut], mask).astype(bf16)
                mixes.append(dot(soft, value[:, cut], 1, 0))
            head_mix[rng, pl.ds(pl.multiple_of(k * 128, 128), 128)] = jnp.concatenate(
                mixes, 1
            ).astype(bf16)
            return 0

        lax.fori_loop(0, hq // 128, heads, 0)

    def out_project(k, _):
        rng = pl.ds(pl.multiple_of(k * wide, wide), wide)
        parts[:, rng] = dot(head_mix[...], one[rng, pl.ds(3 * hq, hq)], 1, 1).astype(bf16)
        return 0

    lax.fori_loop(0, one.shape[0] // wide, out_project, 0)


def attention_forward(token_rows, one, table):
    tokens, width = token_rows.shape
    hq = (one.shape[1] - EXTRA) // 4
    full = pl.BlockSpec(memory_space=VMEM)
    return pl.pallas_call(
        attention_forward_kernel,
        out_shape=(
            jax.ShapeDtypeStruct((tokens, width), bf16),
            jax.ShapeDtypeStruct((2, tokens, 1), f32),
            jax.ShapeDtypeStruct((tokens, 3 * hq), bf16),
            jax.ShapeDtypeStruct((tokens, hq), bf16),
            jax.ShapeDtypeStruct((tokens, width), bf16),
            jax.ShapeDtypeStruct((4, width), f32),
        ),
        in_specs=[full] * 3,
        out_specs=(full,) * 6,
        scratch_shapes=[VMEM((12, 128), f32)],
        compiler_params=pltpu.CompilerParams(vmem_limit_bytes=VMEM_LIMIT),
    )(token_rows, one, table)


def attention_backward_kernel(
    resid, one, normed, stats, qkv, head_mix, token_rows, table, second_terms,
    grads, first_parts, grad_mix, grad_proj,
):
    here = resid.shape[0] // 4
    hq = head_mix.shape[1]
    wide = 256

    def mix_back(k, _):
        cols = pl.ds(pl.multiple_of(k * wide, wide), wide)
        grad_mix[:, cols] = dot(
            resid[...], one[:, pl.ds(pl.multiple_of(3 * hq + k * wide, wide), wide)], 1, 0
        ).astype(bf16)
        return 0

    lax.fori_loop(0, hq // wide, mix_back, 0)

    def out_back(k, _):
        rng = pl.ds(pl.multiple_of(k * wide, wide), wide)
        grads[rng, pl.ds(3 * hq, hq)] = dot(resid[:, rng], head_mix[...], 0, 0).astype(bf16)
        return 0

    lax.fori_loop(0, one.shape[0] // wide, out_back, 0)
    for sequence in range(2):
        mask = causal_mask(sequence, here)
        rng = pl.ds(sequence * 2 * here, 2 * here)
        turn = jnp.concatenate(
            [
                table[pl.ds(pl.multiple_of(half_of_place(2 * sequence + k) * here, here), here)]
                for k in range(2)
            ],
            0,
        )

        def heads(k, _):
            def pair(t):
                return pl.ds(pl.multiple_of(t * hq + k * 128, 128), 128)

            q, key, value = qkv[rng, pair(0)], qkv[rng, pair(1)], qkv[rng, pair(2)]
            mix = grad_mix[rng, pair(0)]
            results = ([], [], [])
            for head in range(2):
                cut = slice(head * HEAD_DIM, (head + 1) * HEAD_DIM)
                soft = soft_of(q[:, cut], key[:, cut], mask)
                grad_soft = dot(mix[:, cut], value[:, cut], 1, 1)
                row_dot = jnp.sum(grad_soft * soft, -1, keepdims=True)
                grad_score = (soft * (grad_soft - row_dot)).astype(bf16)
                results[0].append(dot(grad_score, key[:, cut], 1, 0) * SCALE)
                results[1].append(dot(grad_score, q[:, cut], 0, 0) * SCALE)
                results[2].append(dot(soft.astype(bf16), mix[:, cut], 0, 0))
            for t in range(3):
                both = jnp.concatenate(results[t], 1)
                if t < 2:
                    both = turn_heads(both, turn, -1.0)
                grad_proj[rng, pair(t)] = both.astype(bf16)
            return 0

        lax.fori_loop(0, hq // 128, heads, 0)

    bias_rows = [
        jnp.sum(grad_proj[:, pl.ds(k * 128, 128)].astype(f32), 0, keepdims=True)
        for k in range(3 * hq // 128)
    ]
    mean, inverse = stats[0], stats[1]

    def weights_back(k, _):
        rng = pl.ds(pl.multiple_of(k * wide, wide), wide)
        grads[rng, pl.ds(0, 3 * hq)] = dot(normed[:, rng], grad_proj[...], 0, 0).astype(bf16)
        part = dot(grad_proj[...], one[rng, pl.ds(0, 3 * hq)], 1, 1)
        first_parts[:, rng] = part.astype(bf16)
        unit = (token_rows[:, rng].astype(f32) - mean) * inverse
        gain = jnp.sum(part * unit, 0, keepdims=True)
        shift = jnp.sum(part, 0, keepdims=True)
        for tile in range(wide // 128):
            cut = slice(tile * 128, (tile + 1) * 128)
            lanes = pl.ds(pl.multiple_of(k * wide + tile * 128, 128), 128)
            block = jnp.concatenate(
                bias_rows
                + [
                    gain[:, cut],
                    shift[:, cut],
                    second_terms[:, lanes],
                    jnp.zeros((16, 128), f32),
                ],
                0,
            ).astype(bf16)
            for copy in range(4):
                start = pl.multiple_of(k * wide + tile * 128 + copy * 32, 32)
                grads[pl.ds(start, 32), pl.ds(4 * hq, 128)] = block
        return 0

    lax.fori_loop(0, one.shape[0] // wide, weights_back, 0)


def attention_backward(resid, one, normed, stats, qkv, head_mix, token_rows, table, second_terms):
    tokens, width = token_rows.shape
    hq = head_mix.shape[1]
    full = pl.BlockSpec(memory_space=VMEM)
    return pl.pallas_call(
        attention_backward_kernel,
        out_shape=(
            jax.ShapeDtypeStruct(one.shape, bf16),
            jax.ShapeDtypeStruct((tokens, width), bf16),
        ),
        in_specs=[full] * 9,
        out_specs=(full,) * 2,
        scratch_shapes=[VMEM((tokens, hq), bf16), VMEM((tokens, 3 * hq), bf16)],
        compiler_params=pltpu.CompilerParams(vmem_limit_bytes=VMEM_LIMIT),
    )(resid, one, normed, stats, qkv, head_mix, token_rows, table, second_terms)


def feed_forward_kernel(
    normed, cot_rows, cotangent, unit, scale, gains, weights,
    resid, sums, spread, mixed_parts, chip,
    held, pair, hidden, normed_t, cot_t, parts, sib, mid, sent, far, near,
    load_sem, store_sem, core_send, core_recv, y_send, y_recv,
):
    columns, width = held.shape[1] // 3, held.shape[0]
    wide = 256
    rows = sib.shape[1]
    c = lax.axis_index("c")
    y_sems, core_sems = (y_send, y_recv), (core_send, core_recv)
    whole, rest = columns // wide, columns % wide

    def load(k, which, size):
        start = pl.multiple_of(which * columns + k * wide, 128)
        cut = pl.ds(start, size)
        return pltpu.make_async_copy(weights.at[:, cut], held.at[:, cut], load_sem.at[k, which])

    for k in range(whole + (rest > 0)):
        for which in range(3):
            load(k, which, wide if k < whole else rest).start()

    def flip(k, _):
        rng = pl.ds(pl.multiple_of(k * wide, wide), wide)
        normed_t[rng] = normed[:, rng].T
        cot_t[rng] = cot_rows[:, rng].T
        return 0

    lax.fori_loop(0, width // wide, flip, 0)
    greet([at_y(1), at_y(3), sibling()])

    def ahead(k, size):
        def cut(which):
            return pl.ds(pl.multiple_of(which * columns + k * wide, 128), size)

        for which in range(3):
            load(k, which, size).wait()
        gate = dot(normed[...], held[:, cut(0)], 1, 0)
        up = dot(normed[...], held[:, cut(1)], 1, 0)
        grad_hidden = dot(cot_rows[...], held[:, cut(2)], 1, 0)
        sigmoid = jax.nn.sigmoid(gate)
        activated = gate * sigmoid
        hidden[:, cut(0)] = (activated * up).astype(bf16)
        pair[:, cut(0)] = (
            grad_hidden * up * sigmoid * (1.0 + gate * (1.0 - sigmoid))
        ).astype(bf16)
        pair[:, cut(1)] = (grad_hidden * activated).astype(bf16)
        return 0

    lax.fori_loop(0, whole, lambda k, _: ahead(k, wide), 0)
    if rest:
        ahead(whole, rest)

    def second_back(k, _):
        rng = pl.ds(pl.multiple_of(k * wide, wide), wide)
        parts[:, rng] = dot(pair[...], held[rng, pl.ds(0, 2 * columns)], 1, 1).astype(bf16)
        return 0

    lax.fori_loop(0, width // wide, second_back, 0)
    started = ring_sum_start(parts, mid, near, y_sems, 0)

    def mix(k, _):
        rng = pl.ds(pl.multiple_of(k * wide, wide), wide)
        mixed_parts[:, rng] = dot(
            hidden[...], held[rng, pl.ds(2 * columns, columns)], 1, 1
        ).astype(bf16)
        return 0

    lax.fori_loop(0, width // wide, mix, 0)
    middle = ring_sum_middle(parts, started, mid, sent, far, y_sems, 0)

    def to_core(block):
        theirs = pl.ds(pl.multiple_of((2 * block + 1 - c) * rows, rows), rows)
        return remote(held.at[theirs], sib.at[block], core_sems, block, sibling())

    def weights_back(k, _):
        rng = pl.ds(pl.multiple_of(k * wide, wide), wide)
        held[rng, pl.ds(0, 2 * columns)] = dot(normed_t[rng], pair[...], 1, 0).astype(bf16)
        held[rng, pl.ds(2 * columns, columns)] = dot(cot_t[rng], hidden[...], 1, 0).astype(bf16)
        for block in range(wide // (2 * rows)):
            to_core(k * (wide // (2 * rows)) + block).start()
        return 0

    lax.fori_loop(0, width // wide, weights_back, 0)
    finish = ring_sum_finish(parts, started, middle, far, near)
    half = cotangent.shape[0] // 2
    halves = []
    for top in range(2):
        here = pl.ds(top * half, half)
        total = finish(top)
        unit_rows = unit[here]
        incoming = total * gains[0:1]
        result = cotangent[here].astype(f32) + scale[here] * (
            incoming
            - jnp.mean(incoming, -1, keepdims=True)
            - unit_rows * jnp.mean(incoming * unit_rows, -1, keepdims=True)
        )
        resid[here] = result
        spread[here] = result.astype(bf16)
        halves.append(ring_gather_half(spread, top, y_sems, 6))
        both = jnp.concatenate(
            [
                jnp.sum(total * unit_rows, 0, keepdims=True),
                jnp.sum(total, 0, keepdims=True),
            ],
            0,
        )
        sums[...] = both if top == 0 else sums[...] + both

    blocks = sib.shape[0]

    def store(block):
        ours = pl.ds(pl.multiple_of((2 * block + c) * rows, rows), rows)
        return pltpu.make_async_copy(held.at[ours], chip.at[block], store_sem.at[block])

    def add_core(block, _):
        to_core(block).wait_recv()
        ours = pl.ds(pl.multiple_of((2 * block + c) * rows, rows), rows)
        held[ours] = (held[ours].astype(f32) + sib[block].astype(f32)).astype(bf16)
        store(block).start()
        return 0

    lax.fori_loop(0, blocks // 2, add_core, 0)
    passed = ring_gather_pass(spread, halves, y_sems, 6)
    lax.fori_loop(blocks // 2, blocks, add_core, 0)

    def drain(block, _):
        to_core(block).wait_send()
        store(block).wait()
        return 0

    lax.fori_loop(0, blocks, drain, 0)
    for copy in passed + [halves[1][0], halves[0][1]]:
        copy.wait_recv()
    for copy in started + middle + halves[0] + halves[1] + passed:
        copy.wait_send()


def feed_forward(normed, cot_rows, cotangent, unit, scale, gains, weights):
    tokens, width = normed.shape
    here = cotangent.shape[0]
    columns = weights.shape[1] // 3
    blocks, rows = 16, width // 32
    full = pl.BlockSpec(memory_space=VMEM)
    anywhere = pl.BlockSpec(memory_space=pl.ANY)
    tiles = -(-columns // 256)
    return pl.pallas_call(
        feed_forward_kernel,
        out_shape=(
            jax.ShapeDtypeStruct((here, width), f32),
            jax.ShapeDtypeStruct((2, width), f32),
            jax.ShapeDtypeStruct((tokens, width), bf16),
            jax.ShapeDtypeStruct((tokens, width), bf16),
            jax.ShapeDtypeStruct((blocks, rows, 3 * columns), bf16),
        ),
        in_specs=[full] * 6 + [anywhere],
        out_specs=(full,) * 4 + (anywhere,),
        scratch_shapes=[
            VMEM((width, 3 * columns), bf16),
            VMEM((tokens, 2 * columns), bf16),
            VMEM((tokens, columns), bf16),
            VMEM((width, tokens), bf16),
            VMEM((width, tokens), bf16),
            VMEM((tokens, width), bf16),
            VMEM((blocks, rows, 3 * columns), bf16),
        ]
        + [VMEM((2, here // 2, width), bf16)] * 4
        + [DMA((tiles, 3)), DMA((blocks,)), DMA((blocks,)), DMA((blocks,)), DMA((12,)), DMA((12,))],
        compiler_params=pltpu.CompilerParams(
            collective_id=2, has_side_effects=True, vmem_limit_bytes=VMEM_LIMIT
        ),
    )(normed, cot_rows, cotangent, unit, scale, gains, weights)


SAME = [(0, 0), (1, 2), (2, 1), (3, 3)]
CROSS = [(0, 2), (1, 0), (2, 3), (3, 1)]


def from_quarters(rows):
    yl, c = lax.axis_index("yl"), lax.axis_index("c")
    halves = rows.reshape(2, rows.shape[0] // 2, rows.shape[1])
    one = lax.ppermute(
        lax.dynamic_index_in_dim(halves, yl, 0, False), ("yl", "c"), [(b, a) for a, b in SAME]
    )
    two = lax.ppermute(
        lax.dynamic_index_in_dim(halves, 1 - yl, 0, False),
        ("yl", "c"),
        [(b, a) for a, b in CROSS],
    )
    return jnp.stack([jnp.where(c == 0, one, two), jnp.where(c == 0, two, one)])


def shards(
    tokens, cotangent, norm_params, qkv_weight, qkv_bias, out_weight, gate_up_weight, down_weight
):
    yl, yh, c = lax.axis_index("yl"), lax.axis_index("yh"), lax.axis_index("c")
    mine = ((lax.axis_index("z") * 4 + lax.axis_index("x")) * 2 + yl) * 2 + c
    rows = qkv_weight.shape[1]
    hq = qkv_weight.shape[2] // 2
    fq = gate_up_weight.shape[2] // 2
    heads = hq // HEAD_DIM
    pairs = 3 * heads // 2

    qkv_q = qkv_weight.reshape(3, rows, 2, hq).transpose(2, 1, 0, 3).reshape(2, rows, 3 * hq)
    out_q = out_weight.T.reshape(rows, 2, hq).transpose(1, 0, 2)
    gu_q = gate_up_weight.reshape(2, rows, 2, fq).transpose(2, 1, 0, 3).reshape(2, rows, 2 * fq)
    down_q = down_weight.T.reshape(rows, 2, fq).transpose(1, 0, 2)
    other = lax.ppermute(norm_params, "yh", [(0, 1), (1, 0)])
    norm_rows = jnp.where(
        yh == 0,
        jnp.concatenate([norm_params, other], 1),
        jnp.concatenate([other, norm_params], 1),
    )
    norm_high = lax.optimization_barrier(norm_rows.astype(bf16))
    norm_low = (norm_rows - norm_high.astype(f32)).astype(bf16)
    lanes = jnp.arange(EXTRA)
    norm_extra = jnp.where(
        lanes // rows == mine % 4,
        jnp.tile(jnp.concatenate([norm_high, norm_low], 0), (1, EXTRA // rows)),
        0,
    )
    bias_q = qkv_bias.reshape(3, 2, heads).transpose(1, 0, 2).reshape(2, pairs, 2, 1)
    bias_extra = jnp.where(jnp.arange(HEAD_DIM) == mine, bias_q, 0).reshape(2, pairs, EXTRA)
    extra_q = jnp.concatenate(
        [
            bias_extra,
            jnp.broadcast_to(norm_extra[None], (2, *norm_extra.shape)),
            jnp.zeros((2, rows - pairs - 8, EXTRA), bf16),
        ],
        1,
    )
    one, second, token_rows, cot_rows = first_gather(
        jnp.concatenate([qkv_q, out_q, extra_q], axis=2),
        jnp.concatenate([gu_q, down_q], axis=2),
        tokens,
        cotangent,
    )
    second = lax.all_gather(second, ("z", "x", "c"), axis=0, tiled=True)
    table = jnp.asarray(tables())
    normed_one, stats, qkv, head_mix, parts, norm_table = attention_forward(
        token_rows, one, table
    )
    first_sum, unit_two, scale_two, normed_two = second_norm(parts, tokens, norm_table[2:])
    grad_resid, second_terms, resid_rows, mixed_parts, chip = feed_forward(
        normed_two, cot_rows, cotangent, unit_two, scale_two, norm_table[2:], second
    )
    second_sums = lax.psum_scatter(
        chip.reshape(-1, 3 * fq), ("z", "x"), scatter_dimension=0, tiled=True
    )
    grads, first_parts = attention_backward(
        resid_rows, one, normed_one, stats, qkv, head_mix, token_rows, table, second_terms
    )
    first_back, grad_input, mixed = last_sum(
        grads, first_parts, mixed_parts, grad_resid, tokens, stats, norm_table[:2], first_sum
    )

    second_back = from_quarters(second_sums)
    gu_back, down_back = second_back[:, :, : 2 * fq], second_back[:, :, 2 * fq :]
    out_down = down_back.transpose(0, 2, 1).reshape(2 * fq, rows).astype(f32)
    out_gu = (
        gu_back.reshape(2, rows, 2, fq).transpose(2, 1, 0, 3).reshape(2, rows, 2 * fq).astype(f32)
    )
    out_qkv = (
        first_back[:, :, : 3 * hq]
        .reshape(2, rows, 3, hq)
        .transpose(2, 1, 0, 3)
        .reshape(3, rows, 2 * hq)
        .astype(f32)
    )
    out_out = (
        first_back[:, :, 3 * hq : 4 * hq].transpose(0, 2, 1).reshape(2 * hq, rows).astype(f32)
    )
    extra_back = first_back[:, :, 4 * hq :].astype(f32)
    out_bias = (
        lax.dynamic_index_in_dim(
            extra_back[:, :pairs].reshape(2, pairs, 2, HEAD_DIM), mine, 3, False
        )
        .reshape(2, 3, heads)
        .transpose(1, 0, 2)
        .reshape(3, 2 * heads, 1)
    )
    norm_back = lax.dynamic_index_in_dim(
        (extra_back[0] + extra_back[1])[pairs : pairs + 4].reshape(4, EXTRA // rows, rows),
        mine % 4,
        1,
        False,
    ).reshape(4, 2, rows // 2)
    kept = lax.dynamic_index_in_dim(norm_back, yh, 1, False)
    sent = lax.dynamic_index_in_dim(norm_back, 1 - yh, 1, False)
    out_norm = kept + lax.ppermute(sent, "yh", [(0, 1), (1, 0)])
    return (mixed, grad_input, out_norm, out_qkv, out_bias, out_out, out_gu, out_down)


def solution(mesh):
    grid = Mesh(mesh.devices.reshape(4, 4, 2, 2, 2), GRID)
    placed = (
        P(GRID, None),
        P(GRID, None),
        P(None, GRID),
        P(None, ROWS, "yh"),
        P(None, "yh", ROWS),
        P("yh", ROWS),
        P(None, ROWS, "yh"),
        P("yh", ROWS),
    )
    return jax.shard_map(
        shards,
        mesh=grid,
        in_specs=placed,
        out_specs=(
            P(GRID, None),
            P(GRID, None),
            P(None, GRID),
            P(None, ROWS, "yh"),
            P(None, "yh", ROWS),
            P("yh", ROWS),
            P(None, ROWS, "yh"),
            P("yh", ROWS),
        ),
        check_vma=False,
    )
```

```python
import functools

import jax
import jax.numpy as jnp
import numpy as np
from jax import lax
from jax.experimental import pallas as pl
from jax.experimental.pallas import tpu as pltpu
from jax.sharding import Mesh
from jax.sharding import PartitionSpec as P

HEAD_DIM = 64
ROTARY = 16
EPSILON = 1e-05
SCALE = 0.125

GRID = ("z", "x", "yl", "c", "yh")
ROWS = ("z", "x", "yl", "c")
EXTRA = 128

bf16 = jnp.bfloat16
f32 = jnp.float32

MESH = pl.DeviceIdType.MESH
VMEM = pltpu.VMEM
DMA = pltpu.SemaphoreType.DMA
VMEM_LIMIT = 60 * 1024 * 1024


def at_y(k):
    y = (lax.axis_index("yh") * 2 + lax.axis_index("yl") + k) % 4
    return {"yl": y % 2, "yh": y // 2}


def at_z(k):
    return {"z": (lax.axis_index("z") + k) % 4}


def at_x(k):
    return {"x": (lax.axis_index("x") + k) % 4}


def sibling():
    return {"c": 1 - lax.axis_index("c")}


def greet(devices):
    barrier = pltpu.get_barrier_semaphore()
    for device in devices:
        pl.semaphore_signal(barrier, inc=1, device_id=device, device_id_type=MESH)
    pl.semaphore_wait(barrier, len(devices))


def remote(src, dst, sems, index, device):
    send, recv = sems
    return pltpu.make_async_remote_copy(
        src_ref=src,
        dst_ref=dst,
        send_sem=send.at[index],
        recv_sem=recv.at[index],
        device_id=device,
        device_id_type=MESH,
    )


def ring_gather_half(out, top, sems, base):
    here = out.shape[0] // 4
    half = here // 2
    copies = []
    for way, step, block in ((0, 1, 3), (1, -1, 2)):
        copies.append(
            remote(
                out.at[pl.ds(top * half, half)],
                out.at[pl.ds(block * here + top * half, half)],
                sems,
                base + 2 * way + top,
                at_y(step),
            )
        )
        copies[-1].start()
    return copies


def ring_gather_pass(out, halves, sems, base):
    here = out.shape[0] // 4
    half = here // 2
    passed = []
    for way, step, block in ((0, 1, 3), (1, -1, 2)):
        halves[way][way].wait_recv()
        passed.append(
            remote(
                out.at[pl.ds(block * here + way * half, half)],
                out.at[pl.ds(here + way * half, half)],
                sems,
                base + 4 + way,
                at_y(step),
            )
        )
        passed[-1].start()
    return passed


def pair_moves():
    yl, c = lax.axis_index("yl"), lax.axis_index("c")
    return {"yl": c, "c": yl}, {"yl": 1 - c, "c": yl}


def diagonal():
    return {"yl": 1 - lax.axis_index("yl"), "c": 1 - lax.axis_index("c")}


def everyone_near():
    return [at_z(1), at_z(3), at_x(1), at_x(3), at_y(1), at_y(3), sibling(), diagonal()]


def stay_or_go(src, dst, sems, index, device, local_sem):
    yl, c = lax.axis_index("yl"), lax.axis_index("c")

    @pl.when(yl == c)
    def _():
        pltpu.make_async_copy(src, dst, local_sem).start()

    @pl.when(yl != c)
    def _():
        remote(src, dst, sems, index, device).start()


def stay_or_go_wait(src, dst, sems, index, device, local_sem):
    yl, c = lax.axis_index("yl"), lax.axis_index("c")

    @pl.when(yl == c)
    def _():
        pltpu.make_async_copy(src, dst, local_sem).wait()

    @pl.when(yl != c)
    def _():
        copy = remote(src, dst, sems, index, device)
        copy.wait_recv()
        copy.wait_send()


def last_sum_kernel(
    grads, first_parts, mixed_parts, resid, tokens, stats, gains, first_sum,
    result, grad_tokens, mixed,
    sib, mid, sent, far, near, stage, mid2, sent2, far2, near2, packed,
    ymid, ysent, yfar, ynear,
    core_send, core_recv, send, recv, send2, recv2, pair_send, pair_recv, local_sem, y_send, y_recv,
):
    z, x = lax.axis_index("z"), lax.axis_index("x")
    yl, c = lax.axis_index("yl"), lax.axis_index("c")
    core_sems, sems, sems2, pair_sems, y_sems = (
        (core_send, core_recv),
        (send, recv),
        (send2, recv2),
        (pair_send, pair_recv),
        (y_send, y_recv),
    )
    rows = result.shape[1]
    piece = rows // 2
    greet(everyone_near())
    done = []

    def begin(copy):
        copy.start()
        done.append(copy)
        return copy

    def start_of(dz, dx, core):
        return (((z + dz) % 4) * 4 + (x + dx) % 4) * 4 * rows + core * 2 * rows

    order = []
    for d in (2, 1, 3, 0):
        for e in (2, 1, 3, 0):
            for pair in ((d, e), (e, d)):
                if pair not in order:
                    order.append(pair)
    core = {}
    for dz, dx in order:
        core[dz, dx] = begin(
            remote(
                grads.at[pl.ds(start_of(dz, dx, 1 - c), 2 * rows)],
                sib.at[dz, dx],
                core_sems,
                dz * 4 + dx,
                sibling(),
            )
        )
    y_jobs = [
        ring_sum_start(first_parts, ymid.at[0], ynear.at[0], y_sems, 0),
        ring_sum_start(mixed_parts, ymid.at[1], ynear.at[1], y_sems, 6),
    ]
    summed = set()

    def core_sum(dz, dx):
        if (dz, dx) in summed:
            return
        summed.add((dz, dx))
        core[dz, dx].wait_recv()
        sib[dz, dx] = (
            sib[dz, dx].astype(f32)
            + grads[pl.ds(start_of(dz, dx, c), 2 * rows)].astype(f32)
        ).astype(bf16)

    def view(half, df, part):
        rng = pl.ds(half * rows + part * piece, piece)
        return sib.at[df, :, rng] if half == 0 else sib.at[:, df, rng]

    def device(half, axis, step):
        return at_z(step) if (half == 0) == (axis == 0) else at_x(step)

    def ring_first(half, axis, src, mids, nears, some_sems):
        base = half * 6
        got = {}
        for way, step in ((0, 1), (1, -1)):
            got["first", way] = begin(
                remote(src(2, way), mids.at[half, way], some_sems, base + way, device(half, axis, step))
            )
        return got

    def ring_second(half, axis, src, nears, some_sems, got):
        base = half * 6
        for way, step in ((0, 1), (1, -1)):
            got["second", way] = begin(
                remote(
                    src(step % 4, 1 - way), nears.at[half, way], some_sems, base + 2 + way,
                    device(half, axis, step),
                )
            )

    def ring_third(half, axis, src, mids, sents, fars, some_sems, got):
        base = half * 6
        for way, step in ((0, 1), (1, -1)):
            got["first", way].wait_recv()
            sents[half, way] = (
                src(step % 4, way)[...].astype(f32) + mids[half, way].astype(f32)
            ).astype(bf16)
            got["third", way] = begin(
                remote(
                    sents.at[half, way], fars.at[half, way], some_sems, base + 4 + way,
                    device(half, axis, step),
                )
            )

    def ring_last(half, part, src, fars, nears, got):
        got["third", part].wait_recv()
        got["second", 1 - part].wait_recv()
        return (
            src(0, part)[...].astype(f32)
            + fars[half, part].astype(f32)
            + nears[half, 1 - part].astype(f32)
        )

    got = {}
    sources = [functools.partial(view, half) for half in range(2)]
    for half in range(2):
        for d in (2, 1, 3, 0):
            core_sum(*((2, d) if half == 0 else (d, 2)))
        got[half] = ring_first(half, 0, sources[half], mid, near, sems)
    for half in range(2):
        for step in (1, 3):
            for d in (2, 1, 3, 0):
                core_sum(*((step, d) if half == 0 else (d, step)))
        ring_second(half, 0, sources[half], near, sems, got[half])
    y_more = [
        ring_sum_middle(first_parts, y_jobs[0], ymid.at[0], ysent.at[0], yfar.at[0], y_sems, 0)
    ]
    for half in range(2):
        ring_third(half, 0, sources[half], mid, sent, far, sems, got[half])
    core_sum(0, 0)
    y_more.append(
        ring_sum_middle(mixed_parts, y_jobs[1], ymid.at[1], ysent.at[1], yfar.at[1], y_sems, 6)
    )
    finish = ring_sum_finish(first_parts, y_jobs[0], y_more[0], yfar.at[0], ynear.at[0])
    here = grad_tokens.shape[0] // 2
    for top in range(2):
        rng = pl.ds(top * here, here)
        incoming = finish(top) * gains[0:1]
        inverse = stats[1, rng]
        unit_rows = (tokens[rng].astype(f32) - stats[0, rng]) * inverse
        grad_tokens[rng] = resid[rng] + inverse * (
            incoming
            - jnp.mean(incoming, -1, keepdims=True)
            - unit_rows * jnp.mean(incoming * unit_rows, -1, keepdims=True)
        )
    for half in range(2):
        for part in range(2):
            stage[half, :, part * piece : (part + 1) * piece] = ring_last(
                half, part, sources[half], far, near, got[half]
            ).astype(bf16)

    def stage_view(half, dg, part):
        return stage.at[half, dg, pl.ds(part * piece, piece)]

    sources = [functools.partial(stage_view, half) for half in range(2)]
    got = {}
    for half in range(2):
        got[half] = ring_first(half, 1, sources[half], mid2, near2, sems2)
    for half in range(2):
        ring_second(half, 1, sources[half], near2, sems2, got[half])
    for half in range(2):
        ring_third(half, 1, sources[half], mid2, sent2, far2, sems2, got[half])
    finish = ring_sum_finish(mixed_parts, y_jobs[1], y_more[1], yfar.at[1], ynear.at[1])
    for top in range(2):
        rng = pl.ds(top * here, here)
        mixed[rng] = (first_sum[rng] + finish(top)).astype(bf16)
    for half in range(2):
        for part in range(2):
            packed[half, part * piece : (part + 1) * piece] = ring_last(
                half, part, sources[half], far2, near2, got[half]
            ).astype(bf16)

    home, away = {"yl": c, "c": yl}, {"yl": c, "c": 1 - yl}
    stay_or_go(packed.at[yl], result.at[yl], pair_sems, 0, home, local_sem)
    cross = remote(packed.at[1 - yl], result.at[yl], pair_sems, 1, away)
    cross.start()
    cross.wait_recv()
    cross.wait_send()
    stay_or_go_wait(packed.at[yl], result.at[yl], pair_sems, 0, home, local_sem)
    for jobs in y_jobs + y_more:
        for copy in jobs:
            copy.wait_send()
    for copy in done:
        copy.wait_send()


def ring_sum_start(parts, mid, near, sems, base):
    here = parts.shape[0] // 4
    half = here // 2
    copies = []
    for way, step in ((0, 1), (1, -1)):
        copies.append(
            remote(
                parts.at[pl.ds(here + way * half, half)], mid.at[way], sems, base + way, at_y(step)
            )
        )
    for way, step, block in ((0, 1, 2), (1, -1, 3)):
        copies.append(
            remote(
                parts.at[pl.ds(block * here + (1 - way) * half, half)],
                near.at[way],
                sems,
                base + 2 + way,
                at_y(step),
            )
        )
    for copy in copies:
        copy.start()
    return copies


def ring_sum_middle(parts, started, mid, sent, far, sems, base):
    here = parts.shape[0] // 4
    half = here // 2
    copies = []
    for way, step, block in ((0, 1, 2), (1, -1, 3)):
        started[way].wait_recv()
        sent[way] = (
            parts[pl.ds(block * here + way * half, half)].astype(f32) + mid[way].astype(f32)
        ).astype(bf16)
        copies.append(remote(sent.at[way], far.at[way], sems, base + 4 + way, at_y(step)))
        copies[-1].start()
    return copies


def ring_sum_finish(parts, started, middle, far, near):
    half = parts.shape[0] // 8

    def finish(top):
        started[2 + 1 - top].wait_recv()
        middle[top].wait_recv()
        return (
            parts[pl.ds(top * half, half)].astype(f32)
            + far[top].astype(f32)
            + near[1 - top].astype(f32)
        )

    return finish


def last_sum(grads, first_parts, mixed_parts, resid, tokens, stats, gains, first_sum):
    rows = grads.shape[0] // 64
    wide = grads.shape[1]
    here, width = resid.shape
    full = pl.BlockSpec(memory_space=VMEM)
    piece = rows // 2
    return pl.pallas_call(
        last_sum_kernel,
        out_shape=(
            jax.ShapeDtypeStruct((2, rows, wide), bf16),
            jax.ShapeDtypeStruct((here, width), f32),
            jax.ShapeDtypeStruct((here, width), bf16),
        ),
        in_specs=[full] * 8,
        out_specs=(full,) * 3,
        scratch_shapes=[
            VMEM((4, 4, 2 * rows, wide), bf16),
            VMEM((2, 2, 4, piece, wide), bf16),
            VMEM((2, 2, 4, piece, wide), bf16),
            VMEM((2, 2, 4, piece, wide), bf16),
            VMEM((2, 2, 4, piece, wide), bf16),
            VMEM((2, 4, rows, wide), bf16),
            VMEM((2, 2, piece, wide), bf16),
            VMEM((2, 2, piece, wide), bf16),
            VMEM((2, 2, piece, wide), bf16),
            VMEM((2, 2, piece, wide), bf16),
            VMEM((2, rows, wide), bf16),
            VMEM((2, 2, here // 2, width), bf16),
            VMEM((2, 2, here // 2, width), bf16),
            VMEM((2, 2, here // 2, width), bf16),
            VMEM((2, 2, here // 2, width), bf16),
            DMA((16,)), DMA((16,)), DMA((12,)), DMA((12,)), DMA((12,)), DMA((12,)),
            DMA((2,)), DMA((2,)), DMA, DMA((12,)), DMA((12,)),
        ],
        compiler_params=pltpu.CompilerParams(
            collective_id=3, has_side_effects=True, vmem_limit_bytes=VMEM_LIMIT
        ),
    )(grads, first_parts, mixed_parts, resid, tokens, stats, gains, first_sum)


def tables():
    half = ROTARY // 2
    position = np.arange(256, dtype=np.float32)
    frequency = np.power(np.float32(10000.0), -np.arange(half, dtype=np.float32) * np.float32(2.0 / ROTARY))
    angles = position[:, None] * frequency[None, :].astype(np.float32)
    cosine, sine = np.cos(angles), np.sin(angles)
    own = np.ones((256, 2, HEAD_DIM), np.float32)
    up = np.zeros((256, 2, HEAD_DIM), np.float32)
    down = np.zeros((256, 2, HEAD_DIM), np.float32)
    for head in range(2):
        own[:, head, :half] = cosine
        own[:, head, half:ROTARY] = cosine
        up[:, head, :half] = -sine
        down[:, head, half:ROTARY] = sine
    return np.concatenate([a.reshape(256, 128) for a in (own, up, down)], 1)


def dot(a, b, ca, cb):
    return lax.dot_general(a, b, (((ca,), (cb,)), ((), ())), preferred_element_type=f32)


def turn_heads(value, table, sign):
    own, up, down = table[:, :128], table[:, 128:256], table[:, 256:]
    return value * own + sign * (
        pltpu.roll(value, 120, 1) * up + pltpu.roll(value, 8, 1) * down
    )


def half_of_place(place):
    y = lax.axis_index("yh") * 2 + lax.axis_index("yl")
    return ((y + (0, 2, 1, 3)[place]) % 4) // 2


def causal_mask(sequence, here):
    length = 2 * here
    first = half_of_place(2 * sequence)

    def position(dim):
        index = lax.broadcasted_iota(jnp.int32, (length, length), dim)
        return jnp.where(index < here, index + first * here, index - first * here)

    return position(0) >= position(1)


def soft_of(queries, keys, mask):
    scores = dot(queries, keys, 1, 1) * SCALE
    scores = jnp.where(mask, scores, -1000000000.0)
    powers = jnp.exp(scores - jnp.max(scores, -1, keepdims=True))
    return powers * (1.0 / jnp.sum(powers, -1, keepdims=True))


def read_extras(one, first_column, norm_table, bias):
    total = None
    for group in range(one.shape[0] // 128):
        block = one[pl.ds(group * 128, 128), pl.ds(first_column, 128)].astype(f32)
        block = block[0:32] + block[32:64] + block[64:96] + block[96:128]
        norm_table[:, pl.ds(group * 128, 128)] = block[12:16] + block[16:20]
        total = block[0:12] if total is None else total + block[0:12]
    bias[...] = total


def attention_backward_kernel(
    resid, one, normed, stats, qkv, head_mix, token_rows, table, second_terms,
    grads, first_parts, grad_mix, grad_proj,
):
    here = resid.shape[0] // 4
    hq = head_mix.shape[1]
    wide = 256

    def mix_back(k, _):
        cols = pl.ds(pl.multiple_of(k * wide, wide), wide)
        grad_mix[:, cols] = dot(
            resid[...], one[:, pl.ds(pl.multiple_of(3 * hq + k * wide, wide), wide)], 1, 0
        ).astype(bf16)
        return 0

    lax.fori_loop(0, hq // wide, mix_back, 0)

    def out_back(k, _):
        rng = pl.ds(pl.multiple_of(k * wide, wide), wide)
        grads[rng, pl.ds(3 * hq, hq)] = dot(resid[:, rng], head_mix[...], 0, 0).astype(bf16)
        return 0

    lax.fori_loop(0, one.shape[0] // wide, out_back, 0)
    for sequence in range(2):
        mask = causal_mask(sequence, here)
        rng = pl.ds(sequence * 2 * here, 2 * here)
        turn = jnp.concatenate(
            [
                table[pl.ds(pl.multiple_of(half_of_place(2 * sequence + k) * here, here), here)]
                for k in range(2)
            ],
            0,
        )

        def heads(k, _):
            def pair(t):
                return pl.ds(pl.multiple_of(t * hq + k * 128, 128), 128)

            q, key, value = qkv[rng, pair(0)], qkv[rng, pair(1)], qkv[rng, pair(2)]
            mix = grad_mix[rng, pair(0)]
            results = ([], [], [])
            for head in range(2):
                cut = slice(head * HEAD_DIM, (head + 1) * HEAD_DIM)
                soft = soft_of(q[:, cut], key[:, cut], mask)
                grad_soft = dot(mix[:, cut], value[:, cut], 1, 1)
                row_dot = jnp.sum(grad_soft * soft, -1, keepdims=True)
                grad_score = (soft * (grad_soft - row_dot)).astype(bf16)
                results[0].append(dot(grad_score, key[:, cut], 1, 0) * SCALE)
                results[1].append(dot(grad_score, q[:, cut], 0, 0) * SCALE)
                results[2].append(dot(soft.astype(bf16), mix[:, cut], 0, 0))
            for t in range(3):
                both = jnp.concatenate(results[t], 1)
                if t < 2:
                    both = turn_heads(both, turn, -1.0)
                grad_proj[rng, pair(t)] = both.astype(bf16)
            return 0

        lax.fori_loop(0, hq // 128, heads, 0)

    bias_rows = [
        jnp.sum(grad_proj[:, pl.ds(k * 128, 128)].astype(f32), 0, keepdims=True)
        for k in range(3 * hq // 128)
    ]
    mean, inverse = stats[0], stats[1]

    def weights_back(k, _):
        rng = pl.ds(pl.multiple_of(k * wide, wide), wide)
        grads[rng, pl.ds(0, 3 * hq)] = dot(normed[:, rng], grad_proj[...], 0, 0).astype(bf16)
        part = dot(grad_proj[...], one[rng, pl.ds(0, 3 * hq)], 1, 1)
        first_parts[:, rng] = part.astype(bf16)
        unit = (token_rows[:, rng].astype(f32) - mean) * inverse
        gain = jnp.sum(part * unit, 0, keepdims=True)
        shift = jnp.sum(part, 0, keepdims=True)
        for tile in range(wide // 128):
            cut = slice(tile * 128, (tile + 1) * 128)
            lanes = pl.ds(pl.multiple_of(k * wide + tile * 128, 128), 128)
            block = jnp.concatenate(
                bias_rows
                + [
                    gain[:, cut],
                    shift[:, cut],
                    second_terms[:, lanes],
                    jnp.zeros((16, 128), f32),
                ],
                0,
            ).astype(bf16)
            for copy in range(4):
                start = pl.multiple_of(k * wide + tile * 128 + copy * 32, 32)
                grads[pl.ds(start, 32), pl.ds(4 * hq, 128)] = block
        return 0

    lax.fori_loop(0, one.shape[0] // wide, weights_back, 0)


def attention_backward(resid, one, normed, stats, qkv, head_mix, token_rows, table, second_terms):
    tokens, width = token_rows.shape
    hq = head_mix.shape[1]
    full = pl.BlockSpec(memory_space=VMEM)
    return pl.pallas_call(
        attention_backward_kernel,
        out_shape=(
            jax.ShapeDtypeStruct(one.shape, bf16),
            jax.ShapeDtypeStruct((tokens, width), bf16),
        ),
        in_specs=[full] * 9,
        out_specs=(full,) * 2,
        scratch_shapes=[VMEM((tokens, hq), bf16), VMEM((tokens, 3 * hq), bf16)],
        compiler_params=pltpu.CompilerParams(vmem_limit_bytes=VMEM_LIMIT),
    )(resid, one, normed, stats, qkv, head_mix, token_rows, table, second_terms)


def feed_forward_kernel(
    normed, cot_rows, cotangent, unit, scale, gains, weights,
    resid, sums, spread, mixed_parts, chip,
    held, pair, hidden, normed_t, cot_t, parts, sib, mid, sent, far, near,
    load_sem, store_sem, core_send, core_recv, y_send, y_recv,
):
    columns, width = held.shape[1] // 3, held.shape[0]
    wide = 256
    rows = sib.shape[1]
    c = lax.axis_index("c")
    y_sems, core_sems = (y_send, y_recv), (core_send, core_recv)
    whole, rest = columns // wide, columns % wide

    def load(k, which, size):
        start = pl.multiple_of(which * columns + k * wide, 128)
        cut = pl.ds(start, size)
        return pltpu.make_async_copy(weights.at[:, cut], held.at[:, cut], load_sem.at[k, which])

    for k in range(whole + (rest > 0)):
        for which in range(3):
            load(k, which, wide if k < whole else rest).start()

    def flip(k, _):
        rng = pl.ds(pl.multiple_of(k * wide, wide), wide)
        normed_t[rng] = normed[:, rng].T
        cot_t[rng] = cot_rows[:, rng].T
        return 0

    lax.fori_loop(0, width // wide, flip, 0)
    greet([at_y(1), at_y(3), sibling()])

    def ahead(k, size):
        def cut(which):
            return pl.ds(pl.multiple_of(which * columns + k * wide, 128), size)

        for which in range(3):
            load(k, which, size).wait()
        gate = dot(normed[...], held[:, cut(0)], 1, 0)
        up = dot(normed[...], held[:, cut(1)], 1, 0)
        grad_hidden = dot(cot_rows[...], held[:, cut(2)], 1, 0)
        sigmoid = jax.nn.sigmoid(gate)
        activated = gate * sigmoid
        hidden[:, cut(0)] = (activated * up).astype(bf16)
        pair[:, cut(0)] = (
            grad_hidden * up * sigmoid * (1.0 + gate * (1.0 - sigmoid))
        ).astype(bf16)
        pair[:, cut(1)] = (grad_hidden * activated).astype(bf16)
        return 0

    lax.fori_loop(0, whole, lambda k, _: ahead(k, wide), 0)
    if rest:
        ahead(whole, rest)

    def second_back(k, _):
        rng = pl.ds(pl.multiple_of(k * wide, wide), wide)
        parts[:, rng] = dot(pair[...], held[rng, pl.ds(0, 2 * columns)], 1, 1).astype(bf16)
        return 0

    lax.fori_loop(0, width // wide, second_back, 0)
    started = ring_sum_start(parts, mid, near, y_sems, 0)

    def mix(k, _):
        rng = pl.ds(pl.multiple_of(k * wide, wide), wide)
        mixed_parts[:, rng] = dot(
            hidden[...], held[rng, pl.ds(2 * columns, columns)], 1, 1
        ).astype(bf16)
        return 0

    lax.fori_loop(0, width // wide, mix, 0)
    middle = ring_sum_middle(parts, started, mid, sent, far, y_sems, 0)

    def to_core(block):
        theirs = pl.ds(pl.multiple_of((2 * block + 1 - c) * rows, rows), rows)
        return remote(held.at[theirs], sib.at[block], core_sems, block, sibling())

    def weights_back(k, _):
        rng = pl.ds(pl.multiple_of(k * wide, wide), wide)
        held[rng, pl.ds(0, 2 * columns)] = dot(normed_t[rng], pair[...], 1, 0).astype(bf16)
        held[rng, pl.ds(2 * columns, columns)] = dot(cot_t[rng], hidden[...], 1, 0).astype(bf16)
        for block in range(wide // (2 * rows)):
            to_core(k * (wide // (2 * rows)) + block).start()
        return 0

    lax.fori_loop(0, width // wide, weights_back, 0)
    finish = ring_sum_finish(parts, started, middle, far, near)
    half = cotangent.shape[0] // 2
    halves = []
    for top in range(2):
        here = pl.ds(top * half, half)
        total = finish(top)
        unit_rows = unit[here]
        incoming = total * gains[0:1]
        result = cotangent[here].astype(f32) + scale[here] * (
            incoming
            - jnp.mean(incoming, -1, keepdims=True)
            - unit_rows * jnp.mean(incoming * unit_rows, -1, keepdims=True)
        )
        resid[here] = result
        spread[here] = result.astype(bf16)
        halves.append(ring_gather_half(spread, top, y_sems, 6))
        both = jnp.concatenate(
            [
                jnp.sum(total * unit_rows, 0, keepdims=True),
                jnp.sum(total, 0, keepdims=True),
            ],
            0,
        )
        sums[...] = both if top == 0 else sums[...] + both

    blocks = sib.shape[0]

    def store(block):
        ours = pl.ds(pl.multiple_of((2 * block + c) * rows, rows), rows)
        return pltpu.make_async_copy(held.at[ours], chip.at[block], store_sem.at[block])

    def add_core(block, _):
        to_core(block).wait_recv()
        ours = pl.ds(pl.multiple_of((2 * block + c) * rows, rows), rows)
        held[ours] = (held[ours].astype(f32) + sib[block].astype(f32)).astype(bf16)
        store(block).start()
        return 0

    lax.fori_loop(0, blocks // 2, add_core, 0)
    passed = ring_gather_pass(spread, halves, y_sems, 6)
    lax.fori_loop(blocks // 2, blocks, add_core, 0)

    def drain(block, _):
        to_core(block).wait_send()
        store(block).wait()
        return 0

    lax.fori_loop(0, blocks, drain, 0)
    for copy in passed + [halves[1][0], halves[0][1]]:
        copy.wait_recv()
    for copy in started + middle + halves[0] + halves[1] + passed:
        copy.wait_send()


def feed_forward(normed, cot_rows, cotangent, unit, scale, gains, weights):
    tokens, width = normed.shape
    here = cotangent.shape[0]
    columns = weights.shape[1] // 3
    blocks, rows = 16, width // 32
    full = pl.BlockSpec(memory_space=VMEM)
    anywhere = pl.BlockSpec(memory_space=pl.ANY)
    tiles = -(-columns // 256)
    return pl.pallas_call(
        feed_forward_kernel,
        out_shape=(
            jax.ShapeDtypeStruct((here, width), f32),
            jax.ShapeDtypeStruct((2, width), f32),
            jax.ShapeDtypeStruct((tokens, width), bf16),
            jax.ShapeDtypeStruct((tokens, width), bf16),
            jax.ShapeDtypeStruct((blocks, rows, 3 * columns), bf16),
        ),
        in_specs=[full] * 6 + [anywhere],
        out_specs=(full,) * 4 + (anywhere,),
        scratch_shapes=[
            VMEM((width, 3 * columns), bf16),
            VMEM((tokens, 2 * columns), bf16),
            VMEM((tokens, columns), bf16),
            VMEM((width, tokens), bf16),
            VMEM((width, tokens), bf16),
            VMEM((tokens, width), bf16),
            VMEM((blocks, rows, 3 * columns), bf16),
        ]
        + [VMEM((2, here // 2, width), bf16)] * 4
        + [DMA((tiles, 3)), DMA((blocks,)), DMA((blocks,)), DMA((blocks,)), DMA((12,)), DMA((12,))],
        compiler_params=pltpu.CompilerParams(
            collective_id=2, has_side_effects=True, vmem_limit_bytes=VMEM_LIMIT
        ),
    )(normed, cot_rows, cotangent, unit, scale, gains, weights)


def cube():
    yl, c, yh = lax.axis_index("yl"), lax.axis_index("c"), lax.axis_index("yh")
    return [
        {"yl": (yl + a) % 2, "c": (c + b) % 2, "yh": (yh + d) % 2}
        for a in range(2)
        for b in range(2)
        for d in range(2)
        if a + b + d
    ]


class Spread:
    def __init__(self, out, rows, sems, core_sems):
        self.out, self.rows, self.sems, self.core_sems = out, rows, sems, core_sems
        self.done, self.core = [], []

    def cut(self, half, df, dg, part=None):
        z, x = lax.axis_index("z"), lax.axis_index("x")
        dz, dx = (df, dg) if half == 0 else (dg, df)
        place = ((z + dz) % 4) * 4 + (x + dx) % 4
        start = (place * 4 + lax.axis_index("c") * 2 + half) * self.rows
        piece = self.rows // 2
        if part is None:
            return self.out.at[pl.ds(pl.multiple_of(start, self.rows), self.rows)]
        return self.out.at[pl.ds(pl.multiple_of(start + part * piece, piece), piece)]

    def index(self, half, df, dg, part):
        return ((half * 4 + df % 4) * 4 + dg % 4) * 2 + part

    def push(self, half, df, dg, axis, step, part):
        device = at_z(step) if (half == 0) == (axis == 0) else at_x(step)
        to = (df - step, dg) if axis == 0 else (df, dg - step)
        ref = self.cut(half, df, dg, part)
        copy = remote(ref, ref, self.sems, self.index(half, *to, part), device)
        copy.start()
        self.done.append(copy)

    def arrived(self, half, df, dg, part):
        ref = self.cut(half, df, dg, part)
        remote(ref, ref, self.sems, self.index(half, df, dg, part), at_z(1)).wait_recv()

    def to_sibling(self, half, df, dg):
        ref = self.cut(half, df, dg)
        copy = remote(ref, ref, self.core_sems, (half * 4 + df % 4) * 4 + dg % 4, sibling())
        copy.start()
        self.done.append(copy)
        self.core.append(copy)

    def push_all(self, half, df, dg, axis):
        for part in range(2):
            self.push(half, df, dg, axis, 1, part)
            self.push(half, df, dg, axis, -1, 1 - part)

    def start(self):
        for axis in range(2):
            for half in range(2):
                self.push_all(half, 0, 0, axis)
        for half in range(2):
            self.to_sibling(half, 0, 0)

    def first_pass(self):
        for half in range(2):
            self.arrived(half, 3, 0, 0)
            self.push(half, 3, 0, 0, 1, 0)
            self.arrived(half, 1, 0, 1)
            self.push(half, 1, 0, 0, -1, 1)

    def first_rest(self):
        for half in range(2):
            self.arrived(half, 3, 0, 1)
            self.arrived(half, 1, 0, 0)
            for df in (3, 1):
                self.push_all(half, df, 0, 1)
                self.to_sibling(half, df, 0)

    def first_far(self):
        for half in range(2):
            self.arrived(half, 2, 0, 0)
            self.arrived(half, 2, 0, 1)
            self.push_all(half, 2, 0, 1)
            self.to_sibling(half, 2, 0)

    def second_pass(self, df):
        for half in range(2):
            self.arrived(half, df, 3, 0)
            self.push(half, df, 3, 1, 1, 0)
            self.arrived(half, df, 1, 1)
            self.push(half, df, 1, 1, -1, 1)
        for half in range(2):
            self.arrived(half, df, 3, 1)
            self.to_sibling(half, df, 3)
            self.arrived(half, df, 1, 0)
            self.to_sibling(half, df, 1)

    def second_far(self, df):
        for half in range(2):
            for part in range(2):
                self.arrived(half, df, 2, part)
            self.to_sibling(half, df, 2)

    def land(self):
        for copy in self.core:
            copy.wait_recv()

    def close(self):
        for copy in self.done:
            copy.wait_send()


def forward_kernel(
    qkv_weight, out_weight, gate_up_weight, down_weight, extra, tokens, cotangent, table,
    one_out, two, token_rows, cot_rows, normed, stats, qkv, head_mix, norm_table,
    summed, unit, scale, normed_two,
    one_q, two_q, one, norm_in, bias, parts, mid, sent, far, near,
    pair_send, pair_recv, local_sem, y_send, y_recv,
    send_one, recv_one, core_send_one, core_recv_one,
    send_two, recv_two, core_send_two, core_recv_two,
):
    z, x = lax.axis_index("z"), lax.axis_index("x")
    yl, c, yh = lax.axis_index("yl"), lax.axis_index("c"), lax.axis_index("yh")
    rows, here = one_q.shape[1], tokens.shape[0]
    hq, fq = qkv_weight.shape[2] // 2, gate_up_weight.shape[2] // 2
    pair_sems, y_sems = (pair_send, pair_recv), (y_send, y_recv)
    for q in range(2):
        for t in range(3):
            one_q[q, :, t * hq : (t + 1) * hq] = qkv_weight[t, :, q * hq : (q + 1) * hq]
        one_q[q, :, 3 * hq : 4 * hq] = out_weight[:, q * hq : (q + 1) * hq]
        one_q[q, :, 4 * hq :] = extra[q]
    token_rows[pl.ds(0, here)] = tokens[...]
    greet([at_z(1), at_z(3), at_x(1), at_x(3)] + cube())

    same, cross = pair_moves()
    mine = pl.ds(pl.multiple_of((z * 4 + x) * 4 * rows + (yl * 2 + c) * rows, rows), rows)
    moves = [
        (one_q.at[c], one.at[mine], 0, same),
        (one_q.at[1 - c], one.at[mine], 1, cross),
        (two_q.at[c], two.at[mine], 2, same),
        (two_q.at[1 - c], two.at[mine], 3, cross),
    ]

    def launch(k):
        src, dst, index, device = moves[k]
        if device is same:
            stay_or_go(src, dst, pair_sems, index, device, local_sem.at[index // 2])
        else:
            remote(src, dst, pair_sems, index, device).start()

    def land(k):
        src, dst, index, device = moves[k]
        if device is same:
            stay_or_go_wait(src, dst, pair_sems, index, device, local_sem.at[index // 2])
        else:
            copy = remote(src, dst, pair_sems, index, device)
            copy.wait_recv()
            copy.wait_send()

    norm_moves = [
        remote(
            one_q.at[0, :, pl.ds(4 * hq, EXTRA)],
            norm_in.at[c],
            pair_sems,
            4 + which,
            {"yl": target["yl"], "c": target["c"], "yh": 1 - yh},
        )
        for which, target in enumerate((same, cross))
    ]
    launch(0)
    launch(1)
    for move in norm_moves:
        move.start()
    token_halves = [ring_gather_half(token_rows, top, y_sems, 0) for top in range(2)]
    for q in range(2):
        for t in range(2):
            two_q[q, :, t * fq : (t + 1) * fq] = gate_up_weight[t, :, q * fq : (q + 1) * fq]
        two_q[q, :, 2 * fq :] = down_weight[:, q * fq : (q + 1) * fq]
    cot_rows[pl.ds(0, here)] = cotangent[...]
    land(0)
    land(1)
    for move in norm_moves:
        move.wait_recv()
    own = (z * 4 + x) * 4 + 2 * c
    for core in range(2):
        block = pl.ds(pl.multiple_of((own + core) * rows, rows), rows)
        came = norm_in[core].astype(f32)
        place = lax.broadcasted_iota(jnp.int32, came.shape, 0)
        held = one[block, pl.ds(4 * hq, EXTRA)].astype(f32)
        one[block, pl.ds(4 * hq, EXTRA)] = (
            held + jnp.where((place >= 12) & (place < 20), came, 0.0)
        ).astype(bf16)
    first = Spread(one, rows, (send_one, recv_one), (core_send_one, core_recv_one))
    second = Spread(two, rows, (send_two, recv_two), (core_send_two, core_recv_two))
    first.start()
    launch(2)
    launch(3)
    first.first_pass()
    first.first_rest()
    token_passed = ring_gather_pass(token_rows, token_halves, y_sems, 0)
    first.second_pass(0)
    first.first_far()
    first.second_pass(3)
    first.second_pass(1)
    land(2)
    land(3)
    second.start()
    first.second_pass(2)
    for df in (0, 3, 1, 2):
        first.second_far(df)
    for copy in token_passed + [token_halves[1][0], token_halves[0][1]]:
        copy.wait_recv()
    cot_halves = [ring_gather_half(cot_rows, top, y_sems, 6) for top in range(2)]
    first.land()
    keep = pltpu.make_async_copy(one, one_out, local_sem.at[2])
    keep.start()

    read_extras(one, 4 * hq, norm_table, bias)

    def norm_rows(k, _):
        rng = pl.ds(pl.multiple_of(k * here, here), here)
        values = token_rows[rng].astype(f32)
        mean = jnp.mean(values, -1, keepdims=True)
        centered = values - mean
        inverse = lax.rsqrt(jnp.mean(centered * centered, -1, keepdims=True) + EPSILON)
        stats[0, rng] = mean
        stats[1, rng] = inverse
        normed[rng] = (centered * inverse * norm_table[0:1] + norm_table[1:2]).astype(bf16)
        return 0

    lax.fori_loop(0, 4, norm_rows, 0)
    second.first_pass()
    wide = 256

    def project(k, _):
        cols = pl.ds(pl.multiple_of(k * wide, wide), wide)
        value = dot(normed[...], one[:, cols], 1, 0)
        value = value + jnp.concatenate([bias[pl.ds(2 * k, 1)], bias[pl.ds(2 * k + 1, 1)]], 1)

        @pl.when(k < 2 * hq // wide)
        def _():
            for place in range(4):
                rng = pl.ds(place * here, here)
                turn = table[pl.ds(pl.multiple_of(half_of_place(place) * here, here), here)]
                for pair in range(wide // 128):
                    qkv[rng, pl.ds(pl.multiple_of(k * wide + pair * 128, 128), 128)] = turn_heads(
                        value[place * here : (place + 1) * here, pair * 128 : (pair + 1) * 128],
                        turn,
                        1.0,
                    ).astype(bf16)

        @pl.when(k >= 2 * hq // wide)
        def _():
            qkv[:, cols] = value.astype(bf16)

        return 0

    lax.fori_loop(0, 3 * hq // wide, project, 0)
    second.first_rest()
    cot_passed = ring_gather_pass(cot_rows, cot_halves, y_sems, 6)
    for sequence in range(2):
        mask = causal_mask(sequence, here)
        rng = pl.ds(sequence * 2 * here, 2 * here)

        def heads(k, _):
            def pair(t):
                return qkv[rng, pl.ds(pl.multiple_of(t * hq + k * 128, 128), 128)]

            q, key, value = pair(0), pair(1), pair(2)
            mixes = []
            for head in range(2):
                cut = slice(head * HEAD_DIM, (head + 1) * HEAD_DIM)
                soft = soft_of(q[:, cut], key[:, cut], mask).astype(bf16)
                mixes.append(dot(soft, value[:, cut], 1, 0))
            head_mix[rng, pl.ds(pl.multiple_of(k * 128, 128), 128)] = jnp.concatenate(
                mixes, 1
            ).astype(bf16)
            return 0

        lax.fori_loop(0, hq // 128, heads, 0, unroll=2)
        if sequence == 0:
            second.second_pass(0)
    second.first_far()

    def out_project(k, _):
        rng = pl.ds(pl.multiple_of(k * wide, wide), wide)
        parts[:, rng] = dot(head_mix[...], one[rng, pl.ds(3 * hq, hq)], 1, 1).astype(bf16)
        return 0

    lax.fori_loop(0, one.shape[0] // wide, out_project, 0)
    for copy in cot_passed + [cot_halves[1][0], cot_halves[0][1]]:
        copy.wait_recv()

    started = ring_sum_start(parts, mid, near, y_sems, 12)
    second.second_pass(3)
    middle = ring_sum_middle(parts, started, mid, sent, far, y_sems, 12)
    second.second_pass(1)
    finish = ring_sum_finish(parts, started, middle, far, near)
    half = here // 2
    halves = []
    for top in range(2):
        rng = pl.ds(top * half, half)
        total = tokens[rng].astype(f32) + finish(top)
        summed[rng] = total
        centered = total - jnp.mean(total, -1, keepdims=True)
        inverse = lax.rsqrt(jnp.mean(centered * centered, -1, keepdims=True) + EPSILON)
        unit_rows = centered * inverse
        unit[rng] = unit_rows
        scale[rng] = inverse
        normed_two[rng] = (unit_rows * norm_table[2:3] + norm_table[3:4]).astype(bf16)
        halves.append(ring_gather_half(normed_two, top, y_sems, 18))
    second.second_pass(2)
    passed = ring_gather_pass(normed_two, halves, y_sems, 18)
    for df in (0, 3, 1, 2):
        second.second_far(df)
    for copy in passed + [halves[1][0], halves[0][1]]:
        copy.wait_recv()
    second.land()
    keep.wait()
    for move in norm_moves:
        move.wait_send()
    for copies in token_halves + cot_halves + halves + [
        token_passed, cot_passed, started, middle, passed
    ]:
        for copy in copies:
            copy.wait_send()
    first.close()
    second.close()


def forward(qkv_weight, out_weight, gate_up_weight, down_weight, extra, tokens, cotangent, table):
    here, width = tokens.shape
    rows = qkv_weight.shape[1]
    hq, fq = qkv_weight.shape[2] // 2, gate_up_weight.shape[2] // 2
    full = pl.BlockSpec(memory_space=VMEM)
    anywhere = pl.BlockSpec(memory_space=pl.ANY)
    one_wide, two_wide = 4 * hq + EXTRA, 3 * fq

    def shape(*dims, dtype=bf16):
        return jax.ShapeDtypeStruct(dims, dtype)

    return pl.pallas_call(
        forward_kernel,
        out_shape=(
            shape(width, one_wide),
            shape(width, two_wide),
            shape(4 * here, width),
            shape(4 * here, width),
            shape(4 * here, width),
            shape(2, 4 * here, 1, dtype=f32),
            shape(4 * here, 3 * hq),
            shape(4 * here, hq),
            shape(4, width, dtype=f32),
            shape(here, width, dtype=f32),
            shape(here, width, dtype=f32),
            shape(here, 1, dtype=f32),
            shape(4 * here, width),
        ),
        in_specs=[full] * 8,
        out_specs=(anywhere, anywhere) + (full,) * 11,
        scratch_shapes=[
            VMEM((2, rows, one_wide), bf16),
            VMEM((2, rows, two_wide), bf16),
            VMEM((width, one_wide), bf16),
            VMEM((2, rows, EXTRA), bf16),
            VMEM((12, 128), f32),
            VMEM((4 * here, width), bf16),
        ]
        + [VMEM((2, here // 2, width), bf16)] * 4
        + [
            DMA((6,)), DMA((6,)), DMA((3,)), DMA((24,)), DMA((24,)),
            DMA((64,)), DMA((64,)), DMA((32,)), DMA((32,)),
            DMA((64,)), DMA((64,)), DMA((32,)), DMA((32,)),
        ],
        compiler_params=pltpu.CompilerParams(
            collective_id=0, has_side_effects=True, vmem_limit_bytes=VMEM_LIMIT
        ),
    )(qkv_weight, out_weight, gate_up_weight, down_weight, extra, tokens, cotangent, table)


SAME = [(0, 0), (1, 2), (2, 1), (3, 3)]
CROSS = [(0, 2), (1, 0), (2, 3), (3, 1)]


def from_quarters(rows):
    yl, c = lax.axis_index("yl"), lax.axis_index("c")
    halves = rows.reshape(2, rows.shape[0] // 2, rows.shape[1])
    one = lax.ppermute(
        lax.dynamic_index_in_dim(halves, yl, 0, False), ("yl", "c"), [(b, a) for a, b in SAME]
    )
    two = lax.ppermute(
        lax.dynamic_index_in_dim(halves, 1 - yl, 0, False),
        ("yl", "c"),
        [(b, a) for a, b in CROSS],
    )
    return jnp.stack([jnp.where(c == 0, one, two), jnp.where(c == 0, two, one)])


def shards(
    tokens, cotangent, norm_params, qkv_weight, qkv_bias, out_weight, gate_up_weight, down_weight
):
    yl, yh, c = lax.axis_index("yl"), lax.axis_index("yh"), lax.axis_index("c")
    mine = ((lax.axis_index("z") * 4 + lax.axis_index("x")) * 2 + yl) * 2 + c
    rows = qkv_weight.shape[1]
    hq = qkv_weight.shape[2] // 2
    fq = gate_up_weight.shape[2] // 2
    heads = hq // HEAD_DIM
    pairs = 3 * heads // 2

    norm_high = lax.optimization_barrier(norm_params.astype(bf16))
    norm_low = (norm_params - norm_high.astype(f32)).astype(bf16)
    share = norm_params.shape[1]
    norm_extra = jnp.where(
        jnp.arange(EXTRA) // share == mine % 4 * 2 + yh,
        jnp.tile(jnp.concatenate([norm_high, norm_low], 0), (1, EXTRA // share)),
        0,
    )
    bias_q = qkv_bias.reshape(3, 2, heads).transpose(1, 0, 2).reshape(2, pairs, 2, 1)
    bias_extra = jnp.where(jnp.arange(HEAD_DIM) == mine, bias_q, 0).reshape(2, pairs, EXTRA)
    extra = jnp.concatenate(
        [
            bias_extra,
            jnp.broadcast_to(norm_extra[None], (2, *norm_extra.shape)),
            jnp.zeros((2, rows - pairs - 8, EXTRA), bf16),
        ],
        1,
    )
    table = jnp.asarray(tables())
    (
        one, second, token_rows, cot_rows, normed_one, stats, qkv, head_mix, norm_table,
        first_sum, unit_two, scale_two, normed_two,
    ) = forward(
        qkv_weight, out_weight.T, gate_up_weight, down_weight.T, extra, tokens, cotangent, table
    )
    grad_resid, second_terms, resid_rows, mixed_parts, chip = feed_forward(
        normed_two, cot_rows, cotangent, unit_two, scale_two, norm_table[2:], second
    )
    second_sums = lax.psum_scatter(
        chip.reshape(-1, 3 * fq), ("z", "x"), scatter_dimension=0, tiled=True
    )
    grads, first_parts = attention_backward(
        resid_rows, one, normed_one, stats, qkv, head_mix, token_rows, table, second_terms
    )
    first_back, grad_input, mixed = last_sum(
        grads, first_parts, mixed_parts, grad_resid, tokens, stats, norm_table[:2], first_sum
    )

    second_back = from_quarters(second_sums)
    gu_back, down_back = second_back[:, :, : 2 * fq], second_back[:, :, 2 * fq :]
    out_down = down_back.transpose(0, 2, 1).reshape(2 * fq, rows).astype(f32)
    out_gu = (
        gu_back.reshape(2, rows, 2, fq).transpose(2, 1, 0, 3).reshape(2, rows, 2 * fq).astype(f32)
    )
    out_qkv = (
        first_back[:, :, : 3 * hq]
        .reshape(2, rows, 3, hq)
        .transpose(2, 1, 0, 3)
        .reshape(3, rows, 2 * hq)
        .astype(f32)
    )
    out_out = (
        first_back[:, :, 3 * hq : 4 * hq].transpose(0, 2, 1).reshape(2 * hq, rows).astype(f32)
    )
    extra_back = first_back[:, :, 4 * hq :].astype(f32)
    out_bias = (
        lax.dynamic_index_in_dim(
            extra_back[:, :pairs].reshape(2, pairs, 2, HEAD_DIM), mine, 3, False
        )
        .reshape(2, 3, heads)
        .transpose(1, 0, 2)
        .reshape(3, 2 * heads, 1)
    )
    norm_back = lax.dynamic_index_in_dim(
        (extra_back[0] + extra_back[1])[pairs : pairs + 4].reshape(4, EXTRA // rows, rows),
        mine % 4,
        1,
        False,
    ).reshape(4, 2, rows // 2)
    kept = lax.dynamic_index_in_dim(norm_back, yh, 1, False)
    sent = lax.dynamic_index_in_dim(norm_back, 1 - yh, 1, False)
    out_norm = kept + lax.ppermute(sent, "yh", [(0, 1), (1, 0)])
    return (mixed, grad_input, out_norm, out_qkv, out_bias, out_out, out_gu, out_down)


def solution(mesh):
    grid = Mesh(mesh.devices.reshape(4, 4, 2, 2, 2), GRID)
    placed = (
        P(GRID, None),
        P(GRID, None),
        P(None, GRID),
        P(None, ROWS, "yh"),
        P(None, "yh", ROWS),
        P("yh", ROWS),
        P(None, ROWS, "yh"),
        P("yh", ROWS),
    )
    return jax.shard_map(
        shards,
        mesh=grid,
        in_specs=placed,
        out_specs=(
            P(GRID, None),
            P(GRID, None),
            P(None, GRID),
            P(None, ROWS, "yh"),
            P(None, "yh", ROWS),
            P("yh", ROWS),
            P(None, ROWS, "yh"),
            P("yh", ROWS),
        ),
        check_vma=False,
    )
```

```python
import jax
import jax.numpy as jnp
import numpy as np
from jax import lax
from jax.experimental import pallas as pl
from jax.experimental.pallas import tpu as pltpu
from jax.sharding import Mesh
from jax.sharding import PartitionSpec as P

HEAD_DIM = 64
ROTARY = 16
EPSILON = 1e-05
SCALE = 0.125

GRID = ("z", "x", "yl", "c", "yh")
ROWS = ("z", "x", "yl", "c")
EXTRA = 128

bf16 = jnp.bfloat16
f32 = jnp.float32

MESH = pl.DeviceIdType.MESH
VMEM = pltpu.VMEM
DMA = pltpu.SemaphoreType.DMA
VMEM_LIMIT = 60 * 1024 * 1024


def at_y(k):
    y = (lax.axis_index("yh") * 2 + lax.axis_index("yl") + k) % 4
    return {"yl": y % 2, "yh": y // 2}


def at_z(k):
    return {"z": (lax.axis_index("z") + k) % 4}


def at_x(k):
    return {"x": (lax.axis_index("x") + k) % 4}


def sibling():
    return {"c": 1 - lax.axis_index("c")}


def greet(devices):
    barrier = pltpu.get_barrier_semaphore()
    for device in devices:
        pl.semaphore_signal(barrier, inc=1, device_id=device, device_id_type=MESH)
    pl.semaphore_wait(barrier, len(devices))


def remote(src, dst, sems, index, device):
    send, recv = sems
    return pltpu.make_async_remote_copy(
        src_ref=src,
        dst_ref=dst,
        send_sem=send.at[index],
        recv_sem=recv.at[index],
        device_id=device,
        device_id_type=MESH,
    )


def ring_gather_half(out, top, sems, base):
    here = out.shape[0] // 4
    half = here // 2
    copies = []
    for way, step, block in ((0, 1, 3), (1, -1, 2)):
        copies.append(
            remote(
                out.at[pl.ds(top * half, half)],
                out.at[pl.ds(block * here + top * half, half)],
                sems,
                base + 2 * way + top,
                at_y(step),
            )
        )
        copies[-1].start()
    return copies


def ring_gather_pass(out, halves, sems, base):
    here = out.shape[0] // 4
    half = here // 2
    passed = []
    for way, step, block in ((0, 1, 3), (1, -1, 2)):
        halves[way][way].wait_recv()
        passed.append(
            remote(
                out.at[pl.ds(block * here + way * half, half)],
                out.at[pl.ds(here + way * half, half)],
                sems,
                base + 4 + way,
                at_y(step),
            )
        )
        passed[-1].start()
    return passed


def pair_moves():
    yl, c = lax.axis_index("yl"), lax.axis_index("c")
    return {"yl": c, "c": yl}, {"yl": 1 - c, "c": yl}


def stay_or_go(src, dst, sems, index, device, local_sem):
    yl, c = lax.axis_index("yl"), lax.axis_index("c")

    @pl.when(yl == c)
    def _():
        pltpu.make_async_copy(src, dst, local_sem).start()

    @pl.when(yl != c)
    def _():
        remote(src, dst, sems, index, device).start()


def stay_or_go_wait(src, dst, sems, index, device, local_sem):
    yl, c = lax.axis_index("yl"), lax.axis_index("c")

    @pl.when(yl == c)
    def _():
        pltpu.make_async_copy(src, dst, local_sem).wait()

    @pl.when(yl != c)
    def _():
        copy = remote(src, dst, sems, index, device)
        copy.wait_recv()
        copy.wait_send()


def ring_sum_start(parts, mid, near, sems, base):
    here = parts.shape[0] // 4
    half = here // 2
    copies = []
    for way, step in ((0, 1), (1, -1)):
        copies.append(
            remote(
                parts.at[pl.ds(here + way * half, half)], mid.at[way], sems, base + way, at_y(step)
            )
        )
    for way, step, block in ((0, 1, 2), (1, -1, 3)):
        copies.append(
            remote(
                parts.at[pl.ds(block * here + (1 - way) * half, half)],
                near.at[way],
                sems,
                base + 2 + way,
                at_y(step),
            )
        )
    for copy in copies:
        copy.start()
    return copies


def ring_sum_middle(parts, started, mid, sent, far, sems, base):
    here = parts.shape[0] // 4
    half = here // 2
    copies = []
    for way, step, block in ((0, 1, 2), (1, -1, 3)):
        started[way].wait_recv()
        sent[way] = (
            parts[pl.ds(block * here + way * half, half)].astype(f32) + mid[way].astype(f32)
        ).astype(bf16)
        copies.append(remote(sent.at[way], far.at[way], sems, base + 4 + way, at_y(step)))
        copies[-1].start()
    return copies


def ring_sum_finish(parts, started, middle, far, near):
    half = parts.shape[0] // 8

    def finish(top):
        started[2 + 1 - top].wait_recv()
        middle[top].wait_recv()
        return (
            parts[pl.ds(top * half, half)].astype(f32)
            + far[top].astype(f32)
            + near[1 - top].astype(f32)
        )

    return finish


def tables():
    half = ROTARY // 2
    position = np.arange(256, dtype=np.float32)
    frequency = np.power(np.float32(10000.0), -np.arange(half, dtype=np.float32) * np.float32(2.0 / ROTARY))
    angles = position[:, None] * frequency[None, :].astype(np.float32)
    cosine, sine = np.cos(angles), np.sin(angles)
    own = np.ones((256, 2, HEAD_DIM), np.float32)
    up = np.zeros((256, 2, HEAD_DIM), np.float32)
    down = np.zeros((256, 2, HEAD_DIM), np.float32)
    for head in range(2):
        own[:, head, :half] = cosine
        own[:, head, half:ROTARY] = cosine
        up[:, head, :half] = -sine
        down[:, head, half:ROTARY] = sine
    return np.concatenate([a.reshape(256, 128) for a in (own, up, down)], 1)


def dot(a, b, ca, cb):
    return lax.dot_general(a, b, (((ca,), (cb,)), ((), ())), preferred_element_type=f32)


def turn_heads(value, table, sign):
    own, up, down = table[:, :128], table[:, 128:256], table[:, 256:]
    return value * own + sign * (
        pltpu.roll(value, 120, 1) * up + pltpu.roll(value, 8, 1) * down
    )


def half_of_place(place):
    y = lax.axis_index("yh") * 2 + lax.axis_index("yl")
    return ((y + (0, 2, 1, 3)[place]) % 4) // 2


def causal_mask(sequence, here):
    length = 2 * here
    first = half_of_place(2 * sequence)

    def position(dim):
        index = lax.broadcasted_iota(jnp.int32, (length, length), dim)
        return jnp.where(index < here, index + first * here, index - first * here)

    return position(0) >= position(1)


def soft_of(queries, keys, mask):
    scores = dot(queries, keys, 1, 1) * SCALE
    scores = jnp.where(mask, scores, -1000000000.0)
    powers = jnp.exp(scores - jnp.max(scores, -1, keepdims=True))
    return powers * (1.0 / jnp.sum(powers, -1, keepdims=True))


def read_extras(one, first_column, norm_table, bias):
    total = None
    for group in range(one.shape[0] // 128):
        block = one[pl.ds(group * 128, 128), pl.ds(first_column, 128)].astype(f32)
        block = block[0:32] + block[32:64] + block[64:96] + block[96:128]
        norm_table[:, pl.ds(group * 128, 128)] = block[12:16] + block[16:20]
        total = block[0:12] if total is None else total + block[0:12]
    bias[...] = total


def feed_forward_kernel(
    normed, cot_rows, cotangent, unit, scale, gains, weights,
    resid, sums, spread, mixed_parts, chip,
    held, pair, hidden, normed_t, cot_t, parts, sib, mid, sent, far, near,
    load_sem, store_sem, core_send, core_recv, y_send, y_recv,
):
    columns, width = held.shape[1] // 3, held.shape[0]
    wide = 256
    rows = sib.shape[1]
    c = lax.axis_index("c")
    y_sems, core_sems = (y_send, y_recv), (core_send, core_recv)
    whole, rest = columns // wide, columns % wide

    def load(k, which, size):
        start = pl.multiple_of(which * columns + k * wide, 128)
        cut = pl.ds(start, size)
        return pltpu.make_async_copy(weights.at[:, cut], held.at[:, cut], load_sem.at[k, which])

    for k in range(whole + (rest > 0)):
        for which in range(3):
            load(k, which, wide if k < whole else rest).start()

    def flip(k, _):
        rng = pl.ds(pl.multiple_of(k * wide, wide), wide)
        normed_t[rng] = normed[:, rng].T
        cot_t[rng] = cot_rows[:, rng].T
        return 0

    lax.fori_loop(0, width // wide, flip, 0)
    greet([at_y(1), at_y(3), sibling()])

    def ahead(k, size):
        def cut(which):
            return pl.ds(pl.multiple_of(which * columns + k * wide, 128), size)

        for which in range(3):
            load(k, which, size).wait()
        gate = dot(normed[...], held[:, cut(0)], 1, 0)
        up = dot(normed[...], held[:, cut(1)], 1, 0)
        grad_hidden = dot(cot_rows[...], held[:, cut(2)], 1, 0)
        sigmoid = jax.nn.sigmoid(gate)
        activated = gate * sigmoid
        hidden[:, cut(0)] = (activated * up).astype(bf16)
        pair[:, cut(0)] = (
            grad_hidden * up * sigmoid * (1.0 + gate * (1.0 - sigmoid))
        ).astype(bf16)
        pair[:, cut(1)] = (grad_hidden * activated).astype(bf16)
        return 0

    lax.fori_loop(0, whole, lambda k, _: ahead(k, wide), 0)
    if rest:
        ahead(whole, rest)

    def second_back(k, _):
        rng = pl.ds(pl.multiple_of(k * wide, wide), wide)
        parts[:, rng] = dot(pair[...], held[rng, pl.ds(0, 2 * columns)], 1, 1).astype(bf16)
        return 0

    lax.fori_loop(0, width // wide, second_back, 0)
    started = ring_sum_start(parts, mid, near, y_sems, 0)

    def mix(k, _):
        rng = pl.ds(pl.multiple_of(k * wide, wide), wide)
        mixed_parts[:, rng] = dot(
            hidden[...], held[rng, pl.ds(2 * columns, columns)], 1, 1
        ).astype(bf16)
        return 0

    lax.fori_loop(0, width // wide, mix, 0)
    middle = ring_sum_middle(parts, started, mid, sent, far, y_sems, 0)

    def to_core(block):
        theirs = pl.ds(pl.multiple_of((2 * block + 1 - c) * rows, rows), rows)
        return remote(held.at[theirs], sib.at[block], core_sems, block, sibling())

    def weights_back(k, _):
        rng = pl.ds(pl.multiple_of(k * wide, wide), wide)
        held[rng, pl.ds(0, 2 * columns)] = dot(normed_t[rng], pair[...], 1, 0).astype(bf16)
        held[rng, pl.ds(2 * columns, columns)] = dot(cot_t[rng], hidden[...], 1, 0).astype(bf16)
        for block in range(wide // (2 * rows)):
            to_core(k * (wide // (2 * rows)) + block).start()
        return 0

    lax.fori_loop(0, width // wide, weights_back, 0)
    finish = ring_sum_finish(parts, started, middle, far, near)
    half = cotangent.shape[0] // 2
    halves = []
    for top in range(2):
        here = pl.ds(top * half, half)
        total = finish(top)
        unit_rows = unit[here]
        incoming = total * gains[0:1]
        result = cotangent[here].astype(f32) + scale[here] * (
            incoming
            - jnp.mean(incoming, -1, keepdims=True)
            - unit_rows * jnp.mean(incoming * unit_rows, -1, keepdims=True)
        )
        resid[here] = result
        spread[here] = result.astype(bf16)
        halves.append(ring_gather_half(spread, top, y_sems, 6))
        both = jnp.concatenate(
            [
                jnp.sum(total * unit_rows, 0, keepdims=True),
                jnp.sum(total, 0, keepdims=True),
            ],
            0,
        )
        sums[...] = both if top == 0 else sums[...] + both

    blocks = sib.shape[0]

    def store(block):
        ours = pl.ds(pl.multiple_of((2 * block + c) * rows, rows), rows)
        return pltpu.make_async_copy(held.at[ours], chip.at[block], store_sem.at[block])

    def add_core(block, _):
        to_core(block).wait_recv()
        ours = pl.ds(pl.multiple_of((2 * block + c) * rows, rows), rows)
        held[ours] = (held[ours].astype(f32) + sib[block].astype(f32)).astype(bf16)
        store(block).start()
        return 0

    lax.fori_loop(0, blocks // 2, add_core, 0)
    passed = ring_gather_pass(spread, halves, y_sems, 6)
    lax.fori_loop(blocks // 2, blocks, add_core, 0)

    def drain(block, _):
        to_core(block).wait_send()
        store(block).wait()
        return 0

    lax.fori_loop(0, blocks, drain, 0)
    for copy in passed + [halves[1][0], halves[0][1]]:
        copy.wait_recv()
    for copy in started + middle + halves[0] + halves[1] + passed:
        copy.wait_send()


def feed_forward(normed, cot_rows, cotangent, unit, scale, gains, weights):
    tokens, width = normed.shape
    here = cotangent.shape[0]
    columns = weights.shape[1] // 3
    blocks, rows = 16, width // 32
    full = pl.BlockSpec(memory_space=VMEM)
    anywhere = pl.BlockSpec(memory_space=pl.ANY)
    tiles = -(-columns // 256)
    return pl.pallas_call(
        feed_forward_kernel,
        out_shape=(
            jax.ShapeDtypeStruct((here, width), f32),
            jax.ShapeDtypeStruct((2, width), f32),
            jax.ShapeDtypeStruct((tokens, width), bf16),
            jax.ShapeDtypeStruct((tokens, width), bf16),
            jax.ShapeDtypeStruct((blocks, rows, 3 * columns), bf16),
        ),
        in_specs=[full] * 6 + [anywhere],
        out_specs=(full,) * 4 + (anywhere,),
        scratch_shapes=[
            VMEM((width, 3 * columns), bf16),
            VMEM((tokens, 2 * columns), bf16),
            VMEM((tokens, columns), bf16),
            VMEM((width, tokens), bf16),
            VMEM((width, tokens), bf16),
            VMEM((tokens, width), bf16),
            VMEM((blocks, rows, 3 * columns), bf16),
        ]
        + [VMEM((2, here // 2, width), bf16)] * 4
        + [DMA((tiles, 3)), DMA((blocks,)), DMA((blocks,)), DMA((blocks,)), DMA((12,)), DMA((12,))],
        compiler_params=pltpu.CompilerParams(
            collective_id=2, has_side_effects=True, vmem_limit_bytes=VMEM_LIMIT
        ),
    )(normed, cot_rows, cotangent, unit, scale, gains, weights)


def cube():
    yl, c, yh = lax.axis_index("yl"), lax.axis_index("c"), lax.axis_index("yh")
    return [
        {"yl": (yl + a) % 2, "c": (c + b) % 2, "yh": (yh + d) % 2}
        for a in range(2)
        for b in range(2)
        for d in range(2)
        if a + b + d
    ]


class Spread:
    def __init__(self, out, rows, sems, core_sems):
        self.out, self.rows, self.sems, self.core_sems = out, rows, sems, core_sems
        self.done, self.core = [], []

    def cut(self, half, df, dg, part=None):
        z, x = lax.axis_index("z"), lax.axis_index("x")
        dz, dx = (df, dg) if half == 0 else (dg, df)
        place = ((z + dz) % 4) * 4 + (x + dx) % 4
        start = (place * 4 + lax.axis_index("c") * 2 + half) * self.rows
        piece = self.rows // 2
        if part is None:
            return self.out.at[pl.ds(pl.multiple_of(start, self.rows), self.rows)]
        return self.out.at[pl.ds(pl.multiple_of(start + part * piece, piece), piece)]

    def index(self, half, df, dg, part):
        return ((half * 4 + df % 4) * 4 + dg % 4) * 2 + part

    def push(self, half, df, dg, axis, step, part):
        device = at_z(step) if (half == 0) == (axis == 0) else at_x(step)
        to = (df - step, dg) if axis == 0 else (df, dg - step)
        ref = self.cut(half, df, dg, part)
        copy = remote(ref, ref, self.sems, self.index(half, *to, part), device)
        copy.start()
        self.done.append(copy)

    def arrived(self, half, df, dg, part):
        ref = self.cut(half, df, dg, part)
        remote(ref, ref, self.sems, self.index(half, df, dg, part), at_z(1)).wait_recv()

    def to_sibling(self, half, df, dg):
        ref = self.cut(half, df, dg)
        copy = remote(ref, ref, self.core_sems, (half * 4 + df % 4) * 4 + dg % 4, sibling())
        copy.start()
        self.done.append(copy)
        self.core.append(copy)

    def push_all(self, half, df, dg, axis):
        for part in range(2):
            self.push(half, df, dg, axis, 1, part)
            self.push(half, df, dg, axis, -1, 1 - part)

    def start(self):
        for axis in range(2):
            for half in range(2):
                self.push_all(half, 0, 0, axis)
        for half in range(2):
            self.to_sibling(half, 0, 0)

    def first_pass(self):
        for half in range(2):
            self.arrived(half, 3, 0, 0)
            self.push(half, 3, 0, 0, 1, 0)
            self.arrived(half, 1, 0, 1)
            self.push(half, 1, 0, 0, -1, 1)

    def first_rest(self):
        for half in range(2):
            self.arrived(half, 3, 0, 1)
            self.arrived(half, 1, 0, 0)
            for df in (3, 1):
                self.push_all(half, df, 0, 1)
                self.to_sibling(half, df, 0)

    def first_far(self):
        for half in range(2):
            self.arrived(half, 2, 0, 0)
            self.arrived(half, 2, 0, 1)
            self.push_all(half, 2, 0, 1)
            self.to_sibling(half, 2, 0)

    def second_pass(self, df):
        for half in range(2):
            self.arrived(half, df, 3, 0)
            self.push(half, df, 3, 1, 1, 0)
            self.arrived(half, df, 1, 1)
            self.push(half, df, 1, 1, -1, 1)
        for half in range(2):
            self.arrived(half, df, 3, 1)
            self.to_sibling(half, df, 3)
            self.arrived(half, df, 1, 0)
            self.to_sibling(half, df, 1)

    def second_far(self, df):
        for half in range(2):
            for part in range(2):
                self.arrived(half, df, 2, part)
            self.to_sibling(half, df, 2)

    def land(self):
        for copy in self.core:
            copy.wait_recv()

    def close(self):
        for copy in self.done:
            copy.wait_send()


def forward_kernel(
    qkv_weight, out_weight, gate_up_weight, down_weight, extra, tokens, cotangent, table,
    one_out, two, token_rows, cot_rows, stats, qkv, head_mix, norm_table,
    summed, unit, scale, normed_two,
    one_q, two_q, one, norm_in, bias, normed, parts, mid, sent, far, near,
    pair_send, pair_recv, local_sem, y_send, y_recv,
    send_one, recv_one, core_send_one, core_recv_one,
    send_two, recv_two, core_send_two, core_recv_two,
):
    z, x = lax.axis_index("z"), lax.axis_index("x")
    yl, c, yh = lax.axis_index("yl"), lax.axis_index("c"), lax.axis_index("yh")
    rows, here = one_q.shape[1], tokens.shape[0]
    hq, fq = qkv_weight.shape[2] // 2, gate_up_weight.shape[2] // 2
    pair_sems, y_sems = (pair_send, pair_recv), (y_send, y_recv)
    for q in range(2):
        for t in range(3):
            one_q[q, :, t * hq : (t + 1) * hq] = qkv_weight[t, :, q * hq : (q + 1) * hq]
        one_q[q, :, 3 * hq : 4 * hq] = out_weight[:, q * hq : (q + 1) * hq]
        one_q[q, :, 4 * hq :] = extra[q]
    token_rows[pl.ds(0, here)] = tokens[...]
    greet([at_z(1), at_z(3), at_x(1), at_x(3)] + cube())

    same, cross = pair_moves()
    mine = pl.ds(pl.multiple_of((z * 4 + x) * 4 * rows + (yl * 2 + c) * rows, rows), rows)
    moves = [
        (one_q.at[c], one.at[mine], 0, same),
        (one_q.at[1 - c], one.at[mine], 1, cross),
        (two_q.at[c], two.at[mine], 2, same),
        (two_q.at[1 - c], two.at[mine], 3, cross),
    ]

    def launch(k):
        src, dst, index, device = moves[k]
        if device is same:
            stay_or_go(src, dst, pair_sems, index, device, local_sem.at[index // 2])
        else:
            remote(src, dst, pair_sems, index, device).start()

    def land(k):
        src, dst, index, device = moves[k]
        if device is same:
            stay_or_go_wait(src, dst, pair_sems, index, device, local_sem.at[index // 2])
        else:
            copy = remote(src, dst, pair_sems, index, device)
            copy.wait_recv()
            copy.wait_send()

    norm_moves = [
        remote(
            one_q.at[0, :, pl.ds(4 * hq, EXTRA)],
            norm_in.at[c],
            pair_sems,
            4 + which,
            {"yl": target["yl"], "c": target["c"], "yh": 1 - yh},
        )
        for which, target in enumerate((same, cross))
    ]
    launch(0)
    launch(1)
    for move in norm_moves:
        move.start()
    token_halves = [ring_gather_half(token_rows, top, y_sems, 0) for top in range(2)]
    for q in range(2):
        for t in range(2):
            two_q[q, :, t * fq : (t + 1) * fq] = gate_up_weight[t, :, q * fq : (q + 1) * fq]
        two_q[q, :, 2 * fq :] = down_weight[:, q * fq : (q + 1) * fq]
    cot_rows[pl.ds(0, here)] = cotangent[...]
    land(0)
    land(1)
    for move in norm_moves:
        move.wait_recv()
    own = (z * 4 + x) * 4 + 2 * c
    for core in range(2):
        block = pl.ds(pl.multiple_of((own + core) * rows, rows), rows)
        came = norm_in[core].astype(f32)
        place = lax.broadcasted_iota(jnp.int32, came.shape, 0)
        held = one[block, pl.ds(4 * hq, EXTRA)].astype(f32)
        one[block, pl.ds(4 * hq, EXTRA)] = (
            held + jnp.where((place >= 12) & (place < 20), came, 0.0)
        ).astype(bf16)
    first = Spread(one, rows, (send_one, recv_one), (core_send_one, core_recv_one))
    second = Spread(two, rows, (send_two, recv_two), (core_send_two, core_recv_two))
    first.start()
    launch(2)
    launch(3)
    first.first_pass()
    first.first_rest()
    token_passed = ring_gather_pass(token_rows, token_halves, y_sems, 0)
    first.second_pass(0)
    first.first_far()
    first.second_pass(3)
    first.second_pass(1)
    land(2)
    land(3)
    second.start()
    first.second_pass(2)
    for df in (0, 3, 1, 2):
        first.second_far(df)
    for copy in token_passed + [token_halves[1][0], token_halves[0][1]]:
        copy.wait_recv()
    cot_halves = [ring_gather_half(cot_rows, top, y_sems, 6) for top in range(2)]
    first.land()
    keep = pltpu.make_async_copy(one, one_out, local_sem.at[2])
    keep.start()

    read_extras(one, 4 * hq, norm_table, bias)

    def norm_rows(k, _):
        rng = pl.ds(pl.multiple_of(k * here, here), here)
        values = token_rows[rng].astype(f32)
        mean = jnp.mean(values, -1, keepdims=True)
        centered = values - mean
        inverse = lax.rsqrt(jnp.mean(centered * centered, -1, keepdims=True) + EPSILON)
        stats[0, rng] = mean
        stats[1, rng] = inverse
        normed[rng] = (centered * inverse * norm_table[0:1] + norm_table[1:2]).astype(bf16)
        return 0

    lax.fori_loop(0, 4, norm_rows, 0)
    second.first_pass()
    wide = 256

    def project(k, _):
        cols = pl.ds(pl.multiple_of(k * wide, wide), wide)
        value = dot(normed[...], one[:, cols], 1, 0)
        value = value + jnp.concatenate([bias[pl.ds(2 * k, 1)], bias[pl.ds(2 * k + 1, 1)]], 1)

        @pl.when(k < 2 * hq // wide)
        def _():
            for place in range(4):
                rng = pl.ds(place * here, here)
                turn = table[pl.ds(pl.multiple_of(half_of_place(place) * here, here), here)]
                for pair in range(wide // 128):
                    qkv[rng, pl.ds(pl.multiple_of(k * wide + pair * 128, 128), 128)] = turn_heads(
                        value[place * here : (place + 1) * here, pair * 128 : (pair + 1) * 128],
                        turn,
                        1.0,
                    ).astype(bf16)

        @pl.when(k >= 2 * hq // wide)
        def _():
            qkv[:, cols] = value.astype(bf16)

        return 0

    lax.fori_loop(0, 3 * hq // wide, project, 0)
    second.first_rest()
    cot_passed = ring_gather_pass(cot_rows, cot_halves, y_sems, 6)
    for sequence in range(2):
        mask = causal_mask(sequence, here)
        rng = pl.ds(sequence * 2 * here, 2 * here)

        def heads(k, _):
            def pair(t):
                return qkv[rng, pl.ds(pl.multiple_of(t * hq + k * 128, 128), 128)]

            q, key, value = pair(0), pair(1), pair(2)
            mixes = []
            for head in range(2):
                cut = slice(head * HEAD_DIM, (head + 1) * HEAD_DIM)
                soft = soft_of(q[:, cut], key[:, cut], mask).astype(bf16)
                mixes.append(dot(soft, value[:, cut], 1, 0))
            head_mix[rng, pl.ds(pl.multiple_of(k * 128, 128), 128)] = jnp.concatenate(
                mixes, 1
            ).astype(bf16)
            return 0

        lax.fori_loop(0, hq // 128, heads, 0, unroll=2)
        if sequence == 0:
            second.second_pass(0)
    second.first_far()

    def out_project(k, _):
        rng = pl.ds(pl.multiple_of(k * wide, wide), wide)
        parts[:, rng] = dot(head_mix[...], one[rng, pl.ds(3 * hq, hq)], 1, 1).astype(bf16)
        return 0

    lax.fori_loop(0, one.shape[0] // wide, out_project, 0)
    for copy in cot_passed + [cot_halves[1][0], cot_halves[0][1]]:
        copy.wait_recv()

    started = ring_sum_start(parts, mid, near, y_sems, 12)
    second.second_pass(3)
    middle = ring_sum_middle(parts, started, mid, sent, far, y_sems, 12)
    second.second_pass(1)
    finish = ring_sum_finish(parts, started, middle, far, near)
    half = here // 2
    halves = []
    for top in range(2):
        rng = pl.ds(top * half, half)
        total = tokens[rng].astype(f32) + finish(top)
        summed[rng] = total
        centered = total - jnp.mean(total, -1, keepdims=True)
        inverse = lax.rsqrt(jnp.mean(centered * centered, -1, keepdims=True) + EPSILON)
        unit_rows = centered * inverse
        unit[rng] = unit_rows
        scale[rng] = inverse
        normed_two[rng] = (unit_rows * norm_table[2:3] + norm_table[3:4]).astype(bf16)
        halves.append(ring_gather_half(normed_two, top, y_sems, 18))
    second.second_pass(2)
    passed = ring_gather_pass(normed_two, halves, y_sems, 18)
    for df in (0, 3, 1, 2):
        second.second_far(df)
    for copy in passed + [halves[1][0], halves[0][1]]:
        copy.wait_recv()
    second.land()
    keep.wait()
    for move in norm_moves:
        move.wait_send()
    for copies in token_halves + cot_halves + halves + [
        token_passed, cot_passed, started, middle, passed
    ]:
        for copy in copies:
            copy.wait_send()
    first.close()
    second.close()


def forward(qkv_weight, out_weight, gate_up_weight, down_weight, extra, tokens, cotangent, table):
    here, width = tokens.shape
    rows = qkv_weight.shape[1]
    hq, fq = qkv_weight.shape[2] // 2, gate_up_weight.shape[2] // 2
    full = pl.BlockSpec(memory_space=VMEM)
    anywhere = pl.BlockSpec(memory_space=pl.ANY)
    one_wide, two_wide = 4 * hq + EXTRA, 3 * fq

    def shape(*dims, dtype=bf16):
        return jax.ShapeDtypeStruct(dims, dtype)

    return pl.pallas_call(
        forward_kernel,
        out_shape=(
            shape(width, one_wide),
            shape(width, two_wide),
            shape(4 * here, width),
            shape(4 * here, width),
            shape(2, 4 * here, 1, dtype=f32),
            shape(4 * here, 3 * hq),
            shape(4 * here, hq),
            shape(4, width, dtype=f32),
            shape(here, width, dtype=f32),
            shape(here, width, dtype=f32),
            shape(here, 1, dtype=f32),
            shape(4 * here, width),
        ),
        in_specs=[full] * 8,
        out_specs=(anywhere, anywhere) + (full,) * 10,
        scratch_shapes=[
            VMEM((2, rows, one_wide), bf16),
            VMEM((2, rows, two_wide), bf16),
            VMEM((width, one_wide), bf16),
            VMEM((2, rows, EXTRA), bf16),
            VMEM((12, 128), f32),
            VMEM((4 * here, width), bf16),
            VMEM((4 * here, width), bf16),
        ]
        + [VMEM((2, here // 2, width), bf16)] * 4
        + [
            DMA((6,)), DMA((6,)), DMA((3,)), DMA((24,)), DMA((24,)),
            DMA((64,)), DMA((64,)), DMA((32,)), DMA((32,)),
            DMA((64,)), DMA((64,)), DMA((32,)), DMA((32,)),
        ],
        compiler_params=pltpu.CompilerParams(
            collective_id=0, has_side_effects=True, vmem_limit_bytes=VMEM_LIMIT
        ),
    )(qkv_weight, out_weight, gate_up_weight, down_weight, extra, tokens, cotangent, table)


class Reduce:
    def __init__(self, src, mid, far, near, sems, mid2, far2, near2, sems2):
        self.src, self.rows = src, src.shape[2] // 2
        self.rings = ((mid, far, near, sems), (mid2, far2, near2, sems2))
        self.done, self.got = [], {}

    def view(self, stage, half, d, part):
        piece = self.rows // 2
        rng = pl.ds(half * self.rows + part * piece, piece)
        if stage == 0:
            return self.src.at[d, :, rng] if half == 0 else self.src.at[:, d, rng]
        return self.src.at[0, d, rng] if half == 0 else self.src.at[d, 0, rng]

    def send(self, name, stage, half, way, src, dst, index):
        step = (1, -1)[way]
        device = at_z(step) if (half == 0) == (stage == 0) else at_x(step)
        copy = remote(src, dst, self.rings[stage][3], half * 6 + index * 2 + way, device)
        copy.start()
        self.done.append(copy)
        self.got[name, stage, half, way] = copy

    def far_rows(self, stage, half):
        mid = self.rings[stage][0]
        for way in range(2):
            self.send("mid", stage, half, way, self.view(stage, half, 2, way), mid.at[half, way], 0)

    def near_rows(self, stage, half):
        near = self.rings[stage][2]
        for way in range(2):
            src = self.view(stage, half, (1, 3)[way], 1 - way)
            self.send("near", stage, half, way, src, near.at[half, way], 1)

    def combine(self, stage, half):
        mid, far = self.rings[stage][:2]
        for way in range(2):
            self.got["mid", stage, half, way].wait_recv()
            ref = self.view(stage, half, (1, 3)[way], way)
            ref[...] = (ref[...].astype(f32) + mid[half, way].astype(f32)).astype(bf16)
            self.send("far", stage, half, way, ref, far.at[half, way], 2)

    def settle(self, stage, half, out=None):
        far, near = self.rings[stage][1:3]
        piece = self.rows // 2
        for part in range(2):
            self.got["far", stage, half, part].wait_recv()
            self.got["near", stage, half, 1 - part].wait_recv()
            ref = self.view(stage, half, 0, part)
            total = (
                ref[...].astype(f32)
                + far[half, part].astype(f32)
                + near[half, 1 - part].astype(f32)
            ).astype(bf16)
            if out is None:
                ref[...] = total
            else:
                out[half, pl.ds(part * piece, piece)] = total

    def close(self):
        for copy in self.done:
            copy.wait_send()


def backward_kernel(
    one, resid_rows, chip, qkv, head_mix, token_rows, stats, table, second_terms, norm_table,
    mixed_parts, resid, first_sum,
    result_one, result_two, norm_back, grad_tokens, mixed,
    held, spare, grad_mix, grad_proj, sib, mid_a, far_a, near_a, mid_b, far_b, near_b,
    blocks, mid_c, far_c, near_c, mid_d, far_d, near_d, packed_one, packed_two,
    ymid, ysent, yfar, ynear,
    load_sem, block_sem, core_send, core_recv, send_a, recv_a, send_b, recv_b,
    send_c, recv_c, send_d, recv_d, pair_send, pair_recv, local_sem, y_send, y_recv,
):
    z, x = lax.axis_index("z"), lax.axis_index("x")
    yl, c, yh = lax.axis_index("yl"), lax.axis_index("c"), lax.axis_index("yh")
    here = resid.shape[0]
    rows = result_one.shape[1]
    hq = head_mix.shape[1]
    width = held.shape[0]
    core_sems, pair_sems, y_sems = (core_send, core_recv), (pair_send, pair_recv), (y_send, y_recv)
    wide = 256

    def place_of(dz, dx):
        return ((z + dz) % 4) * 4 + (x + dx) % 4

    loads = [
        pltpu.make_async_copy(
            one.at[:, pl.ds(start, size)], held.at[:, pl.ds(start, size)], load_sem.at[k]
        )
        for k, (start, size) in enumerate(((3 * hq, hq), (0, 3 * hq)))
    ]
    loads.append(pltpu.make_async_copy(resid_rows, spare, load_sem.at[2]))
    order = []
    for d in (2, 1, 3, 0):
        for e in (2, 1, 3, 0):
            for pair in ((d, e), (e, d)):
                if pair not in order:
                    order.append(pair)
    block_loads = {
        (dz, dx): pltpu.make_async_copy(
            chip.at[place_of(dz, dx)], blocks.at[dz, dx], block_sem.at[dz * 4 + dx]
        )
        for dz, dx in order
    }
    loads[2].start()
    loads[0].start()
    for pair in order:
        block_loads[pair].start()
    loads[1].start()
    greet([at_z(1), at_z(3), at_x(1), at_x(3)] + cube())
    mixed_started = ring_sum_start(mixed_parts, ymid.at[0], ynear.at[0], y_sems, 0)
    second = Reduce(blocks, mid_c, far_c, near_c, (send_c, recv_c), mid_d, far_d, near_d, (send_d, recv_d))
    first = Reduce(sib, mid_a, far_a, near_a, (send_a, recv_a), mid_b, far_b, near_b, (send_b, recv_b))
    for pair in order:
        block_loads[pair].wait()
    for half in range(2):
        second.far_rows(0, half)
    for half in range(2):
        second.near_rows(0, half)

    loads[2].wait()
    loads[0].wait()

    def mix_back(k, _):
        cols = pl.ds(pl.multiple_of(k * wide, wide), wide)
        grad_mix[:, cols] = dot(
            spare[...], held[:, pl.ds(pl.multiple_of(3 * hq + k * wide, wide), wide)], 1, 0
        ).astype(bf16)
        return 0

    lax.fori_loop(0, hq // wide, mix_back, 0)

    def out_back(k, _):
        rng = pl.ds(pl.multiple_of(k * 2 * wide, 2 * wide), 2 * wide)
        held[rng, pl.ds(3 * hq, hq)] = dot(spare[:, rng], head_mix[...], 0, 0).astype(bf16)
        return 0

    lax.fori_loop(0, width // (2 * wide), out_back, 0)
    mixed_middle = ring_sum_middle(
        mixed_parts, mixed_started, ymid.at[0], ysent.at[0], yfar.at[0], y_sems, 0
    )
    for sequence in range(2):
        mask = causal_mask(sequence, here)
        rng = pl.ds(sequence * 2 * here, 2 * here)
        turn = jnp.concatenate(
            [
                table[pl.ds(pl.multiple_of(half_of_place(2 * sequence + k) * here, here), here)]
                for k in range(2)
            ],
            0,
        )

        def heads(k, _):
            def pair(t):
                return pl.ds(pl.multiple_of(t * hq + k * 128, 128), 128)

            q, key, value = qkv[rng, pair(0)], qkv[rng, pair(1)], qkv[rng, pair(2)]
            mix = grad_mix[rng, pair(0)]
            results = ([], [], [])
            for head in range(2):
                cut = slice(head * HEAD_DIM, (head + 1) * HEAD_DIM)
                soft = soft_of(q[:, cut], key[:, cut], mask)
                grad_soft = dot(mix[:, cut], value[:, cut], 1, 1)
                row_dot = jnp.sum(grad_soft * soft, -1, keepdims=True)
                grad_score = (soft * (grad_soft - row_dot)).astype(bf16)
                results[0].append(dot(grad_score, key[:, cut], 1, 0) * SCALE)
                results[1].append(dot(grad_score, q[:, cut], 0, 0) * SCALE)
                results[2].append(dot(soft.astype(bf16), mix[:, cut], 0, 0))
            for t in range(3):
                both = jnp.concatenate(results[t], 1)
                if t < 2:
                    both = turn_heads(both, turn, -1.0)
                grad_proj[rng, pair(t)] = both.astype(bf16)
            return 0

        lax.fori_loop(0, hq // 128, heads, 0, unroll=2)
        second.combine(0, sequence)

    bias_rows = [
        jnp.sum(grad_proj[:, pl.ds(k * 128, 128)].astype(f32), 0, keepdims=True)
        for k in range(3 * hq // 128)
    ]
    mean, inverse = stats[0], stats[1]
    loads[1].wait()

    def to_core(block):
        theirs = pl.ds(pl.multiple_of((2 * block + 1 - c) * 2 * rows, 2 * rows), 2 * rows)
        dz, dx = (block // 4 - z + 4) % 4, (block % 4 - x + 4) % 4
        return remote(held.at[theirs], sib.at[dz, dx], core_sems, block, sibling())

    def weights_back(k, _):
        rng = pl.ds(pl.multiple_of(k * wide, wide), wide)
        part = dot(grad_proj[...], held[rng, pl.ds(0, 3 * hq)], 1, 1)
        spare[:, rng] = part.astype(bf16)
        unit = (token_rows[:, rng].astype(f32) - mean) * inverse
        normed = (unit * norm_table[0:1, rng] + norm_table[1:2, rng]).astype(bf16)
        held[rng, pl.ds(0, 3 * hq)] = dot(normed, grad_proj[...], 0, 0).astype(bf16)
        gain = jnp.sum(part * unit, 0, keepdims=True)
        shift = jnp.sum(part, 0, keepdims=True)
        for tile in range(wide // 128):
            cut = slice(tile * 128, (tile + 1) * 128)
            lanes = pl.ds(pl.multiple_of(k * wide + tile * 128, 128), 128)
            extra = jnp.concatenate(
                bias_rows
                + [
                    gain[:, cut],
                    shift[:, cut],
                    second_terms[:, lanes],
                    jnp.zeros((rows - 16, 128), f32),
                ],
                0,
            ).astype(bf16)
            for copy in range(128 // rows):
                start = pl.multiple_of(k * wide + tile * 128 + copy * rows, rows)
                held[pl.ds(start, rows), pl.ds(4 * hq, EXTRA)] = extra
        for block in range(wide // (4 * rows)):
            to_core(k * (wide // (4 * rows)) + block).start()
        return 0

    lax.fori_loop(0, width // wide, weights_back, 0)
    first_started = ring_sum_start(spare, ymid.at[1], ynear.at[1], y_sems, 6)

    summed = set()

    def core_sum(dz, dx):
        if (dz, dx) in summed:
            return
        summed.add((dz, dx))
        block = place_of(dz, dx)
        to_core(block).wait_recv()
        ours = pl.ds(pl.multiple_of((2 * block + c) * 2 * rows, 2 * rows), 2 * rows)
        sib[dz, dx] = (sib[dz, dx].astype(f32) + held[ours].astype(f32)).astype(bf16)

    for half in range(2):
        for d in (2, 1, 3, 0):
            core_sum(*((2, d) if half == 0 else (d, 2)))
        first.far_rows(0, half)
    for half in range(2):
        for step in (1, 3):
            for d in (2, 1, 3, 0):
                core_sum(*((step, d) if half == 0 else (d, step)))
        first.near_rows(0, half)
    core_sum(0, 0)
    for half in range(2):
        second.settle(0, half)
        second.far_rows(1, half)
        second.near_rows(1, half)
    first_middle = ring_sum_middle(
        spare, first_started, ymid.at[1], ysent.at[1], yfar.at[1], y_sems, 6
    )
    for half in range(2):
        first.combine(0, half)
    for half in range(2):
        second.combine(1, half)
    half_here = here // 2
    finish = ring_sum_finish(mixed_parts, mixed_started, mixed_middle, yfar.at[0], ynear.at[0])
    for top in range(2):
        rng = pl.ds(top * half_here, half_here)
        mixed[rng] = (first_sum[rng] + finish(top)).astype(bf16)
    finish = ring_sum_finish(spare, first_started, first_middle, yfar.at[1], ynear.at[1])
    for top in range(2):
        rng = pl.ds(top * half_here, half_here)
        incoming = finish(top) * norm_table[0:1]
        unit_rows = (token_rows[rng].astype(f32) - stats[0, rng]) * stats[1, rng]
        grad_tokens[rng] = resid[rng] + stats[1, rng] * (
            incoming
            - jnp.mean(incoming, -1, keepdims=True)
            - unit_rows * jnp.mean(incoming * unit_rows, -1, keepdims=True)
        )

    home, away = {"yl": c, "c": yl}, {"yl": c, "c": 1 - yl}
    for half in range(2):
        second.settle(1, half, packed_two)
    stay_or_go(packed_two.at[yl], result_two.at[yl], pair_sems, 0, home, local_sem.at[0])
    cross_two = remote(packed_two.at[1 - yl], result_two.at[yl], pair_sems, 1, away)
    cross_two.start()
    for half in range(2):
        first.settle(0, half)
        first.far_rows(1, half)
        first.near_rows(1, half)
    for half in range(2):
        first.combine(1, half)
    for half in range(2):
        first.settle(1, half, packed_one)
    stay_or_go(packed_one.at[yl], result_one.at[yl], pair_sems, 2, home, local_sem.at[1])
    cross_one = remote(packed_one.at[1 - yl], result_one.at[yl], pair_sems, 3, away)
    cross_one.start()
    extras = pl.ds(4 * hq, EXTRA)
    norm_moves = [
        remote(
            packed_one.at[core, :, extras],
            norm_back.at[yl],
            pair_sems,
            4 + which,
            {"yl": c, "c": core, "yh": 1 - yh},
        )
        for which, core in enumerate((yl, 1 - yl))
    ]
    for move in norm_moves:
        move.start()
    for copy in [cross_two, cross_one] + norm_moves:
        copy.wait_recv()
        copy.wait_send()
    stay_or_go_wait(packed_two.at[yl], result_two.at[yl], pair_sems, 0, home, local_sem.at[0])
    stay_or_go_wait(packed_one.at[yl], result_one.at[yl], pair_sems, 2, home, local_sem.at[1])
    for copy in mixed_started + mixed_middle + first_started + first_middle:
        copy.wait_send()

    def drain(block, _):
        to_core(block).wait_send()
        return 0

    lax.fori_loop(0, 16, drain, 0)
    first.close()
    second.close()


def backward(
    one, resid_rows, chip, qkv, head_mix, token_rows, stats, table, second_terms, norm_table,
    mixed_parts, resid, first_sum,
):
    here, width = resid.shape
    hq = head_mix.shape[1]
    rows = width // 64
    piece = rows // 2
    one_wide, two_wide = one.shape[1], chip.shape[2]
    full = pl.BlockSpec(memory_space=VMEM)
    anywhere = pl.BlockSpec(memory_space=pl.ANY)

    def rings(wide):
        return [VMEM((2, 2, 4, piece, wide), bf16)] * 3 + [VMEM((2, 2, piece, wide), bf16)] * 3

    return pl.pallas_call(
        backward_kernel,
        out_shape=(
            jax.ShapeDtypeStruct((2, rows, one_wide), bf16),
            jax.ShapeDtypeStruct((2, rows, two_wide), bf16),
            jax.ShapeDtypeStruct((2, rows, EXTRA), bf16),
            jax.ShapeDtypeStruct((here, width), f32),
            jax.ShapeDtypeStruct((here, width), bf16),
        ),
        in_specs=[anywhere] * 3 + [full] * 10,
        out_specs=(full,) * 5,
        scratch_shapes=[
            VMEM((width, one_wide), bf16),
            VMEM((4 * here, width), bf16),
            VMEM((4 * here, hq), bf16),
            VMEM((4 * here, 3 * hq), bf16),
            VMEM((4, 4, 2 * rows, one_wide), bf16),
        ]
        + rings(one_wide)
        + [VMEM((4, 4, 2 * rows, two_wide), bf16)]
        + rings(two_wide)
        + [VMEM((2, rows, one_wide), bf16), VMEM((2, rows, two_wide), bf16)]
        + [VMEM((2, 2, here // 2, width), bf16)] * 4
        + [DMA((3,)), DMA((16,)), DMA((16,)), DMA((16,))]
        + [DMA((12,))] * 8
        + [DMA((6,)), DMA((6,)), DMA((2,)), DMA((12,)), DMA((12,))],
        compiler_params=pltpu.CompilerParams(
            collective_id=3, has_side_effects=True, vmem_limit_bytes=VMEM_LIMIT
        ),
    )(
        one, resid_rows, chip, qkv, head_mix, token_rows, stats, table, second_terms, norm_table,
        mixed_parts, resid, first_sum,
    )


def shards(
    tokens, cotangent, norm_params, qkv_weight, qkv_bias, out_weight, gate_up_weight, down_weight
):
    yl, yh, c = lax.axis_index("yl"), lax.axis_index("yh"), lax.axis_index("c")
    mine = ((lax.axis_index("z") * 4 + lax.axis_index("x")) * 2 + yl) * 2 + c
    rows = qkv_weight.shape[1]
    hq = qkv_weight.shape[2] // 2
    fq = gate_up_weight.shape[2] // 2
    heads = hq // HEAD_DIM
    pairs = 3 * heads // 2

    norm_high = lax.optimization_barrier(norm_params.astype(bf16))
    norm_low = (norm_params - norm_high.astype(f32)).astype(bf16)
    share = norm_params.shape[1]
    norm_extra = jnp.where(
        jnp.arange(EXTRA) // share == mine % 4 * 2 + yh,
        jnp.tile(jnp.concatenate([norm_high, norm_low], 0), (1, EXTRA // share)),
        0,
    )
    bias_q = qkv_bias.reshape(3, 2, heads).transpose(1, 0, 2).reshape(2, pairs, 2, 1)
    bias_extra = jnp.where(jnp.arange(HEAD_DIM) == mine, bias_q, 0).reshape(2, pairs, EXTRA)
    extra = jnp.concatenate(
        [
            bias_extra,
            jnp.broadcast_to(norm_extra[None], (2, *norm_extra.shape)),
            jnp.zeros((2, rows - pairs - 8, EXTRA), bf16),
        ],
        1,
    )
    table = jnp.asarray(tables())
    (
        one, second, token_rows, cot_rows, stats, qkv, head_mix, norm_table,
        first_sum, unit_two, scale_two, normed_two,
    ) = forward(
        qkv_weight, out_weight.T, gate_up_weight, down_weight.T, extra, tokens, cotangent, table
    )
    grad_resid, second_terms, resid_rows, mixed_parts, chip = feed_forward(
        normed_two, cot_rows, cotangent, unit_two, scale_two, norm_table[2:], second
    )
    first_back, second_back, norm_other, grad_input, mixed = backward(
        one, resid_rows, chip, qkv, head_mix, token_rows, stats, table, second_terms, norm_table,
        mixed_parts, grad_resid, first_sum,
    )

    gu_back, down_back = second_back[:, :, : 2 * fq], second_back[:, :, 2 * fq :]
    out_down = down_back.transpose(0, 2, 1).reshape(2 * fq, rows).astype(f32)
    out_gu = (
        gu_back.reshape(2, rows, 2, fq).transpose(2, 1, 0, 3).reshape(2, rows, 2 * fq).astype(f32)
    )
    out_qkv = (
        first_back[:, :, : 3 * hq]
        .reshape(2, rows, 3, hq)
        .transpose(2, 1, 0, 3)
        .reshape(3, rows, 2 * hq)
        .astype(f32)
    )
    out_out = (
        first_back[:, :, 3 * hq : 4 * hq].transpose(0, 2, 1).reshape(2 * hq, rows).astype(f32)
    )
    extra_back = first_back[:, :, 4 * hq :].astype(f32)
    out_bias = (
        lax.dynamic_index_in_dim(
            extra_back[:, :pairs].reshape(2, pairs, 2, HEAD_DIM), mine, 3, False
        )
        .reshape(2, 3, heads)
        .transpose(1, 0, 2)
        .reshape(3, 2 * heads, 1)
    )
    norm_sums = (extra_back + norm_other.astype(f32)).sum(0)[pairs : pairs + 4]
    out_norm = lax.dynamic_index_in_dim(
        norm_sums.reshape(4, EXTRA // share, share), mine % 4 * 2 + yh, 1, False
    )
    return (mixed, grad_input, out_norm, out_qkv, out_bias, out_out, out_gu, out_down)


def solution(mesh):
    grid = Mesh(mesh.devices.reshape(4, 4, 2, 2, 2), GRID)
    placed = (
        P(GRID, None),
        P(GRID, None),
        P(None, GRID),
        P(None, ROWS, "yh"),
        P(None, "yh", ROWS),
        P("yh", ROWS),
        P(None, ROWS, "yh"),
        P("yh", ROWS),
    )
    return jax.shard_map(
        shards,
        mesh=grid,
        in_specs=placed,
        out_specs=(
            P(GRID, None),
            P(GRID, None),
            P(None, GRID),
            P(None, ROWS, "yh"),
            P(None, "yh", ROWS),
            P("yh", ROWS),
            P(None, ROWS, "yh"),
            P("yh", ROWS),
        ),
        check_vma=False,
    )
```

```python
import jax
import jax.numpy as jnp
import numpy as np
from jax import lax
from jax.experimental import pallas as pl
from jax.experimental.pallas import tpu as pltpu
from jax.sharding import Mesh
from jax.sharding import PartitionSpec as P

HEAD_DIM = 64
ROTARY = 16
EPSILON = 1e-05
SCALE = 0.125

GRID = ("z", "x", "yl", "c", "yh")
ROWS = ("z", "x", "yl", "c")
EXTRA = 128
EARLY = 1408

bf16 = jnp.bfloat16
f32 = jnp.float32

MESH = pl.DeviceIdType.MESH
VMEM = pltpu.VMEM
DMA = pltpu.SemaphoreType.DMA
VMEM_LIMIT = 60 * 1024 * 1024


def at_y(k):
    y = (lax.axis_index("yh") * 2 + lax.axis_index("yl") + k) % 4
    return {"yl": y % 2, "yh": y // 2}


def at_z(k):
    return {"z": (lax.axis_index("z") + k) % 4}


def at_x(k):
    return {"x": (lax.axis_index("x") + k) % 4}


def sibling():
    return {"c": 1 - lax.axis_index("c")}


def greet(devices):
    barrier = pltpu.get_barrier_semaphore()
    for device in devices:
        pl.semaphore_signal(barrier, inc=1, device_id=device, device_id_type=MESH)
    pl.semaphore_wait(barrier, len(devices))


def remote(src, dst, sems, index, device):
    send, recv = sems
    return pltpu.make_async_remote_copy(
        src_ref=src,
        dst_ref=dst,
        send_sem=send.at[index],
        recv_sem=recv.at[index],
        device_id=device,
        device_id_type=MESH,
    )


def ring_gather_half(out, top, sems, base):
    here = out.shape[0] // 4
    half = here // 2
    copies = []
    for way, step, block in ((0, 1, 3), (1, -1, 2)):
        copies.append(
            remote(
                out.at[pl.ds(top * half, half)],
                out.at[pl.ds(block * here + top * half, half)],
                sems,
                base + 2 * way + top,
                at_y(step),
            )
        )
        copies[-1].start()
    return copies


def ring_gather_pass(out, halves, sems, base):
    here = out.shape[0] // 4
    half = here // 2
    passed = []
    for way, step, block in ((0, 1, 3), (1, -1, 2)):
        halves[way][way].wait_recv()
        passed.append(
            remote(
                out.at[pl.ds(block * here + way * half, half)],
                out.at[pl.ds(here + way * half, half)],
                sems,
                base + 4 + way,
                at_y(step),
            )
        )
        passed[-1].start()
    return passed


def pair_moves():
    yl, c = lax.axis_index("yl"), lax.axis_index("c")
    return {"yl": c, "c": yl}, {"yl": 1 - c, "c": yl}


def stay_or_go(src, dst, sems, index, device, local_sem):
    yl, c = lax.axis_index("yl"), lax.axis_index("c")

    @pl.when(yl == c)
    def _():
        pltpu.make_async_copy(src, dst, local_sem).start()

    @pl.when(yl != c)
    def _():
        remote(src, dst, sems, index, device).start()


def stay_or_go_wait(src, dst, sems, index, device, local_sem):
    yl, c = lax.axis_index("yl"), lax.axis_index("c")

    @pl.when(yl == c)
    def _():
        pltpu.make_async_copy(src, dst, local_sem).wait()

    @pl.when(yl != c)
    def _():
        copy = remote(src, dst, sems, index, device)
        copy.wait_recv()
        copy.wait_send()


def ring_sum_start(parts, mid, near, sems, base):
    here = parts.shape[0] // 4
    half = here // 2
    copies = []
    for way, step in ((0, 1), (1, -1)):
        copies.append(
            remote(
                parts.at[pl.ds(here + way * half, half)], mid.at[way], sems, base + way, at_y(step)
            )
        )
    for way, step, block in ((0, 1, 2), (1, -1, 3)):
        copies.append(
            remote(
                parts.at[pl.ds(block * here + (1 - way) * half, half)],
                near.at[way],
                sems,
                base + 2 + way,
                at_y(step),
            )
        )
    for copy in copies:
        copy.start()
    return copies


def ring_sum_middle(parts, started, mid, sent, far, sems, base):
    here = parts.shape[0] // 4
    half = here // 2
    copies = []
    for way, step, block in ((0, 1, 2), (1, -1, 3)):
        started[way].wait_recv()
        sent[way] = (
            parts[pl.ds(block * here + way * half, half)].astype(f32) + mid[way].astype(f32)
        ).astype(bf16)
        copies.append(remote(sent.at[way], far.at[way], sems, base + 4 + way, at_y(step)))
        copies[-1].start()
    return copies


def ring_sum_finish(parts, started, middle, far, near):
    half = parts.shape[0] // 8

    def finish(top):
        started[2 + 1 - top].wait_recv()
        middle[top].wait_recv()
        return (
            parts[pl.ds(top * half, half)].astype(f32)
            + far[top].astype(f32)
            + near[1 - top].astype(f32)
        )

    return finish


def tables():
    half = ROTARY // 2
    position = np.arange(256, dtype=np.float32)
    frequency = np.power(np.float32(10000.0), -np.arange(half, dtype=np.float32) * np.float32(2.0 / ROTARY))
    angles = position[:, None] * frequency[None, :].astype(np.float32)
    cosine, sine = np.cos(angles), np.sin(angles)
    own = np.ones((256, 2, HEAD_DIM), np.float32)
    up = np.zeros((256, 2, HEAD_DIM), np.float32)
    down = np.zeros((256, 2, HEAD_DIM), np.float32)
    for head in range(2):
        own[:, head, :half] = cosine
        own[:, head, half:ROTARY] = cosine
        up[:, head, :half] = -sine
        down[:, head, half:ROTARY] = sine
    return np.concatenate([a.reshape(256, 128) for a in (own, up, down)], 1)


def dot(a, b, ca, cb):
    return lax.dot_general(a, b, (((ca,), (cb,)), ((), ())), preferred_element_type=f32)


def turn_heads(value, table, sign):
    own, up, down = table[:, :128], table[:, 128:256], table[:, 256:]
    return value * own + sign * (
        pltpu.roll(value, 120, 1) * up + pltpu.roll(value, 8, 1) * down
    )


def half_of_place(place):
    y = lax.axis_index("yh") * 2 + lax.axis_index("yl")
    return ((y + (0, 2, 1, 3)[place]) % 4) // 2


def causal_mask(sequence, here):
    length = 2 * here
    first = half_of_place(2 * sequence)

    def position(dim):
        index = lax.broadcasted_iota(jnp.int32, (length, length), dim)
        return jnp.where(index < here, index + first * here, index - first * here)

    return position(0) >= position(1)


def soft_of(queries, keys, mask):
    scores = dot(queries, keys, 1, 1) * SCALE
    scores = jnp.where(mask, scores, -1000000000.0)
    powers = jnp.exp(scores - jnp.max(scores, -1, keepdims=True))
    return powers * (1.0 / jnp.sum(powers, -1, keepdims=True))


def read_extras(one, first_column, norm_table, bias):
    total = None
    for group in range(one.shape[0] // 128):
        block = one[pl.ds(group * 128, 128), pl.ds(first_column, 128)].astype(f32)
        block = block[0:32] + block[32:64] + block[64:96] + block[96:128]
        norm_table[:, pl.ds(group * 128, 128)] = block[12:16] + block[16:20]
        total = block[0:12] if total is None else total + block[0:12]
    bias[...] = total


class Reduce:
    def __init__(self, view, rows, rings):
        self.view, self.rows, self.rings = view, rows, rings
        self.done, self.got = [], {}

    def send(self, name, stage, half, way, src, dst, index):
        step = (1, -1)[way]
        device = at_z(step) if (half == 0) == (stage == 0) else at_x(step)
        copy = remote(src, dst, self.rings[stage][3], half * 6 + index * 2 + way, device)
        copy.start()
        self.done.append(copy)
        self.got[name, stage, half, way] = copy

    def begin(self, stage):
        mid, _, near, _ = self.rings[stage]
        for half in range(2):
            for way in range(2):
                src = self.view(stage, half, 2, way)
                self.send("mid", stage, half, way, src, mid.at[half, way], 0)
        for half in range(2):
            for way in range(2):
                src = self.view(stage, half, (1, 3)[way], 1 - way)
                self.send("near", stage, half, way, src, near.at[half, way], 1)

    def combine(self, stage):
        mid, far = self.rings[stage][:2]
        for half in range(2):
            for way in range(2):
                self.got["mid", stage, half, way].wait_recv()
                ref = self.view(stage, half, (1, 3)[way], way)
                ref[...] = (ref[...].astype(f32) + mid[half, way].astype(f32)).astype(bf16)
                self.send("far", stage, half, way, ref, far.at[half, way], 2)

    def settle(self, stage, out=None):
        far, near = self.rings[stage][1:3]
        piece = self.rows // 2
        for half in range(2):
            for part in range(2):
                self.got["far", stage, half, part].wait_recv()
                self.got["near", stage, half, 1 - part].wait_recv()
                ref = self.view(stage, half, 0, part)
                total = (
                    ref[...].astype(f32)
                    + far[half, part].astype(f32)
                    + near[half, 1 - part].astype(f32)
                ).astype(bf16)
                if out is None:
                    ref[...] = total
                else:
                    out[half, pl.ds(part * piece, piece)] = total

    def close(self):
        for copy in self.done:
            copy.wait_send()


def ring_buffers(stage, piece, wide):
    dims = (2, 2, 4, piece, wide) if stage == 0 else (2, 2, piece, wide)
    return [VMEM(dims, bf16)] * 3 + [DMA((12,))] * 2


def feed_forward_kernel(
    normed, cot_rows, cotangent, unit, scale, norm_table, weights,
    resid, sums, spread, mixed_parts, chip, settled,
    held, pair, hidden, normed_t, cot_t, parts, sib, mid, sent, far, near,
    rmid, rfar, rnear, r_send, r_recv,
    load_sem, store_sem, core_send, core_recv, y_send, y_recv,
):
    columns, width = held.shape[3] // 3, normed.shape[1]
    wide = 256
    rows = sib.shape[1]
    sub = cotangent.shape[0] // 2
    z, x, c = lax.axis_index("z"), lax.axis_index("x"), lax.axis_index("c")
    y_sems, core_sems = (y_send, y_recv), (core_send, core_recv)
    whole, rest = columns // wide, columns % wide
    all_pair, all_hidden = pl.ds(0, 2 * columns), pl.ds(2 * columns, columns)
    groups = (pl.ds(0, EARLY), pl.ds(EARLY, 3 * columns - EARLY))

    def load(k, which, size):
        start = pl.multiple_of(which * columns + k * wide, 128)
        cut = pl.ds(start, size)
        return pltpu.make_async_copy(
            weights.at[:, :, :, cut], held.at[:, :, :, cut], load_sem.at[k, which]
        )

    for k in range(whole + (rest > 0)):
        for which in range(3):
            load(k, which, wide if k < whole else rest).start()

    def flip(k, _):
        rng = pl.ds(pl.multiple_of(k * wide, wide), wide)
        normed_t[rng] = normed[:, rng].T
        cot_t[rng] = cot_rows[:, rng].T
        return 0

    lax.fori_loop(0, width // wide, flip, 0)
    greet([at_z(1), at_z(3), at_x(1), at_x(3), at_y(1), at_y(3), sibling()])

    tall = width // 4

    def tile(k, cut):
        return k, slice(None), slice(None), cut

    def ahead(part, k, size):
        these = pl.ds(4 * part * sub, 4 * sub)

        def cut(which):
            return pl.ds(pl.multiple_of(which * columns + k * wide, 128), size)

        def weight(which):
            return held[:, :, :, cut(which)].reshape(width, size)

        if part == 0:
            for which in range(3):
                load(k, which, size).wait()
        gate = dot(normed[these], weight(0), 1, 0)
        up = dot(normed[these], weight(1), 1, 0)
        grad_hidden = dot(cot_rows[these], weight(2), 1, 0)
        sigmoid = jax.nn.sigmoid(gate)
        activated = gate * sigmoid
        hidden[these, cut(0)] = (activated * up).astype(bf16)
        pair[these, cut(0)] = (
            grad_hidden * up * sigmoid * (1.0 + gate * (1.0 - sigmoid))
        ).astype(bf16)
        pair[these, cut(1)] = (grad_hidden * activated).astype(bf16)
        return 0

    part_subs = [parts.at[pl.ds(4 * k * sub, 4 * sub)] for k in range(2)]
    started, middle, halves, passed = [], [], [], []

    def ring_middle(part):
        middle.append(
            ring_sum_middle(
                part_subs[part], started[part], mid.at[part], sent.at[part], far.at[part],
                y_sems, 6 * part,
            )
        )

    for part in range(2):
        lax.fori_loop(0, whole, lambda k, _: ahead(part, k, wide), 0)
        if rest:
            ahead(part, whole, rest)
        if part == 1:
            ring_middle(0)

        def second_back(k, _):
            rng = pl.ds(pl.multiple_of(k * tall, tall), tall)
            weight = held[tile(k, all_pair)].reshape(tall, 2 * columns)
            these = pl.ds(4 * part * sub, 4 * sub)
            parts[these, rng] = dot(pair[these], weight, 1, 1).astype(bf16)
            return 0

        lax.fori_loop(0, 4, second_back, 0)
        started.append(
            ring_sum_start(part_subs[part], mid.at[part], near.at[part], y_sems, 6 * part)
        )

    def to_core(block, which):
        theirs = pl.ds(pl.multiple_of((1 - c) * rows, rows), rows)
        return remote(
            held.at[block // 4, block % 4, theirs, groups[which]],
            sib.at[block, :, groups[which]],
            core_sems,
            block + 16 * which,
            sibling(),
        )

    ours = pl.ds(pl.multiple_of(c * rows, rows), rows)

    def core_sum(block, which):
        to_core(block, which).wait_recv()
        mine = (block // 4, block % 4, ours, groups[which])
        held[mine] = (
            held[mine].astype(f32) + sib[block, :, groups[which]].astype(f32)
        ).astype(bf16)

    def early_weights(k, _):
        rng = pl.ds(pl.multiple_of(k * tall, tall), tall)
        grad = dot(normed_t[rng], pair[:, pl.ds(0, EARLY)], 1, 0).astype(bf16)
        held[tile(k, groups[0])] = grad.reshape(4, 2 * rows, EARLY)
        for block in range(4):
            to_core(4 * k + block, 0).start()

        @pl.when(k > 0)
        def _():
            for block in range(4):
                core_sum(4 * k - 4 + block, 0)

        return 0

    def settle_rows(part):
        finish = ring_sum_finish(
            part_subs[part], started[part], middle[part], far.at[part], near.at[part]
        )
        here = pl.ds(part * sub, sub)
        total = jnp.concatenate([finish(0), finish(1)], 0)
        unit_rows = unit[here]
        incoming = total * norm_table[2:3]
        result = cotangent[here].astype(f32) + scale[here] * (
            incoming
            - jnp.mean(incoming, -1, keepdims=True)
            - unit_rows * jnp.mean(incoming * unit_rows, -1, keepdims=True)
        )
        resid[here] = result
        spread[pl.ds(4 * part * sub, sub)] = result.astype(bf16)
        out = spread.at[pl.ds(4 * part * sub, 4 * sub)]
        halves.append([ring_gather_half(out, top, y_sems, 12 + 6 * part) for top in range(2)])
        both = jnp.concatenate(
            [
                jnp.sum(total * unit_rows, 0, keepdims=True),
                jnp.sum(total, 0, keepdims=True),
            ],
            0,
        )
        sums[...] = both if part == 0 else sums[...] + both

    def gather_pass(part):
        out = spread.at[pl.ds(4 * part * sub, 4 * sub)]
        passed.append(ring_gather_pass(out, halves[part], y_sems, 12 + 6 * part))

    lax.fori_loop(0, 3, early_weights, 0)
    ring_middle(1)
    lax.fori_loop(3, 4, early_weights, 0)
    for block in range(12, 16):
        core_sum(block, 0)

    def view(stage, half, d, part):
        start = c * rows + half * (rows // 2) + part * (rows // 4)
        rng = pl.ds(pl.multiple_of(start, rows // 4), rows // 4)
        if half == 0:
            return held.at[(z + d) % 4, :, rng, groups[0]]
        return held.at[:, (x + d) % 4, rng, groups[0]]

    reduce = Reduce(view, rows // 2, {0: (rmid, rfar, rnear, (r_send, r_recv))})
    reduce.begin(0)
    settle_rows(0)

    def mix(k, _):
        rng = pl.ds(pl.multiple_of(k * tall, tall), tall)
        weight = held[tile(k, all_hidden)].reshape(tall, columns)
        value = dot(hidden[...], weight, 1, 1).astype(bf16)
        for part in range(2):
            for block in range(4):
                start = (part * 4 + block) * sub
                mixed_parts[pl.ds((2 * block + part) * sub, sub), rng] = value[start : start + sub]
        return 0

    lax.fori_loop(0, 4, mix, 0)
    settle_rows(1)
    gather_pass(0)
    reduce.combine(0)

    def late_weights(k, _):
        rng = pl.ds(pl.multiple_of(k * tall, tall), tall)
        if EARLY < 2 * columns:
            left = pl.ds(EARLY, 2 * columns - EARLY)
            grad = dot(normed_t[rng], pair[:, left], 1, 0).astype(bf16)
            held[tile(k, left)] = grad.reshape(4, 2 * rows, 2 * columns - EARLY)
        grad = dot(cot_t[rng], hidden[...], 1, 0).astype(bf16)
        held[tile(k, all_hidden)] = grad.reshape(4, 2 * rows, columns)
        for block in range(4):
            to_core(4 * k + block, 1).start()

        @pl.when(k > 0)
        def _():
            for block in range(4):
                add_core(4 * k - 4 + block)

        return 0

    def store(block):
        return pltpu.make_async_copy(
            held.at[block // 4, block % 4, ours, groups[1]], chip.at[block], store_sem.at[block]
        )

    def add_core(block):
        core_sum(block, 1)
        store(block).start()

    lax.fori_loop(0, 2, late_weights, 0)
    gather_pass(1)
    lax.fori_loop(2, 4, late_weights, 0)
    for block in range(12, 16):
        add_core(block)
    reduce.settle(0)
    top_rows = pl.ds(pl.multiple_of(c * rows, rows // 2), rows // 2)
    low_rows = pl.ds(pl.multiple_of(c * rows + rows // 2, rows // 2), rows // 2)
    keep = [
        pltpu.make_async_copy(held.at[z, :, top_rows, groups[0]], settled.at[0], store_sem.at[16]),
        pltpu.make_async_copy(held.at[:, x, low_rows, groups[0]], settled.at[1], store_sem.at[17]),
    ]
    for copy in keep:
        copy.start()

    def drain(block, _):
        to_core(block, 0).wait_send()
        to_core(block, 1).wait_send()
        store(block).wait()
        return 0

    lax.fori_loop(0, 16, drain, 0)
    for k in range(2):
        for copy in passed[k] + [halves[k][1][0], halves[k][0][1]]:
            copy.wait_recv()
        for copy in started[k] + middle[k] + halves[k][0] + halves[k][1] + passed[k]:
            copy.wait_send()
    reduce.close()
    for copy in keep:
        copy.wait()


def feed_forward(normed, cot_rows, cotangent, unit, scale, norm_table, weights):
    tokens, width = normed.shape
    here = cotangent.shape[0]
    columns = weights.shape[1] // 3
    rows = width // 32
    full = pl.BlockSpec(memory_space=VMEM)
    anywhere = pl.BlockSpec(memory_space=pl.ANY)
    tiles = -(-columns // 256)
    return pl.pallas_call(
        feed_forward_kernel,
        out_shape=(
            jax.ShapeDtypeStruct((here, width), f32),
            jax.ShapeDtypeStruct((2, width), f32),
            jax.ShapeDtypeStruct((tokens, width), bf16),
            jax.ShapeDtypeStruct((tokens, width), bf16),
            jax.ShapeDtypeStruct((16, rows, 3 * columns - EARLY), bf16),
            jax.ShapeDtypeStruct((2, 4, rows // 2, EARLY), bf16),
        ),
        in_specs=[full] * 6 + [anywhere],
        out_specs=(full,) * 4 + (anywhere,) * 2,
        scratch_shapes=[
            VMEM((4, 4, 2 * rows, 3 * columns), bf16),
            VMEM((tokens, 2 * columns), bf16),
            VMEM((tokens, columns), bf16),
            VMEM((width, tokens), bf16),
            VMEM((width, tokens), bf16),
            VMEM((tokens, width), bf16),
            VMEM((16, rows, 3 * columns), bf16),
        ]
        + [VMEM((2, 2, here // 4, width), bf16)] * 4
        + ring_buffers(0, rows // 4, EARLY)
        + [DMA((tiles, 3)), DMA((18,)), DMA((32,)), DMA((32,)), DMA((24,)), DMA((24,))],
        compiler_params=pltpu.CompilerParams(
            collective_id=2, has_side_effects=True, vmem_limit_bytes=VMEM_LIMIT
        ),
    )(
        normed, cot_rows, cotangent, unit, scale, norm_table,
        weights.reshape(4, 4, 2 * rows, 3 * columns),
    )


def cube():
    yl, c, yh = lax.axis_index("yl"), lax.axis_index("c"), lax.axis_index("yh")
    return [
        {"yl": (yl + a) % 2, "c": (c + b) % 2, "yh": (yh + d) % 2}
        for a in range(2)
        for b in range(2)
        for d in range(2)
        if a + b + d
    ]


class Spread:
    def __init__(self, out, rows, sems, core_sems):
        self.out, self.rows, self.sems, self.core_sems = out, rows, sems, core_sems
        self.done, self.core = [], []

    def cut(self, half, df, dg, part=None):
        z, x = lax.axis_index("z"), lax.axis_index("x")
        dz, dx = (df, dg) if half == 0 else (dg, df)
        place = ((z + dz) % 4) * 4 + (x + dx) % 4
        start = (place * 4 + lax.axis_index("c") * 2 + half) * self.rows
        piece = self.rows // 2
        if part is None:
            return self.out.at[pl.ds(pl.multiple_of(start, self.rows), self.rows)]
        return self.out.at[pl.ds(pl.multiple_of(start + part * piece, piece), piece)]

    def index(self, half, df, dg, part):
        return ((half * 4 + df % 4) * 4 + dg % 4) * 2 + part

    def push(self, half, df, dg, axis, step, part):
        device = at_z(step) if (half == 0) == (axis == 0) else at_x(step)
        to = (df - step, dg) if axis == 0 else (df, dg - step)
        ref = self.cut(half, df, dg, part)
        copy = remote(ref, ref, self.sems, self.index(half, *to, part), device)
        copy.start()
        self.done.append(copy)

    def arrived(self, half, df, dg, part):
        ref = self.cut(half, df, dg, part)
        remote(ref, ref, self.sems, self.index(half, df, dg, part), at_z(1)).wait_recv()

    def to_sibling(self, half, df, dg):
        ref = self.cut(half, df, dg)
        copy = remote(ref, ref, self.core_sems, (half * 4 + df % 4) * 4 + dg % 4, sibling())
        copy.start()
        self.done.append(copy)
        self.core.append(copy)

    def push_all(self, half, df, dg, axis):
        for part in range(2):
            self.push(half, df, dg, axis, 1, part)
            self.push(half, df, dg, axis, -1, 1 - part)

    def start(self):
        for axis in range(2):
            for half in range(2):
                self.push_all(half, 0, 0, axis)
        for half in range(2):
            self.to_sibling(half, 0, 0)

    def first_pass(self):
        for half in range(2):
            self.arrived(half, 3, 0, 0)
            self.push(half, 3, 0, 0, 1, 0)
            self.arrived(half, 1, 0, 1)
            self.push(half, 1, 0, 0, -1, 1)

    def first_rest(self):
        for half in range(2):
            self.arrived(half, 3, 0, 1)
            self.arrived(half, 1, 0, 0)
            for df in (3, 1):
                self.push_all(half, df, 0, 1)
                self.to_sibling(half, df, 0)

    def first_far(self):
        for half in range(2):
            self.arrived(half, 2, 0, 0)
            self.arrived(half, 2, 0, 1)
            self.push_all(half, 2, 0, 1)
            self.to_sibling(half, 2, 0)

    def second_pass(self, df):
        for half in range(2):
            self.arrived(half, df, 3, 0)
            self.push(half, df, 3, 1, 1, 0)
            self.arrived(half, df, 1, 1)
            self.push(half, df, 1, 1, -1, 1)
        for half in range(2):
            self.arrived(half, df, 3, 1)
            self.to_sibling(half, df, 3)
            self.arrived(half, df, 1, 0)
            self.to_sibling(half, df, 1)

    def second_far(self, df):
        for half in range(2):
            for part in range(2):
                self.arrived(half, df, 2, part)
            self.to_sibling(half, df, 2)

    def land(self):
        for copy in self.core:
            copy.wait_recv()

    def close(self):
        for copy in self.done:
            copy.wait_send()


def forward_kernel(
    qkv_weight, out_weight, gate_up_weight, down_weight, extra, tokens, cotangent, table,
    one_out, two, token_rows, cot_rows, stats, qkv, head_mix, norm_table,
    summed, unit, scale, normed_two,
    one_q, two_q, one, norm_in, bias, normed, parts, mid, sent, far, near,
    pair_send, pair_recv, local_sem, y_send, y_recv,
    send_one, recv_one, core_send_one, core_recv_one,
    send_two, recv_two, core_send_two, core_recv_two,
):
    z, x = lax.axis_index("z"), lax.axis_index("x")
    yl, c, yh = lax.axis_index("yl"), lax.axis_index("c"), lax.axis_index("yh")
    rows, here = one_q.shape[1], tokens.shape[0]
    hq, fq = qkv_weight.shape[2] // 2, gate_up_weight.shape[2] // 2
    pair_sems, y_sems = (pair_send, pair_recv), (y_send, y_recv)
    for q in range(2):
        for t in range(3):
            one_q[q, :, t * hq : (t + 1) * hq] = qkv_weight[t, :, q * hq : (q + 1) * hq]
        one_q[q, :, 3 * hq : 3 * hq + EXTRA] = extra[q]
        one_q[q, :, 3 * hq + EXTRA :] = out_weight[:, q * hq : (q + 1) * hq]
    token_rows[pl.ds(0, here)] = tokens[...]
    greet([at_z(1), at_z(3), at_x(1), at_x(3)] + cube())

    same, cross = pair_moves()
    mine = pl.ds(pl.multiple_of((z * 4 + x) * 4 * rows + (yl * 2 + c) * rows, rows), rows)
    moves = [
        (one_q.at[c], one.at[mine], 0, same),
        (one_q.at[1 - c], one.at[mine], 1, cross),
        (two_q.at[c], two.at[mine], 2, same),
        (two_q.at[1 - c], two.at[mine], 3, cross),
    ]

    def launch(k):
        src, dst, index, device = moves[k]
        if device is same:
            stay_or_go(src, dst, pair_sems, index, device, local_sem.at[index // 2])
        else:
            remote(src, dst, pair_sems, index, device).start()

    def land(k):
        src, dst, index, device = moves[k]
        if device is same:
            stay_or_go_wait(src, dst, pair_sems, index, device, local_sem.at[index // 2])
        else:
            copy = remote(src, dst, pair_sems, index, device)
            copy.wait_recv()
            copy.wait_send()

    norm_moves = [
        remote(
            one_q.at[0, :, pl.ds(3 * hq, EXTRA)],
            norm_in.at[c],
            pair_sems,
            4 + which,
            {"yl": target["yl"], "c": target["c"], "yh": 1 - yh},
        )
        for which, target in enumerate((same, cross))
    ]
    launch(0)
    launch(1)
    for move in norm_moves:
        move.start()
    token_halves = [ring_gather_half(token_rows, top, y_sems, 0) for top in range(2)]
    for q in range(2):
        for t in range(2):
            two_q[q, :, t * fq : (t + 1) * fq] = gate_up_weight[t, :, q * fq : (q + 1) * fq]
        two_q[q, :, 2 * fq :] = down_weight[:, q * fq : (q + 1) * fq]
    sub = here // 2
    for k in range(2):
        cot_rows[pl.ds(4 * k * sub, sub)] = cotangent[pl.ds(k * sub, sub)]
    land(0)
    land(1)
    for move in norm_moves:
        move.wait_recv()
    own = (z * 4 + x) * 4 + 2 * c
    for core in range(2):
        block = pl.ds(pl.multiple_of((own + core) * rows, rows), rows)
        came = norm_in[core].astype(f32)
        place = lax.broadcasted_iota(jnp.int32, came.shape, 0)
        held = one[block, pl.ds(3 * hq, EXTRA)].astype(f32)
        one[block, pl.ds(3 * hq, EXTRA)] = (
            held + jnp.where((place >= 12) & (place < 20), came, 0.0)
        ).astype(bf16)
    first = Spread(one, rows, (send_one, recv_one), (core_send_one, core_recv_one))
    second = Spread(two, rows, (send_two, recv_two), (core_send_two, core_recv_two))
    first.start()
    launch(2)
    launch(3)
    first.first_pass()
    first.first_rest()
    token_passed = ring_gather_pass(token_rows, token_halves, y_sems, 0)
    first.second_pass(0)
    first.first_far()
    first.second_pass(3)
    first.second_pass(1)
    land(2)
    land(3)
    second.start()
    first.second_pass(2)
    for df in (0, 3, 1, 2):
        first.second_far(df)
    for copy in token_passed + [token_halves[1][0], token_halves[0][1]]:
        copy.wait_recv()
    cot_subs = [cot_rows.at[pl.ds(4 * k * sub, 4 * sub)] for k in range(2)]
    cot_halves = [
        [ring_gather_half(cot_subs[k], top, y_sems, 6 + 6 * k) for top in range(2)]
        for k in range(2)
    ]
    first.land()
    keep = pltpu.make_async_copy(one, one_out, local_sem.at[2])
    keep.start()

    read_extras(one, 3 * hq, norm_table, bias)

    def norm_rows(k, _):
        rng = pl.ds(pl.multiple_of(k * here, here), here)
        values = token_rows[rng].astype(f32)
        mean = jnp.mean(values, -1, keepdims=True)
        centered = values - mean
        inverse = lax.rsqrt(jnp.mean(centered * centered, -1, keepdims=True) + EPSILON)
        stats[0, rng] = mean
        stats[1, rng] = inverse
        normed[rng] = (centered * inverse * norm_table[0:1] + norm_table[1:2]).astype(bf16)
        return 0

    lax.fori_loop(0, 4, norm_rows, 0)
    second.first_pass()
    wide = 256

    def project(k, _):
        cols = pl.ds(pl.multiple_of(k * wide, wide), wide)
        value = dot(normed[...], one[:, cols], 1, 0)
        value = value + jnp.concatenate([bias[pl.ds(2 * k, 1)], bias[pl.ds(2 * k + 1, 1)]], 1)

        @pl.when(k < 2 * hq // wide)
        def _():
            for place in range(4):
                rng = pl.ds(place * here, here)
                turn = table[pl.ds(pl.multiple_of(half_of_place(place) * here, here), here)]
                for pair in range(wide // 128):
                    qkv[rng, pl.ds(pl.multiple_of(k * wide + pair * 128, 128), 128)] = turn_heads(
                        value[place * here : (place + 1) * here, pair * 128 : (pair + 1) * 128],
                        turn,
                        1.0,
                    ).astype(bf16)

        @pl.when(k >= 2 * hq // wide)
        def _():
            qkv[:, cols] = value.astype(bf16)

        return 0

    lax.fori_loop(0, 3 * hq // wide, project, 0)
    second.first_rest()
    cot_passed = [
        ring_gather_pass(cot_subs[k], cot_halves[k], y_sems, 6 + 6 * k) for k in range(2)
    ]
    for sequence in range(2):
        mask = causal_mask(sequence, here)
        rng = pl.ds(sequence * 2 * here, 2 * here)

        def heads(k, _):
            def pair(t):
                return qkv[rng, pl.ds(pl.multiple_of(t * hq + k * 128, 128), 128)]

            q, key, value = pair(0), pair(1), pair(2)
            mixes = []
            for head in range(2):
                cut = slice(head * HEAD_DIM, (head + 1) * HEAD_DIM)
                soft = soft_of(q[:, cut], key[:, cut], mask).astype(bf16)
                mixes.append(dot(soft, value[:, cut], 1, 0))
            head_mix[rng, pl.ds(pl.multiple_of(k * 128, 128), 128)] = jnp.concatenate(
                mixes, 1
            ).astype(bf16)
            return 0

        lax.fori_loop(0, hq // 128, heads, 0, unroll=2)
        if sequence == 0:
            second.second_pass(0)
    second.first_far()

    part_subs = [parts.at[pl.ds(4 * k * sub, 4 * sub)] for k in range(2)]
    started, middle = [], []
    for part in range(2):
        mix = jnp.concatenate(
            [head_mix[pl.ds(k * here + part * sub, sub)] for k in range(4)], 0
        )

        def out_project(k, _):
            rng = pl.ds(pl.multiple_of(k * wide, wide), wide)
            parts[pl.ds(4 * part * sub, 4 * sub), rng] = dot(
                mix, one[rng, pl.ds(3 * hq + EXTRA, hq)], 1, 1
            ).astype(bf16)
            return 0

        lax.fori_loop(0, one.shape[0] // wide, out_project, 0)
        started.append(
            ring_sum_start(part_subs[part], mid.at[part], near.at[part], y_sems, 18 + 6 * part)
        )
    second.second_pass(3)
    for part in range(2):
        middle.append(
            ring_sum_middle(
                part_subs[part], started[part], mid.at[part], sent.at[part], far.at[part],
                y_sems, 18 + 6 * part,
            )
        )
    second.second_pass(1)
    halves = []
    for part in range(2):
        finish = ring_sum_finish(
            part_subs[part], started[part], middle[part], far.at[part], near.at[part]
        )
        total = jnp.concatenate([finish(0), finish(1)], 0)
        rng = pl.ds(part * sub, sub)
        total = total + tokens[rng].astype(f32)
        summed[rng] = total
        centered = total - jnp.mean(total, -1, keepdims=True)
        inverse = lax.rsqrt(jnp.mean(centered * centered, -1, keepdims=True) + EPSILON)
        unit_rows = centered * inverse
        unit[rng] = unit_rows
        scale[rng] = inverse
        normed_two[pl.ds(4 * part * sub, sub)] = (
            unit_rows * norm_table[2:3] + norm_table[3:4]
        ).astype(bf16)
        out = normed_two.at[pl.ds(4 * part * sub, 4 * sub)]
        halves.append([ring_gather_half(out, top, y_sems, 30 + 6 * part) for top in range(2)])
    second.second_pass(2)
    passed = [
        ring_gather_pass(
            normed_two.at[pl.ds(4 * k * sub, 4 * sub)], halves[k], y_sems, 30 + 6 * k
        )
        for k in range(2)
    ]
    for df in (0, 3, 1, 2):
        second.second_far(df)
    for k in range(2):
        for copy in passed[k] + [halves[k][1][0], halves[k][0][1]]:
            copy.wait_recv()
        for copy in cot_passed[k] + [cot_halves[k][1][0], cot_halves[k][0][1]]:
            copy.wait_recv()
    second.land()
    keep.wait()
    for move in norm_moves:
        move.wait_send()
    gathers = token_halves + cot_halves[0] + cot_halves[1] + halves[0] + halves[1]
    for copies in gathers + [token_passed] + cot_passed + started + middle + passed:
        for copy in copies:
            copy.wait_send()
    first.close()
    second.close()


def forward(qkv_weight, out_weight, gate_up_weight, down_weight, extra, tokens, cotangent, table):
    here, width = tokens.shape
    rows = qkv_weight.shape[1]
    hq, fq = qkv_weight.shape[2] // 2, gate_up_weight.shape[2] // 2
    full = pl.BlockSpec(memory_space=VMEM)
    anywhere = pl.BlockSpec(memory_space=pl.ANY)
    one_wide, two_wide = 4 * hq + EXTRA, 3 * fq

    def shape(*dims, dtype=bf16):
        return jax.ShapeDtypeStruct(dims, dtype)

    return pl.pallas_call(
        forward_kernel,
        out_shape=(
            shape(width, one_wide),
            shape(width, two_wide),
            shape(4 * here, width),
            shape(4 * here, width),
            shape(2, 4 * here, 1, dtype=f32),
            shape(4 * here, 3 * hq),
            shape(4 * here, hq),
            shape(4, width, dtype=f32),
            shape(here, width, dtype=f32),
            shape(here, width, dtype=f32),
            shape(here, 1, dtype=f32),
            shape(4 * here, width),
        ),
        in_specs=[full] * 8,
        out_specs=(anywhere, anywhere) + (full,) * 10,
        scratch_shapes=[
            VMEM((2, rows, one_wide), bf16),
            VMEM((2, rows, two_wide), bf16),
            VMEM((width, one_wide), bf16),
            VMEM((2, rows, EXTRA), bf16),
            VMEM((12, 128), f32),
            VMEM((4 * here, width), bf16),
            VMEM((4 * here, width), bf16),
        ]
        + [VMEM((2, 2, here // 4, width), bf16)] * 4
        + [
            DMA((6,)), DMA((6,)), DMA((3,)), DMA((42,)), DMA((42,)),
            DMA((64,)), DMA((64,)), DMA((32,)), DMA((32,)),
            DMA((64,)), DMA((64,)), DMA((32,)), DMA((32,)),
        ],
        compiler_params=pltpu.CompilerParams(
            collective_id=0, has_side_effects=True, vmem_limit_bytes=VMEM_LIMIT
        ),
    )(qkv_weight, out_weight, gate_up_weight, down_weight, extra, tokens, cotangent, table)


def backward_kernel(
    one, resid_rows, chip, settled, qkv, head_mix, token_rows, stats, table, second_terms,
    norm_table, mixed_parts, resid, first_sum,
    out_qkv, out_out, out_gu, out_down, out_extra, grad_tokens, mixed,
    result_one, result_two, norm_back, held, spare, grad_mix, grad_proj, sib, blocks, pair_sums,
    *rest,
):
    rings = [rest[5 * k : 5 * k + 5] for k in range(7)]
    rings = [(mid, far, near, (send, recv)) for mid, far, near, send, recv in rings]
    (
        packed_one, packed_two, ymid, ysent, yfar, ynear,
        load_sem, block_sem, core_send, core_recv, pair_send, pair_recv, local_sem, y_send, y_recv,
    ) = rest[35:]
    z, x = lax.axis_index("z"), lax.axis_index("x")
    yl, c, yh = lax.axis_index("yl"), lax.axis_index("c"), lax.axis_index("yh")
    here = resid.shape[0]
    rows = result_one.shape[1]
    hq, fq = head_mix.shape[1], result_two.shape[2] // 3
    early, late = pair_sums.shape[3], blocks.shape[3]
    sub = here // 2
    width = held.shape[0]
    core_sems, pair_sems, y_sems = (core_send, core_recv), (pair_send, pair_recv), (y_send, y_recv)
    wide = 256
    out_start = 3 * hq + EXTRA
    columns = (pl.ds(0, out_start), pl.ds(out_start, hq))

    def place_of(dz, dx):
        return ((z + dz) % 4) * 4 + (x + dx) % 4

    loads = [
        pltpu.make_async_copy(
            one.at[:, pl.ds(start, size)], held.at[:, pl.ds(start, size)], load_sem.at[k]
        )
        for k, (start, size) in enumerate(((out_start, hq), (0, 3 * hq)))
    ]
    loads.append(pltpu.make_async_copy(resid_rows, spare, load_sem.at[2]))
    loads.append(pltpu.make_async_copy(settled, pair_sums, load_sem.at[3]))
    block_loads = [
        pltpu.make_async_copy(
            chip.at[place_of(dz, dx)], blocks.at[dz, dx], block_sem.at[dz * 4 + dx]
        )
        for dz in range(4)
        for dx in range(4)
    ]
    loads[3].start()
    loads[2].start()
    loads[0].start()
    for load in block_loads:
        load.start()
    loads[1].start()
    greet([at_z(1), at_z(3), at_x(1), at_x(3)] + cube())
    mixed_started = ring_sum_start(mixed_parts, ymid.at[0], ynear.at[0], y_sems, 0)

    def cut(half, part):
        return pl.ds(half * rows + part * (rows // 2), rows // 2)

    def pair_view(stage, half, d, part):
        along = x if half == 0 else z
        return pair_sums.at[half, (along + d) % 4, pl.ds(part * (rows // 2), rows // 2)]

    def view_of(ref, cols):
        def view(stage, half, d, part):
            if stage == 0:
                there = (d, slice(None)) if half == 0 else (slice(None), d)
            else:
                there = (0, d) if half == 0 else (d, 0)
            return ref.at[(*there, cut(half, part), cols)]

        return view

    gate_up = Reduce(pair_view, rows, {1: rings[0]})
    down = Reduce(view_of(blocks, pl.ds(0, late)), rows, {0: rings[1], 1: rings[2]})
    out_proj = Reduce(view_of(sib, columns[1]), rows, {0: rings[3], 1: rings[4]})
    attention = Reduce(view_of(sib, columns[0]), rows, {0: rings[5], 1: rings[6]})
    loads[3].wait()
    gate_up.begin(1)
    for load in block_loads:
        load.wait()
    down.begin(0)

    def to_core(block, which):
        theirs = pl.ds(pl.multiple_of((2 * block + 1 - c) * 2 * rows, 2 * rows), 2 * rows)
        dz, dx = (block // 4 - z + 4) % 4, (block % 4 - x + 4) % 4
        return remote(
            held.at[theirs, columns[which]],
            sib.at[dz, dx, :, columns[which]],
            core_sems,
            block + 16 * which,
            sibling(),
        )

    def core_sum(block, which):
        to_core(block, which).wait_recv()
        ours = pl.ds(pl.multiple_of((2 * block + c) * 2 * rows, 2 * rows), 2 * rows)
        there = ((block // 4 - z + 4) % 4, (block % 4 - x + 4) % 4, slice(None), columns[which])
        sib[there] = (sib[there].astype(f32) + held[ours, columns[which]].astype(f32)).astype(
            bf16
        )

    loads[2].wait()
    loads[0].wait()

    mix_order = jnp.concatenate(
        [
            head_mix[pl.ds(block * here + part * sub, sub)]
            for part in range(2)
            for block in range(4)
        ],
        0,
    )

    def mix_back(k, _):
        cols = pl.ds(pl.multiple_of(k * wide, wide), wide)
        value = dot(
            spare[...], held[:, pl.ds(pl.multiple_of(out_start + k * wide, 128), wide)], 1, 0
        ).astype(bf16)
        for part in range(2):
            for block in range(4):
                start = (part * 4 + block) * sub
                grad_mix[pl.ds(block * here + part * sub, sub), cols] = value[start : start + sub]
        return 0

    lax.fori_loop(0, hq // wide, mix_back, 0)

    def out_back(k, _):
        rng = pl.ds(pl.multiple_of(k * 2 * wide, 2 * wide), 2 * wide)
        held[rng, columns[1]] = dot(spare[:, rng], mix_order, 0, 0).astype(bf16)
        for block in range(4):
            to_core(4 * k + block, 1).start()
        return 0

    lax.fori_loop(0, width // (2 * wide), out_back, 0)
    gate_up.combine(1)
    mixed_middle = ring_sum_middle(
        mixed_parts, mixed_started, ymid.at[0], ysent.at[0], yfar.at[0], y_sems, 0
    )

    def out_sum(block, _):
        core_sum(block, 1)
        return 0

    lax.fori_loop(0, 16, out_sum, 0)
    out_proj.begin(0)
    for sequence in range(2):
        mask = causal_mask(sequence, here)
        rng = pl.ds(sequence * 2 * here, 2 * here)
        turn = jnp.concatenate(
            [
                table[pl.ds(pl.multiple_of(half_of_place(2 * sequence + k) * here, here), here)]
                for k in range(2)
            ],
            0,
        )

        def heads(k, _):
            def pair(t):
                return pl.ds(pl.multiple_of(t * hq + k * 128, 128), 128)

            q, key, value = qkv[rng, pair(0)], qkv[rng, pair(1)], qkv[rng, pair(2)]
            mix = grad_mix[rng, pair(0)]
            results = ([], [], [])
            for head in range(2):
                lanes = slice(head * HEAD_DIM, (head + 1) * HEAD_DIM)
                soft = soft_of(q[:, lanes], key[:, lanes], mask)
                grad_soft = dot(mix[:, lanes], value[:, lanes], 1, 1)
                row_dot = jnp.sum(grad_soft * soft, -1, keepdims=True)
                grad_score = (soft * (grad_soft - row_dot)).astype(bf16)
                results[0].append(dot(grad_score, key[:, lanes], 1, 0) * SCALE)
                results[1].append(dot(grad_score, q[:, lanes], 0, 0) * SCALE)
                results[2].append(dot(soft.astype(bf16), mix[:, lanes], 0, 0))
            for t in range(3):
                both = jnp.concatenate(results[t], 1)
                if t < 2:
                    both = turn_heads(both, turn, -1.0)
                grad_proj[rng, pair(t)] = both.astype(bf16)
            return 0

        lax.fori_loop(0, hq // 128, heads, 0, unroll=2)
        if sequence == 0:
            down.combine(0)
    gate_up.settle(1, packed_two.at[:, :, pl.ds(0, early)])

    bias_rows = [
        jnp.sum(grad_proj[:, pl.ds(k * 128, 128)].astype(f32), 0, keepdims=True)
        for k in range(3 * hq // 128)
    ]
    mean, inverse = stats[0], stats[1]
    loads[1].wait()

    def weights_back(k, _):
        rng = pl.ds(pl.multiple_of(k * wide, wide), wide)
        part = dot(grad_proj[...], held[rng, pl.ds(0, 3 * hq)], 1, 1)
        spare[:, rng] = part.astype(bf16)
        unit = (token_rows[:, rng].astype(f32) - mean) * inverse
        normed = (unit * norm_table[0:1, rng] + norm_table[1:2, rng]).astype(bf16)
        held[rng, pl.ds(0, 3 * hq)] = dot(normed, grad_proj[...], 0, 0).astype(bf16)
        gain = jnp.sum(part * unit, 0, keepdims=True)
        shift = jnp.sum(part, 0, keepdims=True)
        for tile in range(wide // 128):
            inner = slice(tile * 128, (tile + 1) * 128)
            lanes = pl.ds(pl.multiple_of(k * wide + tile * 128, 128), 128)
            extra = jnp.concatenate(
                bias_rows
                + [
                    gain[:, inner],
                    shift[:, inner],
                    second_terms[:, lanes],
                    jnp.zeros((rows - 16, 128), f32),
                ],
                0,
            ).astype(bf16)
            for copy in range(128 // rows):
                start = pl.multiple_of(k * wide + tile * 128 + copy * rows, rows)
                held[pl.ds(start, rows), pl.ds(3 * hq, EXTRA)] = extra
        for block in range(2):
            to_core(2 * k + block, 0).start()

        @pl.when(k > 0)
        def _():
            for block in range(2):
                core_sum(2 * k - 2 + block, 0)

        return 0

    lax.fori_loop(0, 5, weights_back, 0)
    out_proj.combine(0)
    down.settle(0)
    down.begin(1)
    lax.fori_loop(5, width // wide, weights_back, 0)
    first_started = ring_sum_start(spare, ymid.at[1], ynear.at[1], y_sems, 6)
    for block in range(14, 16):
        core_sum(block, 0)
    attention.begin(0)
    down.combine(1)
    out_proj.settle(0)
    out_proj.begin(1)
    down.settle(1, packed_two.at[:, :, pl.ds(early, late)])
    home, away = {"yl": c, "c": yl}, {"yl": c, "c": 1 - yl}
    stay_or_go(packed_two.at[yl], result_two.at[yl], pair_sems, 0, home, local_sem.at[0])
    cross_two = remote(packed_two.at[1 - yl], result_two.at[yl], pair_sems, 1, away)
    cross_two.start()
    first_middle = ring_sum_middle(
        spare, first_started, ymid.at[1], ysent.at[1], yfar.at[1], y_sems, 6
    )
    attention.combine(0)
    out_proj.combine(1)
    half_here = here // 2
    finish = ring_sum_finish(mixed_parts, mixed_started, mixed_middle, yfar.at[0], ynear.at[0])
    for top in range(2):
        rng = pl.ds(top * half_here, half_here)
        mixed[rng] = (first_sum[rng] + finish(top)).astype(bf16)
    finish = ring_sum_finish(spare, first_started, first_middle, yfar.at[1], ynear.at[1])
    for top in range(2):
        rng = pl.ds(top * half_here, half_here)
        incoming = finish(top) * norm_table[0:1]
        unit_rows = (token_rows[rng].astype(f32) - stats[0, rng]) * stats[1, rng]
        grad_tokens[rng] = resid[rng] + stats[1, rng] * (
            incoming
            - jnp.mean(incoming, -1, keepdims=True)
            - unit_rows * jnp.mean(incoming * unit_rows, -1, keepdims=True)
        )
    out_proj.settle(1, packed_one.at[:, :, columns[1]])
    attention.settle(0)
    attention.begin(1)
    attention.combine(1)
    attention.settle(1, packed_one.at[:, :, columns[0]])

    stay_or_go(packed_one.at[yl], result_one.at[yl], pair_sems, 2, home, local_sem.at[1])
    cross_one = remote(packed_one.at[1 - yl], result_one.at[yl], pair_sems, 3, away)
    cross_one.start()
    extras = pl.ds(3 * hq, EXTRA)
    norm_moves = [
        remote(
            packed_one.at[core, :, extras],
            norm_back.at[yl],
            pair_sems,
            4 + which,
            {"yl": c, "c": core, "yh": 1 - yh},
        )
        for which, core in enumerate((yl, 1 - yl))
    ]
    for move in norm_moves:
        move.start()
    cross_two.wait_recv()
    stay_or_go_wait(packed_two.at[yl], result_two.at[yl], pair_sems, 0, home, local_sem.at[0])
    for q in range(2):
        for t in range(2):
            out_gu[t, :, q * fq : (q + 1) * fq] = result_two[q, :, t * fq : (t + 1) * fq]
        out_down[:, q * fq : (q + 1) * fq] = result_two[q, :, 2 * fq :]
    for copy in [cross_one] + norm_moves:
        copy.wait_recv()
    stay_or_go_wait(packed_one.at[yl], result_one.at[yl], pair_sems, 2, home, local_sem.at[1])
    for q in range(2):
        for t in range(3):
            out_qkv[t, :, q * hq : (q + 1) * hq] = result_one[q, :, t * hq : (t + 1) * hq]
        out_out[:, q * hq : (q + 1) * hq] = result_one[q, :, out_start:]
        out_extra[q] = result_one[q, :, extras].astype(f32)
    out_extra[2] = (out_extra[0] + out_extra[1]) + (
        norm_back[0].astype(f32) + norm_back[1].astype(f32)
    )
    for copy in [cross_two, cross_one] + norm_moves:
        copy.wait_send()
    for copy in mixed_started + mixed_middle + first_started + first_middle:
        copy.wait_send()

    def drain(block, _):
        to_core(block, 0).wait_send()
        to_core(block, 1).wait_send()
        return 0

    lax.fori_loop(0, 16, drain, 0)
    for sums in (gate_up, down, out_proj, attention):
        sums.close()


def backward(
    one, resid_rows, chip, settled, qkv, head_mix, token_rows, stats, table, second_terms,
    norm_table, mixed_parts, resid, first_sum,
):
    here, width = resid.shape
    hq, early, late = head_mix.shape[1], settled.shape[3], chip.shape[2]
    fq = (early + late) // 3
    rows = width // 64
    piece = rows // 2
    one_wide = one.shape[1]
    full = pl.BlockSpec(memory_space=VMEM)
    anywhere = pl.BlockSpec(memory_space=pl.ANY)
    rings = ring_buffers(1, piece, early)
    for wide in (late, hq, 3 * hq + EXTRA):
        rings += ring_buffers(0, piece, wide) + ring_buffers(1, piece, wide)
    return pl.pallas_call(
        backward_kernel,
        out_shape=(
            jax.ShapeDtypeStruct((3, rows, 2 * hq), bf16),
            jax.ShapeDtypeStruct((rows, 2 * hq), bf16),
            jax.ShapeDtypeStruct((2, rows, 2 * fq), bf16),
            jax.ShapeDtypeStruct((rows, 2 * fq), bf16),
            jax.ShapeDtypeStruct((3, rows, EXTRA), f32),
            jax.ShapeDtypeStruct((here, width), f32),
            jax.ShapeDtypeStruct((here, width), bf16),
        ),
        in_specs=[anywhere] * 4 + [full] * 10,
        out_specs=(full,) * 7,
        scratch_shapes=[
            VMEM((2, rows, one_wide), bf16),
            VMEM((2, rows, 3 * fq), bf16),
            VMEM((2, rows, EXTRA), bf16),
            VMEM((width, one_wide), bf16),
            VMEM((4 * here, width), bf16),
            VMEM((4 * here, hq), bf16),
            VMEM((4 * here, 3 * hq), bf16),
            VMEM((4, 4, 2 * rows, one_wide), bf16),
            VMEM((4, 4, 2 * rows, late), bf16),
            VMEM((2, 4, rows, early), bf16),
        ]
        + rings
        + [VMEM((2, rows, one_wide), bf16), VMEM((2, rows, 3 * fq), bf16)]
        + [VMEM((2, 2, here // 2, width), bf16)] * 4
        + [DMA((4,)), DMA((16,)), DMA((32,)), DMA((32,))]
        + [DMA((6,)), DMA((6,)), DMA((2,)), DMA((12,)), DMA((12,))],
        compiler_params=pltpu.CompilerParams(
            collective_id=3, has_side_effects=True, vmem_limit_bytes=VMEM_LIMIT
        ),
    )(
        one, resid_rows, chip, settled, qkv, head_mix, token_rows, stats, table, second_terms,
        norm_table, mixed_parts, resid, first_sum,
    )


def shards(
    tokens, cotangent, norm_params, qkv_weight, qkv_bias, out_weight, gate_up_weight, down_weight
):
    yl, yh, c = lax.axis_index("yl"), lax.axis_index("yh"), lax.axis_index("c")
    mine = ((lax.axis_index("z") * 4 + lax.axis_index("x")) * 2 + yl) * 2 + c
    rows = qkv_weight.shape[1]
    heads = qkv_weight.shape[2] // 2 // HEAD_DIM
    pairs = 3 * heads // 2

    norm_high = lax.optimization_barrier(norm_params.astype(bf16))
    norm_low = (norm_params - norm_high.astype(f32)).astype(bf16)
    share = norm_params.shape[1]
    norm_extra = jnp.where(
        jnp.arange(EXTRA) // share == mine % 4 * 2 + yh,
        jnp.tile(jnp.concatenate([norm_high, norm_low], 0), (1, EXTRA // share)),
        0,
    )
    bias_q = qkv_bias.reshape(3, 2, heads).transpose(1, 0, 2).reshape(2, pairs, 2, 1)
    bias_extra = jnp.where(jnp.arange(HEAD_DIM) == mine, bias_q, 0).reshape(2, pairs, EXTRA)
    extra = jnp.concatenate(
        [
            bias_extra,
            jnp.broadcast_to(norm_extra[None], (2, *norm_extra.shape)),
            jnp.zeros((2, rows - pairs - 8, EXTRA), bf16),
        ],
        1,
    )
    table = jnp.asarray(tables())
    (
        one, second, token_rows, cot_rows, stats, qkv, head_mix, norm_table,
        first_sum, unit_two, scale_two, normed_two,
    ) = forward(
        qkv_weight, out_weight.T, gate_up_weight, down_weight.T, extra, tokens, cotangent, table
    )
    grad_resid, second_terms, resid_rows, mixed_parts, chip, settled = feed_forward(
        normed_two, cot_rows, cotangent, unit_two, scale_two, norm_table, second
    )
    out_qkv, out_out, out_gu, out_down, out_extra, grad_input, mixed = backward(
        one, resid_rows, chip, settled, qkv, head_mix, token_rows, stats, table, second_terms,
        norm_table, mixed_parts, grad_resid, first_sum,
    )

    bias_sums = out_extra[:2, :pairs].reshape(2, 3, heads // 2, 2, HEAD_DIM)
    out_bias = jnp.sum(jnp.where(jnp.arange(HEAD_DIM) == mine, bias_sums, 0.0), -1)
    out_bias = out_bias.transpose(1, 0, 2, 3).reshape(3, 2 * heads, 1)
    out_norm = lax.dynamic_slice(
        out_extra[2, pairs : pairs + 4], (0, (mine % 4 * 2 + yh) * share), (4, share)
    )
    out_qkv, out_gu = out_qkv.astype(f32), out_gu.astype(f32)
    out_out, out_down = out_out.T.astype(f32), out_down.T.astype(f32)
    return (mixed, grad_input, out_norm, out_qkv, out_bias, out_out, out_gu, out_down)


def solution(mesh):
    grid = Mesh(mesh.devices.reshape(4, 4, 2, 2, 2), GRID)
    placed = (
        P(GRID, None),
        P(GRID, None),
        P(None, GRID),
        P(None, ROWS, "yh"),
        P(None, "yh", ROWS),
        P("yh", ROWS),
        P(None, ROWS, "yh"),
        P("yh", ROWS),
    )
    return jax.shard_map(
        shards,
        mesh=grid,
        in_specs=placed,
        out_specs=(
            P(GRID, None),
            P(GRID, None),
            P(None, GRID),
            P(None, ROWS, "yh"),
            P(None, "yh", ROWS),
            P("yh", ROWS),
            P(None, ROWS, "yh"),
            P("yh", ROWS),
        ),
        check_vma=False,
    )
```

```python
import jax
import jax.numpy as jnp
import numpy as np
from jax import lax
from jax.experimental import pallas as pl
from jax.experimental.pallas import tpu as pltpu
from jax.sharding import Mesh
from jax.sharding import PartitionSpec as P

HEAD_DIM = 64
ROTARY = 16
EPSILON = 1e-05
SCALE = 0.125

GRID = ("z", "x", "yl", "c", "yh")
ROWS = ("z", "x", "yl", "c")
EXTRA = 128

bf16 = jnp.bfloat16
f32 = jnp.float32

MESH = pl.DeviceIdType.MESH
VMEM = pltpu.VMEM
DMA = pltpu.SemaphoreType.DMA
VMEM_LIMIT = 60 * 1024 * 1024


def at_y(k):
    y = (lax.axis_index("yh") * 2 + lax.axis_index("yl") + k) % 4
    return {"yl": y % 2, "yh": y // 2}


def at_z(k):
    return {"z": (lax.axis_index("z") + k) % 4}


def at_x(k):
    return {"x": (lax.axis_index("x") + k) % 4}


def sibling():
    return {"c": 1 - lax.axis_index("c")}


def greet(devices):
    barrier = pltpu.get_barrier_semaphore()
    for device in devices:
        pl.semaphore_signal(barrier, inc=1, device_id=device, device_id_type=MESH)
    pl.semaphore_wait(barrier, len(devices))


def remote(src, dst, sems, index, device):
    send, recv = sems
    return pltpu.make_async_remote_copy(
        src_ref=src,
        dst_ref=dst,
        send_sem=send.at[index],
        recv_sem=recv.at[index],
        device_id=device,
        device_id_type=MESH,
    )


def ring_gather_half(out, top, sems, base):
    here = out.shape[0] // 4
    half = here // 2
    copies = []
    for way, step, block in ((0, 1, 3), (1, -1, 2)):
        copies.append(
            remote(
                out.at[pl.ds(top * half, half)],
                out.at[pl.ds(block * here + top * half, half)],
                sems,
                base + 2 * way + top,
                at_y(step),
            )
        )
        copies[-1].start()
    return copies


def ring_gather_pass(out, halves, sems, base):
    here = out.shape[0] // 4
    half = here // 2
    passed = []
    for way, step, block in ((0, 1, 3), (1, -1, 2)):
        halves[way][way].wait_recv()
        passed.append(
            remote(
                out.at[pl.ds(block * here + way * half, half)],
                out.at[pl.ds(here + way * half, half)],
                sems,
                base + 4 + way,
                at_y(step),
            )
        )
        passed[-1].start()
    return passed


def pair_moves():
    yl, c = lax.axis_index("yl"), lax.axis_index("c")
    return {"yl": c, "c": yl}, {"yl": 1 - c, "c": yl}


def stay_or_go(src, dst, sems, index, device, local_sem):
    yl, c = lax.axis_index("yl"), lax.axis_index("c")

    @pl.when(yl == c)
    def _():
        pltpu.make_async_copy(src, dst, local_sem).start()

    @pl.when(yl != c)
    def _():
        remote(src, dst, sems, index, device).start()


def stay_or_go_wait(src, dst, sems, index, device, local_sem):
    yl, c = lax.axis_index("yl"), lax.axis_index("c")

    @pl.when(yl == c)
    def _():
        pltpu.make_async_copy(src, dst, local_sem).wait()

    @pl.when(yl != c)
    def _():
        copy = remote(src, dst, sems, index, device)
        copy.wait_recv()
        copy.wait_send()


def ring_sum_start(parts, mid, near, sems, base):
    here = parts.shape[0] // 4
    half = here // 2
    copies = []
    for way, step in ((0, 1), (1, -1)):
        copies.append(
            remote(
                parts.at[pl.ds(here + way * half, half)], mid.at[way], sems, base + way, at_y(step)
            )
        )
    for way, step, block in ((0, 1, 2), (1, -1, 3)):
        copies.append(
            remote(
                parts.at[pl.ds(block * here + (1 - way) * half, half)],
                near.at[way],
                sems,
                base + 2 + way,
                at_y(step),
            )
        )
    for copy in copies:
        copy.start()
    return copies


def ring_sum_middle(parts, started, mid, sent, far, sems, base):
    here = parts.shape[0] // 4
    half = here // 2
    copies = []
    for way, step, block in ((0, 1, 2), (1, -1, 3)):
        started[way].wait_recv()
        sent[way] = (
            parts[pl.ds(block * here + way * half, half)].astype(f32) + mid[way].astype(f32)
        ).astype(bf16)
        copies.append(remote(sent.at[way], far.at[way], sems, base + 4 + way, at_y(step)))
        copies[-1].start()
    return copies


def ring_sum_finish(parts, started, middle, far, near):
    half = parts.shape[0] // 8

    def finish(top):
        started[2 + 1 - top].wait_recv()
        middle[top].wait_recv()
        return (
            parts[pl.ds(top * half, half)].astype(f32)
            + far[top].astype(f32)
            + near[1 - top].astype(f32)
        )

    return finish


def tables():
    half = ROTARY // 2
    position = np.arange(256, dtype=np.float32)
    frequency = np.power(np.float32(10000.0), -np.arange(half, dtype=np.float32) * np.float32(2.0 / ROTARY))
    angles = position[:, None] * frequency[None, :].astype(np.float32)
    cosine, sine = np.cos(angles), np.sin(angles)
    own = np.ones((256, 2, HEAD_DIM), np.float32)
    up = np.zeros((256, 2, HEAD_DIM), np.float32)
    down = np.zeros((256, 2, HEAD_DIM), np.float32)
    for head in range(2):
        own[:, head, :half] = cosine
        own[:, head, half:ROTARY] = cosine
        up[:, head, :half] = -sine
        down[:, head, half:ROTARY] = sine
    return np.concatenate([a.reshape(256, 128) for a in (own, up, down)], 1)


def dot(a, b, ca, cb):
    return lax.dot_general(a, b, (((ca,), (cb,)), ((), ())), preferred_element_type=f32)


def turn_heads(value, table, sign):
    own, up, down = table[:, :128], table[:, 128:256], table[:, 256:]
    return value * own + sign * (
        pltpu.roll(value, 120, 1) * up + pltpu.roll(value, 8, 1) * down
    )


def half_of_place(place):
    y = lax.axis_index("yh") * 2 + lax.axis_index("yl")
    return ((y + (0, 2, 1, 3)[place]) % 4) // 2


def causal_mask(sequence, here):
    length = 2 * here
    first = half_of_place(2 * sequence)

    def position(dim):
        index = lax.broadcasted_iota(jnp.int32, (length, length), dim)
        return jnp.where(index < here, index + first * here, index - first * here)

    return position(0) >= position(1)


def soft_of(queries, keys, mask):
    scores = dot(queries, keys, 1, 1) * SCALE
    scores = jnp.where(mask, scores, -1000000000.0)
    powers = jnp.exp(scores - jnp.max(scores, -1, keepdims=True))
    return powers * (1.0 / jnp.sum(powers, -1, keepdims=True))


def read_extras(one, first_column, norm_table, bias):
    total = None
    for group in range(one.shape[0] // 128):
        block = one[pl.ds(group * 128, 128), pl.ds(first_column, 128)].astype(f32)
        block = block[0:32] + block[32:64] + block[64:96] + block[96:128]
        norm_table[:, pl.ds(group * 128, 128)] = block[12:16] + block[16:20]
        total = block[0:12] if total is None else total + block[0:12]
    bias[...] = total


class Reduce:
    def __init__(self, view, rows, rings):
        self.view, self.rows, self.rings = view, rows, rings
        self.done, self.got = [], {}

    def send(self, name, stage, half, way, src, dst, index):
        step = (1, -1)[way]
        device = at_z(step) if (half == 0) == (stage == 0) else at_x(step)
        copy = remote(src, dst, self.rings[stage][3], half * 6 + index * 2 + way, device)
        copy.start()
        self.done.append(copy)
        self.got[name, stage, half, way] = copy

    def begin(self, stage):
        mid, _, near, _ = self.rings[stage]
        for half in range(2):
            for way in range(2):
                src = self.view(stage, half, 2, way)
                self.send("mid", stage, half, way, src, mid.at[half, way], 0)
        for half in range(2):
            for way in range(2):
                src = self.view(stage, half, (1, 3)[way], 1 - way)
                self.send("near", stage, half, way, src, near.at[half, way], 1)

    def combine(self, stage):
        mid, far = self.rings[stage][:2]
        for half in range(2):
            for way in range(2):
                self.got["mid", stage, half, way].wait_recv()
                ref = self.view(stage, half, (1, 3)[way], way)
                ref[...] = (ref[...].astype(f32) + mid[half, way].astype(f32)).astype(bf16)
                self.send("far", stage, half, way, ref, far.at[half, way], 2)

    def settle(self, stage, out=None):
        far, near = self.rings[stage][1:3]
        piece = self.rows // 2
        for half in range(2):
            for part in range(2):
                self.got["far", stage, half, part].wait_recv()
                self.got["near", stage, half, 1 - part].wait_recv()
                ref = self.view(stage, half, 0, part)
                total = (
                    ref[...].astype(f32)
                    + far[half, part].astype(f32)
                    + near[half, 1 - part].astype(f32)
                ).astype(bf16)
                if out is None:
                    ref[...] = total
                else:
                    out[half, pl.ds(part * piece, piece)] = total

    def close(self):
        for copy in self.done:
            copy.wait_send()


def ring_buffers(stage, piece, wide):
    dims = (2, 2, 4, piece, wide) if stage == 0 else (2, 2, piece, wide)
    return [VMEM(dims, bf16)] * 3 + [DMA((12,))] * 2


def feed_forward_kernel(
    normed_in, cot_in, cotangent_in, unit_in, weights, scale, norm_table,
    resid_out, spread_out, mixed_out, chip, settled, sums,
    normed, cot_rows, cotangent, unit, resid, spread, mixed_parts, held, pair, hidden, normed_t, cot_t, parts, sib, mid, sent, far, near,
    *rest,
):
    rings = [rest[5 * k : 5 * k + 5] for k in range(2)]
    rings = [(mid, far, near, (send, recv)) for mid, far, near, send, recv in rings]
    in_sem, save_sem, load_sem, store_sem, core_send, core_recv, y_send, y_recv = rest[10:]
    columns, width = held.shape[3] // 3, normed.shape[1]
    wide = 256
    rows = sib.shape[1]
    sub = cotangent.shape[0] // 2
    z, x, c = lax.axis_index("z"), lax.axis_index("x"), lax.axis_index("c")
    y_sems, core_sems = (y_send, y_recv), (core_send, core_recv)
    whole, left = columns // wide, columns % wide
    all_pair, all_hidden = pl.ds(0, 2 * columns), pl.ds(2 * columns, columns)
    groups = tuple(pl.ds(which * columns, columns) for which in range(3))

    def load(k, which, size):
        start = pl.multiple_of(which * columns + k * wide, 128)
        cut = pl.ds(start, size)
        return pltpu.make_async_copy(
            weights.at[:, :, :, cut], held.at[:, :, :, cut], load_sem.at[k, which]
        )

    ins = [
        pltpu.make_async_copy(src, dst, in_sem.at[k])
        for k, (src, dst) in enumerate(
            ((normed_in, normed), (cot_in, cot_rows), (cotangent_in, cotangent), (unit_in, unit))
        )
    ]
    ins[0].start()
    ins[1].start()
    saves = []

    def save(src, dst):
        saves.append(pltpu.make_async_copy(src, dst, save_sem.at[len(saves)]))
        saves[-1].start()

    def load_tile(k, size):
        for which in range(3):
            load(k, which, size).start()

    load_tile(0, wide)
    load_tile(1, wide)
    ins[0].wait()
    ins[1].wait()

    def flip(k, _):
        rng = pl.ds(pl.multiple_of(k * wide, wide), wide)
        normed_t[rng] = normed[:, rng].T
        cot_t[rng] = cot_rows[:, rng].T
        return 0

    lax.fori_loop(0, width // wide, flip, 0)
    greet([at_z(1), at_z(3), at_x(1), at_x(3), at_y(1), at_y(3), sibling()])

    tall = width // 4

    def tile(k, cut):
        return k, slice(None), slice(None), cut

    def ahead(part, k, size):
        these = pl.ds(4 * part * sub, 4 * sub)

        def cut(which):
            return pl.ds(pl.multiple_of(which * columns + k * wide, 128), size)

        def weight(which):
            return held[:, :, :, cut(which)].reshape(width, size)

        if part == 0:
            if size == wide:
                pl.when(k + 2 < whole)(lambda: load_tile(k + 2, wide))
                if left:
                    pl.when(k + 2 == whole)(lambda: load_tile(whole, left))
            for which in range(3):
                load(k, which, size).wait()
        gate = dot(normed[these], weight(0), 1, 0)
        up = dot(normed[these], weight(1), 1, 0)
        grad_hidden = dot(cot_rows[these], weight(2), 1, 0)
        sigmoid = jax.nn.sigmoid(gate)
        activated = gate * sigmoid
        hidden[these, cut(0)] = (activated * up).astype(bf16)
        pair[these, cut(0)] = (
            grad_hidden * up * sigmoid * (1.0 + gate * (1.0 - sigmoid))
        ).astype(bf16)
        pair[these, cut(1)] = (grad_hidden * activated).astype(bf16)
        return 0

    part_subs = [parts.at[pl.ds(4 * k * sub, 4 * sub)] for k in range(2)]
    started, middle, halves, passed = [], [], [], []

    def ring_middle(part):
        middle.append(
            ring_sum_middle(
                part_subs[part], started[part], mid.at[part], sent.at[part], far.at[part],
                y_sems, 6 * part,
            )
        )

    for part in range(2):
        lax.fori_loop(0, whole, lambda k, _: ahead(part, k, wide), 0)
        if left:
            ahead(part, whole, left)
        if part == 1:
            ring_middle(0)

        def second_back(k, _):
            rng = pl.ds(pl.multiple_of(k * tall, tall), tall)
            weight = held[tile(k, all_pair)].reshape(tall, 2 * columns)
            these = pl.ds(4 * part * sub, 4 * sub)
            parts[these, rng] = dot(pair[these], weight, 1, 1).astype(bf16)
            return 0

        lax.fori_loop(0, 4, second_back, 0)
        started.append(
            ring_sum_start(part_subs[part], mid.at[part], near.at[part], y_sems, 6 * part)
        )

    def to_core(block, which):
        theirs = pl.ds(pl.multiple_of((1 - c) * rows, rows), rows)
        return remote(
            held.at[block // 4, block % 4, theirs, groups[which]],
            sib.at[block, :, groups[which]],
            core_sems,
            block + 16 * which,
            sibling(),
        )

    ours = pl.ds(pl.multiple_of(c * rows, rows), rows)

    def store(block):
        return pltpu.make_async_copy(
            held.at[block // 4, block % 4, ours, groups[2]], chip.at[block], store_sem.at[block]
        )

    def core_sum(block, which):
        to_core(block, which).wait_recv()
        mine = (block // 4, block % 4, ours, groups[which])
        held[mine] = (
            held[mine].astype(f32) + sib[block, :, groups[which]].astype(f32)
        ).astype(bf16)
        if which == 2:
            store(block).start()

    def weights_back(which, k):
        rng = pl.ds(pl.multiple_of(k * tall, tall), tall)
        if which < 2:
            grad = dot(normed_t[rng], pair[:, groups[which]], 1, 0)
        else:
            grad = dot(cot_t[rng], hidden[...], 1, 0)
        held[tile(k, groups[which])] = grad.astype(bf16).reshape(4, 2 * rows, columns)
        for block in range(4):
            to_core(4 * k + block, which).start()

        @pl.when(k > 1)
        def _():
            for block in range(4):
                core_sum(4 * k - 8 + block, which)

        return 0

    def all_weights(which):
        lax.fori_loop(0, 4, lambda k, _: weights_back(which, k), 0)

    def last_sums(which):
        for block in range(8, 16):
            core_sum(block, which)

    def settle_rows(part):
        finish = ring_sum_finish(
            part_subs[part], started[part], middle[part], far.at[part], near.at[part]
        )
        here = pl.ds(part * sub, sub)
        total = jnp.concatenate([finish(0), finish(1)], 0)
        unit_rows = unit[here]
        incoming = total * norm_table[2:3]
        result = cotangent[here].astype(f32) + scale[here] * (
            incoming
            - jnp.mean(incoming, -1, keepdims=True)
            - unit_rows * jnp.mean(incoming * unit_rows, -1, keepdims=True)
        )
        resid[here] = result
        spread[pl.ds(4 * part * sub, sub)] = result.astype(bf16)
        out = spread.at[pl.ds(4 * part * sub, 4 * sub)]
        halves.append([ring_gather_half(out, top, y_sems, 12 + 6 * part) for top in range(2)])
        both = jnp.concatenate(
            [
                jnp.sum(total * unit_rows, 0, keepdims=True),
                jnp.sum(total, 0, keepdims=True),
            ],
            0,
        )
        sums[...] = both if part == 0 else sums[...] + both

    def gather_pass(part):
        out = spread.at[pl.ds(4 * part * sub, 4 * sub)]
        passed.append(ring_gather_pass(out, halves[part], y_sems, 12 + 6 * part))

    def view_of(cols):
        def view(stage, half, d, part):
            start = c * rows + half * (rows // 2) + part * (rows // 4)
            rng = pl.ds(pl.multiple_of(start, rows // 4), rows // 4)
            if half == 0:
                return held.at[(z + d) % 4, :, rng, cols]
            return held.at[:, (x + d) % 4, rng, cols]

        return view

    gate_sums, up_sums = (
        Reduce(view_of(groups[which]), rows // 2, {0: rings[which]}) for which in range(2)
    )
    def mix(k, _):
        rng = pl.ds(pl.multiple_of(k * tall, tall), tall)
        weight = held[tile(k, all_hidden)].reshape(tall, columns)
        value = dot(hidden[...], weight, 1, 1).astype(bf16)
        for part in range(2):
            for block in range(4):
                start = (part * 4 + block) * sub
                mixed_parts[pl.ds((2 * block + part) * sub, sub), rng] = value[start : start + sub]
        return 0

    ins[2].start()
    ins[3].start()
    all_weights(0)
    ring_middle(1)
    last_sums(0)
    gate_sums.begin(0)
    ins[2].wait()
    ins[3].wait()
    settle_rows(0)
    all_weights(1)
    gate_sums.combine(0)
    last_sums(1)
    up_sums.begin(0)
    gather_pass(0)
    lax.fori_loop(0, 4, mix, 0)
    save(mixed_parts, mixed_out)
    settle_rows(1)
    save(resid, resid_out)
    all_weights(2)
    up_sums.combine(0)
    gather_pass(1)
    last_sums(2)
    gate_sums.settle(0)
    up_sums.settle(0)
    top_rows = pl.ds(pl.multiple_of(c * rows, rows // 2), rows // 2)
    low_rows = pl.ds(pl.multiple_of(c * rows + rows // 2, rows // 2), rows // 2)
    keep = [
        pltpu.make_async_copy(held.at[z, :, top_rows, all_pair], settled.at[0], store_sem.at[16]),
        pltpu.make_async_copy(held.at[:, x, low_rows, all_pair], settled.at[1], store_sem.at[17]),
    ]
    for copy in keep:
        copy.start()

    def drain(block, _):
        for which in range(3):
            to_core(block, which).wait_send()
        store(block).wait()
        return 0

    lax.fori_loop(0, 16, drain, 0)
    for k in range(2):
        for copy in passed[k] + [halves[k][1][0], halves[k][0][1]]:
            copy.wait_recv()
        these = pl.ds(4 * k * sub, 4 * sub)
        save(spread.at[these], spread_out.at[these])
        for copy in started[k] + middle[k] + halves[k][0] + halves[k][1] + passed[k]:
            copy.wait_send()
    gate_sums.close()
    up_sums.close()
    for copy in keep + saves:
        copy.wait()


def feed_forward(normed, cot_rows, cotangent, unit, scale, norm_table, weights):
    tokens, width = normed.shape
    here = cotangent.shape[0]
    columns = weights.shape[1] // 3
    rows = width // 32
    full = pl.BlockSpec(memory_space=VMEM)
    anywhere = pl.BlockSpec(memory_space=pl.ANY)
    tiles = -(-columns // 256)
    kept = (
        ((tokens, width), bf16),
        ((tokens, width), bf16),
        ((here, width), bf16),
        ((here, width), f32),
        ((here, width), f32),
        ((tokens, width), bf16),
        ((tokens, width), bf16),
    )
    return pl.pallas_call(
        feed_forward_kernel,
        out_shape=(
            jax.ShapeDtypeStruct((here, width), f32),
            jax.ShapeDtypeStruct((tokens, width), bf16),
            jax.ShapeDtypeStruct((tokens, width), bf16),
            jax.ShapeDtypeStruct((16, rows, columns), bf16),
            jax.ShapeDtypeStruct((2, 4, rows // 2, 2 * columns), bf16),
            jax.ShapeDtypeStruct((2, width), f32),
        ),
        in_specs=[anywhere] * 5 + [full] * 2,
        out_specs=(anywhere,) * 5 + (full,),
        scratch_shapes=[VMEM(dims, dtype) for dims, dtype in kept]
        + [
            VMEM((4, 4, 2 * rows, 3 * columns), bf16),
            VMEM((tokens, 2 * columns), bf16),
            VMEM((tokens, columns), bf16),
            VMEM((width, tokens), bf16),
            VMEM((width, tokens), bf16),
            VMEM((tokens, width), bf16),
            VMEM((16, rows, 3 * columns), bf16),
        ]
        + [VMEM((2, 2, here // 4, width), bf16)] * 4
        + ring_buffers(0, rows // 4, columns) * 2
        + [DMA((4,)), DMA((4,))]
        + [DMA((tiles, 3)), DMA((18,)), DMA((48,)), DMA((48,)), DMA((24,)), DMA((24,))],
        compiler_params=pltpu.CompilerParams(
            collective_id=2, has_side_effects=True, vmem_limit_bytes=VMEM_LIMIT
        ),
    )(
        normed, cot_rows, cotangent, unit, weights.reshape(4, 4, 2 * rows, 3 * columns), scale,
        norm_table,
    )


def cube():
    yl, c, yh = lax.axis_index("yl"), lax.axis_index("c"), lax.axis_index("yh")
    return [
        {"yl": (yl + a) % 2, "c": (c + b) % 2, "yh": (yh + d) % 2}
        for a in range(2)
        for b in range(2)
        for d in range(2)
        if a + b + d
    ]


class Spread:
    def __init__(self, out, rows, sems, core_sems):
        self.out, self.rows, self.sems, self.core_sems = out, rows, sems, core_sems
        self.done, self.core = [], []

    def cut(self, half, df, dg, part=None):
        z, x = lax.axis_index("z"), lax.axis_index("x")
        dz, dx = (df, dg) if half == 0 else (dg, df)
        place = ((z + dz) % 4) * 4 + (x + dx) % 4
        start = (place * 4 + lax.axis_index("c") * 2 + half) * self.rows
        piece = self.rows // 2
        if part is None:
            return self.out.at[pl.ds(pl.multiple_of(start, self.rows), self.rows)]
        return self.out.at[pl.ds(pl.multiple_of(start + part * piece, piece), piece)]

    def index(self, half, df, dg, part):
        return ((half * 4 + df % 4) * 4 + dg % 4) * 2 + part

    def push(self, half, df, dg, axis, step, part):
        device = at_z(step) if (half == 0) == (axis == 0) else at_x(step)
        to = (df - step, dg) if axis == 0 else (df, dg - step)
        ref = self.cut(half, df, dg, part)
        copy = remote(ref, ref, self.sems, self.index(half, *to, part), device)
        copy.start()
        self.done.append(copy)

    def arrived(self, half, df, dg, part):
        ref = self.cut(half, df, dg, part)
        remote(ref, ref, self.sems, self.index(half, df, dg, part), at_z(1)).wait_recv()

    def to_sibling(self, half, df, dg):
        ref = self.cut(half, df, dg)
        copy = remote(ref, ref, self.core_sems, (half * 4 + df % 4) * 4 + dg % 4, sibling())
        copy.start()
        self.done.append(copy)
        self.core.append(copy)

    def push_all(self, half, df, dg, axis):
        for part in range(2):
            self.push(half, df, dg, axis, 1, part)
            self.push(half, df, dg, axis, -1, 1 - part)

    def start(self):
        for axis in range(2):
            for half in range(2):
                self.push_all(half, 0, 0, axis)
        for half in range(2):
            self.to_sibling(half, 0, 0)

    def first_pass(self):
        for half in range(2):
            self.arrived(half, 3, 0, 0)
            self.push(half, 3, 0, 0, 1, 0)
            self.arrived(half, 1, 0, 1)
            self.push(half, 1, 0, 0, -1, 1)

    def first_rest(self):
        for half in range(2):
            self.arrived(half, 3, 0, 1)
            self.arrived(half, 1, 0, 0)
            for df in (3, 1):
                self.push_all(half, df, 0, 1)
                self.to_sibling(half, df, 0)

    def first_far(self):
        for half in range(2):
            self.arrived(half, 2, 0, 0)
            self.arrived(half, 2, 0, 1)
            self.push_all(half, 2, 0, 1)
            self.to_sibling(half, 2, 0)

    def second_pass(self, df):
        for half in range(2):
            self.arrived(half, df, 3, 0)
            self.push(half, df, 3, 1, 1, 0)
            self.arrived(half, df, 1, 1)
            self.push(half, df, 1, 1, -1, 1)
        for half in range(2):
            self.arrived(half, df, 3, 1)
            self.to_sibling(half, df, 3)
            self.arrived(half, df, 1, 0)
            self.to_sibling(half, df, 1)

    def second_far(self, df):
        for half in range(2):
            for part in range(2):
                self.arrived(half, df, 2, part)
            self.to_sibling(half, df, 2)

    def land(self):
        for copy in self.core:
            copy.wait_recv()

    def close(self):
        for copy in self.done:
            copy.wait_send()


def extra_rows(qkv_bias, norm_params, q, rows):
    z, x = lax.axis_index("z"), lax.axis_index("x")
    yl, c, yh = lax.axis_index("yl"), lax.axis_index("c"), lax.axis_index("yh")
    mine = ((z * 4 + x) * 2 + yl) * 2 + c
    lane = lax.broadcasted_iota(jnp.int32, (1, EXTRA), 1)
    heads = qkv_bias.shape[2] // 2
    pieces = []
    for t in range(3):
        for pair in range(heads // 2):
            row = jnp.zeros((1, EXTRA), f32)
            for side in range(2):
                head = q * heads + 2 * pair + side
                value = qkv_bias[t, :, head : head + 1].astype(f32)
                row = row + jnp.where(lane == mine + side * HEAD_DIM, value, 0.0)
            pieces.append(row)
    share = norm_params.shape[1]
    high = norm_params[...].astype(bf16).astype(f32)
    norm = jnp.concatenate([high, norm_params[...] - high], 0)
    norm = jnp.concatenate([norm, jnp.zeros((norm.shape[0], EXTRA - share), f32)], 1)
    norm = pltpu.roll(norm, (mine % 4 * 2 + yh) * share, 1)
    used = len(pieces) + norm.shape[0]
    pieces += [norm, jnp.zeros((rows - used, EXTRA), f32)]
    return jnp.concatenate(pieces, 0).astype(bf16)


def forward_kernel(
    qkv_weight, out_weight, gate_up_weight, down_weight, qkv_bias, norm_params, tokens, cotangent,
    table,
    one_out, two, token_out, cot_out, qkv_out, mix_out, summed_out, unit_out, normed_out,
    stats, norm_table, scale,
    token_rows, cot_rows, qkv, head_mix, summed, unit, normed_two,
    one_q, two_q, one, norm_in, bias, normed, parts, mid, sent, far, near,
    pair_send, pair_recv, local_sem, save_sem, y_send, y_recv,
    send_one, recv_one, core_send_one, core_recv_one,
    send_two, recv_two, core_send_two, core_recv_two,
):
    z, x = lax.axis_index("z"), lax.axis_index("x")
    yl, c, yh = lax.axis_index("yl"), lax.axis_index("c"), lax.axis_index("yh")
    rows, here = one_q.shape[1], tokens.shape[0]
    hq, fq = qkv_weight.shape[2] // 2, gate_up_weight.shape[2] // 2
    pair_sems, y_sems = (pair_send, pair_recv), (y_send, y_recv)
    for q in range(2):
        for group in range(2):
            for t in range(3):
                to, start = (group * 3 + t) * hq // 2, q * hq + group * hq // 2
                one_q[q, :, to : to + hq // 2] = qkv_weight[t, :, start : start + hq // 2]
        one_q[q, :, 3 * hq : 3 * hq + EXTRA] = extra_rows(qkv_bias, norm_params, q, rows)
        one_q[q, :, 3 * hq + EXTRA :] = out_weight[:, q * hq : (q + 1) * hq]
    token_rows[pl.ds(0, here)] = tokens[...]
    greet([at_z(1), at_z(3), at_x(1), at_x(3)] + cube())

    same, cross = pair_moves()
    mine = pl.ds(pl.multiple_of((z * 4 + x) * 4 * rows + (yl * 2 + c) * rows, rows), rows)
    moves = [
        (one_q.at[c], one.at[mine], 0, same),
        (one_q.at[1 - c], one.at[mine], 1, cross),
        (two_q.at[c], two.at[mine], 2, same),
        (two_q.at[1 - c], two.at[mine], 3, cross),
    ]

    def launch(k):
        src, dst, index, device = moves[k]
        if device is same:
            stay_or_go(src, dst, pair_sems, index, device, local_sem.at[index // 2])
        else:
            remote(src, dst, pair_sems, index, device).start()

    def land(k):
        src, dst, index, device = moves[k]
        if device is same:
            stay_or_go_wait(src, dst, pair_sems, index, device, local_sem.at[index // 2])
        else:
            copy = remote(src, dst, pair_sems, index, device)
            copy.wait_recv()
            copy.wait_send()

    norm_moves = [
        remote(
            one_q.at[0, :, pl.ds(3 * hq, EXTRA)],
            norm_in.at[c],
            pair_sems,
            4 + which,
            {"yl": target["yl"], "c": target["c"], "yh": 1 - yh},
        )
        for which, target in enumerate((same, cross))
    ]
    launch(0)
    launch(1)
    for move in norm_moves:
        move.start()
    token_halves = [ring_gather_half(token_rows, top, y_sems, 0) for top in range(2)]
    for q in range(2):
        for t in range(2):
            two_q[q, :, t * fq : (t + 1) * fq] = gate_up_weight[t, :, q * fq : (q + 1) * fq]
        two_q[q, :, 2 * fq :] = down_weight[:, q * fq : (q + 1) * fq]
    sub = here // 2
    for k in range(2):
        cot_rows[pl.ds(4 * k * sub, sub)] = cotangent[pl.ds(k * sub, sub)]
    land(0)
    land(1)
    for move in norm_moves:
        move.wait_recv()
    own = (z * 4 + x) * 4 + 2 * c
    for core in range(2):
        block = pl.ds(pl.multiple_of((own + core) * rows, rows), rows)
        came = norm_in[core].astype(f32)
        place = lax.broadcasted_iota(jnp.int32, came.shape, 0)
        held = one[block, pl.ds(3 * hq, EXTRA)].astype(f32)
        one[block, pl.ds(3 * hq, EXTRA)] = (
            held + jnp.where((place >= 12) & (place < 20), came, 0.0)
        ).astype(bf16)
    first = Spread(one, rows, (send_one, recv_one), (core_send_one, core_recv_one))
    second = Spread(two, rows, (send_two, recv_two), (core_send_two, core_recv_two))
    first.start()
    launch(2)
    launch(3)
    first.first_pass()
    first.first_rest()
    token_passed = ring_gather_pass(token_rows, token_halves, y_sems, 0)
    first.second_pass(0)
    first.first_far()
    first.second_pass(3)
    first.second_pass(1)
    land(2)
    land(3)
    second.start()
    first.second_pass(2)
    for df in (0, 3, 1, 2):
        first.second_far(df)
    for copy in token_passed + [token_halves[1][0], token_halves[0][1]]:
        copy.wait_recv()
    cot_subs = [cot_rows.at[pl.ds(4 * k * sub, 4 * sub)] for k in range(2)]
    cot_halves = [
        [ring_gather_half(cot_subs[k], top, y_sems, 6 + 6 * k) for top in range(2)]
        for k in range(2)
    ]
    first.land()
    keep = pltpu.make_async_copy(one, one_out, local_sem.at[2])
    keep.start()
    saves = []

    def save(src, dst):
        saves.append(pltpu.make_async_copy(src, dst, save_sem.at[len(saves)]))
        saves[-1].start()

    save(token_rows, token_out)

    read_extras(one, 3 * hq, norm_table, bias)

    def norm_rows(k, _):
        rng = pl.ds(pl.multiple_of(k * here, here), here)
        values = token_rows[rng].astype(f32)
        mean = jnp.mean(values, -1, keepdims=True)
        centered = values - mean
        inverse = lax.rsqrt(jnp.mean(centered * centered, -1, keepdims=True) + EPSILON)
        stats[0, rng] = mean
        stats[1, rng] = inverse
        normed[rng] = (centered * inverse * norm_table[0:1] + norm_table[1:2]).astype(bf16)
        return 0

    lax.fori_loop(0, 4, norm_rows, 0)
    second.first_pass()
    wide = 256

    def project(k, _):
        cols = pl.ds(pl.multiple_of(k * wide, wide), wide)
        value = dot(normed[...], one[:, cols], 1, 0)
        row = k % 3 * (hq // 128) + k // 3 * 2
        value = value + jnp.concatenate([bias[pl.ds(row, 1)], bias[pl.ds(row + 1, 1)]], 1)

        @pl.when(k % 3 < 2)
        def _():
            for place in range(4):
                rng = pl.ds(place * here, here)
                turn = table[pl.ds(pl.multiple_of(half_of_place(place) * here, here), here)]
                for pair in range(wide // 128):
                    qkv[rng, pl.ds(pl.multiple_of(k * wide + pair * 128, 128), 128)] = turn_heads(
                        value[place * here : (place + 1) * here, pair * 128 : (pair + 1) * 128],
                        turn,
                        1.0,
                    ).astype(bf16)

        @pl.when(k % 3 == 2)
        def _():
            qkv[:, cols] = value.astype(bf16)

        return 0

    lax.fori_loop(0, 3 * hq // wide, project, 0)
    save(qkv, qkv_out)
    second.first_rest()
    cot_passed = [
        ring_gather_pass(cot_subs[k], cot_halves[k], y_sems, 6 + 6 * k) for k in range(2)
    ]
    for sequence in range(2):
        mask = causal_mask(sequence, here)
        rng = pl.ds(sequence * 2 * here, 2 * here)

        def heads(k, _):
            def pair(t):
                start = k // 2 * (3 * hq // 2) + t * (hq // 2) + k % 2 * 128
                return qkv[rng, pl.ds(pl.multiple_of(start, 128), 128)]

            q, key, value = pair(0), pair(1), pair(2)
            mixes = []
            for head in range(2):
                cut = slice(head * HEAD_DIM, (head + 1) * HEAD_DIM)
                soft = soft_of(q[:, cut], key[:, cut], mask).astype(bf16)
                mixes.append(dot(soft, value[:, cut], 1, 0))
            head_mix[rng, pl.ds(pl.multiple_of(k * 128, 128), 128)] = jnp.concatenate(
                mixes, 1
            ).astype(bf16)
            return 0

        lax.fori_loop(0, hq // 128, heads, 0, unroll=2)
        if sequence == 0:
            second.second_pass(0)
    second.first_far()

    save(head_mix, mix_out)
    for k in range(2):
        for copy in cot_passed[k] + [cot_halves[k][1][0], cot_halves[k][0][1]]:
            copy.wait_recv()
    save(cot_rows, cot_out)
    part_subs = [parts.at[pl.ds(4 * k * sub, 4 * sub)] for k in range(2)]
    started, middle = [], []
    for part in range(2):
        mix = jnp.concatenate(
            [head_mix[pl.ds(k * here + part * sub, sub)] for k in range(4)], 0
        )

        def out_project(k, _):
            rng = pl.ds(pl.multiple_of(k * wide, wide), wide)
            parts[pl.ds(4 * part * sub, 4 * sub), rng] = dot(
                mix, one[rng, pl.ds(3 * hq + EXTRA, hq)], 1, 1
            ).astype(bf16)
            return 0

        lax.fori_loop(0, one.shape[0] // wide, out_project, 0)
        started.append(
            ring_sum_start(part_subs[part], mid.at[part], near.at[part], y_sems, 18 + 6 * part)
        )
    second.second_pass(3)
    for part in range(2):
        middle.append(
            ring_sum_middle(
                part_subs[part], started[part], mid.at[part], sent.at[part], far.at[part],
                y_sems, 18 + 6 * part,
            )
        )
    second.second_pass(1)
    halves = []
    for part in range(2):
        finish = ring_sum_finish(
            part_subs[part], started[part], middle[part], far.at[part], near.at[part]
        )
        total = jnp.concatenate([finish(0), finish(1)], 0)
        rng = pl.ds(part * sub, sub)
        total = total + tokens[rng].astype(f32)
        summed[rng] = total
        centered = total - jnp.mean(total, -1, keepdims=True)
        inverse = lax.rsqrt(jnp.mean(centered * centered, -1, keepdims=True) + EPSILON)
        unit_rows = centered * inverse
        unit[rng] = unit_rows
        scale[rng] = inverse
        normed_two[pl.ds(4 * part * sub, sub)] = (
            unit_rows * norm_table[2:3] + norm_table[3:4]
        ).astype(bf16)
        out = normed_two.at[pl.ds(4 * part * sub, 4 * sub)]
        halves.append([ring_gather_half(out, top, y_sems, 30 + 6 * part) for top in range(2)])
    save(summed, summed_out)
    save(unit, unit_out)
    second.second_pass(2)
    passed = [
        ring_gather_pass(
            normed_two.at[pl.ds(4 * k * sub, 4 * sub)], halves[k], y_sems, 30 + 6 * k
        )
        for k in range(2)
    ]
    for df in (0, 3, 1, 2):
        second.second_far(df)
    for k in range(2):
        for copy in passed[k] + [halves[k][1][0], halves[k][0][1]]:
            copy.wait_recv()
        these = pl.ds(4 * k * sub, 4 * sub)
        save(normed_two.at[these], normed_out.at[these])
    second.land()
    keep.wait()
    for copy in saves:
        copy.wait()
    for move in norm_moves:
        move.wait_send()
    gathers = token_halves + cot_halves[0] + cot_halves[1] + halves[0] + halves[1]
    for copies in gathers + [token_passed] + cot_passed + started + middle + passed:
        for copy in copies:
            copy.wait_send()
    first.close()
    second.close()


def forward(
    qkv_weight, out_weight, gate_up_weight, down_weight, qkv_bias, norm_params, tokens, cotangent,
    table,
):
    here, width = tokens.shape
    rows = qkv_weight.shape[1]
    hq, fq = qkv_weight.shape[2] // 2, gate_up_weight.shape[2] // 2
    full = pl.BlockSpec(memory_space=VMEM)
    anywhere = pl.BlockSpec(memory_space=pl.ANY)
    one_wide, two_wide = 4 * hq + EXTRA, 3 * fq
    kept = (
        ((4 * here, width), bf16),
        ((4 * here, width), bf16),
        ((4 * here, 3 * hq), bf16),
        ((4 * here, hq), bf16),
        ((here, width), f32),
        ((here, width), f32),
        ((4 * here, width), bf16),
    )

    def shape(*dims, dtype=bf16):
        return jax.ShapeDtypeStruct(dims, dtype)

    return pl.pallas_call(
        forward_kernel,
        out_shape=(
            shape(width, one_wide),
            shape(width, two_wide),
            *(shape(*dims, dtype=dtype) for dims, dtype in kept),
            shape(2, 4 * here, 1, dtype=f32),
            shape(4, width, dtype=f32),
            shape(here, 1, dtype=f32),
        ),
        in_specs=[full] * 9,
        out_specs=(anywhere,) * 9 + (full,) * 3,
        scratch_shapes=[VMEM(dims, dtype) for dims, dtype in kept]
        + [
            VMEM((2, rows, one_wide), bf16),
            VMEM((2, rows, two_wide), bf16),
            VMEM((width, one_wide), bf16),
            VMEM((2, rows, EXTRA), bf16),
            VMEM((12, 128), f32),
            VMEM((4 * here, width), bf16),
            VMEM((4 * here, width), bf16),
        ]
        + [VMEM((2, 2, here // 4, width), bf16)] * 4
        + [
            DMA((6,)), DMA((6,)), DMA((3,)), DMA((9,)), DMA((42,)), DMA((42,)),
            DMA((64,)), DMA((64,)), DMA((32,)), DMA((32,)),
            DMA((64,)), DMA((64,)), DMA((32,)), DMA((32,)),
        ],
        compiler_params=pltpu.CompilerParams(
            collective_id=0, has_side_effects=True, vmem_limit_bytes=VMEM_LIMIT
        ),
    )(
        qkv_weight, out_weight, gate_up_weight, down_weight, qkv_bias, norm_params, tokens,
        cotangent, table,
    )


def backward_kernel(
    one, resid_rows, chip, settled, qkv_in, mix_in, token_in, mixed_in, resid_in, sum_in,
    stats, table, second_terms, norm_table,
    result_one, result_two, norm_back, grad_out, mixed_out,
    qkv, head_mix, token_rows, mixed_parts, resid, first_sum, grad_tokens, mixed,
    held, spare, grad_mix, grad_proj, part_sums, sib, blocks, pair_sums,
    *rest,
):
    rings = [rest[5 * k : 5 * k + 5] for k in range(9)]
    rings = [(mid, far, near, (send, recv)) for mid, far, near, send, recv in rings]
    (
        packed_one, packed_two, ymid, ysent, yfar, ynear,
        load_sem, in_sem, save_sem, block_sem, core_send, core_recv, pair_send, pair_recv, local_sem, y_send, y_recv,
    ) = rest[45:]
    z, x = lax.axis_index("z"), lax.axis_index("x")
    yl, c, yh = lax.axis_index("yl"), lax.axis_index("c"), lax.axis_index("yh")
    here = resid.shape[0]
    rows = result_one.shape[1]
    hq, fq = head_mix.shape[1], result_two.shape[2] // 3
    early, late = pair_sums.shape[3], blocks.shape[3]
    sub = here // 2
    width = held.shape[0]
    core_sems, pair_sems, y_sems = (core_send, core_recv), (pair_send, pair_recv), (y_send, y_recv)
    wide = 256
    out_start = 3 * hq + EXTRA
    group = 3 * hq // 2
    columns = (pl.ds(0, group), pl.ds(out_start, hq), pl.ds(group, group + EXTRA))

    def place_of(dz, dx):
        return ((z + dz) % 4) * 4 + (x + dx) % 4

    loads = [
        pltpu.make_async_copy(
            one.at[:, pl.ds(start, size)], held.at[:, pl.ds(start, size)], load_sem.at[k]
        )
        for k, (start, size) in enumerate(((out_start, hq), (0, 3 * hq)))
    ]
    loads.append(pltpu.make_async_copy(resid_rows, spare, load_sem.at[2]))
    loads.append(pltpu.make_async_copy(settled, pair_sums, load_sem.at[3]))
    block_loads = [
        pltpu.make_async_copy(
            chip.at[place_of(dz, dx)], blocks.at[dz, dx], block_sem.at[dz * 4 + dx]
        )
        for dz in range(4)
        for dx in range(4)
    ]
    ins = [
        pltpu.make_async_copy(src, dst, in_sem.at[k])
        for k, (src, dst) in enumerate(
            (
                (mixed_in, mixed_parts), (mix_in, head_mix), (qkv_in, qkv),
                (token_in, token_rows), (resid_in, resid), (sum_in, first_sum),
            )
        )
    ]
    loads[3].start()
    ins[0].start()
    loads[2].start()
    loads[0].start()
    ins[1].start()
    for load in block_loads:
        load.start()
    greet([at_z(1), at_z(3), at_x(1), at_x(3)] + cube())
    ins[0].wait()
    mixed_started = ring_sum_start(mixed_parts, ymid.at[0], ynear.at[0], y_sems, 0)

    def cut(half, part):
        return pl.ds(half * rows + part * (rows // 2), rows // 2)

    def pair_view(stage, half, d, part):
        along = x if half == 0 else z
        return pair_sums.at[half, (along + d) % 4, pl.ds(part * (rows // 2), rows // 2)]

    def view_of(ref, cols):
        def view(stage, half, d, part):
            if stage == 0:
                there = (d, slice(None)) if half == 0 else (slice(None), d)
            else:
                there = (0, d) if half == 0 else (d, 0)
            return ref.at[(*there, cut(half, part), cols)]

        return view

    early_sums = Reduce(pair_view, rows, {1: rings[0]})
    late_sums = Reduce(view_of(blocks, pl.ds(0, late)), rows, {0: rings[1], 1: rings[2]})
    out_proj = Reduce(view_of(sib, columns[1]), rows, {0: rings[3], 1: rings[4]})
    head_sums = [
        Reduce(view_of(sib, columns[0]), rows, {0: rings[5], 1: rings[6]}),
        Reduce(view_of(sib, columns[2]), rows, {0: rings[7], 1: rings[8]}),
    ]
    loads[3].wait()
    early_sums.begin(1)
    for load in block_loads:
        load.wait()
    late_sums.begin(0)

    def to_core(block, which):
        theirs = pl.ds(pl.multiple_of((2 * block + 1 - c) * 2 * rows, 2 * rows), 2 * rows)
        dz, dx = (block // 4 - z + 4) % 4, (block % 4 - x + 4) % 4
        return remote(
            held.at[theirs, columns[which]],
            sib.at[dz, dx, :, columns[which]],
            core_sems,
            block + 16 * which,
            sibling(),
        )

    def core_sum(block, which):
        to_core(block, which).wait_recv()
        ours = pl.ds(pl.multiple_of((2 * block + c) * 2 * rows, 2 * rows), 2 * rows)
        there = ((block // 4 - z + 4) % 4, (block % 4 - x + 4) % 4, slice(None), columns[which])
        sib[there] = (sib[there].astype(f32) + held[ours, columns[which]].astype(f32)).astype(
            bf16
        )

    loads[2].wait()
    loads[0].wait()
    ins[1].wait()

    mix_order = jnp.concatenate(
        [
            head_mix[pl.ds(block * here + part * sub, sub)]
            for part in range(2)
            for block in range(4)
        ],
        0,
    )

    def mix_back(k, _):
        cols = pl.ds(pl.multiple_of(k * wide, wide), wide)
        value = dot(
            spare[...], held[:, pl.ds(pl.multiple_of(out_start + k * wide, 128), wide)], 1, 0
        ).astype(bf16)
        for part in range(2):
            for block in range(4):
                start = (part * 4 + block) * sub
                grad_mix[pl.ds(block * here + part * sub, sub), cols] = value[start : start + sub]
        return 0

    ins[2].start()
    loads[1].start()
    lax.fori_loop(0, hq // wide, mix_back, 0)
    for load in ins[3:]:
        load.start()

    def out_back(k, _):
        rng = pl.ds(pl.multiple_of(k * 2 * wide, 2 * wide), 2 * wide)
        held[rng, columns[1]] = dot(spare[:, rng], mix_order, 0, 0).astype(bf16)
        for block in range(4):
            to_core(4 * k + block, 1).start()
        return 0

    lax.fori_loop(0, width // (2 * wide), out_back, 0)
    early_sums.combine(1)
    mixed_middle = ring_sum_middle(
        mixed_parts, mixed_started, ymid.at[0], ysent.at[0], yfar.at[0], y_sems, 0
    )

    def out_sum(block, _):
        core_sum(block, 1)
        return 0

    lax.fori_loop(0, 16, out_sum, 0)
    out_proj.begin(0)
    masks = [causal_mask(sequence, here) for sequence in range(2)]
    turns = [
        jnp.concatenate(
            [
                table[pl.ds(pl.multiple_of(half_of_place(2 * sequence + k) * here, here), here)]
                for k in range(2)
            ],
            0,
        )
        for sequence in range(2)
    ]

    def heads_back(half, sequence):
        mask, turn = masks[sequence], turns[sequence]
        rng = pl.ds(sequence * 2 * here, 2 * here)
        for k in range(hq // 256):

            def pair(t):
                return pl.ds(half * group + t * (hq // 2) + k * 128, 128)

            q, key, value = qkv[rng, pair(0)], qkv[rng, pair(1)], qkv[rng, pair(2)]
            mix = grad_mix[rng, pl.ds(half * (hq // 2) + k * 128, 128)]
            results = ([], [], [])
            for head in range(2):
                lanes = slice(head * HEAD_DIM, (head + 1) * HEAD_DIM)
                soft = soft_of(q[:, lanes], key[:, lanes], mask)
                grad_soft = dot(mix[:, lanes], value[:, lanes], 1, 1)
                row_dot = jnp.sum(grad_soft * soft, -1, keepdims=True)
                grad_score = (soft * (grad_soft - row_dot)).astype(bf16)
                results[0].append(dot(grad_score, key[:, lanes], 1, 0) * SCALE)
                results[1].append(dot(grad_score, q[:, lanes], 0, 0) * SCALE)
                results[2].append(dot(soft.astype(bf16), mix[:, lanes], 0, 0))
            for t in range(3):
                both = jnp.concatenate(results[t], 1)
                if t < 2:
                    both = turn_heads(both, turn, -1.0)
                grad_proj[rng, pair(t)] = both.astype(bf16)

    def bias_sum(t, k):
        start = k // 2 * group + t * (hq // 2) + k % 2 * 128
        return jnp.sum(grad_proj[:, pl.ds(start, 128)].astype(f32), 0, keepdims=True)

    mean, inverse = stats[0], stats[1]
    tall = 512

    def weights_back(half, k, bias_rows):
        rng = pl.ds(pl.multiple_of(k * tall, tall), tall)
        these = pl.ds(half * group, group)
        part = dot(grad_proj[:, these], held[rng, these], 1, 1)
        unit = (token_rows[:, rng].astype(f32) - mean) * inverse
        normed = (unit * norm_table[0:1, rng] + norm_table[1:2, rng]).astype(bf16)
        held[rng, these] = dot(normed, grad_proj[:, these], 0, 0).astype(bf16)
        if half == 0:
            part_sums[:, rng] = part
        else:
            part = part + part_sums[:, rng]
            spare[:, rng] = part.astype(bf16)
            gain = jnp.sum(part * unit, 0, keepdims=True)
            shift = jnp.sum(part, 0, keepdims=True)
            for tile in range(tall // 128):
                inner = slice(tile * 128, (tile + 1) * 128)
                lanes = pl.ds(pl.multiple_of(k * tall + tile * 128, 128), 128)
                extra = jnp.concatenate(
                    bias_rows
                    + [
                        gain[:, inner],
                        shift[:, inner],
                        second_terms[:, lanes],
                        jnp.zeros((rows - 16, 128), f32),
                    ],
                    0,
                ).astype(bf16)
                for copy in range(128 // rows):
                    start = pl.multiple_of(k * tall + tile * 128 + copy * rows, rows)
                    held[pl.ds(start, rows), pl.ds(3 * hq, EXTRA)] = extra
        for block in range(4):
            to_core(4 * k + block, 2 * half).start()

        @pl.when(k > 0)
        def _():
            for block in range(4):
                core_sum(4 * k - 4 + block, 2 * half)

        return 0

    ins[2].wait()
    for sequence in range(2):
        heads_back(0, sequence)
    late_sums.combine(0)
    loads[1].wait()
    for load in ins[3:]:
        load.wait()
    lax.fori_loop(0, width // tall, lambda k, _: weights_back(0, k, None), 0)
    for block in range(12, 16):
        core_sum(block, 0)
    head_sums[0].begin(0)
    early_sums.settle(1, packed_two.at[:, :, pl.ds(0, early)])
    heads_back(1, 0)
    out_proj.combine(0)
    late_sums.settle(0)
    late_sums.begin(1)
    heads_back(1, 1)
    head_sums[0].combine(0)
    bias_rows = [bias_sum(t, k) for t in range(3) for k in range(hq // 128)]
    lax.fori_loop(0, width // tall, lambda k, _: weights_back(1, k, bias_rows), 0)
    first_started = ring_sum_start(spare, ymid.at[1], ynear.at[1], y_sems, 6)
    for block in range(12, 16):
        core_sum(block, 2)
    head_sums[1].begin(0)
    out_proj.settle(0)
    out_proj.begin(1)
    late_sums.combine(1)
    head_sums[0].settle(0)
    head_sums[0].begin(1)
    late_sums.settle(1, packed_two.at[:, :, pl.ds(early, late)])
    home, away = {"yl": c, "c": yl}, {"yl": c, "c": 1 - yl}
    stay_or_go(packed_two.at[yl], result_two.at[yl], pair_sems, 0, home, local_sem.at[0])
    cross_two = remote(packed_two.at[1 - yl], result_two.at[yl], pair_sems, 1, away)
    cross_two.start()
    first_middle = ring_sum_middle(
        spare, first_started, ymid.at[1], ysent.at[1], yfar.at[1], y_sems, 6
    )
    out_proj.combine(1)
    head_sums[1].combine(0)
    head_sums[0].combine(1)
    half_here = here // 2
    finish = ring_sum_finish(mixed_parts, mixed_started, mixed_middle, yfar.at[0], ynear.at[0])
    for top in range(2):
        rng = pl.ds(top * half_here, half_here)
        mixed[rng] = (first_sum[rng] + finish(top)).astype(bf16)
    saves = [pltpu.make_async_copy(mixed, mixed_out, save_sem.at[0])]
    saves[0].start()
    finish = ring_sum_finish(spare, first_started, first_middle, yfar.at[1], ynear.at[1])
    for top in range(2):
        rng = pl.ds(top * half_here, half_here)
        incoming = finish(top) * norm_table[0:1]
        unit_rows = (token_rows[rng].astype(f32) - stats[0, rng]) * stats[1, rng]
        grad_tokens[rng] = resid[rng] + stats[1, rng] * (
            incoming
            - jnp.mean(incoming, -1, keepdims=True)
            - unit_rows * jnp.mean(incoming * unit_rows, -1, keepdims=True)
        )
    saves.append(pltpu.make_async_copy(grad_tokens, grad_out, save_sem.at[1]))
    saves[1].start()
    out_proj.settle(1, packed_one.at[:, :, columns[1]])
    head_sums[0].settle(1, packed_one.at[:, :, columns[0]])
    head_sums[1].settle(0)
    head_sums[1].begin(1)
    head_sums[1].combine(1)
    head_sums[1].settle(1, packed_one.at[:, :, columns[2]])

    stay_or_go(packed_one.at[yl], result_one.at[yl], pair_sems, 2, home, local_sem.at[1])
    cross_one = remote(packed_one.at[1 - yl], result_one.at[yl], pair_sems, 3, away)
    cross_one.start()
    extras = pl.ds(3 * hq, EXTRA)
    norm_moves = [
        remote(
            packed_one.at[core, :, extras],
            norm_back.at[yl],
            pair_sems,
            4 + which,
            {"yl": c, "c": core, "yh": 1 - yh},
        )
        for which, core in enumerate((yl, 1 - yl))
    ]
    for move in norm_moves:
        move.start()
    for copy in [cross_two, cross_one] + norm_moves:
        copy.wait_recv()
        copy.wait_send()
    stay_or_go_wait(packed_two.at[yl], result_two.at[yl], pair_sems, 0, home, local_sem.at[0])
    stay_or_go_wait(packed_one.at[yl], result_one.at[yl], pair_sems, 2, home, local_sem.at[1])
    for copy in saves:
        copy.wait()
    for copy in mixed_started + mixed_middle + first_started + first_middle:
        copy.wait_send()

    def drain(block, _):
        for which in range(3):
            to_core(block, which).wait_send()
        return 0

    lax.fori_loop(0, 16, drain, 0)
    for sums in [early_sums, late_sums, out_proj] + head_sums:
        sums.close()


def backward(
    one, resid_rows, chip, settled, qkv, head_mix, token_rows, mixed_parts, resid, first_sum,
    stats, table, second_terms, norm_table,
):
    here, width = resid.shape
    hq, early, late = head_mix.shape[1], settled.shape[3], chip.shape[2]
    fq = (early + late) // 3
    rows = width // 64
    piece = rows // 2
    one_wide = one.shape[1]
    full = pl.BlockSpec(memory_space=VMEM)
    anywhere = pl.BlockSpec(memory_space=pl.ANY)
    rings = ring_buffers(1, piece, early)
    for wide in (late, hq, 3 * hq // 2, 3 * hq // 2 + EXTRA):
        rings += ring_buffers(0, piece, wide) + ring_buffers(1, piece, wide)
    return pl.pallas_call(
        backward_kernel,
        out_shape=(
            jax.ShapeDtypeStruct((2, rows, one_wide), bf16),
            jax.ShapeDtypeStruct((2, rows, 3 * fq), bf16),
            jax.ShapeDtypeStruct((2, rows, EXTRA), bf16),
            jax.ShapeDtypeStruct((here, width), f32),
            jax.ShapeDtypeStruct((here, width), bf16),
        ),
        in_specs=[anywhere] * 10 + [full] * 4,
        out_specs=(anywhere,) * 5,
        scratch_shapes=[
            VMEM(qkv.shape, bf16),
            VMEM(head_mix.shape, bf16),
            VMEM(token_rows.shape, bf16),
            VMEM(mixed_parts.shape, bf16),
            VMEM((here, width), f32),
            VMEM((here, width), f32),
            VMEM((here, width), f32),
            VMEM((here, width), bf16),
            VMEM((width, one_wide), bf16),
            VMEM((4 * here, width), bf16),
            VMEM((4 * here, hq), bf16),
            VMEM((4 * here, 3 * hq), bf16),
            VMEM((4 * here, width), f32),
            VMEM((4, 4, 2 * rows, one_wide), bf16),
            VMEM((4, 4, 2 * rows, late), bf16),
            VMEM((2, 4, rows, early), bf16),
        ]
        + rings
        + [VMEM((2, rows, one_wide), bf16), VMEM((2, rows, 3 * fq), bf16)]
        + [VMEM((2, 2, here // 2, width), bf16)] * 4
        + [DMA((4,)), DMA((6,)), DMA((2,)), DMA((16,)), DMA((48,)), DMA((48,))]
        + [DMA((6,)), DMA((6,)), DMA((2,)), DMA((12,)), DMA((12,))],
        compiler_params=pltpu.CompilerParams(
            collective_id=3, has_side_effects=True, vmem_limit_bytes=VMEM_LIMIT
        ),
    )(
        one, resid_rows, chip, settled, qkv, head_mix, token_rows, mixed_parts, resid, first_sum,
        stats, table, second_terms, norm_table,
    )


def finish_kernel(
    one, two, norm_back, tokens_in, mixed_in,
    mixed, grad_tokens, out_norm, out_qkv, out_bias, out_out, out_gate_up, out_down,
):
    z, x = lax.axis_index("z"), lax.axis_index("x")
    yl, c, yh = lax.axis_index("yl"), lax.axis_index("c"), lax.axis_index("yh")
    mine = ((z * 4 + x) * 2 + yl) * 2 + c
    hq, fq = out_out.shape[1] // 2, out_down.shape[1] // 2
    mixed[...] = mixed_in[...]
    grad_tokens[...] = tokens_in[...]
    for q in range(2):
        for group in range(2):
            for t in range(3):
                start, to = (group * 3 + t) * hq // 2, q * hq + group * hq // 2
                out_qkv[t, :, to : to + hq // 2] = one[q, :, start : start + hq // 2].astype(f32)
        out_out[:, q * hq : (q + 1) * hq] = one[q, :, 3 * hq + EXTRA :].astype(f32)
        for t in range(2):
            out_gate_up[t, :, q * fq : (q + 1) * fq] = two[q, :, t * fq : (t + 1) * fq].astype(f32)
        out_down[:, q * fq : (q + 1) * fq] = two[q, :, 2 * fq :].astype(f32)
    extras = [one[q, :, 3 * hq : 3 * hq + EXTRA].astype(f32) for q in range(2)]
    heads = hq // HEAD_DIM
    pairs = 3 * heads // 2
    share = out_norm.shape[1]
    sums = extras[0] + extras[1] + (norm_back[0].astype(f32) + norm_back[1].astype(f32))
    sums = pltpu.roll(sums, EXTRA - (mine % 4 * 2 + yh) * share, 1)
    out_norm[...] = sums[pairs : pairs + 4, :share]
    lane = lax.broadcasted_iota(jnp.int32, extras[0].shape, 1)
    place = lax.broadcasted_iota(jnp.int32, (1, 2 * heads), 1)
    totals = [jnp.zeros((1, 2 * heads), f32) for _ in range(3)]
    for q in range(2):
        for side in range(2):
            value = jnp.sum(
                jnp.where(lane == mine + side * HEAD_DIM, extras[q], 0.0), 1, keepdims=True
            )
            for t in range(3):
                for pair in range(heads // 2):
                    row = t * (heads // 2) + pair
                    head = q * heads + 2 * pair + side
                    totals[t] = totals[t] + jnp.where(place == head, value[row : row + 1], 0.0)
    for t in range(3):
        out_bias[t] = totals[t]


def finish(one, two, norm_back, grad_tokens, mixed, share):
    rows = one.shape[1]
    hq, fq = (one.shape[2] - EXTRA) // 4, two.shape[2] // 3
    full = pl.BlockSpec(memory_space=VMEM)
    return pl.pallas_call(
        finish_kernel,
        out_shape=(
            jax.ShapeDtypeStruct(mixed.shape, bf16),
            jax.ShapeDtypeStruct(grad_tokens.shape, f32),
            jax.ShapeDtypeStruct((4, share), f32),
            jax.ShapeDtypeStruct((3, rows, 2 * hq), f32),
            jax.ShapeDtypeStruct((3, 1, 2 * hq // HEAD_DIM), f32),
            jax.ShapeDtypeStruct((rows, 2 * hq), f32),
            jax.ShapeDtypeStruct((2, rows, 2 * fq), f32),
            jax.ShapeDtypeStruct((rows, 2 * fq), f32),
        ),
        in_specs=[full] * 5,
        out_specs=(full,) * 8,
        compiler_params=pltpu.CompilerParams(vmem_limit_bytes=VMEM_LIMIT),
    )(one, two, norm_back, grad_tokens, mixed)


def shards(
    tokens, cotangent, norm_params, qkv_weight, qkv_bias, out_weight, gate_up_weight, down_weight
):
    table = jnp.asarray(tables())
    (
        one, second, token_rows, cot_rows, qkv, head_mix, first_sum, unit_two, normed_two,
        stats, norm_table, scale_two,
    ) = forward(
        qkv_weight, out_weight.T, gate_up_weight, down_weight.T, qkv_bias.transpose(0, 2, 1),
        norm_params, tokens, cotangent, table,
    )
    grad_resid, resid_rows, mixed_parts, chip, settled, second_terms = feed_forward(
        normed_two, cot_rows, cotangent, unit_two, scale_two, norm_table, second
    )
    one_back, two_back, norm_back, grad_tokens, mixed = backward(
        one, resid_rows, chip, settled, qkv, head_mix, token_rows, mixed_parts, grad_resid,
        first_sum, stats, table, second_terms, norm_table,
    )
    mixed, grad_tokens, out_norm, out_qkv, out_bias, out_out, out_gate_up, out_down = finish(
        one_back, two_back, norm_back, grad_tokens, mixed, norm_params.shape[1]
    )
    return (
        mixed, grad_tokens, out_norm, out_qkv, out_bias.transpose(0, 2, 1), out_out.T,
        out_gate_up, out_down.T,
    )


def solution(mesh):
    grid = Mesh(mesh.devices.reshape(4, 4, 2, 2, 2), GRID)
    placed = (
        P(GRID, None),
        P(GRID, None),
        P(None, GRID),
        P(None, ROWS, "yh"),
        P(None, "yh", ROWS),
        P("yh", ROWS),
        P(None, ROWS, "yh"),
        P("yh", ROWS),
    )
    return jax.shard_map(
        shards,
        mesh=grid,
        in_specs=placed,
        out_specs=(
            P(GRID, None),
            P(GRID, None),
            P(None, GRID),
            P(None, ROWS, "yh"),
            P(None, "yh", ROWS),
            P("yh", ROWS),
            P(None, ROWS, "yh"),
            P("yh", ROWS),
        ),
        check_vma=False,
    )
```

```python
import jax
import jax.numpy as jnp
import numpy as np
from jax import lax
from jax.experimental import pallas as pl
from jax.experimental.pallas import tpu as pltpu
from jax.sharding import Mesh
from jax.sharding import PartitionSpec as P

HEAD_DIM = 64
ROTARY = 16
EPSILON = 1e-05
SCALE = 0.125

GRID = ("z", "x", "yl", "c", "yh")
ROWS = ("z", "x", "yl", "c")
EXTRA = 128

bf16 = jnp.bfloat16
f32 = jnp.float32

MESH = pl.DeviceIdType.MESH
VMEM = pltpu.VMEM
DMA = pltpu.SemaphoreType.DMA
VMEM_LIMIT = 60 * 1024 * 1024


def at_y(k):
    y = (lax.axis_index("yh") * 2 + lax.axis_index("yl") + k) % 4
    return {"yl": y % 2, "yh": y // 2}


def at_z(k):
    return {"z": (lax.axis_index("z") + k) % 4}


def at_x(k):
    return {"x": (lax.axis_index("x") + k) % 4}


def sibling():
    return {"c": 1 - lax.axis_index("c")}


def greet(devices):
    barrier = pltpu.get_barrier_semaphore()
    for device in devices:
        pl.semaphore_signal(barrier, inc=1, device_id=device, device_id_type=MESH)
    pl.semaphore_wait(barrier, len(devices))


def remote(src, dst, sems, index, device):
    send, recv = sems
    return pltpu.make_async_remote_copy(
        src_ref=src,
        dst_ref=dst,
        send_sem=send.at[index],
        recv_sem=recv.at[index],
        device_id=device,
        device_id_type=MESH,
    )


def ring_gather_half(out, top, sems, base):
    here = out.shape[0] // 4
    half = here // 2
    copies = []
    for way, step, block in ((0, 1, 3), (1, -1, 2)):
        copies.append(
            remote(
                out.at[pl.ds(top * half, half)],
                out.at[pl.ds(block * here + top * half, half)],
                sems,
                base + 2 * way + top,
                at_y(step),
            )
        )
        copies[-1].start()
    return copies


def ring_gather_pass(out, halves, sems, base):
    here = out.shape[0] // 4
    half = here // 2
    passed = []
    for way, step, block in ((0, 1, 3), (1, -1, 2)):
        halves[way][way].wait_recv()
        passed.append(
            remote(
                out.at[pl.ds(block * here + way * half, half)],
                out.at[pl.ds(here + way * half, half)],
                sems,
                base + 4 + way,
                at_y(step),
            )
        )
        passed[-1].start()
    return passed


def pair_moves():
    yl, c = lax.axis_index("yl"), lax.axis_index("c")
    return {"yl": c, "c": yl}, {"yl": 1 - c, "c": yl}


def stay_or_go(src, dst, sems, index, device, local_sem):
    yl, c = lax.axis_index("yl"), lax.axis_index("c")

    @pl.when(yl == c)
    def _():
        pltpu.make_async_copy(src, dst, local_sem).start()

    @pl.when(yl != c)
    def _():
        remote(src, dst, sems, index, device).start()


def stay_or_go_wait(src, dst, sems, index, device, local_sem):
    yl, c = lax.axis_index("yl"), lax.axis_index("c")

    @pl.when(yl == c)
    def _():
        pltpu.make_async_copy(src, dst, local_sem).wait()

    @pl.when(yl != c)
    def _():
        copy = remote(src, dst, sems, index, device)
        copy.wait_recv()
        copy.wait_send()


def ring_sum_start(parts, mid, near, sems, base):
    here = parts.shape[0] // 4
    half = here // 2
    copies = []
    for way, step in ((0, 1), (1, -1)):
        copies.append(
            remote(
                parts.at[pl.ds(here + way * half, half)], mid.at[way], sems, base + way, at_y(step)
            )
        )
    for way, step, block in ((0, 1, 2), (1, -1, 3)):
        copies.append(
            remote(
                parts.at[pl.ds(block * here + (1 - way) * half, half)],
                near.at[way],
                sems,
                base + 2 + way,
                at_y(step),
            )
        )
    for copy in copies:
        copy.start()
    return copies


def ring_sum_middle(parts, started, mid, sent, far, sems, base):
    here = parts.shape[0] // 4
    half = here // 2
    copies = []
    for way, step, block in ((0, 1, 2), (1, -1, 3)):
        started[way].wait_recv()
        sent[way] = (
            parts[pl.ds(block * here + way * half, half)].astype(f32) + mid[way].astype(f32)
        ).astype(bf16)
        copies.append(remote(sent.at[way], far.at[way], sems, base + 4 + way, at_y(step)))
        copies[-1].start()
    return copies


def ring_sum_finish(parts, started, middle, far, near):
    half = parts.shape[0] // 8

    def finish(top):
        started[2 + 1 - top].wait_recv()
        middle[top].wait_recv()
        return (
            parts[pl.ds(top * half, half)].astype(f32)
            + far[top].astype(f32)
            + near[1 - top].astype(f32)
        )

    return finish


def tables():
    half = ROTARY // 2
    position = np.arange(256, dtype=np.float32)
    frequency = np.power(np.float32(10000.0), -np.arange(half, dtype=np.float32) * np.float32(2.0 / ROTARY))
    angles = position[:, None] * frequency[None, :].astype(np.float32)
    cosine, sine = np.cos(angles), np.sin(angles)
    own = np.ones((256, 2, HEAD_DIM), np.float32)
    up = np.zeros((256, 2, HEAD_DIM), np.float32)
    down = np.zeros((256, 2, HEAD_DIM), np.float32)
    for head in range(2):
        own[:, head, :half] = cosine
        own[:, head, half:ROTARY] = cosine
        up[:, head, :half] = -sine
        down[:, head, half:ROTARY] = sine
    return np.concatenate([a.reshape(256, 128) for a in (own, up, down)], 1)


def dot(a, b, ca, cb):
    return lax.dot_general(a, b, (((ca,), (cb,)), ((), ())), preferred_element_type=f32)


def turn_heads(value, table, sign):
    own, up, down = table[:, :128], table[:, 128:256], table[:, 256:]
    return value * own + sign * (
        pltpu.roll(value, 120, 1) * up + pltpu.roll(value, 8, 1) * down
    )


def half_of_place(place):
    y = lax.axis_index("yh") * 2 + lax.axis_index("yl")
    return ((y + (0, 2, 1, 3)[place]) % 4) // 2


def causal_mask(sequence, here):
    length = 2 * here
    first = half_of_place(2 * sequence)

    def position(dim):
        index = lax.broadcasted_iota(jnp.int32, (length, length), dim)
        return jnp.where(index < here, index + first * here, index - first * here)

    return position(0) >= position(1)


def soft_of(queries, keys, mask):
    scores = dot(queries, keys, 1, 1) * SCALE
    scores = jnp.where(mask, scores, -1000000000.0)
    powers = jnp.exp(scores - jnp.max(scores, -1, keepdims=True))
    return powers * (1.0 / jnp.sum(powers, -1, keepdims=True))


def read_extras(one, first_column, norm_table, bias):
    total = None
    for group in range(one.shape[0] // 128):
        block = one[pl.ds(group * 128, 128), pl.ds(first_column, 128)].astype(f32)
        block = block[0:32] + block[32:64] + block[64:96] + block[96:128]
        norm_table[:, pl.ds(group * 128, 128)] = block[12:16] + block[16:20]
        total = block[0:12] if total is None else total + block[0:12]
    bias[...] = total


class Reduce:
    def __init__(self, view, rows, rings):
        self.view, self.rows, self.rings = view, rows, rings
        self.done, self.got = [], {}

    def send(self, name, stage, half, way, src, dst, index):
        step = (1, -1)[way]
        device = at_z(step) if (half == 0) == (stage == 0) else at_x(step)
        copy = remote(src, dst, self.rings[stage][3], half * 6 + index * 2 + way, device)
        copy.start()
        self.done.append(copy)
        self.got[name, stage, half, way] = copy

    def begin(self, stage):
        mid, _, near, _ = self.rings[stage]
        for half in range(2):
            for way in range(2):
                src = self.view(stage, half, 2, way)
                self.send("mid", stage, half, way, src, mid.at[half, way], 0)
        for half in range(2):
            for way in range(2):
                src = self.view(stage, half, (1, 3)[way], 1 - way)
                self.send("near", stage, half, way, src, near.at[half, way], 1)

    def combine(self, stage):
        mid, far = self.rings[stage][:2]
        for half in range(2):
            for way in range(2):
                self.got["mid", stage, half, way].wait_recv()
                ref = self.view(stage, half, (1, 3)[way], way)
                ref[...] = (ref[...].astype(f32) + mid[half, way].astype(f32)).astype(bf16)
                self.send("far", stage, half, way, ref, far.at[half, way], 2)

    def settle(self, stage, out=None):
        far, near = self.rings[stage][1:3]
        piece = self.rows // 2
        for half in range(2):
            for part in range(2):
                self.got["far", stage, half, part].wait_recv()
                self.got["near", stage, half, 1 - part].wait_recv()
                ref = self.view(stage, half, 0, part)
                total = (
                    ref[...].astype(f32)
                    + far[half, part].astype(f32)
                    + near[half, 1 - part].astype(f32)
                ).astype(bf16)
                if out is None:
                    ref[...] = total
                else:
                    out[half, pl.ds(part * piece, piece)] = total

    def close(self):
        for copy in self.done:
            copy.wait_send()


def ring_buffers(stage, piece, wide):
    dims = (2, 2, 4, piece, wide) if stage == 0 else (2, 2, piece, wide)
    return [VMEM(dims, bf16)] * 3 + [DMA((12,))] * 2


def feed_forward_kernel(
    normed_in, cot_in, cotangent_in, unit_in, weights, scale, norm_table,
    resid_out, spread_out, mixed_out, chip, settled, sums,
    normed, cot_rows, cotangent, unit, resid, spread, mixed_parts, held, pair, hidden, normed_t, cot_t, parts, sib, mid, sent, far, near,
    *rest,
):
    rings = [rest[5 * k : 5 * k + 5] for k in range(2)]
    rings = [(mid, far, near, (send, recv)) for mid, far, near, send, recv in rings]
    in_sem, save_sem, load_sem, store_sem, core_send, core_recv, y_send, y_recv = rest[10:]
    columns, width = held.shape[3] // 3, normed.shape[1]
    wide = 256
    rows = sib.shape[1]
    sub = cotangent.shape[0] // 2
    z, x, c = lax.axis_index("z"), lax.axis_index("x"), lax.axis_index("c")
    y_sems, core_sems = (y_send, y_recv), (core_send, core_recv)
    whole, left = columns // wide, columns % wide
    all_pair, all_hidden = pl.ds(0, 2 * columns), pl.ds(2 * columns, columns)
    groups = tuple(pl.ds(which * columns, columns) for which in range(3))

    def load(k, which, size):
        start = pl.multiple_of(which * columns + k * wide, 128)
        cut = pl.ds(start, size)
        return pltpu.make_async_copy(
            weights.at[:, :, :, cut], held.at[:, :, :, cut], load_sem.at[k, which]
        )

    ins = [
        pltpu.make_async_copy(src, dst, in_sem.at[k])
        for k, (src, dst) in enumerate(
            ((normed_in, normed), (cot_in, cot_rows), (cotangent_in, cotangent), (unit_in, unit))
        )
    ]
    ins[0].start()
    ins[1].start()
    saves = []

    def save(src, dst):
        saves.append(pltpu.make_async_copy(src, dst, save_sem.at[len(saves)]))
        saves[-1].start()

    def load_tile(k, size):
        for which in range(3):
            load(k, which, size).start()

    load_tile(0, wide)
    load_tile(1, wide)
    ins[0].wait()
    ins[1].wait()

    def flip(k, _):
        rng = pl.ds(pl.multiple_of(k * wide, wide), wide)
        normed_t[rng] = normed[:, rng].T
        cot_t[rng] = cot_rows[:, rng].T
        return 0

    lax.fori_loop(0, width // wide, flip, 0)
    greet([at_z(1), at_z(3), at_x(1), at_x(3), at_y(1), at_y(3), sibling()])

    tall = width // 4

    def tile(k, cut):
        return k, slice(None), slice(None), cut

    def ahead(part, k, size):
        these = pl.ds(4 * part * sub, 4 * sub)

        def cut(which):
            return pl.ds(pl.multiple_of(which * columns + k * wide, 128), size)

        def weight(which):
            return held[:, :, :, cut(which)].reshape(width, size)

        if part == 0:
            if size == wide:
                pl.when(k + 2 < whole)(lambda: load_tile(k + 2, wide))
                if left:
                    pl.when(k + 2 == whole)(lambda: load_tile(whole, left))
            for which in range(3):
                load(k, which, size).wait()
        gate = dot(normed[these], weight(0), 1, 0)
        up = dot(normed[these], weight(1), 1, 0)
        grad_hidden = dot(cot_rows[these], weight(2), 1, 0)
        sigmoid = jax.nn.sigmoid(gate)
        activated = gate * sigmoid
        hidden[these, cut(0)] = (activated * up).astype(bf16)
        pair[these, cut(0)] = (
            grad_hidden * up * sigmoid * (1.0 + gate * (1.0 - sigmoid))
        ).astype(bf16)
        pair[these, cut(1)] = (grad_hidden * activated).astype(bf16)
        return 0

    part_subs = [parts.at[pl.ds(4 * k * sub, 4 * sub)] for k in range(2)]
    started, middle, halves, passed = [], [], [], []

    def ring_middle(part):
        middle.append(
            ring_sum_middle(
                part_subs[part], started[part], mid.at[part], sent.at[part], far.at[part],
                y_sems, 6 * part,
            )
        )

    for part in range(2):
        lax.fori_loop(0, whole, lambda k, _: ahead(part, k, wide), 0)
        if left:
            ahead(part, whole, left)
        if part == 1:
            ring_middle(0)

        def second_back(k, _):
            rng = pl.ds(pl.multiple_of(k * tall, tall), tall)
            weight = held[tile(k, all_pair)].reshape(tall, 2 * columns)
            these = pl.ds(4 * part * sub, 4 * sub)
            parts[these, rng] = dot(pair[these], weight, 1, 1).astype(bf16)
            return 0

        lax.fori_loop(0, 4, second_back, 0)
        started.append(
            ring_sum_start(part_subs[part], mid.at[part], near.at[part], y_sems, 6 * part)
        )

    def to_core(block, which):
        theirs = pl.ds(pl.multiple_of((1 - c) * rows, rows), rows)
        return remote(
            held.at[block // 4, block % 4, theirs, groups[which]],
            sib.at[block, :, groups[which]],
            core_sems,
            block + 16 * which,
            sibling(),
        )

    ours = pl.ds(pl.multiple_of(c * rows, rows), rows)

    def store(block):
        return pltpu.make_async_copy(
            held.at[block // 4, block % 4, ours, groups[2]], chip.at[block], store_sem.at[block]
        )

    def core_sum(block, which):
        to_core(block, which).wait_recv()
        mine = (block // 4, block % 4, ours, groups[which])
        held[mine] = (
            held[mine].astype(f32) + sib[block, :, groups[which]].astype(f32)
        ).astype(bf16)
        if which == 2:
            store(block).start()

    def weights_back(which, k):
        rng = pl.ds(pl.multiple_of(k * tall, tall), tall)
        if which < 2:
            grad = dot(normed_t[rng], pair[:, groups[which]], 1, 0)
        else:
            grad = dot(cot_t[rng], hidden[...], 1, 0)
        held[tile(k, groups[which])] = grad.astype(bf16).reshape(4, 2 * rows, columns)
        for block in range(4):
            to_core(4 * k + block, which).start()

        @pl.when(k > 1)
        def _():
            for block in range(4):
                core_sum(4 * k - 8 + block, which)

        return 0

    def all_weights(which):
        lax.fori_loop(0, 4, lambda k, _: weights_back(which, k), 0)

    def last_sums(which):
        for block in range(8, 16):
            core_sum(block, which)

    def settle_rows(part):
        finish = ring_sum_finish(
            part_subs[part], started[part], middle[part], far.at[part], near.at[part]
        )
        here = pl.ds(part * sub, sub)
        total = jnp.concatenate([finish(0), finish(1)], 0)
        unit_rows = unit[here]
        incoming = total * norm_table[2:3]
        result = cotangent[here].astype(f32) + scale[here] * (
            incoming
            - jnp.mean(incoming, -1, keepdims=True)
            - unit_rows * jnp.mean(incoming * unit_rows, -1, keepdims=True)
        )
        resid[here] = result
        spread[pl.ds(4 * part * sub, sub)] = result.astype(bf16)
        out = spread.at[pl.ds(4 * part * sub, 4 * sub)]
        halves.append([ring_gather_half(out, top, y_sems, 12 + 6 * part) for top in range(2)])
        both = jnp.concatenate(
            [
                jnp.sum(total * unit_rows, 0, keepdims=True),
                jnp.sum(total, 0, keepdims=True),
            ],
            0,
        )
        sums[...] = both if part == 0 else sums[...] + both

    def gather_pass(part):
        out = spread.at[pl.ds(4 * part * sub, 4 * sub)]
        passed.append(ring_gather_pass(out, halves[part], y_sems, 12 + 6 * part))

    def view_of(cols):
        def view(stage, half, d, part):
            start = c * rows + half * (rows // 2) + part * (rows // 4)
            rng = pl.ds(pl.multiple_of(start, rows // 4), rows // 4)
            if half == 0:
                return held.at[(z + d) % 4, :, rng, cols]
            return held.at[:, (x + d) % 4, rng, cols]

        return view

    gate_sums, up_sums = (
        Reduce(view_of(groups[which]), rows // 2, {0: rings[which]}) for which in range(2)
    )
    def mix(k, _):
        rng = pl.ds(pl.multiple_of(k * tall, tall), tall)
        weight = held[tile(k, all_hidden)].reshape(tall, columns)
        value = dot(hidden[...], weight, 1, 1).astype(bf16)
        for part in range(2):
            for block in range(4):
                start = (part * 4 + block) * sub
                mixed_parts[pl.ds((2 * block + part) * sub, sub), rng] = value[start : start + sub]
        return 0

    ins[2].start()
    ins[3].start()
    all_weights(0)
    ring_middle(1)
    last_sums(0)
    gate_sums.begin(0)
    ins[2].wait()
    ins[3].wait()
    settle_rows(0)
    all_weights(1)
    gate_sums.combine(0)
    last_sums(1)
    up_sums.begin(0)
    gather_pass(0)
    lax.fori_loop(0, 4, mix, 0)
    save(mixed_parts, mixed_out)
    settle_rows(1)
    save(resid, resid_out)
    all_weights(2)
    up_sums.combine(0)
    gather_pass(1)
    last_sums(2)
    gate_sums.settle(0)
    up_sums.settle(0)
    top_rows = pl.ds(pl.multiple_of(c * rows, rows // 2), rows // 2)
    low_rows = pl.ds(pl.multiple_of(c * rows + rows // 2, rows // 2), rows // 2)
    keep = [
        pltpu.make_async_copy(held.at[z, :, top_rows, all_pair], settled.at[0], store_sem.at[16]),
        pltpu.make_async_copy(held.at[:, x, low_rows, all_pair], settled.at[1], store_sem.at[17]),
    ]
    for copy in keep:
        copy.start()

    def drain(block, _):
        for which in range(3):
            to_core(block, which).wait_send()
        store(block).wait()
        return 0

    lax.fori_loop(0, 16, drain, 0)
    for k in range(2):
        for copy in passed[k] + [halves[k][1][0], halves[k][0][1]]:
            copy.wait_recv()
        these = pl.ds(4 * k * sub, 4 * sub)
        save(spread.at[these], spread_out.at[these])
        for copy in started[k] + middle[k] + halves[k][0] + halves[k][1] + passed[k]:
            copy.wait_send()
    gate_sums.close()
    up_sums.close()
    for copy in keep + saves:
        copy.wait()


def feed_forward(normed, cot_rows, cotangent, unit, scale, norm_table, weights):
    tokens, width = normed.shape
    here = cotangent.shape[0]
    columns = weights.shape[1] // 3
    rows = width // 32
    full = pl.BlockSpec(memory_space=VMEM)
    anywhere = pl.BlockSpec(memory_space=pl.ANY)
    tiles = -(-columns // 256)
    kept = (
        ((tokens, width), bf16),
        ((tokens, width), bf16),
        ((here, width), bf16),
        ((here, width), f32),
        ((here, width), f32),
        ((tokens, width), bf16),
        ((tokens, width), bf16),
    )
    return pl.pallas_call(
        feed_forward_kernel,
        out_shape=(
            jax.ShapeDtypeStruct((here, width), f32),
            jax.ShapeDtypeStruct((tokens, width), bf16),
            jax.ShapeDtypeStruct((tokens, width), bf16),
            jax.ShapeDtypeStruct((16, rows, columns), bf16),
            jax.ShapeDtypeStruct((2, 4, rows // 2, 2 * columns), bf16),
            jax.ShapeDtypeStruct((2, width), f32),
        ),
        in_specs=[anywhere] * 5 + [full] * 2,
        out_specs=(anywhere,) * 5 + (full,),
        scratch_shapes=[VMEM(dims, dtype) for dims, dtype in kept]
        + [
            VMEM((4, 4, 2 * rows, 3 * columns), bf16),
            VMEM((tokens, 2 * columns), bf16),
            VMEM((tokens, columns), bf16),
            VMEM((width, tokens), bf16),
            VMEM((width, tokens), bf16),
            VMEM((tokens, width), bf16),
            VMEM((16, rows, 3 * columns), bf16),
        ]
        + [VMEM((2, 2, here // 4, width), bf16)] * 4
        + ring_buffers(0, rows // 4, columns) * 2
        + [DMA((4,)), DMA((4,))]
        + [DMA((tiles, 3)), DMA((18,)), DMA((48,)), DMA((48,)), DMA((24,)), DMA((24,))],
        compiler_params=pltpu.CompilerParams(
            collective_id=2, has_side_effects=True, vmem_limit_bytes=VMEM_LIMIT
        ),
    )(
        normed, cot_rows, cotangent, unit, weights.reshape(4, 4, 2 * rows, 3 * columns), scale,
        norm_table,
    )


def cube():
    yl, c, yh = lax.axis_index("yl"), lax.axis_index("c"), lax.axis_index("yh")
    return [
        {"yl": (yl + a) % 2, "c": (c + b) % 2, "yh": (yh + d) % 2}
        for a in range(2)
        for b in range(2)
        for d in range(2)
        if a + b + d
    ]


class Spread:
    def __init__(self, out, rows, sems, core_sems):
        self.out, self.rows, self.sems, self.core_sems = out, rows, sems, core_sems
        self.done, self.core = [], []

    def cut(self, half, df, dg, part=None):
        z, x = lax.axis_index("z"), lax.axis_index("x")
        dz, dx = (df, dg) if half == 0 else (dg, df)
        place = ((z + dz) % 4) * 4 + (x + dx) % 4
        start = (place * 4 + lax.axis_index("c") * 2 + half) * self.rows
        piece = self.rows // 2
        if part is None:
            return self.out.at[pl.ds(pl.multiple_of(start, self.rows), self.rows)]
        return self.out.at[pl.ds(pl.multiple_of(start + part * piece, piece), piece)]

    def index(self, half, df, dg, part):
        return ((half * 4 + df % 4) * 4 + dg % 4) * 2 + part

    def push(self, half, df, dg, axis, step, part):
        device = at_z(step) if (half == 0) == (axis == 0) else at_x(step)
        to = (df - step, dg) if axis == 0 else (df, dg - step)
        ref = self.cut(half, df, dg, part)
        copy = remote(ref, ref, self.sems, self.index(half, *to, part), device)
        copy.start()
        self.done.append(copy)

    def arrived(self, half, df, dg, part):
        ref = self.cut(half, df, dg, part)
        remote(ref, ref, self.sems, self.index(half, df, dg, part), at_z(1)).wait_recv()

    def to_sibling(self, half, df, dg):
        ref = self.cut(half, df, dg)
        copy = remote(ref, ref, self.core_sems, (half * 4 + df % 4) * 4 + dg % 4, sibling())
        copy.start()
        self.done.append(copy)
        self.core.append(copy)

    def push_all(self, half, df, dg, axis):
        for part in range(2):
            self.push(half, df, dg, axis, 1, part)
            self.push(half, df, dg, axis, -1, 1 - part)

    def start(self):
        for axis in range(2):
            for half in range(2):
                self.push_all(half, 0, 0, axis)
        for half in range(2):
            self.to_sibling(half, 0, 0)

    def first_pass(self):
        for half in range(2):
            self.arrived(half, 3, 0, 0)
            self.push(half, 3, 0, 0, 1, 0)
            self.arrived(half, 1, 0, 1)
            self.push(half, 1, 0, 0, -1, 1)

    def first_rest(self):
        for half in range(2):
            self.arrived(half, 3, 0, 1)
            self.arrived(half, 1, 0, 0)
            for df in (3, 1):
                self.push_all(half, df, 0, 1)
                self.to_sibling(half, df, 0)

    def first_far(self):
        for half in range(2):
            self.arrived(half, 2, 0, 0)
            self.arrived(half, 2, 0, 1)
            self.push_all(half, 2, 0, 1)
            self.to_sibling(half, 2, 0)

    def second_pass(self, df):
        for half in range(2):
            self.arrived(half, df, 3, 0)
            self.push(half, df, 3, 1, 1, 0)
            self.arrived(half, df, 1, 1)
            self.push(half, df, 1, 1, -1, 1)
        for half in range(2):
            self.arrived(half, df, 3, 1)
            self.to_sibling(half, df, 3)
            self.arrived(half, df, 1, 0)
            self.to_sibling(half, df, 1)

    def second_far(self, df):
        for half in range(2):
            for part in range(2):
                self.arrived(half, df, 2, part)
            self.to_sibling(half, df, 2)

    def land(self):
        for copy in self.core:
            copy.wait_recv()

    def close(self):
        for copy in self.done:
            copy.wait_send()


def extra_rows(qkv_bias, norm_params, q, rows):
    z, x = lax.axis_index("z"), lax.axis_index("x")
    yl, c, yh = lax.axis_index("yl"), lax.axis_index("c"), lax.axis_index("yh")
    mine = ((z * 4 + x) * 2 + yl) * 2 + c
    lane = lax.broadcasted_iota(jnp.int32, (1, EXTRA), 1)
    heads = qkv_bias.shape[2] // 2
    pieces = []
    for t in range(3):
        for pair in range(heads // 2):
            row = jnp.zeros((1, EXTRA), f32)
            for side in range(2):
                head = q * heads + 2 * pair + side
                value = qkv_bias[t, :, head : head + 1].astype(f32)
                row = row + jnp.where(lane == mine + side * HEAD_DIM, value, 0.0)
            pieces.append(row)
    share = norm_params.shape[1]
    high = norm_params[...].astype(bf16).astype(f32)
    norm = jnp.concatenate([high, norm_params[...] - high], 0)
    norm = jnp.concatenate([norm, jnp.zeros((norm.shape[0], EXTRA - share), f32)], 1)
    norm = pltpu.roll(norm, (mine % 4 * 2 + yh) * share, 1)
    used = len(pieces) + norm.shape[0]
    pieces += [norm, jnp.zeros((rows - used, EXTRA), f32)]
    return jnp.concatenate(pieces, 0).astype(bf16)


def forward_kernel(
    qkv_weight, out_weight, gate_up_weight, down_weight, qkv_bias, norm_params, tokens, cotangent,
    table,
    one_out, two, token_out, cot_out, qkv_out, mix_out, summed_out, unit_out, normed_out,
    stats, norm_table, scale,
    token_rows, cot_rows, qkv, head_mix, summed, unit, normed_two,
    one_q, two_q, one, norm_in, bias, normed, parts, mid, sent, far, near,
    pair_send, pair_recv, local_sem, save_sem, y_send, y_recv,
    send_one, recv_one, core_send_one, core_recv_one,
    send_two, recv_two, core_send_two, core_recv_two,
):
    z, x = lax.axis_index("z"), lax.axis_index("x")
    yl, c, yh = lax.axis_index("yl"), lax.axis_index("c"), lax.axis_index("yh")
    rows, here = one_q.shape[1], tokens.shape[0]
    hq, fq = qkv_weight.shape[2] // 2, gate_up_weight.shape[2] // 2
    pair_sems, y_sems = (pair_send, pair_recv), (y_send, y_recv)
    for q in range(2):
        for group in range(2):
            for t in range(3):
                to, start = (group * 3 + t) * hq // 2, q * hq + group * hq // 2
                one_q[q, :, to : to + hq // 2] = qkv_weight[t, :, start : start + hq // 2]
        one_q[q, :, 3 * hq : 3 * hq + EXTRA] = extra_rows(qkv_bias, norm_params, q, rows)
        one_q[q, :, 3 * hq + EXTRA :] = out_weight[:, q * hq : (q + 1) * hq]
    token_rows[pl.ds(0, here)] = tokens[...]
    greet([at_z(1), at_z(3), at_x(1), at_x(3)] + cube())

    same, cross = pair_moves()
    mine = pl.ds(pl.multiple_of((z * 4 + x) * 4 * rows + (yl * 2 + c) * rows, rows), rows)
    moves = [
        (one_q.at[c], one.at[mine], 0, same),
        (one_q.at[1 - c], one.at[mine], 1, cross),
        (two_q.at[c], two.at[mine], 2, same),
        (two_q.at[1 - c], two.at[mine], 3, cross),
    ]

    def launch(k):
        src, dst, index, device = moves[k]
        if device is same:
            stay_or_go(src, dst, pair_sems, index, device, local_sem.at[index // 2])
        else:
            remote(src, dst, pair_sems, index, device).start()

    def land(k):
        src, dst, index, device = moves[k]
        if device is same:
            stay_or_go_wait(src, dst, pair_sems, index, device, local_sem.at[index // 2])
        else:
            copy = remote(src, dst, pair_sems, index, device)
            copy.wait_recv()
            copy.wait_send()

    norm_moves = [
        remote(
            one_q.at[0, :, pl.ds(3 * hq, EXTRA)],
            norm_in.at[c],
            pair_sems,
            4 + which,
            {"yl": target["yl"], "c": target["c"], "yh": 1 - yh},
        )
        for which, target in enumerate((same, cross))
    ]
    launch(0)
    launch(1)
    for move in norm_moves:
        move.start()
    token_halves = [ring_gather_half(token_rows, top, y_sems, 0) for top in range(2)]
    for q in range(2):
        for t in range(2):
            two_q[q, :, t * fq : (t + 1) * fq] = gate_up_weight[t, :, q * fq : (q + 1) * fq]
        two_q[q, :, 2 * fq :] = down_weight[:, q * fq : (q + 1) * fq]
    sub = here // 2
    for k in range(2):
        cot_rows[pl.ds(4 * k * sub, sub)] = cotangent[pl.ds(k * sub, sub)]
    land(0)
    land(1)
    for move in norm_moves:
        move.wait_recv()
    own = (z * 4 + x) * 4 + 2 * c
    for core in range(2):
        block = pl.ds(pl.multiple_of((own + core) * rows, rows), rows)
        came = norm_in[core].astype(f32)
        place = lax.broadcasted_iota(jnp.int32, came.shape, 0)
        held = one[block, pl.ds(3 * hq, EXTRA)].astype(f32)
        one[block, pl.ds(3 * hq, EXTRA)] = (
            held + jnp.where((place >= 12) & (place < 20), came, 0.0)
        ).astype(bf16)
    first = Spread(one, rows, (send_one, recv_one), (core_send_one, core_recv_one))
    second = Spread(two, rows, (send_two, recv_two), (core_send_two, core_recv_two))
    first.start()
    launch(2)
    launch(3)
    first.first_pass()
    first.first_rest()
    token_passed = ring_gather_pass(token_rows, token_halves, y_sems, 0)
    first.second_pass(0)
    first.first_far()
    first.second_pass(3)
    first.second_pass(1)
    first.second_pass(2)
    for df in (0, 3, 1, 2):
        first.second_far(df)
    land(2)
    land(3)
    second.start()
    for copy in token_passed + [token_halves[1][0], token_halves[0][1]]:
        copy.wait_recv()
    cot_subs = [cot_rows.at[pl.ds(4 * k * sub, 4 * sub)] for k in range(2)]
    cot_halves = [
        [ring_gather_half(cot_subs[k], top, y_sems, 6 + 6 * k) for top in range(2)]
        for k in range(2)
    ]
    first.land()
    keep = pltpu.make_async_copy(one, one_out, local_sem.at[2])
    keep.start()
    saves = []

    def save(src, dst):
        saves.append(pltpu.make_async_copy(src, dst, save_sem.at[len(saves)]))
        saves[-1].start()

    save(token_rows, token_out)

    read_extras(one, 3 * hq, norm_table, bias)

    def norm_rows(k, _):
        rng = pl.ds(pl.multiple_of(k * here, here), here)
        values = token_rows[rng].astype(f32)
        mean = jnp.mean(values, -1, keepdims=True)
        centered = values - mean
        inverse = lax.rsqrt(jnp.mean(centered * centered, -1, keepdims=True) + EPSILON)
        stats[0, rng] = mean
        stats[1, rng] = inverse
        normed[rng] = (centered * inverse * norm_table[0:1] + norm_table[1:2]).astype(bf16)
        return 0

    lax.fori_loop(0, 4, norm_rows, 0)
    second.first_pass()
    wide = 256

    def project(k, _):
        cols = pl.ds(pl.multiple_of(k * wide, wide), wide)
        value = dot(normed[...], one[:, cols], 1, 0)
        row = k % 3 * (hq // 128) + k // 3 * 2
        value = value + jnp.concatenate([bias[pl.ds(row, 1)], bias[pl.ds(row + 1, 1)]], 1)

        @pl.when(k % 3 < 2)
        def _():
            for place in range(4):
                rng = pl.ds(place * here, here)
                turn = table[pl.ds(pl.multiple_of(half_of_place(place) * here, here), here)]
                for pair in range(wide // 128):
                    qkv[rng, pl.ds(pl.multiple_of(k * wide + pair * 128, 128), 128)] = turn_heads(
                        value[place * here : (place + 1) * here, pair * 128 : (pair + 1) * 128],
                        turn,
                        1.0,
                    ).astype(bf16)

        @pl.when(k % 3 == 2)
        def _():
            qkv[:, cols] = value.astype(bf16)

        return 0

    lax.fori_loop(0, 3 * hq // wide, project, 0)
    save(qkv, qkv_out)
    second.first_rest()
    cot_passed = [
        ring_gather_pass(cot_subs[k], cot_halves[k], y_sems, 6 + 6 * k) for k in range(2)
    ]
    for sequence in range(2):
        mask = causal_mask(sequence, here)
        rng = pl.ds(sequence * 2 * here, 2 * here)

        def heads(k, _):
            def pair(t):
                start = k // 2 * (3 * hq // 2) + t * (hq // 2) + k % 2 * 128
                return qkv[rng, pl.ds(pl.multiple_of(start, 128), 128)]

            q, key, value = pair(0), pair(1), pair(2)
            mixes = []
            for head in range(2):
                cut = slice(head * HEAD_DIM, (head + 1) * HEAD_DIM)
                soft = soft_of(q[:, cut], key[:, cut], mask).astype(bf16)
                mixes.append(dot(soft, value[:, cut], 1, 0))
            head_mix[rng, pl.ds(pl.multiple_of(k * 128, 128), 128)] = jnp.concatenate(
                mixes, 1
            ).astype(bf16)
            return 0

        lax.fori_loop(0, hq // 128, heads, 0, unroll=2)
        if sequence == 0:
            second.second_pass(0)
    second.first_far()

    save(head_mix, mix_out)
    for k in range(2):
        for copy in cot_passed[k] + [cot_halves[k][1][0], cot_halves[k][0][1]]:
            copy.wait_recv()
    save(cot_rows, cot_out)
    part_subs = [parts.at[pl.ds(4 * k * sub, 4 * sub)] for k in range(2)]
    started, middle = [], []
    for part in range(2):
        mix = jnp.concatenate(
            [head_mix[pl.ds(k * here + part * sub, sub)] for k in range(4)], 0
        )

        def out_project(k, _):
            rng = pl.ds(pl.multiple_of(k * wide, wide), wide)
            parts[pl.ds(4 * part * sub, 4 * sub), rng] = dot(
                mix, one[rng, pl.ds(3 * hq + EXTRA, hq)], 1, 1
            ).astype(bf16)
            return 0

        lax.fori_loop(0, one.shape[0] // wide, out_project, 0)
        started.append(
            ring_sum_start(part_subs[part], mid.at[part], near.at[part], y_sems, 18 + 6 * part)
        )
    second.second_pass(3)
    for part in range(2):
        middle.append(
            ring_sum_middle(
                part_subs[part], started[part], mid.at[part], sent.at[part], far.at[part],
                y_sems, 18 + 6 * part,
            )
        )
    second.second_pass(1)
    halves = []
    for part in range(2):
        finish = ring_sum_finish(
            part_subs[part], started[part], middle[part], far.at[part], near.at[part]
        )
        total = jnp.concatenate([finish(0), finish(1)], 0)
        rng = pl.ds(part * sub, sub)
        total = total + tokens[rng].astype(f32)
        summed[rng] = total
        centered = total - jnp.mean(total, -1, keepdims=True)
        inverse = lax.rsqrt(jnp.mean(centered * centered, -1, keepdims=True) + EPSILON)
        unit_rows = centered * inverse
        unit[rng] = unit_rows
        scale[rng] = inverse
        normed_two[pl.ds(4 * part * sub, sub)] = (
            unit_rows * norm_table[2:3] + norm_table[3:4]
        ).astype(bf16)
        out = normed_two.at[pl.ds(4 * part * sub, 4 * sub)]
        halves.append([ring_gather_half(out, top, y_sems, 30 + 6 * part) for top in range(2)])
    save(summed, summed_out)
    save(unit, unit_out)
    second.second_pass(2)
    passed = [
        ring_gather_pass(
            normed_two.at[pl.ds(4 * k * sub, 4 * sub)], halves[k], y_sems, 30 + 6 * k
        )
        for k in range(2)
    ]
    for df in (0, 3, 1, 2):
        second.second_far(df)
    for k in range(2):
        for copy in passed[k] + [halves[k][1][0], halves[k][0][1]]:
            copy.wait_recv()
        these = pl.ds(4 * k * sub, 4 * sub)
        save(normed_two.at[these], normed_out.at[these])
    second.land()
    keep.wait()
    for copy in saves:
        copy.wait()
    for move in norm_moves:
        move.wait_send()
    gathers = token_halves + cot_halves[0] + cot_halves[1] + halves[0] + halves[1]
    for copies in gathers + [token_passed] + cot_passed + started + middle + passed:
        for copy in copies:
            copy.wait_send()
    first.close()
    second.close()


def forward(
    qkv_weight, out_weight, gate_up_weight, down_weight, qkv_bias, norm_params, tokens, cotangent,
    table,
):
    here, width = tokens.shape
    rows = qkv_weight.shape[1]
    hq, fq = qkv_weight.shape[2] // 2, gate_up_weight.shape[2] // 2
    full = pl.BlockSpec(memory_space=VMEM)
    anywhere = pl.BlockSpec(memory_space=pl.ANY)
    one_wide, two_wide = 4 * hq + EXTRA, 3 * fq
    kept = (
        ((4 * here, width), bf16),
        ((4 * here, width), bf16),
        ((4 * here, 3 * hq), bf16),
        ((4 * here, hq), bf16),
        ((here, width), f32),
        ((here, width), f32),
        ((4 * here, width), bf16),
    )

    def shape(*dims, dtype=bf16):
        return jax.ShapeDtypeStruct(dims, dtype)

    return pl.pallas_call(
        forward_kernel,
        out_shape=(
            shape(width, one_wide),
            shape(width, two_wide),
            *(shape(*dims, dtype=dtype) for dims, dtype in kept),
            shape(2, 4 * here, 1, dtype=f32),
            shape(4, width, dtype=f32),
            shape(here, 1, dtype=f32),
        ),
        in_specs=[full] * 9,
        out_specs=(anywhere,) * 9 + (full,) * 3,
        scratch_shapes=[VMEM(dims, dtype) for dims, dtype in kept]
        + [
            VMEM((2, rows, one_wide), bf16),
            VMEM((2, rows, two_wide), bf16),
            VMEM((width, one_wide), bf16),
            VMEM((2, rows, EXTRA), bf16),
            VMEM((12, 128), f32),
            VMEM((4 * here, width), bf16),
            VMEM((4 * here, width), bf16),
        ]
        + [VMEM((2, 2, here // 4, width), bf16)] * 4
        + [
            DMA((6,)), DMA((6,)), DMA((3,)), DMA((9,)), DMA((42,)), DMA((42,)),
            DMA((64,)), DMA((64,)), DMA((32,)), DMA((32,)),
            DMA((64,)), DMA((64,)), DMA((32,)), DMA((32,)),
        ],
        compiler_params=pltpu.CompilerParams(
            collective_id=0, has_side_effects=True, vmem_limit_bytes=VMEM_LIMIT
        ),
    )(
        qkv_weight, out_weight, gate_up_weight, down_weight, qkv_bias, norm_params, tokens,
        cotangent, table,
    )


def backward_kernel(
    one, resid_rows, chip, settled, qkv_in, mix_in, token_in, mixed_in, resid_in, sum_in,
    stats, table, second_terms, norm_table,
    result_one, result_two, norm_back, grad_out, mixed_out,
    qkv, head_mix, token_rows, mixed_parts, resid, first_sum, grad_tokens, mixed,
    held, spare, grad_mix, grad_proj, part_sums, sib, blocks, pair_sums,
    *rest,
):
    rings = [rest[5 * k : 5 * k + 5] for k in range(9)]
    rings = [(mid, far, near, (send, recv)) for mid, far, near, send, recv in rings]
    (
        packed_one, packed_two, ymid, ysent, yfar, ynear,
        load_sem, in_sem, save_sem, block_sem, core_send, core_recv, pair_send, pair_recv, local_sem, y_send, y_recv,
    ) = rest[45:]
    z, x = lax.axis_index("z"), lax.axis_index("x")
    yl, c, yh = lax.axis_index("yl"), lax.axis_index("c"), lax.axis_index("yh")
    here = resid.shape[0]
    rows = result_one.shape[1]
    hq, fq = head_mix.shape[1], result_two.shape[2] // 3
    early, late = pair_sums.shape[3], blocks.shape[3]
    sub = here // 2
    width = held.shape[0]
    core_sems, pair_sems, y_sems = (core_send, core_recv), (pair_send, pair_recv), (y_send, y_recv)
    wide = 256
    out_start = 3 * hq + EXTRA
    group = 3 * hq // 2
    columns = (pl.ds(0, group), pl.ds(out_start, hq), pl.ds(group, group + EXTRA))

    def place_of(dz, dx):
        return ((z + dz) % 4) * 4 + (x + dx) % 4

    loads = [
        pltpu.make_async_copy(
            one.at[:, pl.ds(start, size)], held.at[:, pl.ds(start, size)], load_sem.at[k]
        )
        for k, (start, size) in enumerate(((out_start, hq), (0, 3 * hq)))
    ]
    loads.append(pltpu.make_async_copy(resid_rows, spare, load_sem.at[2]))
    loads.append(pltpu.make_async_copy(settled, pair_sums, load_sem.at[3]))
    block_loads = [
        pltpu.make_async_copy(
            chip.at[place_of(dz, dx)], blocks.at[dz, dx], block_sem.at[dz * 4 + dx]
        )
        for dz in range(4)
        for dx in range(4)
    ]
    ins = [
        pltpu.make_async_copy(src, dst, in_sem.at[k])
        for k, (src, dst) in enumerate(
            (
                (mixed_in, mixed_parts), (mix_in, head_mix), (qkv_in, qkv),
                (token_in, token_rows), (resid_in, resid), (sum_in, first_sum),
            )
        )
    ]
    loads[3].start()
    ins[0].start()
    loads[2].start()
    loads[0].start()
    ins[1].start()
    for load in block_loads:
        load.start()
    greet([at_z(1), at_z(3), at_x(1), at_x(3)] + cube())
    ins[0].wait()
    mixed_started = ring_sum_start(mixed_parts, ymid.at[0], ynear.at[0], y_sems, 0)

    def cut(half, part):
        return pl.ds(half * rows + part * (rows // 2), rows // 2)

    def pair_view(stage, half, d, part):
        along = x if half == 0 else z
        return pair_sums.at[half, (along + d) % 4, pl.ds(part * (rows // 2), rows // 2)]

    def view_of(ref, cols):
        def view(stage, half, d, part):
            if stage == 0:
                there = (d, slice(None)) if half == 0 else (slice(None), d)
            else:
                there = (0, d) if half == 0 else (d, 0)
            return ref.at[(*there, cut(half, part), cols)]

        return view

    early_sums = Reduce(pair_view, rows, {1: rings[0]})
    late_sums = Reduce(view_of(blocks, pl.ds(0, late)), rows, {0: rings[1], 1: rings[2]})
    out_proj = Reduce(view_of(sib, columns[1]), rows, {0: rings[3], 1: rings[4]})
    head_sums = [
        Reduce(view_of(sib, columns[0]), rows, {0: rings[5], 1: rings[6]}),
        Reduce(view_of(sib, columns[2]), rows, {0: rings[7], 1: rings[8]}),
    ]
    loads[3].wait()
    early_sums.begin(1)
    for load in block_loads:
        load.wait()
    late_sums.begin(0)

    def to_core(block, which):
        theirs = pl.ds(pl.multiple_of((2 * block + 1 - c) * 2 * rows, 2 * rows), 2 * rows)
        dz, dx = (block // 4 - z + 4) % 4, (block % 4 - x + 4) % 4
        return remote(
            held.at[theirs, columns[which]],
            sib.at[dz, dx, :, columns[which]],
            core_sems,
            block + 16 * which,
            sibling(),
        )

    def core_sum(block, which):
        to_core(block, which).wait_recv()
        ours = pl.ds(pl.multiple_of((2 * block + c) * 2 * rows, 2 * rows), 2 * rows)
        there = ((block // 4 - z + 4) % 4, (block % 4 - x + 4) % 4, slice(None), columns[which])
        sib[there] = (sib[there].astype(f32) + held[ours, columns[which]].astype(f32)).astype(
            bf16
        )

    loads[2].wait()
    loads[0].wait()
    ins[1].wait()

    mix_order = jnp.concatenate(
        [
            head_mix[pl.ds(block * here + part * sub, sub)]
            for part in range(2)
            for block in range(4)
        ],
        0,
    )

    def mix_back(k, _):
        cols = pl.ds(pl.multiple_of(k * wide, wide), wide)
        value = dot(
            spare[...], held[:, pl.ds(pl.multiple_of(out_start + k * wide, 128), wide)], 1, 0
        ).astype(bf16)
        for part in range(2):
            for block in range(4):
                start = (part * 4 + block) * sub
                grad_mix[pl.ds(block * here + part * sub, sub), cols] = value[start : start + sub]
        return 0

    ins[2].start()
    loads[1].start()
    lax.fori_loop(0, hq // wide, mix_back, 0)
    for load in ins[3:]:
        load.start()

    def out_back(k, _):
        rng = pl.ds(pl.multiple_of(k * 2 * wide, 2 * wide), 2 * wide)
        held[rng, columns[1]] = dot(spare[:, rng], mix_order, 0, 0).astype(bf16)
        for block in range(4):
            to_core(4 * k + block, 1).start()
        return 0

    lax.fori_loop(0, width // (2 * wide), out_back, 0)
    early_sums.combine(1)
    mixed_middle = ring_sum_middle(
        mixed_parts, mixed_started, ymid.at[0], ysent.at[0], yfar.at[0], y_sems, 0
    )

    def out_sum(block, _):
        core_sum(block, 1)
        return 0

    lax.fori_loop(0, 16, out_sum, 0)
    out_proj.begin(0)
    masks = [causal_mask(sequence, here) for sequence in range(2)]
    turns = [
        jnp.concatenate(
            [
                table[pl.ds(pl.multiple_of(half_of_place(2 * sequence + k) * here, here), here)]
                for k in range(2)
            ],
            0,
        )
        for sequence in range(2)
    ]

    def heads_back(half, sequence):
        mask, turn = masks[sequence], turns[sequence]
        rng = pl.ds(sequence * 2 * here, 2 * here)
        for k in range(hq // 256):

            def pair(t):
                return pl.ds(half * group + t * (hq // 2) + k * 128, 128)

            q, key, value = qkv[rng, pair(0)], qkv[rng, pair(1)], qkv[rng, pair(2)]
            mix = grad_mix[rng, pl.ds(half * (hq // 2) + k * 128, 128)]
            results = ([], [], [])
            for head in range(2):
                lanes = slice(head * HEAD_DIM, (head + 1) * HEAD_DIM)
                soft = soft_of(q[:, lanes], key[:, lanes], mask)
                grad_soft = dot(mix[:, lanes], value[:, lanes], 1, 1)
                row_dot = jnp.sum(grad_soft * soft, -1, keepdims=True)
                grad_score = (soft * (grad_soft - row_dot)).astype(bf16)
                results[0].append(dot(grad_score, key[:, lanes], 1, 0) * SCALE)
                results[1].append(dot(grad_score, q[:, lanes], 0, 0) * SCALE)
                results[2].append(dot(soft.astype(bf16), mix[:, lanes], 0, 0))
            for t in range(3):
                both = jnp.concatenate(results[t], 1)
                if t < 2:
                    both = turn_heads(both, turn, -1.0)
                grad_proj[rng, pair(t)] = both.astype(bf16)

    def bias_sum(t, k):
        start = k // 2 * group + t * (hq // 2) + k % 2 * 128
        return jnp.sum(grad_proj[:, pl.ds(start, 128)].astype(f32), 0, keepdims=True)

    mean, inverse = stats[0], stats[1]
    tall = 512

    def weights_back(half, k, bias_rows):
        rng = pl.ds(pl.multiple_of(k * tall, tall), tall)
        these = pl.ds(half * group, group)
        part = dot(grad_proj[:, these], held[rng, these], 1, 1)
        unit = (token_rows[:, rng].astype(f32) - mean) * inverse
        normed = (unit * norm_table[0:1, rng] + norm_table[1:2, rng]).astype(bf16)
        held[rng, these] = dot(normed, grad_proj[:, these], 0, 0).astype(bf16)
        if half == 0:
            part_sums[:, rng] = part
        else:
            part = part + part_sums[:, rng]
            spare[:, rng] = part.astype(bf16)
            gain = jnp.sum(part * unit, 0, keepdims=True)
            shift = jnp.sum(part, 0, keepdims=True)
            for tile in range(tall // 128):
                inner = slice(tile * 128, (tile + 1) * 128)
                lanes = pl.ds(pl.multiple_of(k * tall + tile * 128, 128), 128)
                extra = jnp.concatenate(
                    bias_rows
                    + [
                        gain[:, inner],
                        shift[:, inner],
                        second_terms[:, lanes],
                        jnp.zeros((rows - 16, 128), f32),
                    ],
                    0,
                ).astype(bf16)
                for copy in range(128 // rows):
                    start = pl.multiple_of(k * tall + tile * 128 + copy * rows, rows)
                    held[pl.ds(start, rows), pl.ds(3 * hq, EXTRA)] = extra
        for block in range(4):
            to_core(4 * k + block, 2 * half).start()

        @pl.when(k > 0)
        def _():
            for block in range(4):
                core_sum(4 * k - 4 + block, 2 * half)

        return 0

    ins[2].wait()
    for sequence in range(2):
        heads_back(0, sequence)
    late_sums.combine(0)
    loads[1].wait()
    for load in ins[3:]:
        load.wait()
    lax.fori_loop(0, width // tall, lambda k, _: weights_back(0, k, None), 0)
    for block in range(12, 16):
        core_sum(block, 0)
    head_sums[0].begin(0)
    early_sums.settle(1, packed_two.at[:, :, pl.ds(0, early)])
    heads_back(1, 0)
    out_proj.combine(0)
    late_sums.settle(0)
    late_sums.begin(1)
    heads_back(1, 1)
    head_sums[0].combine(0)
    bias_rows = [bias_sum(t, k) for t in range(3) for k in range(hq // 128)]
    lax.fori_loop(0, 2, lambda k, _: weights_back(1, k, bias_rows), 0)
    out_proj.settle(0)
    out_proj.begin(1)
    late_sums.combine(1)
    lax.fori_loop(2, 4, lambda k, _: weights_back(1, k, bias_rows), 0)
    first_started = ring_sum_start(spare, ymid.at[1], ynear.at[1], y_sems, 6)
    for block in range(12, 16):
        core_sum(block, 2)
    head_sums[1].begin(0)
    head_sums[0].settle(0)
    head_sums[0].begin(1)
    late_sums.settle(1, packed_two.at[:, :, pl.ds(early, late)])
    home, away = {"yl": c, "c": yl}, {"yl": c, "c": 1 - yl}
    stay_or_go(packed_two.at[yl], result_two.at[yl], pair_sems, 0, home, local_sem.at[0])
    cross_two = remote(packed_two.at[1 - yl], result_two.at[yl], pair_sems, 1, away)
    cross_two.start()
    out_proj.combine(1)
    head_sums[1].combine(0)
    first_middle = ring_sum_middle(
        spare, first_started, ymid.at[1], ysent.at[1], yfar.at[1], y_sems, 6
    )
    head_sums[0].combine(1)
    half_here = here // 2
    finish = ring_sum_finish(mixed_parts, mixed_started, mixed_middle, yfar.at[0], ynear.at[0])
    for top in range(2):
        rng = pl.ds(top * half_here, half_here)
        mixed[rng] = (first_sum[rng] + finish(top)).astype(bf16)
    saves = [pltpu.make_async_copy(mixed, mixed_out, save_sem.at[0])]
    saves[0].start()
    out_proj.settle(1, packed_one.at[:, :, columns[1]])
    head_sums[1].settle(0)
    head_sums[1].begin(1)
    head_sums[0].settle(1, packed_one.at[:, :, columns[0]])
    head_sums[1].combine(1)
    head_sums[1].settle(1, packed_one.at[:, :, columns[2]])

    stay_or_go(packed_one.at[yl], result_one.at[yl], pair_sems, 2, home, local_sem.at[1])
    cross_one = remote(packed_one.at[1 - yl], result_one.at[yl], pair_sems, 3, away)
    cross_one.start()
    extras = pl.ds(3 * hq, EXTRA)
    norm_moves = [
        remote(
            packed_one.at[core, :, extras],
            norm_back.at[yl],
            pair_sems,
            4 + which,
            {"yl": c, "c": core, "yh": 1 - yh},
        )
        for which, core in enumerate((yl, 1 - yl))
    ]
    for move in norm_moves:
        move.start()
    finish = ring_sum_finish(spare, first_started, first_middle, yfar.at[1], ynear.at[1])
    for top in range(2):
        rng = pl.ds(top * half_here, half_here)
        incoming = finish(top) * norm_table[0:1]
        unit_rows = (token_rows[rng].astype(f32) - stats[0, rng]) * stats[1, rng]
        grad_tokens[rng] = resid[rng] + stats[1, rng] * (
            incoming
            - jnp.mean(incoming, -1, keepdims=True)
            - unit_rows * jnp.mean(incoming * unit_rows, -1, keepdims=True)
        )
    saves.append(pltpu.make_async_copy(grad_tokens, grad_out, save_sem.at[1]))
    saves[1].start()
    for copy in [cross_two, cross_one] + norm_moves:
        copy.wait_recv()
        copy.wait_send()
    stay_or_go_wait(packed_two.at[yl], result_two.at[yl], pair_sems, 0, home, local_sem.at[0])
    stay_or_go_wait(packed_one.at[yl], result_one.at[yl], pair_sems, 2, home, local_sem.at[1])
    for copy in saves:
        copy.wait()
    for copy in mixed_started + mixed_middle + first_started + first_middle:
        copy.wait_send()

    def drain(block, _):
        for which in range(3):
            to_core(block, which).wait_send()
        return 0

    lax.fori_loop(0, 16, drain, 0)
    for sums in [early_sums, late_sums, out_proj] + head_sums:
        sums.close()


def backward(
    one, resid_rows, chip, settled, qkv, head_mix, token_rows, mixed_parts, resid, first_sum,
    stats, table, second_terms, norm_table,
):
    here, width = resid.shape
    hq, early, late = head_mix.shape[1], settled.shape[3], chip.shape[2]
    fq = (early + late) // 3
    rows = width // 64
    piece = rows // 2
    one_wide = one.shape[1]
    full = pl.BlockSpec(memory_space=VMEM)
    anywhere = pl.BlockSpec(memory_space=pl.ANY)
    rings = ring_buffers(1, piece, early)
    for wide in (late, hq, 3 * hq // 2, 3 * hq // 2 + EXTRA):
        rings += ring_buffers(0, piece, wide) + ring_buffers(1, piece, wide)
    return pl.pallas_call(
        backward_kernel,
        out_shape=(
            jax.ShapeDtypeStruct((2, rows, one_wide), bf16),
            jax.ShapeDtypeStruct((2, rows, 3 * fq), bf16),
            jax.ShapeDtypeStruct((2, rows, EXTRA), bf16),
            jax.ShapeDtypeStruct((here, width), f32),
            jax.ShapeDtypeStruct((here, width), bf16),
        ),
        in_specs=[anywhere] * 10 + [full] * 4,
        out_specs=(anywhere,) * 5,
        scratch_shapes=[
            VMEM(qkv.shape, bf16),
            VMEM(head_mix.shape, bf16),
            VMEM(token_rows.shape, bf16),
            VMEM(mixed_parts.shape, bf16),
            VMEM((here, width), f32),
            VMEM((here, width), f32),
            VMEM((here, width), f32),
            VMEM((here, width), bf16),
            VMEM((width, one_wide), bf16),
            VMEM((4 * here, width), bf16),
            VMEM((4 * here, hq), bf16),
            VMEM((4 * here, 3 * hq), bf16),
            VMEM((4 * here, width), f32),
            VMEM((4, 4, 2 * rows, one_wide), bf16),
            VMEM((4, 4, 2 * rows, late), bf16),
            VMEM((2, 4, rows, early), bf16),
        ]
        + rings
        + [VMEM((2, rows, one_wide), bf16), VMEM((2, rows, 3 * fq), bf16)]
        + [VMEM((2, 2, here // 2, width), bf16)] * 4
        + [DMA((4,)), DMA((6,)), DMA((2,)), DMA((16,)), DMA((48,)), DMA((48,))]
        + [DMA((6,)), DMA((6,)), DMA((2,)), DMA((12,)), DMA((12,))],
        compiler_params=pltpu.CompilerParams(
            collective_id=3, has_side_effects=True, vmem_limit_bytes=VMEM_LIMIT
        ),
    )(
        one, resid_rows, chip, settled, qkv, head_mix, token_rows, mixed_parts, resid, first_sum,
        stats, table, second_terms, norm_table,
    )


def finish_kernel(
    one, two, norm_back, tokens_in, mixed_in,
    mixed, grad_tokens, out_norm, out_qkv, out_bias, out_out, out_gate_up, out_down,
):
    z, x = lax.axis_index("z"), lax.axis_index("x")
    yl, c, yh = lax.axis_index("yl"), lax.axis_index("c"), lax.axis_index("yh")
    mine = ((z * 4 + x) * 2 + yl) * 2 + c
    hq, fq = out_out.shape[1] // 2, out_down.shape[1] // 2
    mixed[...] = mixed_in[...]
    grad_tokens[...] = tokens_in[...]
    for q in range(2):
        for group in range(2):
            for t in range(3):
                start, to = (group * 3 + t) * hq // 2, q * hq + group * hq // 2
                out_qkv[t, :, to : to + hq // 2] = one[q, :, start : start + hq // 2].astype(f32)
        out_out[:, q * hq : (q + 1) * hq] = one[q, :, 3 * hq + EXTRA :].astype(f32)
        for t in range(2):
            out_gate_up[t, :, q * fq : (q + 1) * fq] = two[q, :, t * fq : (t + 1) * fq].astype(f32)
        out_down[:, q * fq : (q + 1) * fq] = two[q, :, 2 * fq :].astype(f32)
    extras = [one[q, :, 3 * hq : 3 * hq + EXTRA].astype(f32) for q in range(2)]
    heads = hq // HEAD_DIM
    pairs = 3 * heads // 2
    share = out_norm.shape[1]
    sums = extras[0] + extras[1] + (norm_back[0].astype(f32) + norm_back[1].astype(f32))
    sums = pltpu.roll(sums, EXTRA - (mine % 4 * 2 + yh) * share, 1)
    out_norm[...] = sums[pairs : pairs + 4, :share]
    lane = lax.broadcasted_iota(jnp.int32, extras[0].shape, 1)
    place = lax.broadcasted_iota(jnp.int32, (1, 2 * heads), 1)
    totals = [jnp.zeros((1, 2 * heads), f32) for _ in range(3)]
    for q in range(2):
        for side in range(2):
            value = jnp.sum(
                jnp.where(lane == mine + side * HEAD_DIM, extras[q], 0.0), 1, keepdims=True
            )
            for t in range(3):
                for pair in range(heads // 2):
                    row = t * (heads // 2) + pair
                    head = q * heads + 2 * pair + side
                    totals[t] = totals[t] + jnp.where(place == head, value[row : row + 1], 0.0)
    for t in range(3):
        out_bias[t] = totals[t]


def finish(one, two, norm_back, grad_tokens, mixed, share):
    rows = one.shape[1]
    hq, fq = (one.shape[2] - EXTRA) // 4, two.shape[2] // 3
    full = pl.BlockSpec(memory_space=VMEM)
    return pl.pallas_call(
        finish_kernel,
        out_shape=(
            jax.ShapeDtypeStruct(mixed.shape, bf16),
            jax.ShapeDtypeStruct(grad_tokens.shape, f32),
            jax.ShapeDtypeStruct((4, share), f32),
            jax.ShapeDtypeStruct((3, rows, 2 * hq), f32),
            jax.ShapeDtypeStruct((3, 1, 2 * hq // HEAD_DIM), f32),
            jax.ShapeDtypeStruct((rows, 2 * hq), f32),
            jax.ShapeDtypeStruct((2, rows, 2 * fq), f32),
            jax.ShapeDtypeStruct((rows, 2 * fq), f32),
        ),
        in_specs=[full] * 5,
        out_specs=(full,) * 8,
        compiler_params=pltpu.CompilerParams(vmem_limit_bytes=VMEM_LIMIT),
    )(one, two, norm_back, grad_tokens, mixed)


def shards(
    tokens, cotangent, norm_params, qkv_weight, qkv_bias, out_weight, gate_up_weight, down_weight
):
    table = jnp.asarray(tables())
    (
        one, second, token_rows, cot_rows, qkv, head_mix, first_sum, unit_two, normed_two,
        stats, norm_table, scale_two,
    ) = forward(
        qkv_weight, out_weight.T, gate_up_weight, down_weight.T, qkv_bias.transpose(0, 2, 1),
        norm_params, tokens, cotangent, table,
    )
    grad_resid, resid_rows, mixed_parts, chip, settled, second_terms = feed_forward(
        normed_two, cot_rows, cotangent, unit_two, scale_two, norm_table, second
    )
    one_back, two_back, norm_back, grad_tokens, mixed = backward(
        one, resid_rows, chip, settled, qkv, head_mix, token_rows, mixed_parts, grad_resid,
        first_sum, stats, table, second_terms, norm_table,
    )
    mixed, grad_tokens, out_norm, out_qkv, out_bias, out_out, out_gate_up, out_down = finish(
        one_back, two_back, norm_back, grad_tokens, mixed, norm_params.shape[1]
    )
    return (
        mixed, grad_tokens, out_norm, out_qkv, out_bias.transpose(0, 2, 1), out_out.T,
        out_gate_up, out_down.T,
    )


def solution(mesh):
    grid = Mesh(mesh.devices.reshape(4, 4, 2, 2, 2), GRID)
    placed = (
        P(GRID, None),
        P(GRID, None),
        P(None, GRID),
        P(None, ROWS, "yh"),
        P(None, "yh", ROWS),
        P("yh", ROWS),
        P(None, ROWS, "yh"),
        P("yh", ROWS),
    )
    return jax.shard_map(
        shards,
        mesh=grid,
        in_specs=placed,
        out_specs=(
            P(GRID, None),
            P(GRID, None),
            P(None, GRID),
            P(None, ROWS, "yh"),
            P(None, "yh", ROWS),
            P("yh", ROWS),
            P(None, ROWS, "yh"),
            P("yh", ROWS),
        ),
        check_vma=False,
    )
```

```python
import jax
import jax.numpy as jnp
import numpy as np
from jax import lax
from jax.experimental import pallas as pl
from jax.experimental.pallas import tpu as pltpu
from jax.sharding import Mesh
from jax.sharding import PartitionSpec as P

HEAD_DIM = 64
ROTARY = 16
EPSILON = 1e-05
SCALE = 0.125

GRID = ("z", "x", "yl", "c", "yh")
ROWS = ("z", "x", "yl", "c")
EXTRA = 128

bf16 = jnp.bfloat16
f32 = jnp.float32

MESH = pl.DeviceIdType.MESH
VMEM = pltpu.VMEM
DMA = pltpu.SemaphoreType.DMA
VMEM_LIMIT = 60 * 1024 * 1024


def at_y(k):
    y = (lax.axis_index("yh") * 2 + lax.axis_index("yl") + k) % 4
    return {"yl": y % 2, "yh": y // 2}


def at_z(k):
    return {"z": (lax.axis_index("z") + k) % 4}


def at_x(k):
    return {"x": (lax.axis_index("x") + k) % 4}


def sibling():
    return {"c": 1 - lax.axis_index("c")}


def greet(devices):
    barrier = pltpu.get_barrier_semaphore()
    for device in devices:
        pl.semaphore_signal(barrier, inc=1, device_id=device, device_id_type=MESH)
    pl.semaphore_wait(barrier, len(devices))


def remote(src, dst, sems, index, device):
    send, recv = sems
    return pltpu.make_async_remote_copy(
        src_ref=src,
        dst_ref=dst,
        send_sem=send.at[index],
        recv_sem=recv.at[index],
        device_id=device,
        device_id_type=MESH,
    )


def ring_gather_half(out, top, sems, base):
    here = out.shape[0] // 4
    half = here // 2
    copies = []
    for way, step, block in ((0, 1, 3), (1, -1, 2)):
        copies.append(
            remote(
                out.at[pl.ds(top * half, half)],
                out.at[pl.ds(block * here + top * half, half)],
                sems,
                base + 2 * way + top,
                at_y(step),
            )
        )
        copies[-1].start()
    return copies


def ring_gather_pass(out, halves, sems, base):
    here = out.shape[0] // 4
    half = here // 2
    passed = []
    for way, step, block in ((0, 1, 3), (1, -1, 2)):
        halves[way][way].wait_recv()
        passed.append(
            remote(
                out.at[pl.ds(block * here + way * half, half)],
                out.at[pl.ds(here + way * half, half)],
                sems,
                base + 4 + way,
                at_y(step),
            )
        )
        passed[-1].start()
    return passed


def pair_moves():
    yl, c = lax.axis_index("yl"), lax.axis_index("c")
    return {"yl": c, "c": yl}, {"yl": 1 - c, "c": yl}


def stay_or_go(src, dst, sems, index, device, local_sem):
    yl, c = lax.axis_index("yl"), lax.axis_index("c")

    @pl.when(yl == c)
    def _():
        pltpu.make_async_copy(src, dst, local_sem).start()

    @pl.when(yl != c)
    def _():
        remote(src, dst, sems, index, device).start()


def stay_or_go_wait(src, dst, sems, index, device, local_sem):
    yl, c = lax.axis_index("yl"), lax.axis_index("c")

    @pl.when(yl == c)
    def _():
        pltpu.make_async_copy(src, dst, local_sem).wait()

    @pl.when(yl != c)
    def _():
        copy = remote(src, dst, sems, index, device)
        copy.wait_recv()
        copy.wait_send()


def ring_sum_start(parts, mid, near, sems, base):
    here = parts.shape[0] // 4
    half = here // 2
    copies = []
    for way, step in ((0, 1), (1, -1)):
        copies.append(
            remote(
                parts.at[pl.ds(here + way * half, half)], mid.at[way], sems, base + way, at_y(step)
            )
        )
    for way, step, block in ((0, 1, 2), (1, -1, 3)):
        copies.append(
            remote(
                parts.at[pl.ds(block * here + (1 - way) * half, half)],
                near.at[way],
                sems,
                base + 2 + way,
                at_y(step),
            )
        )
    for copy in copies:
        copy.start()
    return copies


def ring_sum_middle(parts, started, mid, sent, far, sems, base):
    here = parts.shape[0] // 4
    half = here // 2
    copies = []
    for way, step, block in ((0, 1, 2), (1, -1, 3)):
        started[way].wait_recv()
        sent[way] = (
            parts[pl.ds(block * here + way * half, half)].astype(f32) + mid[way].astype(f32)
        ).astype(bf16)
        copies.append(remote(sent.at[way], far.at[way], sems, base + 4 + way, at_y(step)))
        copies[-1].start()
    return copies


def ring_sum_finish(parts, started, middle, far, near):
    half = parts.shape[0] // 8

    def finish(top):
        started[2 + 1 - top].wait_recv()
        middle[top].wait_recv()
        return (
            parts[pl.ds(top * half, half)].astype(f32)
            + far[top].astype(f32)
            + near[1 - top].astype(f32)
        )

    return finish


def tables():
    half = ROTARY // 2
    position = np.arange(256, dtype=np.float32)
    frequency = np.power(np.float32(10000.0), -np.arange(half, dtype=np.float32) * np.float32(2.0 / ROTARY))
    angles = position[:, None] * frequency[None, :].astype(np.float32)
    cosine, sine = np.cos(angles), np.sin(angles)
    own = np.ones((256, 2, HEAD_DIM), np.float32)
    up = np.zeros((256, 2, HEAD_DIM), np.float32)
    down = np.zeros((256, 2, HEAD_DIM), np.float32)
    for head in range(2):
        own[:, head, :half] = cosine
        own[:, head, half:ROTARY] = cosine
        up[:, head, :half] = -sine
        down[:, head, half:ROTARY] = sine
    return np.concatenate([a.reshape(256, 128) for a in (own, up, down)], 1)


def dot(a, b, ca, cb):
    return lax.dot_general(a, b, (((ca,), (cb,)), ((), ())), preferred_element_type=f32)


def turn_heads(value, table, sign):
    own, up, down = table[:, :128], table[:, 128:256], table[:, 256:]
    return value * own + sign * (
        pltpu.roll(value, 120, 1) * up + pltpu.roll(value, 8, 1) * down
    )


def half_of_place(place):
    y = lax.axis_index("yh") * 2 + lax.axis_index("yl")
    return ((y + (0, 2, 1, 3)[place]) % 4) // 2


def causal_mask(sequence, here):
    length = 2 * here
    first = half_of_place(2 * sequence)

    def position(dim):
        index = lax.broadcasted_iota(jnp.int32, (length, length), dim)
        return jnp.where(index < here, index + first * here, index - first * here)

    return position(0) >= position(1)


def causal_rows(sequence, here, part):
    sub = here // 2
    shape = (2 * sub, 2 * here)
    first = half_of_place(2 * sequence)
    row = lax.broadcasted_iota(jnp.int32, shape, 0)
    row = jnp.where(row < sub, row + part * sub, row + here - sub + part * sub)
    col = lax.broadcasted_iota(jnp.int32, shape, 1)
    row, col = (
        jnp.where(index < here, index + first * here, index - first * here) for index in (row, col)
    )
    return row >= col


def soft_of(queries, keys, mask):
    scores = dot(queries, keys, 1, 1) * SCALE
    scores = jnp.where(mask, scores, -1000000000.0)
    powers = jnp.exp(scores - jnp.max(scores, -1, keepdims=True))
    return powers * (1.0 / jnp.sum(powers, -1, keepdims=True))


def read_extras(one, first_column, norm_table, bias):
    total = None
    for group in range(one.shape[0] // 128):
        block = one[pl.ds(group * 128, 128), pl.ds(first_column, 128)].astype(f32)
        block = block[0:32] + block[32:64] + block[64:96] + block[96:128]
        norm_table[:, pl.ds(group * 128, 128)] = block[12:16] + block[16:20]
        total = block[0:12] if total is None else total + block[0:12]
    bias[...] = total


class Reduce:
    def __init__(self, view, rows, rings):
        self.view, self.rows, self.rings = view, rows, rings
        self.done, self.got = [], {}

    def send(self, name, stage, half, way, src, dst, index):
        step = (1, -1)[way]
        device = at_z(step) if (half == 0) == (stage == 0) else at_x(step)
        copy = remote(src, dst, self.rings[stage][3], half * 6 + index * 2 + way, device)
        copy.start()
        self.done.append(copy)
        self.got[name, stage, half, way] = copy

    def begin(self, stage):
        mid, _, near, _ = self.rings[stage]
        for half in range(2):
            for way in range(2):
                src = self.view(stage, half, 2, way)
                self.send("mid", stage, half, way, src, mid.at[half, way], 0)
        for half in range(2):
            for way in range(2):
                src = self.view(stage, half, (1, 3)[way], 1 - way)
                self.send("near", stage, half, way, src, near.at[half, way], 1)

    def combine(self, stage):
        mid, far = self.rings[stage][:2]
        for half in range(2):
            for way in range(2):
                self.got["mid", stage, half, way].wait_recv()
                ref = self.view(stage, half, (1, 3)[way], way)
                ref[...] = (ref[...].astype(f32) + mid[half, way].astype(f32)).astype(bf16)
                self.send("far", stage, half, way, ref, far.at[half, way], 2)

    def settle(self, stage, out=None):
        far, near = self.rings[stage][1:3]
        piece = self.rows // 2
        for half in range(2):
            for part in range(2):
                self.got["far", stage, half, part].wait_recv()
                self.got["near", stage, half, 1 - part].wait_recv()
                ref = self.view(stage, half, 0, part)
                total = (
                    ref[...].astype(f32)
                    + far[half, part].astype(f32)
                    + near[half, 1 - part].astype(f32)
                ).astype(bf16)
                if out is None:
                    ref[...] = total
                else:
                    out[half, pl.ds(part * piece, piece)] = total

    def close(self):
        for copy in self.done:
            copy.wait_send()


def ring_buffers(stage, piece, wide):
    dims = (2, 2, 4, piece, wide) if stage == 0 else (2, 2, piece, wide)
    return [VMEM(dims, bf16)] * 3 + [DMA((12,))] * 2


def feed_forward_kernel(
    normed_in, cot_in, cotangent_in, unit_in, weights, scale, norm_table,
    resid_out, spread_out, mixed_out, chip, settled, sums,
    normed, cot_rows, cotangent, unit, resid, spread, mixed_parts, held, pair, hidden, normed_t, cot_t, parts, sib, mid, sent, far, near,
    *rest,
):
    rings = [rest[5 * k : 5 * k + 5] for k in range(2)]
    rings = [(mid, far, near, (send, recv)) for mid, far, near, send, recv in rings]
    in_sem, save_sem, load_sem, store_sem, core_send, core_recv, y_send, y_recv = rest[10:]
    columns, width = held.shape[3] // 3, normed.shape[1]
    wide = 256
    rows = sib.shape[1]
    sub = cotangent.shape[0] // 2
    z, x, c = lax.axis_index("z"), lax.axis_index("x"), lax.axis_index("c")
    y_sems, core_sems = (y_send, y_recv), (core_send, core_recv)
    whole, left = columns // wide, columns % wide
    all_pair, all_hidden = pl.ds(0, 2 * columns), pl.ds(2 * columns, columns)
    groups = tuple(pl.ds(which * columns, columns) for which in range(3))

    def load(k, which, size):
        start = pl.multiple_of(which * columns + k * wide, 128)
        cut = pl.ds(start, size)
        return pltpu.make_async_copy(
            weights.at[:, :, :, cut], held.at[:, :, :, cut], load_sem.at[k, which]
        )

    ins = [
        pltpu.make_async_copy(src, dst, in_sem.at[k])
        for k, (src, dst) in enumerate(
            ((normed_in, normed), (cot_in, cot_rows), (cotangent_in, cotangent), (unit_in, unit))
        )
    ]
    ins[0].start()
    ins[1].start()
    saves = []

    def save(src, dst):
        saves.append(pltpu.make_async_copy(src, dst, save_sem.at[len(saves)]))
        saves[-1].start()

    def load_tile(k, size):
        for which in range(3):
            load(k, which, size).start()

    load_tile(0, wide)
    load_tile(1, wide)
    ins[0].wait()
    ins[1].wait()

    def flip(k, _):
        rng = pl.ds(pl.multiple_of(k * wide, wide), wide)
        normed_t[rng] = normed[:, rng].T
        cot_t[rng] = cot_rows[:, rng].T
        return 0

    lax.fori_loop(0, width // wide, flip, 0)
    greet([at_z(1), at_z(3), at_x(1), at_x(3), at_y(1), at_y(3), sibling()])

    tall = width // 4

    def tile(k, cut):
        return k, slice(None), slice(None), cut

    def ahead(part, k, size):
        these = pl.ds(4 * part * sub, 4 * sub)

        def cut(which):
            return pl.ds(pl.multiple_of(which * columns + k * wide, 128), size)

        def weight(which):
            return held[:, :, :, cut(which)].reshape(width, size)

        if part == 0:
            if size == wide:
                pl.when(k + 2 < whole)(lambda: load_tile(k + 2, wide))
                if left:
                    pl.when(k + 2 == whole)(lambda: load_tile(whole, left))
            for which in range(3):
                load(k, which, size).wait()
        gate = dot(normed[these], weight(0), 1, 0)
        up = dot(normed[these], weight(1), 1, 0)
        grad_hidden = dot(cot_rows[these], weight(2), 1, 0)
        sigmoid = jax.nn.sigmoid(gate)
        activated = gate * sigmoid
        hidden[these, cut(0)] = (activated * up).astype(bf16)
        pair[these, cut(0)] = (
            grad_hidden * up * sigmoid * (1.0 + gate * (1.0 - sigmoid))
        ).astype(bf16)
        pair[these, cut(1)] = (grad_hidden * activated).astype(bf16)
        return 0

    part_subs = [parts.at[pl.ds(4 * k * sub, 4 * sub)] for k in range(2)]
    started, middle, halves, passed = [], [], [], []

    def ring_middle(part):
        middle.append(
            ring_sum_middle(
                part_subs[part], started[part], mid.at[part], sent.at[part], far.at[part],
                y_sems, 6 * part,
            )
        )

    for part in range(2):
        lax.fori_loop(0, whole, lambda k, _: ahead(part, k, wide), 0)
        if left:
            ahead(part, whole, left)
        if part == 1:
            ring_middle(0)

        def second_back(k, _):
            rng = pl.ds(pl.multiple_of(k * tall, tall), tall)
            weight = held[tile(k, all_pair)].reshape(tall, 2 * columns)
            these = pl.ds(4 * part * sub, 4 * sub)
            parts[these, rng] = dot(pair[these], weight, 1, 1).astype(bf16)
            return 0

        lax.fori_loop(0, 4, second_back, 0)
        started.append(
            ring_sum_start(part_subs[part], mid.at[part], near.at[part], y_sems, 6 * part)
        )

    def to_core(block, which):
        theirs = pl.ds(pl.multiple_of((1 - c) * rows, rows), rows)
        return remote(
            held.at[block // 4, block % 4, theirs, groups[which]],
            sib.at[block, :, groups[which]],
            core_sems,
            block + 16 * which,
            sibling(),
        )

    ours = pl.ds(pl.multiple_of(c * rows, rows), rows)

    def store(block):
        return pltpu.make_async_copy(
            held.at[block // 4, block % 4, ours, groups[2]], chip.at[block], store_sem.at[block]
        )

    def core_sum(block, which):
        to_core(block, which).wait_recv()
        mine = (block // 4, block % 4, ours, groups[which])
        held[mine] = (
            held[mine].astype(f32) + sib[block, :, groups[which]].astype(f32)
        ).astype(bf16)
        if which == 2:
            store(block).start()

    def weights_back(which, k):
        rng = pl.ds(pl.multiple_of(k * tall, tall), tall)
        if which < 2:
            grad = dot(normed_t[rng], pair[:, groups[which]], 1, 0)
        else:
            grad = dot(cot_t[rng], hidden[...], 1, 0)
        held[tile(k, groups[which])] = grad.astype(bf16).reshape(4, 2 * rows, columns)
        for block in range(4):
            to_core(4 * k + block, which).start()

        @pl.when(k > 1)
        def _():
            for block in range(4):
                core_sum(4 * k - 8 + block, which)

        return 0

    def all_weights(which):
        lax.fori_loop(0, 4, lambda k, _: weights_back(which, k), 0)

    def last_sums(which):
        for block in range(8, 16):
            core_sum(block, which)

    def settle_rows(part):
        finish = ring_sum_finish(
            part_subs[part], started[part], middle[part], far.at[part], near.at[part]
        )
        here = pl.ds(part * sub, sub)
        total = jnp.concatenate([finish(0), finish(1)], 0)
        unit_rows = unit[here]
        incoming = total * norm_table[2:3]
        result = cotangent[here].astype(f32) + scale[here] * (
            incoming
            - jnp.mean(incoming, -1, keepdims=True)
            - unit_rows * jnp.mean(incoming * unit_rows, -1, keepdims=True)
        )
        resid[here] = result
        spread[pl.ds(4 * part * sub, sub)] = result.astype(bf16)
        out = spread.at[pl.ds(4 * part * sub, 4 * sub)]
        halves.append([ring_gather_half(out, top, y_sems, 12 + 6 * part) for top in range(2)])
        both = jnp.concatenate(
            [
                jnp.sum(total * unit_rows, 0, keepdims=True),
                jnp.sum(total, 0, keepdims=True),
            ],
            0,
        )
        sums[...] = both if part == 0 else sums[...] + both

    def gather_pass(part):
        out = spread.at[pl.ds(4 * part * sub, 4 * sub)]
        passed.append(ring_gather_pass(out, halves[part], y_sems, 12 + 6 * part))

    def view_of(cols):
        def view(stage, half, d, part):
            start = c * rows + half * (rows // 2) + part * (rows // 4)
            rng = pl.ds(pl.multiple_of(start, rows // 4), rows // 4)
            if half == 0:
                return held.at[(z + d) % 4, :, rng, cols]
            return held.at[:, (x + d) % 4, rng, cols]

        return view

    gate_sums, up_sums = (
        Reduce(view_of(groups[which]), rows // 2, {0: rings[which]}) for which in range(2)
    )
    def mix(k, _):
        rng = pl.ds(pl.multiple_of(k * tall, tall), tall)
        weight = held[tile(k, all_hidden)].reshape(tall, columns)
        value = dot(hidden[...], weight, 1, 1).astype(bf16)
        for part in range(2):
            for block in range(4):
                start = (part * 4 + block) * sub
                mixed_parts[pl.ds((2 * block + part) * sub, sub), rng] = value[start : start + sub]
        return 0

    ins[2].start()
    ins[3].start()
    all_weights(0)
    ring_middle(1)
    last_sums(0)
    gate_sums.begin(0)
    ins[2].wait()
    ins[3].wait()
    settle_rows(0)
    all_weights(1)
    gate_sums.combine(0)
    last_sums(1)
    up_sums.begin(0)
    gather_pass(0)
    lax.fori_loop(0, 4, mix, 0)
    save(mixed_parts, mixed_out)
    settle_rows(1)
    save(resid, resid_out)
    all_weights(2)
    up_sums.combine(0)
    gather_pass(1)
    last_sums(2)
    gate_sums.settle(0)
    up_sums.settle(0)
    top_rows = pl.ds(pl.multiple_of(c * rows, rows // 2), rows // 2)
    low_rows = pl.ds(pl.multiple_of(c * rows + rows // 2, rows // 2), rows // 2)
    keep = [
        pltpu.make_async_copy(held.at[z, :, top_rows, all_pair], settled.at[0], store_sem.at[16]),
        pltpu.make_async_copy(held.at[:, x, low_rows, all_pair], settled.at[1], store_sem.at[17]),
    ]
    for copy in keep:
        copy.start()

    def drain(block, _):
        for which in range(3):
            to_core(block, which).wait_send()
        store(block).wait()
        return 0

    lax.fori_loop(0, 16, drain, 0)
    for k in range(2):
        for copy in passed[k] + [halves[k][1][0], halves[k][0][1]]:
            copy.wait_recv()
        these = pl.ds(4 * k * sub, 4 * sub)
        save(spread.at[these], spread_out.at[these])
        for copy in started[k] + middle[k] + halves[k][0] + halves[k][1] + passed[k]:
            copy.wait_send()
    gate_sums.close()
    up_sums.close()
    for copy in keep + saves:
        copy.wait()


def feed_forward(normed, cot_rows, cotangent, unit, scale, norm_table, weights):
    tokens, width = normed.shape
    here = cotangent.shape[0]
    columns = weights.shape[1] // 3
    rows = width // 32
    full = pl.BlockSpec(memory_space=VMEM)
    anywhere = pl.BlockSpec(memory_space=pl.ANY)
    tiles = -(-columns // 256)
    kept = (
        ((tokens, width), bf16),
        ((tokens, width), bf16),
        ((here, width), bf16),
        ((here, width), f32),
        ((here, width), f32),
        ((tokens, width), bf16),
        ((tokens, width), bf16),
    )
    return pl.pallas_call(
        feed_forward_kernel,
        out_shape=(
            jax.ShapeDtypeStruct((here, width), f32),
            jax.ShapeDtypeStruct((tokens, width), bf16),
            jax.ShapeDtypeStruct((tokens, width), bf16),
            jax.ShapeDtypeStruct((16, rows, columns), bf16),
            jax.ShapeDtypeStruct((2, 4, rows // 2, 2 * columns), bf16),
            jax.ShapeDtypeStruct((2, width), f32),
        ),
        in_specs=[anywhere] * 5 + [full] * 2,
        out_specs=(anywhere,) * 5 + (full,),
        scratch_shapes=[VMEM(dims, dtype) for dims, dtype in kept]
        + [
            VMEM((4, 4, 2 * rows, 3 * columns), bf16),
            VMEM((tokens, 2 * columns), bf16),
            VMEM((tokens, columns), bf16),
            VMEM((width, tokens), bf16),
            VMEM((width, tokens), bf16),
            VMEM((tokens, width), bf16),
            VMEM((16, rows, 3 * columns), bf16),
        ]
        + [VMEM((2, 2, here // 4, width), bf16)] * 4
        + ring_buffers(0, rows // 4, columns) * 2
        + [DMA((4,)), DMA((4,))]
        + [DMA((tiles, 3)), DMA((18,)), DMA((48,)), DMA((48,)), DMA((24,)), DMA((24,))],
        compiler_params=pltpu.CompilerParams(
            collective_id=2, has_side_effects=True, vmem_limit_bytes=VMEM_LIMIT
        ),
    )(
        normed, cot_rows, cotangent, unit, weights.reshape(4, 4, 2 * rows, 3 * columns), scale,
        norm_table,
    )


def cube():
    yl, c, yh = lax.axis_index("yl"), lax.axis_index("c"), lax.axis_index("yh")
    return [
        {"yl": (yl + a) % 2, "c": (c + b) % 2, "yh": (yh + d) % 2}
        for a in range(2)
        for b in range(2)
        for d in range(2)
        if a + b + d
    ]


class Spread:
    def __init__(self, out, rows, sems, core_sems):
        self.out, self.rows, self.sems, self.core_sems = out, rows, sems, core_sems
        self.done, self.core = [], []

    def cut(self, half, df, dg, part=None):
        z, x = lax.axis_index("z"), lax.axis_index("x")
        dz, dx = (df, dg) if half == 0 else (dg, df)
        place = ((z + dz) % 4) * 4 + (x + dx) % 4
        start = (place * 4 + lax.axis_index("c") * 2 + half) * self.rows
        piece = self.rows // 2
        if part is None:
            return self.out.at[pl.ds(pl.multiple_of(start, self.rows), self.rows)]
        return self.out.at[pl.ds(pl.multiple_of(start + part * piece, piece), piece)]

    def index(self, half, df, dg, part):
        return ((half * 4 + df % 4) * 4 + dg % 4) * 2 + part

    def push(self, half, df, dg, axis, step, part):
        device = at_z(step) if (half == 0) == (axis == 0) else at_x(step)
        to = (df - step, dg) if axis == 0 else (df, dg - step)
        ref = self.cut(half, df, dg, part)
        copy = remote(ref, ref, self.sems, self.index(half, *to, part), device)
        copy.start()
        self.done.append(copy)

    def arrived(self, half, df, dg, part):
        ref = self.cut(half, df, dg, part)
        remote(ref, ref, self.sems, self.index(half, df, dg, part), at_z(1)).wait_recv()

    def to_sibling(self, half, df, dg):
        ref = self.cut(half, df, dg)
        copy = remote(ref, ref, self.core_sems, (half * 4 + df % 4) * 4 + dg % 4, sibling())
        copy.start()
        self.done.append(copy)
        self.core.append(copy)

    def push_all(self, half, df, dg, axis):
        for part in range(2):
            self.push(half, df, dg, axis, 1, part)
            self.push(half, df, dg, axis, -1, 1 - part)

    def start(self):
        for axis in range(2):
            for half in range(2):
                self.push_all(half, 0, 0, axis)
        for half in range(2):
            self.to_sibling(half, 0, 0)

    def first_pass(self):
        for half in range(2):
            self.arrived(half, 3, 0, 0)
            self.push(half, 3, 0, 0, 1, 0)
            self.arrived(half, 1, 0, 1)
            self.push(half, 1, 0, 0, -1, 1)

    def first_rest(self):
        for half in range(2):
            self.arrived(half, 3, 0, 1)
            self.arrived(half, 1, 0, 0)
            for df in (3, 1):
                self.push_all(half, df, 0, 1)
                self.to_sibling(half, df, 0)

    def first_far(self):
        for half in range(2):
            self.arrived(half, 2, 0, 0)
            self.arrived(half, 2, 0, 1)
            self.push_all(half, 2, 0, 1)
            self.to_sibling(half, 2, 0)

    def second_pass(self, df):
        for half in range(2):
            self.arrived(half, df, 3, 0)
            self.push(half, df, 3, 1, 1, 0)
            self.arrived(half, df, 1, 1)
            self.push(half, df, 1, 1, -1, 1)
        for half in range(2):
            self.arrived(half, df, 3, 1)
            self.to_sibling(half, df, 3)
            self.arrived(half, df, 1, 0)
            self.to_sibling(half, df, 1)

    def second_far(self, df):
        for half in range(2):
            for part in range(2):
                self.arrived(half, df, 2, part)
            self.to_sibling(half, df, 2)

    def land(self):
        for copy in self.core:
            copy.wait_recv()

    def close(self):
        for copy in self.done:
            copy.wait_send()


def extra_rows(qkv_bias, norm_params, q, rows):
    z, x = lax.axis_index("z"), lax.axis_index("x")
    yl, c, yh = lax.axis_index("yl"), lax.axis_index("c"), lax.axis_index("yh")
    mine = ((z * 4 + x) * 2 + yl) * 2 + c
    lane = lax.broadcasted_iota(jnp.int32, (1, EXTRA), 1)
    heads = qkv_bias.shape[2] // 2
    pieces = []
    for t in range(3):
        for pair in range(heads // 2):
            row = jnp.zeros((1, EXTRA), f32)
            for side in range(2):
                head = q * heads + 2 * pair + side
                value = qkv_bias[t, :, head : head + 1].astype(f32)
                row = row + jnp.where(lane == mine + side * HEAD_DIM, value, 0.0)
            pieces.append(row)
    share = norm_params.shape[1]
    high = norm_params[...].astype(bf16).astype(f32)
    norm = jnp.concatenate([high, norm_params[...] - high], 0)
    norm = jnp.concatenate([norm, jnp.zeros((norm.shape[0], EXTRA - share), f32)], 1)
    norm = pltpu.roll(norm, (mine % 4 * 2 + yh) * share, 1)
    used = len(pieces) + norm.shape[0]
    pieces += [norm, jnp.zeros((rows - used, EXTRA), f32)]
    return jnp.concatenate(pieces, 0).astype(bf16)


def forward_kernel(
    qkv_weight, out_weight, gate_up_weight, down_weight, qkv_bias, norm_params, tokens, cotangent,
    table,
    one_out, two, token_out, cot_out, qkv_out, mix_out, summed_out, unit_out, normed_out,
    stats, norm_table, scale,
    token_rows, cot_rows, qkv, head_mix, summed, unit, normed_two,
    one_q, two_q, one, norm_in, bias, normed, parts, mid, sent, far, near,
    pair_send, pair_recv, local_sem, save_sem, y_send, y_recv,
    send_one, recv_one, core_send_one, core_recv_one,
    send_two, recv_two, core_send_two, core_recv_two,
):
    z, x = lax.axis_index("z"), lax.axis_index("x")
    yl, c, yh = lax.axis_index("yl"), lax.axis_index("c"), lax.axis_index("yh")
    rows, here = one_q.shape[1], tokens.shape[0]
    hq, fq = qkv_weight.shape[2] // 2, gate_up_weight.shape[2] // 2
    pair_sems, y_sems = (pair_send, pair_recv), (y_send, y_recv)
    for q in range(2):
        for group in range(2):
            for t in range(3):
                to, start = (group * 3 + t) * hq // 2, q * hq + group * hq // 2
                one_q[q, :, to : to + hq // 2] = qkv_weight[t, :, start : start + hq // 2]
        one_q[q, :, 3 * hq : 3 * hq + EXTRA] = extra_rows(qkv_bias, norm_params, q, rows)
        one_q[q, :, 3 * hq + EXTRA :] = out_weight[:, q * hq : (q + 1) * hq]
    token_rows[pl.ds(0, here)] = tokens[...]
    greet([at_z(1), at_z(3), at_x(1), at_x(3)] + cube())

    same, cross = pair_moves()
    mine = pl.ds(pl.multiple_of((z * 4 + x) * 4 * rows + (yl * 2 + c) * rows, rows), rows)
    moves = [
        (one_q.at[c], one.at[mine], 0, same),
        (one_q.at[1 - c], one.at[mine], 1, cross),
        (two_q.at[c], two.at[mine], 2, same),
        (two_q.at[1 - c], two.at[mine], 3, cross),
    ]

    def launch(k):
        src, dst, index, device = moves[k]
        if device is same:
            stay_or_go(src, dst, pair_sems, index, device, local_sem.at[index // 2])
        else:
            remote(src, dst, pair_sems, index, device).start()

    def land(k):
        src, dst, index, device = moves[k]
        if device is same:
            stay_or_go_wait(src, dst, pair_sems, index, device, local_sem.at[index // 2])
        else:
            copy = remote(src, dst, pair_sems, index, device)
            copy.wait_recv()
            copy.wait_send()

    norm_moves = [
        remote(
            one_q.at[0, :, pl.ds(3 * hq, EXTRA)],
            norm_in.at[c],
            pair_sems,
            4 + which,
            {"yl": target["yl"], "c": target["c"], "yh": 1 - yh},
        )
        for which, target in enumerate((same, cross))
    ]
    launch(0)
    launch(1)
    for move in norm_moves:
        move.start()
    token_halves = [ring_gather_half(token_rows, top, y_sems, 0) for top in range(2)]
    for q in range(2):
        for t in range(2):
            two_q[q, :, t * fq : (t + 1) * fq] = gate_up_weight[t, :, q * fq : (q + 1) * fq]
        two_q[q, :, 2 * fq :] = down_weight[:, q * fq : (q + 1) * fq]
    sub = here // 2
    for k in range(2):
        cot_rows[pl.ds(4 * k * sub, sub)] = cotangent[pl.ds(k * sub, sub)]
    land(0)
    land(1)
    for move in norm_moves:
        move.wait_recv()
    own = (z * 4 + x) * 4 + 2 * c
    for core in range(2):
        block = pl.ds(pl.multiple_of((own + core) * rows, rows), rows)
        came = norm_in[core].astype(f32)
        place = lax.broadcasted_iota(jnp.int32, came.shape, 0)
        held = one[block, pl.ds(3 * hq, EXTRA)].astype(f32)
        one[block, pl.ds(3 * hq, EXTRA)] = (
            held + jnp.where((place >= 12) & (place < 20), came, 0.0)
        ).astype(bf16)
    first = Spread(one, rows, (send_one, recv_one), (core_send_one, core_recv_one))
    second = Spread(two, rows, (send_two, recv_two), (core_send_two, core_recv_two))
    first.start()
    launch(2)
    launch(3)
    first.first_pass()
    first.first_rest()
    token_passed = ring_gather_pass(token_rows, token_halves, y_sems, 0)
    first.second_pass(0)
    first.first_far()
    first.second_pass(3)
    first.second_pass(1)
    first.second_pass(2)
    for df in (0, 3, 1, 2):
        first.second_far(df)
    land(2)
    land(3)
    second.start()
    for copy in token_passed + [token_halves[1][0], token_halves[0][1]]:
        copy.wait_recv()
    cot_subs = [cot_rows.at[pl.ds(4 * k * sub, 4 * sub)] for k in range(2)]
    cot_halves = [
        [ring_gather_half(cot_subs[k], top, y_sems, 6 + 6 * k) for top in range(2)]
        for k in range(2)
    ]
    first.land()
    keep = pltpu.make_async_copy(one, one_out, local_sem.at[2])
    keep.start()
    saves = []

    def save(src, dst):
        saves.append(pltpu.make_async_copy(src, dst, save_sem.at[len(saves)]))
        saves[-1].start()

    save(token_rows, token_out)

    read_extras(one, 3 * hq, norm_table, bias)

    def norm_rows(k, _):
        rng = pl.ds(pl.multiple_of(k * here, here), here)
        values = token_rows[rng].astype(f32)
        mean = jnp.mean(values, -1, keepdims=True)
        centered = values - mean
        inverse = lax.rsqrt(jnp.mean(centered * centered, -1, keepdims=True) + EPSILON)
        stats[0, rng] = mean
        stats[1, rng] = inverse
        normed[rng] = (centered * inverse * norm_table[0:1] + norm_table[1:2]).astype(bf16)
        return 0

    lax.fori_loop(0, 4, norm_rows, 0)
    second.first_pass()
    wide = 256

    def project(k, _):
        cols = pl.ds(pl.multiple_of(k * wide, wide), wide)
        value = dot(normed[...], one[:, cols], 1, 0)
        row = k % 3 * (hq // 128) + k // 3 * 2
        value = value + jnp.concatenate([bias[pl.ds(row, 1)], bias[pl.ds(row + 1, 1)]], 1)

        @pl.when(k % 3 < 2)
        def _():
            for place in range(4):
                rng = pl.ds(place * here, here)
                turn = table[pl.ds(pl.multiple_of(half_of_place(place) * here, here), here)]
                for pair in range(wide // 128):
                    qkv[rng, pl.ds(pl.multiple_of(k * wide + pair * 128, 128), 128)] = turn_heads(
                        value[place * here : (place + 1) * here, pair * 128 : (pair + 1) * 128],
                        turn,
                        1.0,
                    ).astype(bf16)

        @pl.when(k % 3 == 2)
        def _():
            qkv[:, cols] = value.astype(bf16)

        return 0

    lax.fori_loop(0, 3 * hq // wide, project, 0)
    save(qkv, qkv_out)
    second.first_rest()
    cot_passed = [
        ring_gather_pass(cot_subs[k], cot_halves[k], y_sems, 6 + 6 * k) for k in range(2)
    ]
    part_subs = [parts.at[pl.ds(4 * k * sub, 4 * sub)] for k in range(2)]
    started, middle = [], []
    for part in range(2):
        for sequence in range(2):
            mask = causal_rows(sequence, here, part)
            rng = pl.ds(sequence * 2 * here, 2 * here)
            lower = pl.ds(sequence * 2 * here + part * sub, sub)
            upper = pl.ds(sequence * 2 * here + here + part * sub, sub)

            def heads(k, _):
                def cols(t):
                    start = k // 2 * (3 * hq // 2) + t * (hq // 2) + k % 2 * 128
                    return pl.ds(pl.multiple_of(start, 128), 128)

                q = jnp.concatenate([qkv[lower, cols(0)], qkv[upper, cols(0)]], 0)
                key, value = qkv[rng, cols(1)], qkv[rng, cols(2)]
                mixes = []
                for head in range(2):
                    cut = slice(head * HEAD_DIM, (head + 1) * HEAD_DIM)
                    soft = soft_of(q[:, cut], key[:, cut], mask).astype(bf16)
                    mixes.append(dot(soft, value[:, cut], 1, 0))
                mixed = jnp.concatenate(mixes, 1).astype(bf16)
                there = pl.ds(pl.multiple_of(k * 128, 128), 128)
                head_mix[lower, there] = mixed[:sub]
                head_mix[upper, there] = mixed[sub:]
                return 0

            lax.fori_loop(0, hq // 128, heads, 0, unroll=2)
        mix = jnp.concatenate(
            [head_mix[pl.ds(k * here + part * sub, sub)] for k in range(4)], 0
        )

        def out_project(k, _):
            rng = pl.ds(pl.multiple_of(k * wide, wide), wide)
            parts[pl.ds(4 * part * sub, 4 * sub), rng] = dot(
                mix, one[rng, pl.ds(3 * hq + EXTRA, hq)], 1, 1
            ).astype(bf16)
            return 0

        lax.fori_loop(0, one.shape[0] // wide, out_project, 0)
        started.append(
            ring_sum_start(part_subs[part], mid.at[part], near.at[part], y_sems, 18 + 6 * part)
        )
        if part == 0:
            second.second_pass(0)
            second.first_far()
    save(head_mix, mix_out)
    for k in range(2):
        for copy in cot_passed[k] + [cot_halves[k][1][0], cot_halves[k][0][1]]:
            copy.wait_recv()
    save(cot_rows, cot_out)
    second.second_pass(3)
    for part in range(2):
        middle.append(
            ring_sum_middle(
                part_subs[part], started[part], mid.at[part], sent.at[part], far.at[part],
                y_sems, 18 + 6 * part,
            )
        )
    second.second_pass(1)
    halves = []
    for part in range(2):
        finish = ring_sum_finish(
            part_subs[part], started[part], middle[part], far.at[part], near.at[part]
        )
        total = jnp.concatenate([finish(0), finish(1)], 0)
        rng = pl.ds(part * sub, sub)
        total = total + tokens[rng].astype(f32)
        summed[rng] = total
        centered = total - jnp.mean(total, -1, keepdims=True)
        inverse = lax.rsqrt(jnp.mean(centered * centered, -1, keepdims=True) + EPSILON)
        unit_rows = centered * inverse
        unit[rng] = unit_rows
        scale[rng] = inverse
        normed_two[pl.ds(4 * part * sub, sub)] = (
            unit_rows * norm_table[2:3] + norm_table[3:4]
        ).astype(bf16)
        out = normed_two.at[pl.ds(4 * part * sub, 4 * sub)]
        halves.append([ring_gather_half(out, top, y_sems, 30 + 6 * part) for top in range(2)])
    save(summed, summed_out)
    save(unit, unit_out)
    second.second_pass(2)
    passed = [
        ring_gather_pass(
            normed_two.at[pl.ds(4 * k * sub, 4 * sub)], halves[k], y_sems, 30 + 6 * k
        )
        for k in range(2)
    ]
    for df in (0, 3, 1, 2):
        second.second_far(df)
    for k in range(2):
        for copy in passed[k] + [halves[k][1][0], halves[k][0][1]]:
            copy.wait_recv()
        these = pl.ds(4 * k * sub, 4 * sub)
        save(normed_two.at[these], normed_out.at[these])
    second.land()
    keep.wait()
    for copy in saves:
        copy.wait()
    for move in norm_moves:
        move.wait_send()
    gathers = token_halves + cot_halves[0] + cot_halves[1] + halves[0] + halves[1]
    for copies in gathers + [token_passed] + cot_passed + started + middle + passed:
        for copy in copies:
            copy.wait_send()
    first.close()
    second.close()


def forward(
    qkv_weight, out_weight, gate_up_weight, down_weight, qkv_bias, norm_params, tokens, cotangent,
    table,
):
    here, width = tokens.shape
    rows = qkv_weight.shape[1]
    hq, fq = qkv_weight.shape[2] // 2, gate_up_weight.shape[2] // 2
    full = pl.BlockSpec(memory_space=VMEM)
    anywhere = pl.BlockSpec(memory_space=pl.ANY)
    one_wide, two_wide = 4 * hq + EXTRA, 3 * fq
    kept = (
        ((4 * here, width), bf16),
        ((4 * here, width), bf16),
        ((4 * here, 3 * hq), bf16),
        ((4 * here, hq), bf16),
        ((here, width), f32),
        ((here, width), f32),
        ((4 * here, width), bf16),
    )

    def shape(*dims, dtype=bf16):
        return jax.ShapeDtypeStruct(dims, dtype)

    return pl.pallas_call(
        forward_kernel,
        out_shape=(
            shape(width, one_wide),
            shape(width, two_wide),
            *(shape(*dims, dtype=dtype) for dims, dtype in kept),
            shape(2, 4 * here, 1, dtype=f32),
            shape(4, width, dtype=f32),
            shape(here, 1, dtype=f32),
        ),
        in_specs=[full] * 9,
        out_specs=(anywhere,) * 9 + (full,) * 3,
        scratch_shapes=[VMEM(dims, dtype) for dims, dtype in kept]
        + [
            VMEM((2, rows, one_wide), bf16),
            VMEM((2, rows, two_wide), bf16),
            VMEM((width, one_wide), bf16),
            VMEM((2, rows, EXTRA), bf16),
            VMEM((12, 128), f32),
            VMEM((4 * here, width), bf16),
            VMEM((4 * here, width), bf16),
        ]
        + [VMEM((2, 2, here // 4, width), bf16)] * 4
        + [
            DMA((6,)), DMA((6,)), DMA((3,)), DMA((9,)), DMA((42,)), DMA((42,)),
            DMA((64,)), DMA((64,)), DMA((32,)), DMA((32,)),
            DMA((64,)), DMA((64,)), DMA((32,)), DMA((32,)),
        ],
        compiler_params=pltpu.CompilerParams(
            collective_id=0, has_side_effects=True, vmem_limit_bytes=VMEM_LIMIT
        ),
    )(
        qkv_weight, out_weight, gate_up_weight, down_weight, qkv_bias, norm_params, tokens,
        cotangent, table,
    )


def backward_kernel(
    one, resid_rows, chip, settled, qkv_in, mix_in, token_in, mixed_in, resid_in, sum_in,
    stats, table, second_terms, norm_table,
    result_one, result_two, norm_back, grad_out, mixed_out,
    qkv, head_mix, token_rows, mixed_parts, resid, first_sum, grad_tokens, mixed,
    held, spare, grad_mix, grad_proj, part_sums, sib, blocks, pair_sums,
    *rest,
):
    rings = [rest[5 * k : 5 * k + 5] for k in range(9)]
    rings = [(mid, far, near, (send, recv)) for mid, far, near, send, recv in rings]
    (
        packed_one, packed_two, ymid, ysent, yfar, ynear,
        load_sem, in_sem, save_sem, block_sem, core_send, core_recv, pair_send, pair_recv, local_sem, y_send, y_recv,
    ) = rest[45:]
    z, x = lax.axis_index("z"), lax.axis_index("x")
    yl, c, yh = lax.axis_index("yl"), lax.axis_index("c"), lax.axis_index("yh")
    here = resid.shape[0]
    rows = result_one.shape[1]
    hq, fq = head_mix.shape[1], result_two.shape[2] // 3
    early, late = pair_sums.shape[3], blocks.shape[3]
    sub = here // 2
    width = held.shape[0]
    core_sems, pair_sems, y_sems = (core_send, core_recv), (pair_send, pair_recv), (y_send, y_recv)
    wide = 256
    out_start = 3 * hq + EXTRA
    group = 3 * hq // 2
    columns = (pl.ds(0, group), pl.ds(out_start, hq), pl.ds(group, group + EXTRA))

    def place_of(dz, dx):
        return ((z + dz) % 4) * 4 + (x + dx) % 4

    loads = [
        pltpu.make_async_copy(
            one.at[:, pl.ds(start, size)], held.at[:, pl.ds(start, size)], load_sem.at[k]
        )
        for k, (start, size) in enumerate(((out_start, hq), (0, 3 * hq)))
    ]
    loads.append(pltpu.make_async_copy(resid_rows, spare, load_sem.at[2]))
    loads.append(pltpu.make_async_copy(settled, pair_sums, load_sem.at[3]))
    block_loads = [
        pltpu.make_async_copy(
            chip.at[place_of(dz, dx)], blocks.at[dz, dx], block_sem.at[dz * 4 + dx]
        )
        for dz in range(4)
        for dx in range(4)
    ]
    ins = [
        pltpu.make_async_copy(src, dst, in_sem.at[k])
        for k, (src, dst) in enumerate(
            (
                (mixed_in, mixed_parts), (mix_in, head_mix), (qkv_in, qkv),
                (token_in, token_rows), (resid_in, resid), (sum_in, first_sum),
            )
        )
    ]
    loads[3].start()
    ins[0].start()
    loads[2].start()
    loads[0].start()
    ins[1].start()
    for load in block_loads:
        load.start()
    greet([at_z(1), at_z(3), at_x(1), at_x(3)] + cube())
    ins[0].wait()
    mixed_started = ring_sum_start(mixed_parts, ymid.at[0], ynear.at[0], y_sems, 0)

    def cut(half, part):
        return pl.ds(half * rows + part * (rows // 2), rows // 2)

    def pair_view(stage, half, d, part):
        along = x if half == 0 else z
        return pair_sums.at[half, (along + d) % 4, pl.ds(part * (rows // 2), rows // 2)]

    def view_of(ref, cols):
        def view(stage, half, d, part):
            if stage == 0:
                there = (d, slice(None)) if half == 0 else (slice(None), d)
            else:
                there = (0, d) if half == 0 else (d, 0)
            return ref.at[(*there, cut(half, part), cols)]

        return view

    early_sums = Reduce(pair_view, rows, {1: rings[0]})
    late_sums = Reduce(view_of(blocks, pl.ds(0, late)), rows, {0: rings[1], 1: rings[2]})
    out_proj = Reduce(view_of(sib, columns[1]), rows, {0: rings[3], 1: rings[4]})
    head_sums = [
        Reduce(view_of(sib, columns[0]), rows, {0: rings[5], 1: rings[6]}),
        Reduce(view_of(sib, columns[2]), rows, {0: rings[7], 1: rings[8]}),
    ]
    loads[3].wait()
    early_sums.begin(1)
    for load in block_loads:
        load.wait()
    late_sums.begin(0)

    def to_core(block, which):
        theirs = pl.ds(pl.multiple_of((2 * block + 1 - c) * 2 * rows, 2 * rows), 2 * rows)
        dz, dx = (block // 4 - z + 4) % 4, (block % 4 - x + 4) % 4
        return remote(
            held.at[theirs, columns[which]],
            sib.at[dz, dx, :, columns[which]],
            core_sems,
            block + 16 * which,
            sibling(),
        )

    def core_sum(block, which):
        to_core(block, which).wait_recv()
        ours = pl.ds(pl.multiple_of((2 * block + c) * 2 * rows, 2 * rows), 2 * rows)
        there = ((block // 4 - z + 4) % 4, (block % 4 - x + 4) % 4, slice(None), columns[which])
        sib[there] = (sib[there].astype(f32) + held[ours, columns[which]].astype(f32)).astype(
            bf16
        )

    loads[2].wait()
    loads[0].wait()
    ins[1].wait()

    mix_order = jnp.concatenate(
        [
            head_mix[pl.ds(block * here + part * sub, sub)]
            for part in range(2)
            for block in range(4)
        ],
        0,
    )

    def mix_back(k, _):
        cols = pl.ds(pl.multiple_of(k * wide, wide), wide)
        value = dot(
            spare[...], held[:, pl.ds(pl.multiple_of(out_start + k * wide, 128), wide)], 1, 0
        ).astype(bf16)
        for part in range(2):
            for block in range(4):
                start = (part * 4 + block) * sub
                grad_mix[pl.ds(block * here + part * sub, sub), cols] = value[start : start + sub]
        return 0

    ins[2].start()
    loads[1].start()
    lax.fori_loop(0, hq // wide, mix_back, 0)
    for load in ins[3:]:
        load.start()

    def out_back(k, _):
        rng = pl.ds(pl.multiple_of(k * 2 * wide, 2 * wide), 2 * wide)
        held[rng, columns[1]] = dot(spare[:, rng], mix_order, 0, 0).astype(bf16)
        for block in range(4):
            to_core(4 * k + block, 1).start()
        return 0

    lax.fori_loop(0, width // (2 * wide), out_back, 0)
    early_sums.combine(1)
    mixed_middle = ring_sum_middle(
        mixed_parts, mixed_started, ymid.at[0], ysent.at[0], yfar.at[0], y_sems, 0
    )

    def out_sum(block, _):
        core_sum(block, 1)
        return 0

    lax.fori_loop(0, 16, out_sum, 0)
    out_proj.begin(0)
    masks = [causal_mask(sequence, here) for sequence in range(2)]
    turns = [
        jnp.concatenate(
            [
                table[pl.ds(pl.multiple_of(half_of_place(2 * sequence + k) * here, here), here)]
                for k in range(2)
            ],
            0,
        )
        for sequence in range(2)
    ]

    def heads_back(half, sequence):
        mask, turn = masks[sequence], turns[sequence]
        rng = pl.ds(sequence * 2 * here, 2 * here)
        for k in range(hq // 256):

            def pair(t):
                return pl.ds(half * group + t * (hq // 2) + k * 128, 128)

            q, key, value = qkv[rng, pair(0)], qkv[rng, pair(1)], qkv[rng, pair(2)]
            mix = grad_mix[rng, pl.ds(half * (hq // 2) + k * 128, 128)]
            results = ([], [], [])
            for head in range(2):
                lanes = slice(head * HEAD_DIM, (head + 1) * HEAD_DIM)
                soft = soft_of(q[:, lanes], key[:, lanes], mask)
                grad_soft = dot(mix[:, lanes], value[:, lanes], 1, 1)
                row_dot = jnp.sum(grad_soft * soft, -1, keepdims=True)
                grad_score = (soft * (grad_soft - row_dot)).astype(bf16)
                results[0].append(dot(grad_score, key[:, lanes], 1, 0) * SCALE)
                results[1].append(dot(grad_score, q[:, lanes], 0, 0) * SCALE)
                results[2].append(dot(soft.astype(bf16), mix[:, lanes], 0, 0))
            for t in range(3):
                both = jnp.concatenate(results[t], 1)
                if t < 2:
                    both = turn_heads(both, turn, -1.0)
                grad_proj[rng, pair(t)] = both.astype(bf16)

    def bias_sum(t, k):
        start = k // 2 * group + t * (hq // 2) + k % 2 * 128
        return jnp.sum(grad_proj[:, pl.ds(start, 128)].astype(f32), 0, keepdims=True)

    mean, inverse = stats[0], stats[1]
    tall = 512

    def weights_back(half, k, bias_rows):
        rng = pl.ds(pl.multiple_of(k * tall, tall), tall)
        these = pl.ds(half * group, group)
        part = dot(grad_proj[:, these], held[rng, these], 1, 1)
        unit = (token_rows[:, rng].astype(f32) - mean) * inverse
        normed = (unit * norm_table[0:1, rng] + norm_table[1:2, rng]).astype(bf16)
        held[rng, these] = dot(normed, grad_proj[:, these], 0, 0).astype(bf16)
        if half == 0:
            part_sums[:, rng] = part
        else:
            part = part + part_sums[:, rng]
            spare[:, rng] = part.astype(bf16)
            gain = jnp.sum(part * unit, 0, keepdims=True)
            shift = jnp.sum(part, 0, keepdims=True)
            for tile in range(tall // 128):
                inner = slice(tile * 128, (tile + 1) * 128)
                lanes = pl.ds(pl.multiple_of(k * tall + tile * 128, 128), 128)
                extra = jnp.concatenate(
                    bias_rows
                    + [
                        gain[:, inner],
                        shift[:, inner],
                        second_terms[:, lanes],
                        jnp.zeros((rows - 16, 128), f32),
                    ],
                    0,
                ).astype(bf16)
                for copy in range(128 // rows):
                    start = pl.multiple_of(k * tall + tile * 128 + copy * rows, rows)
                    held[pl.ds(start, rows), pl.ds(3 * hq, EXTRA)] = extra
        for block in range(4):
            to_core(4 * k + block, 2 * half).start()

        @pl.when(k > 0)
        def _():
            for block in range(4):
                core_sum(4 * k - 4 + block, 2 * half)

        return 0

    ins[2].wait()
    for sequence in range(2):
        heads_back(0, sequence)
    late_sums.combine(0)
    loads[1].wait()
    for load in ins[3:]:
        load.wait()
    lax.fori_loop(0, width // tall, lambda k, _: weights_back(0, k, None), 0)
    for block in range(12, 16):
        core_sum(block, 0)
    head_sums[0].begin(0)
    early_sums.settle(1, packed_two.at[:, :, pl.ds(0, early)])
    heads_back(1, 0)
    out_proj.combine(0)
    late_sums.settle(0)
    late_sums.begin(1)
    heads_back(1, 1)
    head_sums[0].combine(0)
    bias_rows = [bias_sum(t, k) for t in range(3) for k in range(hq // 128)]
    lax.fori_loop(0, 2, lambda k, _: weights_back(1, k, bias_rows), 0)
    out_proj.settle(0)
    out_proj.begin(1)
    late_sums.combine(1)
    lax.fori_loop(2, 4, lambda k, _: weights_back(1, k, bias_rows), 0)
    first_started = ring_sum_start(spare, ymid.at[1], ynear.at[1], y_sems, 6)
    for block in range(12, 16):
        core_sum(block, 2)
    head_sums[1].begin(0)
    head_sums[0].settle(0)
    head_sums[0].begin(1)
    late_sums.settle(1, packed_two.at[:, :, pl.ds(early, late)])
    home, away = {"yl": c, "c": yl}, {"yl": c, "c": 1 - yl}
    stay_or_go(packed_two.at[yl], result_two.at[yl], pair_sems, 0, home, local_sem.at[0])
    cross_two = remote(packed_two.at[1 - yl], result_two.at[yl], pair_sems, 1, away)
    cross_two.start()
    out_proj.combine(1)
    head_sums[1].combine(0)
    first_middle = ring_sum_middle(
        spare, first_started, ymid.at[1], ysent.at[1], yfar.at[1], y_sems, 6
    )
    head_sums[0].combine(1)
    half_here = here // 2
    finish = ring_sum_finish(mixed_parts, mixed_started, mixed_middle, yfar.at[0], ynear.at[0])
    for top in range(2):
        rng = pl.ds(top * half_here, half_here)
        mixed[rng] = (first_sum[rng] + finish(top)).astype(bf16)
    saves = [pltpu.make_async_copy(mixed, mixed_out, save_sem.at[0])]
    saves[0].start()
    out_proj.settle(1, packed_one.at[:, :, columns[1]])
    head_sums[1].settle(0)
    head_sums[1].begin(1)
    head_sums[0].settle(1, packed_one.at[:, :, columns[0]])
    head_sums[1].combine(1)
    head_sums[1].settle(1, packed_one.at[:, :, columns[2]])

    stay_or_go(packed_one.at[yl], result_one.at[yl], pair_sems, 2, home, local_sem.at[1])
    cross_one = remote(packed_one.at[1 - yl], result_one.at[yl], pair_sems, 3, away)
    cross_one.start()
    extras = pl.ds(3 * hq, EXTRA)
    norm_moves = [
        remote(
            packed_one.at[core, :, extras],
            norm_back.at[yl],
            pair_sems,
            4 + which,
            {"yl": c, "c": core, "yh": 1 - yh},
        )
        for which, core in enumerate((yl, 1 - yl))
    ]
    for move in norm_moves:
        move.start()
    finish = ring_sum_finish(spare, first_started, first_middle, yfar.at[1], ynear.at[1])
    for top in range(2):
        rng = pl.ds(top * half_here, half_here)
        incoming = finish(top) * norm_table[0:1]
        unit_rows = (token_rows[rng].astype(f32) - stats[0, rng]) * stats[1, rng]
        grad_tokens[rng] = resid[rng] + stats[1, rng] * (
            incoming
            - jnp.mean(incoming, -1, keepdims=True)
            - unit_rows * jnp.mean(incoming * unit_rows, -1, keepdims=True)
        )
    saves.append(pltpu.make_async_copy(grad_tokens, grad_out, save_sem.at[1]))
    saves[1].start()
    for copy in [cross_two, cross_one] + norm_moves:
        copy.wait_recv()
        copy.wait_send()
    stay_or_go_wait(packed_two.at[yl], result_two.at[yl], pair_sems, 0, home, local_sem.at[0])
    stay_or_go_wait(packed_one.at[yl], result_one.at[yl], pair_sems, 2, home, local_sem.at[1])
    for copy in saves:
        copy.wait()
    for copy in mixed_started + mixed_middle + first_started + first_middle:
        copy.wait_send()

    def drain(block, _):
        for which in range(3):
            to_core(block, which).wait_send()
        return 0

    lax.fori_loop(0, 16, drain, 0)
    for sums in [early_sums, late_sums, out_proj] + head_sums:
        sums.close()


def backward(
    one, resid_rows, chip, settled, qkv, head_mix, token_rows, mixed_parts, resid, first_sum,
    stats, table, second_terms, norm_table,
):
    here, width = resid.shape
    hq, early, late = head_mix.shape[1], settled.shape[3], chip.shape[2]
    fq = (early + late) // 3
    rows = width // 64
    piece = rows // 2
    one_wide = one.shape[1]
    full = pl.BlockSpec(memory_space=VMEM)
    anywhere = pl.BlockSpec(memory_space=pl.ANY)
    rings = ring_buffers(1, piece, early)
    for wide in (late, hq, 3 * hq // 2, 3 * hq // 2 + EXTRA):
        rings += ring_buffers(0, piece, wide) + ring_buffers(1, piece, wide)
    return pl.pallas_call(
        backward_kernel,
        out_shape=(
            jax.ShapeDtypeStruct((2, rows, one_wide), bf16),
            jax.ShapeDtypeStruct((2, rows, 3 * fq), bf16),
            jax.ShapeDtypeStruct((2, rows, EXTRA), bf16),
            jax.ShapeDtypeStruct((here, width), f32),
            jax.ShapeDtypeStruct((here, width), bf16),
        ),
        in_specs=[anywhere] * 10 + [full] * 4,
        out_specs=(anywhere,) * 5,
        scratch_shapes=[
            VMEM(qkv.shape, bf16),
            VMEM(head_mix.shape, bf16),
            VMEM(token_rows.shape, bf16),
            VMEM(mixed_parts.shape, bf16),
            VMEM((here, width), f32),
            VMEM((here, width), f32),
            VMEM((here, width), f32),
            VMEM((here, width), bf16),
            VMEM((width, one_wide), bf16),
            VMEM((4 * here, width), bf16),
            VMEM((4 * here, hq), bf16),
            VMEM((4 * here, 3 * hq), bf16),
            VMEM((4 * here, width), f32),
            VMEM((4, 4, 2 * rows, one_wide), bf16),
            VMEM((4, 4, 2 * rows, late), bf16),
            VMEM((2, 4, rows, early), bf16),
        ]
        + rings
        + [VMEM((2, rows, one_wide), bf16), VMEM((2, rows, 3 * fq), bf16)]
        + [VMEM((2, 2, here // 2, width), bf16)] * 4
        + [DMA((4,)), DMA((6,)), DMA((2,)), DMA((16,)), DMA((48,)), DMA((48,))]
        + [DMA((6,)), DMA((6,)), DMA((2,)), DMA((12,)), DMA((12,))],
        compiler_params=pltpu.CompilerParams(
            collective_id=3, has_side_effects=True, vmem_limit_bytes=VMEM_LIMIT
        ),
    )(
        one, resid_rows, chip, settled, qkv, head_mix, token_rows, mixed_parts, resid, first_sum,
        stats, table, second_terms, norm_table,
    )


def finish_kernel(
    one, two, norm_back,
    out_norm, out_qkv, out_bias, out_out, out_gate_up, out_down,
):
    z, x = lax.axis_index("z"), lax.axis_index("x")
    yl, c, yh = lax.axis_index("yl"), lax.axis_index("c"), lax.axis_index("yh")
    mine = ((z * 4 + x) * 2 + yl) * 2 + c
    hq, fq = out_out.shape[1] // 2, out_down.shape[1] // 2
    for q in range(2):
        for group in range(2):
            for t in range(3):
                start, to = (group * 3 + t) * hq // 2, q * hq + group * hq // 2
                out_qkv[t, :, to : to + hq // 2] = one[q, :, start : start + hq // 2].astype(f32)
        out_out[:, q * hq : (q + 1) * hq] = one[q, :, 3 * hq + EXTRA :].astype(f32)
        for t in range(2):
            out_gate_up[t, :, q * fq : (q + 1) * fq] = two[q, :, t * fq : (t + 1) * fq].astype(f32)
        out_down[:, q * fq : (q + 1) * fq] = two[q, :, 2 * fq :].astype(f32)
    extras = [one[q, :, 3 * hq : 3 * hq + EXTRA].astype(f32) for q in range(2)]
    heads = hq // HEAD_DIM
    pairs = 3 * heads // 2
    share = out_norm.shape[1]
    sums = extras[0] + extras[1] + (norm_back[0].astype(f32) + norm_back[1].astype(f32))
    sums = pltpu.roll(sums, EXTRA - (mine % 4 * 2 + yh) * share, 1)
    out_norm[...] = sums[pairs : pairs + 4, :share]
    lane = lax.broadcasted_iota(jnp.int32, extras[0].shape, 1)
    place = lax.broadcasted_iota(jnp.int32, (1, 2 * heads), 1)
    totals = [jnp.zeros((1, 2 * heads), f32) for _ in range(3)]
    for q in range(2):
        for side in range(2):
            value = jnp.sum(
                jnp.where(lane == mine + side * HEAD_DIM, extras[q], 0.0), 1, keepdims=True
            )
            for t in range(3):
                for pair in range(heads // 2):
                    row = t * (heads // 2) + pair
                    head = q * heads + 2 * pair + side
                    totals[t] = totals[t] + jnp.where(place == head, value[row : row + 1], 0.0)
    for t in range(3):
        out_bias[t] = totals[t]


def finish(one, two, norm_back, share):
    rows = one.shape[1]
    hq, fq = (one.shape[2] - EXTRA) // 4, two.shape[2] // 3
    full = pl.BlockSpec(memory_space=VMEM)
    return pl.pallas_call(
        finish_kernel,
        out_shape=(
            jax.ShapeDtypeStruct((4, share), f32),
            jax.ShapeDtypeStruct((3, rows, 2 * hq), f32),
            jax.ShapeDtypeStruct((3, 1, 2 * hq // HEAD_DIM), f32),
            jax.ShapeDtypeStruct((rows, 2 * hq), f32),
            jax.ShapeDtypeStruct((2, rows, 2 * fq), f32),
            jax.ShapeDtypeStruct((rows, 2 * fq), f32),
        ),
        in_specs=[full] * 3,
        out_specs=(full,) * 6,
        compiler_params=pltpu.CompilerParams(vmem_limit_bytes=VMEM_LIMIT),
    )(one, two, norm_back)


def shards(
    tokens, cotangent, norm_params, qkv_weight, qkv_bias, out_weight, gate_up_weight, down_weight
):
    table = jnp.asarray(tables())
    (
        one, second, token_rows, cot_rows, qkv, head_mix, first_sum, unit_two, normed_two,
        stats, norm_table, scale_two,
    ) = forward(
        qkv_weight, out_weight.T, gate_up_weight, down_weight.T, qkv_bias.transpose(0, 2, 1),
        norm_params, tokens, cotangent, table,
    )
    grad_resid, resid_rows, mixed_parts, chip, settled, second_terms = feed_forward(
        normed_two, cot_rows, cotangent, unit_two, scale_two, norm_table, second
    )
    one_back, two_back, norm_back, grad_tokens, mixed = backward(
        one, resid_rows, chip, settled, qkv, head_mix, token_rows, mixed_parts, grad_resid,
        first_sum, stats, table, second_terms, norm_table,
    )
    out_norm, out_qkv, out_bias, out_out, out_gate_up, out_down = finish(
        one_back, two_back, norm_back, norm_params.shape[1]
    )
    return (
        mixed, grad_tokens, out_norm, out_qkv, out_bias.transpose(0, 2, 1), out_out.T,
        out_gate_up, out_down.T,
    )


def solution(mesh):
    grid = Mesh(mesh.devices.reshape(4, 4, 2, 2, 2), GRID)
    placed = (
        P(GRID, None),
        P(GRID, None),
        P(None, GRID),
        P(None, ROWS, "yh"),
        P(None, "yh", ROWS),
        P("yh", ROWS),
        P(None, ROWS, "yh"),
        P("yh", ROWS),
    )
    return jax.shard_map(
        shards,
        mesh=grid,
        in_specs=placed,
        out_specs=(
            P(GRID, None),
            P(GRID, None),
            P(None, GRID),
            P(None, ROWS, "yh"),
            P(None, "yh", ROWS),
            P("yh", ROWS),
            P(None, ROWS, "yh"),
            P("yh", ROWS),
        ),
        check_vma=False,
    )
```

```python
import jax
import jax.numpy as jnp
import numpy as np
from jax import lax
from jax.experimental import pallas as pl
from jax.experimental.pallas import tpu as pltpu
from jax.sharding import Mesh
from jax.sharding import PartitionSpec as P

HEAD_DIM = 64
ROTARY = 16
EPSILON = 1e-05
SCALE = 0.125

GRID = ("z", "x", "yl", "c", "yh")
ROWS = ("z", "x", "yl", "c")
EXTRA = 128

bf16 = jnp.bfloat16
f32 = jnp.float32

MESH = pl.DeviceIdType.MESH
VMEM = pltpu.VMEM
DMA = pltpu.SemaphoreType.DMA
VMEM_LIMIT = 60 * 1024 * 1024


def at_y(k):
    y = (lax.axis_index("yh") * 2 + lax.axis_index("yl") + k) % 4
    return {"yl": y % 2, "yh": y // 2}


def at_z(k):
    return {"z": (lax.axis_index("z") + k) % 4}


def at_x(k):
    return {"x": (lax.axis_index("x") + k) % 4}


def sibling():
    return {"c": 1 - lax.axis_index("c")}


def greet(devices):
    barrier = pltpu.get_barrier_semaphore()
    for device in devices:
        pl.semaphore_signal(barrier, inc=1, device_id=device, device_id_type=MESH)
    pl.semaphore_wait(barrier, len(devices))


def remote(src, dst, sems, index, device):
    send, recv = sems
    return pltpu.make_async_remote_copy(
        src_ref=src,
        dst_ref=dst,
        send_sem=send.at[index],
        recv_sem=recv.at[index],
        device_id=device,
        device_id_type=MESH,
    )


def ring_gather_half(out, top, sems, base):
    here = out.shape[0] // 4
    half = here // 2
    copies = []
    for way, step, block in ((0, 1, 3), (1, -1, 2)):
        copies.append(
            remote(
                out.at[pl.ds(top * half, half)],
                out.at[pl.ds(block * here + top * half, half)],
                sems,
                base + 2 * way + top,
                at_y(step),
            )
        )
        copies[-1].start()
    return copies


def ring_gather_pass(out, halves, sems, base):
    here = out.shape[0] // 4
    half = here // 2
    passed = []
    for way, step, block in ((0, 1, 3), (1, -1, 2)):
        halves[way][way].wait_recv()
        passed.append(
            remote(
                out.at[pl.ds(block * here + way * half, half)],
                out.at[pl.ds(here + way * half, half)],
                sems,
                base + 4 + way,
                at_y(step),
            )
        )
        passed[-1].start()
    return passed


def pair_moves():
    yl, c = lax.axis_index("yl"), lax.axis_index("c")
    return {"yl": c, "c": yl}, {"yl": 1 - c, "c": yl}


def stay_or_go(src, dst, sems, index, device, local_sem):
    yl, c = lax.axis_index("yl"), lax.axis_index("c")

    @pl.when(yl == c)
    def _():
        pltpu.make_async_copy(src, dst, local_sem).start()

    @pl.when(yl != c)
    def _():
        remote(src, dst, sems, index, device).start()


def stay_or_go_wait(src, dst, sems, index, device, local_sem):
    yl, c = lax.axis_index("yl"), lax.axis_index("c")

    @pl.when(yl == c)
    def _():
        pltpu.make_async_copy(src, dst, local_sem).wait()

    @pl.when(yl != c)
    def _():
        copy = remote(src, dst, sems, index, device)
        copy.wait_recv()
        copy.wait_send()


def ring_sum_start(parts, mid, near, sems, base):
    here = parts.shape[0] // 4
    half = here // 2
    copies = []
    for way, step in ((0, 1), (1, -1)):
        copies.append(
            remote(
                parts.at[pl.ds(here + way * half, half)], mid.at[way], sems, base + way, at_y(step)
            )
        )
    for way, step, block in ((0, 1, 2), (1, -1, 3)):
        copies.append(
            remote(
                parts.at[pl.ds(block * here + (1 - way) * half, half)],
                near.at[way],
                sems,
                base + 2 + way,
                at_y(step),
            )
        )
    for copy in copies:
        copy.start()
    return copies


def ring_sum_middle(parts, started, mid, sent, far, sems, base):
    here = parts.shape[0] // 4
    half = here // 2
    copies = []
    for way, step, block in ((0, 1, 2), (1, -1, 3)):
        started[way].wait_recv()
        sent[way] = (
            parts[pl.ds(block * here + way * half, half)].astype(f32) + mid[way].astype(f32)
        ).astype(bf16)
        copies.append(remote(sent.at[way], far.at[way], sems, base + 4 + way, at_y(step)))
        copies[-1].start()
    return copies


def ring_sum_finish(parts, started, middle, far, near):
    half = parts.shape[0] // 8

    def finish(top):
        started[2 + 1 - top].wait_recv()
        middle[top].wait_recv()
        return (
            parts[pl.ds(top * half, half)].astype(f32)
            + far[top].astype(f32)
            + near[1 - top].astype(f32)
        )

    return finish


def tables():
    half = ROTARY // 2
    position = np.arange(256, dtype=np.float32)
    frequency = np.power(np.float32(10000.0), -np.arange(half, dtype=np.float32) * np.float32(2.0 / ROTARY))
    angles = position[:, None] * frequency[None, :].astype(np.float32)
    cosine, sine = np.cos(angles), np.sin(angles)
    own = np.ones((256, 2, HEAD_DIM), np.float32)
    up = np.zeros((256, 2, HEAD_DIM), np.float32)
    down = np.zeros((256, 2, HEAD_DIM), np.float32)
    for head in range(2):
        own[:, head, :half] = cosine
        own[:, head, half:ROTARY] = cosine
        up[:, head, :half] = -sine
        down[:, head, half:ROTARY] = sine
    return np.concatenate([a.reshape(256, 128) for a in (own, up, down)], 1)


def dot(a, b, ca, cb):
    return lax.dot_general(a, b, (((ca,), (cb,)), ((), ())), preferred_element_type=f32)


def turn_heads(value, table, sign):
    own, up, down = table[:, :128], table[:, 128:256], table[:, 256:]
    return value * own + sign * (
        pltpu.roll(value, 120, 1) * up + pltpu.roll(value, 8, 1) * down
    )


def half_of_place(place):
    y = lax.axis_index("yh") * 2 + lax.axis_index("yl")
    return ((y + place % 2 * 2 + place // 2) % 4) // 2


def causal_mask(sequence, here):
    length = 2 * here
    first = half_of_place(2 * sequence)

    def position(dim):
        index = lax.broadcasted_iota(jnp.int32, (length, length), dim)
        return jnp.where(index < here, index + first * here, index - first * here)

    return position(0) >= position(1)


def causal_rows(sequence, here, part):
    sub = here // 2
    shape = (2 * sub, 2 * here)
    first = half_of_place(2 * sequence)
    row = lax.broadcasted_iota(jnp.int32, shape, 0)
    row = jnp.where(row < sub, row + part * sub, row + here - sub + part * sub)
    col = lax.broadcasted_iota(jnp.int32, shape, 1)
    row, col = (
        jnp.where(index < here, index + first * here, index - first * here) for index in (row, col)
    )
    return row >= col


def soft_of(queries, keys, mask):
    scores = dot(queries, keys, 1, 1) * SCALE
    scores = jnp.where(mask, scores, -1000000000.0)
    powers = jnp.exp(scores - jnp.max(scores, -1, keepdims=True))
    return powers * (1.0 / jnp.sum(powers, -1, keepdims=True))


def read_extras(one, first_column, norm_table, bias):
    total = None
    for group in range(one.shape[0] // 128):
        block = one[pl.ds(group * 128, 128), pl.ds(first_column, 128)].astype(f32)
        block = block[0:32] + block[32:64] + block[64:96] + block[96:128]
        norm_table[:, pl.ds(group * 128, 128)] = block[12:16] + block[16:20]
        total = block[0:12] if total is None else total + block[0:12]
    bias[...] = total


class Reduce:
    def __init__(self, view, rows, rings):
        self.view, self.rows, self.rings = view, rows, rings
        self.done, self.got = [], {}

    def send(self, name, stage, half, way, src, dst, index):
        step = (1, -1)[way]
        device = at_z(step) if (half == 0) == (stage == 0) else at_x(step)
        copy = remote(src, dst, self.rings[stage][3], half * 6 + index * 2 + way, device)
        copy.start()
        self.done.append(copy)
        self.got[name, stage, half, way] = copy

    def begin(self, stage):
        mid, _, near, _ = self.rings[stage]
        for half in range(2):
            for way in range(2):
                src = self.view(stage, half, 2, way)
                self.send("mid", stage, half, way, src, mid.at[half, way], 0)
        for half in range(2):
            for way in range(2):
                src = self.view(stage, half, (1, 3)[way], 1 - way)
                self.send("near", stage, half, way, src, near.at[half, way], 1)

    def combine(self, stage):
        mid, far = self.rings[stage][:2]
        for half in range(2):
            for way in range(2):
                self.got["mid", stage, half, way].wait_recv()
                ref = self.view(stage, half, (1, 3)[way], way)
                ref[...] = (ref[...].astype(f32) + mid[half, way].astype(f32)).astype(bf16)
                self.send("far", stage, half, way, ref, far.at[half, way], 2)

    def settle(self, stage, out=None):
        far, near = self.rings[stage][1:3]
        piece = self.rows // 2
        for half in range(2):
            for part in range(2):
                self.got["far", stage, half, part].wait_recv()
                self.got["near", stage, half, 1 - part].wait_recv()
                ref = self.view(stage, half, 0, part)
                total = (
                    ref[...].astype(f32)
                    + far[half, part].astype(f32)
                    + near[half, 1 - part].astype(f32)
                ).astype(bf16)
                if out is None:
                    ref[...] = total
                else:
                    out[half, pl.ds(part * piece, piece)] = total

    def close(self):
        for copy in self.done:
            copy.wait_send()


def ring_buffers(stage, piece, wide):
    dims = (2, 2, 4, piece, wide) if stage == 0 else (2, 2, piece, wide)
    return [VMEM(dims, bf16)] * 3 + [DMA((12,))] * 2


def feed_forward_kernel(
    normed_in, cot_in, cotangent_in, unit_in, weights, scale, norm_table,
    resid_out, spread_out, mixed_out, chip, settled, sums,
    normed, cot_rows, cotangent, unit, resid, spread, mixed_parts, held, pair, hidden, normed_t, cot_t, parts, sib, mid, sent, far, near,
    *rest,
):
    rings = [rest[5 * k : 5 * k + 5] for k in range(2)]
    rings = [(mid, far, near, (send, recv)) for mid, far, near, send, recv in rings]
    in_sem, save_sem, load_sem, store_sem, core_send, core_recv, y_send, y_recv = rest[10:]
    columns, width = held.shape[3] // 3, normed.shape[1]
    wide = 256
    rows = sib.shape[1]
    sub = cotangent.shape[0] // 2
    z, x, c = lax.axis_index("z"), lax.axis_index("x"), lax.axis_index("c")
    y_sems, core_sems = (y_send, y_recv), (core_send, core_recv)
    whole, left = columns // wide, columns % wide
    all_pair, all_hidden = pl.ds(0, 2 * columns), pl.ds(2 * columns, columns)
    groups = tuple(pl.ds(which * columns, columns) for which in range(3))

    def load(k, which, size):
        start = pl.multiple_of(which * columns + k * wide, 128)
        cut = pl.ds(start, size)
        return pltpu.make_async_copy(
            weights.at[:, :, :, cut], held.at[:, :, :, cut], load_sem.at[k, which]
        )

    ins = [
        pltpu.make_async_copy(src, dst, in_sem.at[k])
        for k, (src, dst) in enumerate(
            ((normed_in, normed), (cot_in, cot_rows), (cotangent_in, cotangent), (unit_in, unit))
        )
    ]
    ins[0].start()
    ins[1].start()
    saves = []

    def save(src, dst):
        saves.append(pltpu.make_async_copy(src, dst, save_sem.at[len(saves)]))
        saves[-1].start()

    def load_tile(k, size):
        for which in range(3):
            load(k, which, size).start()

    load_tile(0, wide)
    load_tile(1, wide)
    ins[0].wait()
    ins[1].wait()

    def flip(k, _):
        rng = pl.ds(pl.multiple_of(k * wide, wide), wide)
        normed_t[rng] = normed[:, rng].T
        cot_t[rng] = cot_rows[:, rng].T
        return 0

    lax.fori_loop(0, width // wide, flip, 0)
    greet([at_z(1), at_z(3), at_x(1), at_x(3), at_y(1), at_y(3), sibling()])

    tall = width // 4

    def tile(k, cut):
        return k, slice(None), slice(None), cut

    def ahead(part, k, size):
        these = pl.ds(4 * part * sub, 4 * sub)

        def cut(which):
            return pl.ds(pl.multiple_of(which * columns + k * wide, 128), size)

        def weight(which):
            return held[:, :, :, cut(which)].reshape(width, size)

        if part == 0:
            if size == wide:
                pl.when(k + 2 < whole)(lambda: load_tile(k + 2, wide))
                if left:
                    pl.when(k + 2 == whole)(lambda: load_tile(whole, left))
            for which in range(3):
                load(k, which, size).wait()
        gate = dot(normed[these], weight(0), 1, 0)
        up = dot(normed[these], weight(1), 1, 0)
        grad_hidden = dot(cot_rows[these], weight(2), 1, 0)
        sigmoid = jax.nn.sigmoid(gate)
        activated = gate * sigmoid
        hidden[these, cut(0)] = (activated * up).astype(bf16)
        pair[these, cut(0)] = (
            grad_hidden * up * sigmoid * (1.0 + gate * (1.0 - sigmoid))
        ).astype(bf16)
        pair[these, cut(1)] = (grad_hidden * activated).astype(bf16)
        return 0

    part_subs = [parts.at[pl.ds(4 * k * sub, 4 * sub)] for k in range(2)]
    started, middle, halves, passed = [], [], [], []

    def ring_middle(part):
        middle.append(
            ring_sum_middle(
                part_subs[part], started[part], mid.at[part], sent.at[part], far.at[part],
                y_sems, 6 * part,
            )
        )

    for part in range(2):
        lax.fori_loop(0, whole, lambda k, _: ahead(part, k, wide), 0)
        if left:
            ahead(part, whole, left)
        if part == 1:
            ring_middle(0)

        def second_back(k, _):
            rng = pl.ds(pl.multiple_of(k * tall, tall), tall)
            weight = held[tile(k, all_pair)].reshape(tall, 2 * columns)
            these = pl.ds(4 * part * sub, 4 * sub)
            parts[these, rng] = dot(pair[these], weight, 1, 1).astype(bf16)
            return 0

        lax.fori_loop(0, 4, second_back, 0)
        started.append(
            ring_sum_start(part_subs[part], mid.at[part], near.at[part], y_sems, 6 * part)
        )

    def to_core(block, which):
        theirs = pl.ds(pl.multiple_of((1 - c) * rows, rows), rows)
        return remote(
            held.at[block // 4, block % 4, theirs, groups[which]],
            sib.at[block, :, groups[which]],
            core_sems,
            block + 16 * which,
            sibling(),
        )

    ours = pl.ds(pl.multiple_of(c * rows, rows), rows)

    def store(block):
        return pltpu.make_async_copy(
            held.at[block // 4, block % 4, ours, groups[2]], chip.at[block], store_sem.at[block]
        )

    def core_sum(block, which):
        to_core(block, which).wait_recv()
        mine = (block // 4, block % 4, ours, groups[which])
        held[mine] = (
            held[mine].astype(f32) + sib[block, :, groups[which]].astype(f32)
        ).astype(bf16)
        if which == 2:
            store(block).start()

    def weights_back(which, k):
        rng = pl.ds(pl.multiple_of(k * tall, tall), tall)
        if which < 2:
            grad = dot(normed_t[rng], pair[:, groups[which]], 1, 0)
        else:
            grad = dot(cot_t[rng], hidden[...], 1, 0)
        held[tile(k, groups[which])] = grad.astype(bf16).reshape(4, 2 * rows, columns)
        for block in range(4):
            to_core(4 * k + block, which).start()

        @pl.when(k > 1)
        def _():
            for block in range(4):
                core_sum(4 * k - 8 + block, which)

        return 0

    def all_weights(which):
        lax.fori_loop(0, 4, lambda k, _: weights_back(which, k), 0)

    def last_sums(which):
        for block in range(8, 16):
            core_sum(block, which)

    def settle_rows(part):
        finish = ring_sum_finish(
            part_subs[part], started[part], middle[part], far.at[part], near.at[part]
        )
        here = pl.ds(part * sub, sub)
        total = jnp.concatenate([finish(0), finish(1)], 0)
        unit_rows = unit[here]
        incoming = total * norm_table[2:3]
        result = cotangent[here].astype(f32) + scale[here] * (
            incoming
            - jnp.mean(incoming, -1, keepdims=True)
            - unit_rows * jnp.mean(incoming * unit_rows, -1, keepdims=True)
        )
        resid[here] = result
        spread[pl.ds(4 * part * sub, sub)] = result.astype(bf16)
        out = spread.at[pl.ds(4 * part * sub, 4 * sub)]
        halves.append([ring_gather_half(out, top, y_sems, 12 + 6 * part) for top in range(2)])
        both = jnp.concatenate(
            [
                jnp.sum(total * unit_rows, 0, keepdims=True),
                jnp.sum(total, 0, keepdims=True),
            ],
            0,
        )
        sums[...] = both if part == 0 else sums[...] + both

    def gather_pass(part):
        out = spread.at[pl.ds(4 * part * sub, 4 * sub)]
        passed.append(ring_gather_pass(out, halves[part], y_sems, 12 + 6 * part))

    def view_of(cols):
        def view(stage, half, d, part):
            start = c * rows + half * (rows // 2) + part * (rows // 4)
            rng = pl.ds(pl.multiple_of(start, rows // 4), rows // 4)
            if half == 0:
                return held.at[(z + d) % 4, :, rng, cols]
            return held.at[:, (x + d) % 4, rng, cols]

        return view

    gate_sums, up_sums = (
        Reduce(view_of(groups[which]), rows // 2, {0: rings[which]}) for which in range(2)
    )
    def mix(k, _):
        rng = pl.ds(pl.multiple_of(k * tall, tall), tall)
        weight = held[tile(k, all_hidden)].reshape(tall, columns)
        value = dot(hidden[...], weight, 1, 1).astype(bf16)
        for part in range(2):
            for block in range(4):
                start = (part * 4 + block) * sub
                mixed_parts[pl.ds((2 * block + part) * sub, sub), rng] = value[start : start + sub]
        return 0

    ins[2].start()
    ins[3].start()
    all_weights(0)
    ring_middle(1)
    last_sums(0)
    gate_sums.begin(0)
    ins[2].wait()
    ins[3].wait()
    settle_rows(0)
    all_weights(1)
    gate_sums.combine(0)
    last_sums(1)
    up_sums.begin(0)
    gather_pass(0)
    lax.fori_loop(0, 4, mix, 0)
    save(mixed_parts, mixed_out)
    settle_rows(1)
    save(resid, resid_out)
    all_weights(2)
    up_sums.combine(0)
    gather_pass(1)
    last_sums(2)
    gate_sums.settle(0)
    up_sums.settle(0)
    top_rows = pl.ds(pl.multiple_of(c * rows, rows // 2), rows // 2)
    low_rows = pl.ds(pl.multiple_of(c * rows + rows // 2, rows // 2), rows // 2)
    keep = [
        pltpu.make_async_copy(held.at[z, :, top_rows, all_pair], settled.at[0], store_sem.at[16]),
        pltpu.make_async_copy(held.at[:, x, low_rows, all_pair], settled.at[1], store_sem.at[17]),
    ]
    for copy in keep:
        copy.start()

    def drain(block, _):
        for which in range(3):
            to_core(block, which).wait_send()
        store(block).wait()
        return 0

    lax.fori_loop(0, 16, drain, 0)
    for k in range(2):
        for copy in passed[k] + [halves[k][1][0], halves[k][0][1]]:
            copy.wait_recv()
        these = pl.ds(4 * k * sub, 4 * sub)
        save(spread.at[these], spread_out.at[these])
        for copy in started[k] + middle[k] + halves[k][0] + halves[k][1] + passed[k]:
            copy.wait_send()
    gate_sums.close()
    up_sums.close()
    for copy in keep + saves:
        copy.wait()


def feed_forward(normed, cot_rows, cotangent, unit, scale, norm_table, weights):
    tokens, width = normed.shape
    here = cotangent.shape[0]
    columns = weights.shape[1] // 3
    rows = width // 32
    full = pl.BlockSpec(memory_space=VMEM)
    anywhere = pl.BlockSpec(memory_space=pl.ANY)
    tiles = -(-columns // 256)
    kept = (
        ((tokens, width), bf16),
        ((tokens, width), bf16),
        ((here, width), bf16),
        ((here, width), f32),
        ((here, width), f32),
        ((tokens, width), bf16),
        ((tokens, width), bf16),
    )
    return pl.pallas_call(
        feed_forward_kernel,
        out_shape=(
            jax.ShapeDtypeStruct((here, width), f32),
            jax.ShapeDtypeStruct((tokens, width), bf16),
            jax.ShapeDtypeStruct((tokens, width), bf16),
            jax.ShapeDtypeStruct((16, rows, columns), bf16),
            jax.ShapeDtypeStruct((2, 4, rows // 2, 2 * columns), bf16),
            jax.ShapeDtypeStruct((2, width), f32),
        ),
        in_specs=[anywhere] * 5 + [full] * 2,
        out_specs=(anywhere,) * 5 + (full,),
        scratch_shapes=[VMEM(dims, dtype) for dims, dtype in kept]
        + [
            VMEM((4, 4, 2 * rows, 3 * columns), bf16),
            VMEM((tokens, 2 * columns), bf16),
            VMEM((tokens, columns), bf16),
            VMEM((width, tokens), bf16),
            VMEM((width, tokens), bf16),
            VMEM((tokens, width), bf16),
            VMEM((16, rows, 3 * columns), bf16),
        ]
        + [VMEM((2, 2, here // 4, width), bf16)] * 4
        + ring_buffers(0, rows // 4, columns) * 2
        + [DMA((4,)), DMA((4,))]
        + [DMA((tiles, 3)), DMA((18,)), DMA((48,)), DMA((48,)), DMA((24,)), DMA((24,))],
        compiler_params=pltpu.CompilerParams(
            collective_id=2, has_side_effects=True, vmem_limit_bytes=VMEM_LIMIT
        ),
    )(
        normed, cot_rows, cotangent, unit, weights.reshape(4, 4, 2 * rows, 3 * columns), scale,
        norm_table,
    )


def cube():
    yl, c, yh = lax.axis_index("yl"), lax.axis_index("c"), lax.axis_index("yh")
    return [
        {"yl": (yl + a) % 2, "c": (c + b) % 2, "yh": (yh + d) % 2}
        for a in range(2)
        for b in range(2)
        for d in range(2)
        if a + b + d
    ]


class Spread:
    def __init__(self, out, rows, sems, core_sems):
        self.out, self.rows, self.sems, self.core_sems = out, rows, sems, core_sems
        self.done, self.core = [], []

    def cut(self, half, df, dg, part=None):
        z, x = lax.axis_index("z"), lax.axis_index("x")
        dz, dx = (df, dg) if half == 0 else (dg, df)
        place = ((z + dz) % 4) * 4 + (x + dx) % 4
        start = (place * 4 + lax.axis_index("c") * 2 + half) * self.rows
        piece = self.rows // 2
        if part is None:
            return self.out.at[pl.ds(pl.multiple_of(start, self.rows), self.rows)]
        return self.out.at[pl.ds(pl.multiple_of(start + part * piece, piece), piece)]

    def index(self, half, df, dg, part):
        return ((half * 4 + df % 4) * 4 + dg % 4) * 2 + part

    def push(self, half, df, dg, axis, step, part):
        device = at_z(step) if (half == 0) == (axis == 0) else at_x(step)
        to = (df - step, dg) if axis == 0 else (df, dg - step)
        ref = self.cut(half, df, dg, part)
        copy = remote(ref, ref, self.sems, self.index(half, *to, part), device)
        copy.start()
        self.done.append(copy)

    def arrived(self, half, df, dg, part):
        ref = self.cut(half, df, dg, part)
        remote(ref, ref, self.sems, self.index(half, df, dg, part), at_z(1)).wait_recv()

    def to_sibling(self, half, df, dg):
        ref = self.cut(half, df, dg)
        copy = remote(ref, ref, self.core_sems, (half * 4 + df % 4) * 4 + dg % 4, sibling())
        copy.start()
        self.done.append(copy)
        self.core.append(copy)

    def push_all(self, half, df, dg, axis):
        for part in range(2):
            self.push(half, df, dg, axis, 1, part)
            self.push(half, df, dg, axis, -1, 1 - part)

    def start(self):
        for axis in range(2):
            for half in range(2):
                self.push_all(half, 0, 0, axis)
        for half in range(2):
            self.to_sibling(half, 0, 0)

    def first_pass(self):
        for half in range(2):
            self.arrived(half, 3, 0, 0)
            self.push(half, 3, 0, 0, 1, 0)
            self.arrived(half, 1, 0, 1)
            self.push(half, 1, 0, 0, -1, 1)

    def first_rest(self):
        for half in range(2):
            self.arrived(half, 3, 0, 1)
            self.arrived(half, 1, 0, 0)
            for df in (3, 1):
                self.push_all(half, df, 0, 1)
                self.to_sibling(half, df, 0)

    def first_far(self):
        for half in range(2):
            self.arrived(half, 2, 0, 0)
            self.arrived(half, 2, 0, 1)
            self.push_all(half, 2, 0, 1)
            self.to_sibling(half, 2, 0)

    def second_pass(self, df):
        for half in range(2):
            self.arrived(half, df, 3, 0)
            self.push(half, df, 3, 1, 1, 0)
            self.arrived(half, df, 1, 1)
            self.push(half, df, 1, 1, -1, 1)
        for half in range(2):
            self.arrived(half, df, 3, 1)
            self.to_sibling(half, df, 3)
            self.arrived(half, df, 1, 0)
            self.to_sibling(half, df, 1)

    def second_far(self, df):
        for half in range(2):
            for part in range(2):
                self.arrived(half, df, 2, part)
            self.to_sibling(half, df, 2)

    def land(self):
        for copy in self.core:
            copy.wait_recv()

    def close(self):
        for copy in self.done:
            copy.wait_send()


def extra_rows(qkv_bias, norm_params, q, rows):
    z, x = lax.axis_index("z"), lax.axis_index("x")
    yl, c, yh = lax.axis_index("yl"), lax.axis_index("c"), lax.axis_index("yh")
    mine = ((z * 4 + x) * 2 + yl) * 2 + c
    lane = lax.broadcasted_iota(jnp.int32, (1, EXTRA), 1)
    heads = qkv_bias.shape[2] // 2
    pieces = []
    for t in range(3):
        for pair in range(heads // 2):
            row = jnp.zeros((1, EXTRA), f32)
            for side in range(2):
                head = q * heads + 2 * pair + side
                value = qkv_bias[t, :, head : head + 1].astype(f32)
                row = row + jnp.where(lane == mine + side * HEAD_DIM, value, 0.0)
            pieces.append(row)
    share = norm_params.shape[1]
    high = norm_params[...].astype(bf16).astype(f32)
    norm = jnp.concatenate([high, norm_params[...] - high], 0)
    norm = jnp.concatenate([norm, jnp.zeros((norm.shape[0], EXTRA - share), f32)], 1)
    norm = pltpu.roll(norm, (mine % 4 * 2 + yh) * share, 1)
    used = len(pieces) + norm.shape[0]
    pieces += [norm, jnp.zeros((rows - used, EXTRA), f32)]
    return jnp.concatenate(pieces, 0).astype(bf16)


def forward_kernel(
    qkv_weight, out_weight, gate_up_weight, down_weight, qkv_bias, norm_params, tokens, cotangent,
    table,
    one_out, two, token_out, cot_out, qkv_out, mix_out, summed_out, unit_out, normed_out,
    stats, norm_table, scale,
    token_rows, cot_rows, qkv, head_mix, summed, unit, normed_two,
    one_q, two_q, one, norm_in, bias, normed, parts, mid, sent, far, near,
    pair_send, pair_recv, local_sem, save_sem, y_send, y_recv,
    send_one, recv_one, core_send_one, core_recv_one,
    send_two, recv_two, core_send_two, core_recv_two,
):
    z, x = lax.axis_index("z"), lax.axis_index("x")
    yl, c, yh = lax.axis_index("yl"), lax.axis_index("c"), lax.axis_index("yh")
    rows, here = one_q.shape[1], tokens.shape[0]
    hq, fq = qkv_weight.shape[2] // 2, gate_up_weight.shape[2] // 2
    pair_sems, y_sems = (pair_send, pair_recv), (y_send, y_recv)
    for q in range(2):
        for group in range(2):
            for t in range(3):
                to, start = (group * 3 + t) * hq // 2, q * hq + group * hq // 2
                one_q[q, :, to : to + hq // 2] = qkv_weight[t, :, start : start + hq // 2]
        one_q[q, :, 3 * hq : 3 * hq + EXTRA] = extra_rows(qkv_bias, norm_params, q, rows)
        one_q[q, :, 3 * hq + EXTRA :] = out_weight[:, q * hq : (q + 1) * hq]
    token_rows[pl.ds(0, here)] = tokens[...]
    greet([at_z(1), at_z(3), at_x(1), at_x(3)] + cube())

    same, cross = pair_moves()
    mine = pl.ds(pl.multiple_of((z * 4 + x) * 4 * rows + (yl * 2 + c) * rows, rows), rows)
    moves = [
        (one_q.at[c], one.at[mine], 0, same),
        (one_q.at[1 - c], one.at[mine], 1, cross),
        (two_q.at[c], two.at[mine], 2, same),
        (two_q.at[1 - c], two.at[mine], 3, cross),
    ]

    def launch(k):
        src, dst, index, device = moves[k]
        if device is same:
            stay_or_go(src, dst, pair_sems, index, device, local_sem.at[index // 2])
        else:
            remote(src, dst, pair_sems, index, device).start()

    def land(k):
        src, dst, index, device = moves[k]
        if device is same:
            stay_or_go_wait(src, dst, pair_sems, index, device, local_sem.at[index // 2])
        else:
            copy = remote(src, dst, pair_sems, index, device)
            copy.wait_recv()
            copy.wait_send()

    norm_moves = [
        remote(
            one_q.at[0, :, pl.ds(3 * hq, EXTRA)],
            norm_in.at[c],
            pair_sems,
            4 + which,
            {"yl": target["yl"], "c": target["c"], "yh": 1 - yh},
        )
        for which, target in enumerate((same, cross))
    ]
    launch(0)
    launch(1)
    for move in norm_moves:
        move.start()
    token_halves = [ring_gather_half(token_rows, top, y_sems, 0) for top in range(2)]
    for q in range(2):
        for t in range(2):
            two_q[q, :, t * fq : (t + 1) * fq] = gate_up_weight[t, :, q * fq : (q + 1) * fq]
        two_q[q, :, 2 * fq :] = down_weight[:, q * fq : (q + 1) * fq]
    sub = here // 2
    for k in range(2):
        cot_rows[pl.ds(4 * k * sub, sub)] = cotangent[pl.ds(k * sub, sub)]
    land(0)
    land(1)
    for move in norm_moves:
        move.wait_recv()
    own = (z * 4 + x) * 4 + 2 * c
    for core in range(2):
        block = pl.ds(pl.multiple_of((own + core) * rows, rows), rows)
        came = norm_in[core].astype(f32)
        place = lax.broadcasted_iota(jnp.int32, came.shape, 0)
        held = one[block, pl.ds(3 * hq, EXTRA)].astype(f32)
        one[block, pl.ds(3 * hq, EXTRA)] = (
            held + jnp.where((place >= 12) & (place < 20), came, 0.0)
        ).astype(bf16)
    first = Spread(one, rows, (send_one, recv_one), (core_send_one, core_recv_one))
    second = Spread(two, rows, (send_two, recv_two), (core_send_two, core_recv_two))
    first.start()
    launch(2)
    launch(3)
    first.first_pass()
    first.first_rest()
    token_passed = ring_gather_pass(token_rows, token_halves, y_sems, 0)
    first.second_pass(0)
    first.first_far()
    first.second_pass(3)
    first.second_pass(1)
    first.second_pass(2)
    for df in (0, 3, 1, 2):
        first.second_far(df)
    land(2)
    land(3)
    second.start()
    for copy in token_passed + [token_halves[1][0], token_halves[0][1]]:
        copy.wait_recv()
    cot_subs = [cot_rows.at[pl.ds(4 * k * sub, 4 * sub)] for k in range(2)]
    cot_halves = [
        [ring_gather_half(cot_subs[k], top, y_sems, 6 + 6 * k) for top in range(2)]
        for k in range(2)
    ]
    first.land()
    keep = pltpu.make_async_copy(one, one_out, local_sem.at[2])
    keep.start()
    saves = []

    def save(src, dst):
        saves.append(pltpu.make_async_copy(src, dst, save_sem.at[len(saves)]))
        saves[-1].start()

    save(token_rows, token_out)

    read_extras(one, 3 * hq, norm_table, bias)

    def norm_rows(k, _):
        rng = pl.ds(pl.multiple_of(k * here, here), here)
        values = token_rows[rng].astype(f32)
        mean = jnp.mean(values, -1, keepdims=True)
        centered = values - mean
        inverse = lax.rsqrt(jnp.mean(centered * centered, -1, keepdims=True) + EPSILON)
        stats[0, rng] = mean
        stats[1, rng] = inverse
        normed[rng] = (centered * inverse * norm_table[0:1] + norm_table[1:2]).astype(bf16)
        return 0

    lax.fori_loop(0, 4, norm_rows, 0)
    second.first_pass()
    wide = 256

    def project(k, _):
        cols = pl.ds(pl.multiple_of(k * wide, wide), wide)
        value = dot(normed[...], one[:, cols], 1, 0)
        row = k % 3 * (hq // 128) + k // 3 * 2
        value = value + jnp.concatenate([bias[pl.ds(row, 1)], bias[pl.ds(row + 1, 1)]], 1)

        @pl.when(k % 3 < 2)
        def _():
            for place in range(4):
                rng = pl.ds(place * here, here)
                turn = table[pl.ds(pl.multiple_of(half_of_place(place) * here, here), here)]
                for pair in range(wide // 128):
                    qkv[rng, pl.ds(pl.multiple_of(k * wide + pair * 128, 128), 128)] = turn_heads(
                        value[place * here : (place + 1) * here, pair * 128 : (pair + 1) * 128],
                        turn,
                        1.0,
                    ).astype(bf16)

        @pl.when(k % 3 == 2)
        def _():
            qkv[:, cols] = value.astype(bf16)

        return 0

    lax.fori_loop(0, 3 * hq // wide, project, 0)
    save(qkv, qkv_out)
    second.first_rest()
    cot_passed = [
        ring_gather_pass(cot_subs[k], cot_halves[k], y_sems, 6 + 6 * k) for k in range(2)
    ]
    part_subs = [parts.at[pl.ds(4 * k * sub, 4 * sub)] for k in range(2)]
    started, middle = [], []
    for part in range(2):
        def attend(sequence, _):
            mask = causal_rows(sequence, here, part)
            rng = pl.ds(pl.multiple_of(sequence * 2 * here, 2 * here), 2 * here)
            lower = pl.ds(pl.multiple_of(sequence * 2 * here + part * sub, sub), sub)
            upper = pl.ds(pl.multiple_of(sequence * 2 * here + here + part * sub, sub), sub)

            def heads(k, _):
                def cols(t):
                    start = k // 2 * (3 * hq // 2) + t * (hq // 2) + k % 2 * 128
                    return pl.ds(pl.multiple_of(start, 128), 128)

                q = jnp.concatenate([qkv[lower, cols(0)], qkv[upper, cols(0)]], 0)
                key, value = qkv[rng, cols(1)], qkv[rng, cols(2)]
                mixes = []
                for head in range(2):
                    cut = slice(head * HEAD_DIM, (head + 1) * HEAD_DIM)
                    soft = soft_of(q[:, cut], key[:, cut], mask).astype(bf16)
                    mixes.append(dot(soft, value[:, cut], 1, 0))
                mixed = jnp.concatenate(mixes, 1).astype(bf16)
                there = pl.ds(pl.multiple_of(k * 128, 128), 128)
                head_mix[lower, there] = mixed[:sub]
                head_mix[upper, there] = mixed[sub:]
                return 0

            lax.fori_loop(0, hq // 128, heads, 0, unroll=2)
            return 0

        lax.fori_loop(0, 2, attend, 0)
        mix = jnp.concatenate(
            [head_mix[pl.ds(k * here + part * sub, sub)] for k in range(4)], 0
        )

        def out_project(k, _):
            rng = pl.ds(pl.multiple_of(k * wide, wide), wide)
            parts[pl.ds(4 * part * sub, 4 * sub), rng] = dot(
                mix, one[rng, pl.ds(3 * hq + EXTRA, hq)], 1, 1
            ).astype(bf16)
            return 0

        lax.fori_loop(0, one.shape[0] // wide, out_project, 0)
        started.append(
            ring_sum_start(part_subs[part], mid.at[part], near.at[part], y_sems, 18 + 6 * part)
        )
        if part == 0:
            second.second_pass(0)
            second.first_far()
    save(head_mix, mix_out)
    for k in range(2):
        for copy in cot_passed[k] + [cot_halves[k][1][0], cot_halves[k][0][1]]:
            copy.wait_recv()
    save(cot_rows, cot_out)
    second.second_pass(3)
    for part in range(2):
        middle.append(
            ring_sum_middle(
                part_subs[part], started[part], mid.at[part], sent.at[part], far.at[part],
                y_sems, 18 + 6 * part,
            )
        )
    second.second_pass(1)
    halves = []
    for part in range(2):
        finish = ring_sum_finish(
            part_subs[part], started[part], middle[part], far.at[part], near.at[part]
        )
        total = jnp.concatenate([finish(0), finish(1)], 0)
        rng = pl.ds(part * sub, sub)
        total = total + tokens[rng].astype(f32)
        summed[rng] = total
        centered = total - jnp.mean(total, -1, keepdims=True)
        inverse = lax.rsqrt(jnp.mean(centered * centered, -1, keepdims=True) + EPSILON)
        unit_rows = centered * inverse
        unit[rng] = unit_rows
        scale[rng] = inverse
        normed_two[pl.ds(4 * part * sub, sub)] = (
            unit_rows * norm_table[2:3] + norm_table[3:4]
        ).astype(bf16)
        out = normed_two.at[pl.ds(4 * part * sub, 4 * sub)]
        halves.append([ring_gather_half(out, top, y_sems, 30 + 6 * part) for top in range(2)])
    save(summed, summed_out)
    save(unit, unit_out)
    second.second_pass(2)
    passed = [
        ring_gather_pass(
            normed_two.at[pl.ds(4 * k * sub, 4 * sub)], halves[k], y_sems, 30 + 6 * k
        )
        for k in range(2)
    ]
    for df in (0, 3, 1, 2):
        second.second_far(df)
    for k in range(2):
        for copy in passed[k] + [halves[k][1][0], halves[k][0][1]]:
            copy.wait_recv()
        these = pl.ds(4 * k * sub, 4 * sub)
        save(normed_two.at[these], normed_out.at[these])
    second.land()
    keep.wait()
    for copy in saves:
        copy.wait()
    for move in norm_moves:
        move.wait_send()
    gathers = token_halves + cot_halves[0] + cot_halves[1] + halves[0] + halves[1]
    for copies in gathers + [token_passed] + cot_passed + started + middle + passed:
        for copy in copies:
            copy.wait_send()
    first.close()
    second.close()


def forward(
    qkv_weight, out_weight, gate_up_weight, down_weight, qkv_bias, norm_params, tokens, cotangent,
    table,
):
    here, width = tokens.shape
    rows = qkv_weight.shape[1]
    hq, fq = qkv_weight.shape[2] // 2, gate_up_weight.shape[2] // 2
    full = pl.BlockSpec(memory_space=VMEM)
    anywhere = pl.BlockSpec(memory_space=pl.ANY)
    one_wide, two_wide = 4 * hq + EXTRA, 3 * fq
    kept = (
        ((4 * here, width), bf16),
        ((4 * here, width), bf16),
        ((4 * here, 3 * hq), bf16),
        ((4 * here, hq), bf16),
        ((here, width), f32),
        ((here, width), f32),
        ((4 * here, width), bf16),
    )

    def shape(*dims, dtype=bf16):
        return jax.ShapeDtypeStruct(dims, dtype)

    return pl.pallas_call(
        forward_kernel,
        out_shape=(
            shape(width, one_wide),
            shape(width, two_wide),
            *(shape(*dims, dtype=dtype) for dims, dtype in kept),
            shape(2, 4 * here, 1, dtype=f32),
            shape(4, width, dtype=f32),
            shape(here, 1, dtype=f32),
        ),
        in_specs=[full] * 9,
        out_specs=(anywhere,) * 9 + (full,) * 3,
        scratch_shapes=[VMEM(dims, dtype) for dims, dtype in kept]
        + [
            VMEM((2, rows, one_wide), bf16),
            VMEM((2, rows, two_wide), bf16),
            VMEM((width, one_wide), bf16),
            VMEM((2, rows, EXTRA), bf16),
            VMEM((12, 128), f32),
            VMEM((4 * here, width), bf16),
            VMEM((4 * here, width), bf16),
        ]
        + [VMEM((2, 2, here // 4, width), bf16)] * 4
        + [
            DMA((6,)), DMA((6,)), DMA((3,)), DMA((9,)), DMA((42,)), DMA((42,)),
            DMA((64,)), DMA((64,)), DMA((32,)), DMA((32,)),
            DMA((64,)), DMA((64,)), DMA((32,)), DMA((32,)),
        ],
        compiler_params=pltpu.CompilerParams(
            collective_id=0, has_side_effects=True, vmem_limit_bytes=VMEM_LIMIT
        ),
    )(
        qkv_weight, out_weight, gate_up_weight, down_weight, qkv_bias, norm_params, tokens,
        cotangent, table,
    )


def backward_kernel(
    one, resid_rows, chip, settled, qkv_in, mix_in, token_in, mixed_in, resid_in, sum_in,
    stats, table, second_terms, norm_table,
    result_one, result_two, norm_back, grad_out, mixed_out,
    qkv, head_mix, token_rows, mixed_parts, resid, first_sum, grad_tokens, mixed,
    held, spare, grad_mix, grad_proj, part_sums, sib, blocks, pair_sums,
    *rest,
):
    rings = [rest[5 * k : 5 * k + 5] for k in range(9)]
    rings = [(mid, far, near, (send, recv)) for mid, far, near, send, recv in rings]
    (
        packed_one, packed_two, ymid, ysent, yfar, ynear,
        load_sem, in_sem, save_sem, block_sem, core_send, core_recv, pair_send, pair_recv, local_sem, y_send, y_recv,
    ) = rest[45:]
    z, x = lax.axis_index("z"), lax.axis_index("x")
    yl, c, yh = lax.axis_index("yl"), lax.axis_index("c"), lax.axis_index("yh")
    here = resid.shape[0]
    rows = result_one.shape[1]
    hq, fq = head_mix.shape[1], result_two.shape[2] // 3
    early, late = pair_sums.shape[3], blocks.shape[3]
    sub = here // 2
    width = held.shape[0]
    core_sems, pair_sems, y_sems = (core_send, core_recv), (pair_send, pair_recv), (y_send, y_recv)
    wide = 256
    out_start = 3 * hq + EXTRA
    group = 3 * hq // 2
    columns = (pl.ds(0, group), pl.ds(out_start, hq), pl.ds(group, group + EXTRA))

    def place_of(dz, dx):
        return ((z + dz) % 4) * 4 + (x + dx) % 4

    loads = [
        pltpu.make_async_copy(
            one.at[:, pl.ds(start, size)], held.at[:, pl.ds(start, size)], load_sem.at[k]
        )
        for k, (start, size) in enumerate(((out_start, hq), (0, 3 * hq)))
    ]
    loads.append(pltpu.make_async_copy(resid_rows, spare, load_sem.at[2]))
    loads.append(pltpu.make_async_copy(settled, pair_sums, load_sem.at[3]))
    block_loads = [
        pltpu.make_async_copy(
            chip.at[place_of(dz, dx)], blocks.at[dz, dx], block_sem.at[dz * 4 + dx]
        )
        for dz in range(4)
        for dx in range(4)
    ]
    ins = [
        pltpu.make_async_copy(src, dst, in_sem.at[k])
        for k, (src, dst) in enumerate(
            (
                (mixed_in, mixed_parts), (mix_in, head_mix), (qkv_in, qkv),
                (token_in, token_rows), (resid_in, resid), (sum_in, first_sum),
            )
        )
    ]
    loads[3].start()
    ins[0].start()
    loads[2].start()
    loads[0].start()
    ins[1].start()
    for load in block_loads:
        load.start()
    greet([at_z(1), at_z(3), at_x(1), at_x(3)] + cube())
    ins[0].wait()
    mixed_started = ring_sum_start(mixed_parts, ymid.at[0], ynear.at[0], y_sems, 0)

    def cut(half, part):
        return pl.ds(half * rows + part * (rows // 2), rows // 2)

    def pair_view(stage, half, d, part):
        along = x if half == 0 else z
        return pair_sums.at[half, (along + d) % 4, pl.ds(part * (rows // 2), rows // 2)]

    def view_of(ref, cols):
        def view(stage, half, d, part):
            if stage == 0:
                there = (d, slice(None)) if half == 0 else (slice(None), d)
            else:
                there = (0, d) if half == 0 else (d, 0)
            return ref.at[(*there, cut(half, part), cols)]

        return view

    early_sums = Reduce(pair_view, rows, {1: rings[0]})
    late_sums = Reduce(view_of(blocks, pl.ds(0, late)), rows, {0: rings[1], 1: rings[2]})
    out_proj = Reduce(view_of(sib, columns[1]), rows, {0: rings[3], 1: rings[4]})
    head_sums = [
        Reduce(view_of(sib, columns[0]), rows, {0: rings[5], 1: rings[6]}),
        Reduce(view_of(sib, columns[2]), rows, {0: rings[7], 1: rings[8]}),
    ]
    loads[3].wait()
    early_sums.begin(1)
    for load in block_loads:
        load.wait()
    late_sums.begin(0)

    def to_core(block, which):
        theirs = pl.ds(pl.multiple_of((2 * block + 1 - c) * 2 * rows, 2 * rows), 2 * rows)
        dz, dx = (block // 4 - z + 4) % 4, (block % 4 - x + 4) % 4
        return remote(
            held.at[theirs, columns[which]],
            sib.at[dz, dx, :, columns[which]],
            core_sems,
            block + 16 * which,
            sibling(),
        )

    def core_sum(block, which):
        to_core(block, which).wait_recv()
        ours = pl.ds(pl.multiple_of((2 * block + c) * 2 * rows, 2 * rows), 2 * rows)
        there = ((block // 4 - z + 4) % 4, (block % 4 - x + 4) % 4, slice(None), columns[which])
        sib[there] = (sib[there].astype(f32) + held[ours, columns[which]].astype(f32)).astype(
            bf16
        )

    loads[2].wait()
    loads[0].wait()
    ins[1].wait()

    mix_order = jnp.concatenate(
        [
            head_mix[pl.ds(block * here + part * sub, sub)]
            for part in range(2)
            for block in range(4)
        ],
        0,
    )

    def mix_back(k, _):
        cols = pl.ds(pl.multiple_of(k * wide, wide), wide)
        value = dot(
            spare[...], held[:, pl.ds(pl.multiple_of(out_start + k * wide, 128), wide)], 1, 0
        ).astype(bf16)
        for part in range(2):
            for block in range(4):
                start = (part * 4 + block) * sub
                grad_mix[pl.ds(block * here + part * sub, sub), cols] = value[start : start + sub]
        return 0

    ins[2].start()
    loads[1].start()
    lax.fori_loop(0, hq // wide, mix_back, 0)
    for load in ins[3:]:
        load.start()

    def out_back(k, _):
        rng = pl.ds(pl.multiple_of(k * 2 * wide, 2 * wide), 2 * wide)
        held[rng, columns[1]] = dot(spare[:, rng], mix_order, 0, 0).astype(bf16)
        for block in range(4):
            to_core(4 * k + block, 1).start()
        return 0

    lax.fori_loop(0, width // (2 * wide), out_back, 0)
    early_sums.combine(1)
    mixed_middle = ring_sum_middle(
        mixed_parts, mixed_started, ymid.at[0], ysent.at[0], yfar.at[0], y_sems, 0
    )

    def out_sum(block, _):
        core_sum(block, 1)
        return 0

    lax.fori_loop(0, 16, out_sum, 0)
    out_proj.begin(0)
    def heads_back(half, sequence):
        mask = causal_mask(sequence, here)
        turn = jnp.concatenate(
            [
                table[pl.ds(pl.multiple_of(half_of_place(2 * sequence + k) * here, here), here)]
                for k in range(2)
            ],
            0,
        )
        rng = pl.ds(pl.multiple_of(sequence * 2 * here, 2 * here), 2 * here)
        for k in range(hq // 256):

            def pair(t):
                return pl.ds(half * group + t * (hq // 2) + k * 128, 128)

            q, key, value = qkv[rng, pair(0)], qkv[rng, pair(1)], qkv[rng, pair(2)]
            mix = grad_mix[rng, pl.ds(half * (hq // 2) + k * 128, 128)]
            results = ([], [], [])
            for head in range(2):
                lanes = slice(head * HEAD_DIM, (head + 1) * HEAD_DIM)
                soft = soft_of(q[:, lanes], key[:, lanes], mask)
                grad_soft = dot(mix[:, lanes], value[:, lanes], 1, 1)
                row_dot = jnp.sum(grad_soft * soft, -1, keepdims=True)
                grad_score = (soft * (grad_soft - row_dot)).astype(bf16)
                results[0].append(dot(grad_score, key[:, lanes], 1, 0) * SCALE)
                results[1].append(dot(grad_score, q[:, lanes], 0, 0) * SCALE)
                results[2].append(dot(soft.astype(bf16), mix[:, lanes], 0, 0))
            for t in range(3):
                both = jnp.concatenate(results[t], 1)
                if t < 2:
                    both = turn_heads(both, turn, -1.0)
                grad_proj[rng, pair(t)] = both.astype(bf16)
        return 0

    def bias_sum(t, k):
        start = k // 2 * group + t * (hq // 2) + k % 2 * 128
        return jnp.sum(grad_proj[:, pl.ds(start, 128)].astype(f32), 0, keepdims=True)

    mean, inverse = stats[0], stats[1]
    tall = 512

    def weights_back(half, k, bias_rows):
        rng = pl.ds(pl.multiple_of(k * tall, tall), tall)
        these = pl.ds(half * group, group)
        part = dot(grad_proj[:, these], held[rng, these], 1, 1)
        unit = (token_rows[:, rng].astype(f32) - mean) * inverse
        normed = (unit * norm_table[0:1, rng] + norm_table[1:2, rng]).astype(bf16)
        held[rng, these] = dot(normed, grad_proj[:, these], 0, 0).astype(bf16)
        if half == 0:
            part_sums[:, rng] = part
        else:
            part = part + part_sums[:, rng]
            spare[:, rng] = part.astype(bf16)
            gain = jnp.sum(part * unit, 0, keepdims=True)
            shift = jnp.sum(part, 0, keepdims=True)
            for tile in range(tall // 128):
                inner = slice(tile * 128, (tile + 1) * 128)
                lanes = pl.ds(pl.multiple_of(k * tall + tile * 128, 128), 128)
                extra = jnp.concatenate(
                    bias_rows
                    + [
                        gain[:, inner],
                        shift[:, inner],
                        second_terms[:, lanes],
                        jnp.zeros((rows - 16, 128), f32),
                    ],
                    0,
                ).astype(bf16)
                for copy in range(128 // rows):
                    start = pl.multiple_of(k * tall + tile * 128 + copy * rows, rows)
                    held[pl.ds(start, rows), pl.ds(3 * hq, EXTRA)] = extra
        for block in range(4):
            to_core(4 * k + block, 2 * half).start()

        @pl.when(k > 0)
        def _():
            for block in range(4):
                core_sum(4 * k - 4 + block, 2 * half)

        return 0

    ins[2].wait()
    lax.fori_loop(0, 2, lambda sequence, _: heads_back(0, sequence), 0)
    late_sums.combine(0)
    loads[1].wait()
    for load in ins[3:]:
        load.wait()
    lax.fori_loop(0, width // tall, lambda k, _: weights_back(0, k, None), 0)
    for block in range(12, 16):
        core_sum(block, 0)
    head_sums[0].begin(0)
    early_sums.settle(1, packed_two.at[:, :, pl.ds(0, early)])
    out_proj.combine(0)
    lax.fori_loop(0, 2, lambda sequence, _: heads_back(1, sequence), 0)
    late_sums.settle(0)
    late_sums.begin(1)
    head_sums[0].combine(0)
    bias_rows = [bias_sum(t, k) for t in range(3) for k in range(hq // 128)]
    lax.fori_loop(0, 2, lambda k, _: weights_back(1, k, bias_rows), 0)
    out_proj.settle(0)
    out_proj.begin(1)
    late_sums.combine(1)
    lax.fori_loop(2, 4, lambda k, _: weights_back(1, k, bias_rows), 0)
    first_started = ring_sum_start(spare, ymid.at[1], ynear.at[1], y_sems, 6)
    for block in range(12, 16):
        core_sum(block, 2)
    head_sums[1].begin(0)
    head_sums[0].settle(0)
    head_sums[0].begin(1)
    late_sums.settle(1, packed_two.at[:, :, pl.ds(early, late)])
    home, away = {"yl": c, "c": yl}, {"yl": c, "c": 1 - yl}
    stay_or_go(packed_two.at[yl], result_two.at[yl], pair_sems, 0, home, local_sem.at[0])
    cross_two = remote(packed_two.at[1 - yl], result_two.at[yl], pair_sems, 1, away)
    cross_two.start()
    out_proj.combine(1)
    head_sums[1].combine(0)
    first_middle = ring_sum_middle(
        spare, first_started, ymid.at[1], ysent.at[1], yfar.at[1], y_sems, 6
    )
    head_sums[0].combine(1)
    half_here = here // 2
    finish = ring_sum_finish(mixed_parts, mixed_started, mixed_middle, yfar.at[0], ynear.at[0])
    for top in range(2):
        rng = pl.ds(top * half_here, half_here)
        mixed[rng] = (first_sum[rng] + finish(top)).astype(bf16)
    saves = [pltpu.make_async_copy(mixed, mixed_out, save_sem.at[0])]
    saves[0].start()
    out_proj.settle(1, packed_one.at[:, :, columns[1]])
    head_sums[1].settle(0)
    head_sums[1].begin(1)
    head_sums[0].settle(1, packed_one.at[:, :, columns[0]])
    head_sums[1].combine(1)
    head_sums[1].settle(1, packed_one.at[:, :, columns[2]])

    stay_or_go(packed_one.at[yl], result_one.at[yl], pair_sems, 2, home, local_sem.at[1])
    cross_one = remote(packed_one.at[1 - yl], result_one.at[yl], pair_sems, 3, away)
    cross_one.start()
    extras = pl.ds(3 * hq, EXTRA)
    norm_moves = [
        remote(
            packed_one.at[core, :, extras],
            norm_back.at[yl],
            pair_sems,
            4 + which,
            {"yl": c, "c": core, "yh": 1 - yh},
        )
        for which, core in enumerate((yl, 1 - yl))
    ]
    for move in norm_moves:
        move.start()
    finish = ring_sum_finish(spare, first_started, first_middle, yfar.at[1], ynear.at[1])
    for top in range(2):
        rng = pl.ds(top * half_here, half_here)
        incoming = finish(top) * norm_table[0:1]
        unit_rows = (token_rows[rng].astype(f32) - stats[0, rng]) * stats[1, rng]
        grad_tokens[rng] = resid[rng] + stats[1, rng] * (
            incoming
            - jnp.mean(incoming, -1, keepdims=True)
            - unit_rows * jnp.mean(incoming * unit_rows, -1, keepdims=True)
        )
    saves.append(pltpu.make_async_copy(grad_tokens, grad_out, save_sem.at[1]))
    saves[1].start()
    for copy in [cross_two, cross_one] + norm_moves:
        copy.wait_recv()
        copy.wait_send()
    stay_or_go_wait(packed_two.at[yl], result_two.at[yl], pair_sems, 0, home, local_sem.at[0])
    stay_or_go_wait(packed_one.at[yl], result_one.at[yl], pair_sems, 2, home, local_sem.at[1])
    for copy in saves:
        copy.wait()
    for copy in mixed_started + mixed_middle + first_started + first_middle:
        copy.wait_send()

    def drain(block, _):
        for which in range(3):
            to_core(block, which).wait_send()
        return 0

    lax.fori_loop(0, 16, drain, 0)
    for sums in [early_sums, late_sums, out_proj] + head_sums:
        sums.close()


def backward(
    one, resid_rows, chip, settled, qkv, head_mix, token_rows, mixed_parts, resid, first_sum,
    stats, table, second_terms, norm_table,
):
    here, width = resid.shape
    hq, early, late = head_mix.shape[1], settled.shape[3], chip.shape[2]
    fq = (early + late) // 3
    rows = width // 64
    piece = rows // 2
    one_wide = one.shape[1]
    full = pl.BlockSpec(memory_space=VMEM)
    anywhere = pl.BlockSpec(memory_space=pl.ANY)
    rings = ring_buffers(1, piece, early)
    for wide in (late, hq, 3 * hq // 2, 3 * hq // 2 + EXTRA):
        rings += ring_buffers(0, piece, wide) + ring_buffers(1, piece, wide)
    return pl.pallas_call(
        backward_kernel,
        out_shape=(
            jax.ShapeDtypeStruct((2, rows, one_wide), bf16),
            jax.ShapeDtypeStruct((2, rows, 3 * fq), bf16),
            jax.ShapeDtypeStruct((2, rows, EXTRA), bf16),
            jax.ShapeDtypeStruct((here, width), f32),
            jax.ShapeDtypeStruct((here, width), bf16),
        ),
        in_specs=[anywhere] * 10 + [full] * 4,
        out_specs=(anywhere,) * 5,
        scratch_shapes=[
            VMEM(qkv.shape, bf16),
            VMEM(head_mix.shape, bf16),
            VMEM(token_rows.shape, bf16),
            VMEM(mixed_parts.shape, bf16),
            VMEM((here, width), f32),
            VMEM((here, width), f32),
            VMEM((here, width), f32),
            VMEM((here, width), bf16),
            VMEM((width, one_wide), bf16),
            VMEM((4 * here, width), bf16),
            VMEM((4 * here, hq), bf16),
            VMEM((4 * here, 3 * hq), bf16),
            VMEM((4 * here, width), f32),
            VMEM((4, 4, 2 * rows, one_wide), bf16),
            VMEM((4, 4, 2 * rows, late), bf16),
            VMEM((2, 4, rows, early), bf16),
        ]
        + rings
        + [VMEM((2, rows, one_wide), bf16), VMEM((2, rows, 3 * fq), bf16)]
        + [VMEM((2, 2, here // 2, width), bf16)] * 4
        + [DMA((4,)), DMA((6,)), DMA((2,)), DMA((16,)), DMA((48,)), DMA((48,))]
        + [DMA((6,)), DMA((6,)), DMA((2,)), DMA((12,)), DMA((12,))],
        compiler_params=pltpu.CompilerParams(
            collective_id=3, has_side_effects=True, vmem_limit_bytes=VMEM_LIMIT
        ),
    )(
        one, resid_rows, chip, settled, qkv, head_mix, token_rows, mixed_parts, resid, first_sum,
        stats, table, second_terms, norm_table,
    )


def finish_kernel(
    one, two, norm_back, tokens_in, mixed_in,
    mixed, grad_tokens, out_norm, out_qkv, out_bias, out_out, out_gate_up, out_down,
):
    z, x = lax.axis_index("z"), lax.axis_index("x")
    yl, c, yh = lax.axis_index("yl"), lax.axis_index("c"), lax.axis_index("yh")
    mine = ((z * 4 + x) * 2 + yl) * 2 + c
    hq, fq = out_out.shape[1] // 2, out_down.shape[1] // 2
    mixed[...] = mixed_in[...]
    grad_tokens[...] = tokens_in[...]
    for q in range(2):
        for group in range(2):
            for t in range(3):
                start, to = (group * 3 + t) * hq // 2, q * hq + group * hq // 2
                out_qkv[t, :, to : to + hq // 2] = one[q, :, start : start + hq // 2].astype(f32)
        out_out[:, q * hq : (q + 1) * hq] = one[q, :, 3 * hq + EXTRA :].astype(f32)
        for t in range(2):
            out_gate_up[t, :, q * fq : (q + 1) * fq] = two[q, :, t * fq : (t + 1) * fq].astype(f32)
        out_down[:, q * fq : (q + 1) * fq] = two[q, :, 2 * fq :].astype(f32)
    extras = [one[q, :, 3 * hq : 3 * hq + EXTRA].astype(f32) for q in range(2)]
    heads = hq // HEAD_DIM
    pairs = 3 * heads // 2
    share = out_norm.shape[1]
    sums = extras[0] + extras[1] + (norm_back[0].astype(f32) + norm_back[1].astype(f32))
    sums = pltpu.roll(sums, EXTRA - (mine % 4 * 2 + yh) * share, 1)
    out_norm[...] = sums[pairs : pairs + 4, :share]
    lane = lax.broadcasted_iota(jnp.int32, extras[0].shape, 1)
    place = lax.broadcasted_iota(jnp.int32, (1, 2 * heads), 1)
    totals = [jnp.zeros((1, 2 * heads), f32) for _ in range(3)]
    for q in range(2):
        for side in range(2):
            value = jnp.sum(
                jnp.where(lane == mine + side * HEAD_DIM, extras[q], 0.0), 1, keepdims=True
            )
            for t in range(3):
                for pair in range(heads // 2):
                    row = t * (heads // 2) + pair
                    head = q * heads + 2 * pair + side
                    totals[t] = totals[t] + jnp.where(place == head, value[row : row + 1], 0.0)
    for t in range(3):
        out_bias[t] = totals[t]


def finish(one, two, norm_back, grad_tokens, mixed, share):
    rows = one.shape[1]
    hq, fq = (one.shape[2] - EXTRA) // 4, two.shape[2] // 3
    full = pl.BlockSpec(memory_space=VMEM)
    return pl.pallas_call(
        finish_kernel,
        out_shape=(
            jax.ShapeDtypeStruct(mixed.shape, bf16),
            jax.ShapeDtypeStruct(grad_tokens.shape, f32),
            jax.ShapeDtypeStruct((4, share), f32),
            jax.ShapeDtypeStruct((3, rows, 2 * hq), f32),
            jax.ShapeDtypeStruct((3, 1, 2 * hq // HEAD_DIM), f32),
            jax.ShapeDtypeStruct((rows, 2 * hq), f32),
            jax.ShapeDtypeStruct((2, rows, 2 * fq), f32),
            jax.ShapeDtypeStruct((rows, 2 * fq), f32),
        ),
        in_specs=[full] * 5,
        out_specs=(full,) * 8,
        compiler_params=pltpu.CompilerParams(vmem_limit_bytes=VMEM_LIMIT),
    )(one, two, norm_back, grad_tokens, mixed)


def shards(
    tokens, cotangent, norm_params, qkv_weight, qkv_bias, out_weight, gate_up_weight, down_weight
):
    table = jnp.asarray(tables())
    (
        one, second, token_rows, cot_rows, qkv, head_mix, first_sum, unit_two, normed_two,
        stats, norm_table, scale_two,
    ) = forward(
        qkv_weight, out_weight.T, gate_up_weight, down_weight.T, qkv_bias.transpose(0, 2, 1),
        norm_params, tokens, cotangent, table,
    )
    grad_resid, resid_rows, mixed_parts, chip, settled, second_terms = feed_forward(
        normed_two, cot_rows, cotangent, unit_two, scale_two, norm_table, second
    )
    one_back, two_back, norm_back, grad_tokens, mixed = backward(
        one, resid_rows, chip, settled, qkv, head_mix, token_rows, mixed_parts, grad_resid,
        first_sum, stats, table, second_terms, norm_table,
    )
    mixed, grad_tokens, out_norm, out_qkv, out_bias, out_out, out_gate_up, out_down = finish(
        one_back, two_back, norm_back, grad_tokens, mixed, norm_params.shape[1]
    )
    return (
        mixed, grad_tokens, out_norm, out_qkv, out_bias.transpose(0, 2, 1), out_out.T,
        out_gate_up, out_down.T,
    )


def solution(mesh):
    grid = Mesh(mesh.devices.reshape(4, 4, 2, 2, 2), GRID)
    placed = (
        P(GRID, None),
        P(GRID, None),
        P(None, GRID),
        P(None, ROWS, "yh"),
        P(None, "yh", ROWS),
        P("yh", ROWS),
        P(None, ROWS, "yh"),
        P("yh", ROWS),
    )
    return jax.shard_map(
        shards,
        mesh=grid,
        in_specs=placed,
        out_specs=(
            P(GRID, None),
            P(GRID, None),
            P(None, GRID),
            P(None, ROWS, "yh"),
            P(None, "yh", ROWS),
            P("yh", ROWS),
            P(None, ROWS, "yh"),
            P("yh", ROWS),
        ),
        check_vma=False,
    )
```
